32 devices in a mesh: ctx: 8 (over y, x, core), wa: 4 (over z).
Axes of the slice: x: 2, y: 2, z: 4, core: 2. Of those that a mesh axis runs over, the one named last changes fastest.
Arguments:
- tokens: bfloat16 [8, 1024, 768], P('wa', 'ctx'), may hold values from -6 to 6
- doc_lengths: int32 [8], replicated, may hold values from 256 to 1024, as said below
- group_deal: int32 [8, 8], replicated, may hold values from 0 to 7, each once within a row
- qkv_weight: bfloat16 [768, 2304], P('wa'), may hold values from -0.21875 to 0.21875
- out_weight: bfloat16 [768, 768], P('wa'), may hold values from -2.5 to 2.5
- up_weight: bfloat16 [768, 3072], P('wa'), may hold values from -0.21875 to 0.21875
- up_bias: bfloat16 [3072], P('wa'), may hold values from -3 to 3
- down_weight: bfloat16 [3072, 768], P('wa'), may hold values from -0.109375 to 0.109375
- proj_weight: bfloat16 [768, 128], P('wa'), may hold values from -0.21875 to 0.21875
- vectors: bfloat16 [8, 768], P(None, 'wa'), may hold values from -2 to 2
- cotangent: bfloat16 [8, 1024, 128], P('wa', 'ctx'), may hold values from -6 to 6
Outputs:
- embeddings: bfloat16 [8, 1024, 128], P('wa', 'ctx')
- tokens_grad: float32 [8, 1024, 768], P('wa', 'ctx')
- qkv_grad: float32 [768, 2304], P('wa')
- out_grad: float32 [768, 768], P('wa')
- up_grad: float32 [768, 3072], P('wa')
- bias_grad: float32 [3072], P('wa')
- down_grad: float32 [3072, 768], P('wa')
- proj_grad: float32 [768, 128], P('wa')
- vectors_grad: float32 [8, 768], P(None, 'wa')
The draws below stay inside these ranges and needn't reach their ends.
Inputs may be any that keep to these rules, and one draw needn't show every extreme that they name: `doc_lengths`: every draw has a sequence with all 1024 slots valid. `group_deal`: each row is a permutation of the block numbers of a sequence.
All inputs are finite; a program needn't handle non-finite values.
Results may differ from the reference program's by a relative error of at most 0.023.
Values may be sent and summed in bfloat16 or wider, within the bound.
No kernel may reach another device: no remote copies, remote signals or barrier semaphores. Data moves between devices by JAX's collectives and lax.ppermute only.
A program may use at most 256 MiB of HBM per device.

```python
import jax
import jax.numpy as jnp
from jax import lax

D = 768
H = 12
HEAD = 64
FF = 3072
E = 128
GROUP = 128
SEQ_LEN = 1024
NSEQ = 8
N_CTX = 8


def draw_doc_lengths(key, part):
    first, second = jax.random.split(key)
    drawn = jax.random.randint(first, (NSEQ,), SEQ_LEN // 4, SEQ_LEN + 1)
    chosen = jax.random.randint(second, (), 0, NSEQ)
    return jnp.where(jnp.arange(NSEQ) == chosen, SEQ_LEN, drawn).astype(jnp.int32)


def draw_vectors(key, part):
    first, second = jax.random.split(key)
    shifts = jnp.clip(0.45 * jax.random.normal(first, (8, D)), -2.0, 2.0)
    gains = jnp.exp(jax.random.uniform(second, (8, D), minval=-0.5, maxval=0.5))
    rows_index = jnp.arange(8)
    is_gain = (rows_index == 3) | (rows_index == 6)
    return jnp.where(is_gain[:, None], gains, shifts).astype(jnp.float32).astype(jnp.bfloat16)


def block_scale(stream_key, dims, cuts, low, high):
    loudness = 1.0
    for dim, parts in cuts:
        steps = jax.random.uniform(jax.random.fold_in(jax.random.fold_in(stream_key, 6), dim), (parts,), jnp.float32, low / len(cuts), high / len(cuts))
        loudness = loudness * jnp.repeat(jnp.exp(steps), dims[dim] // parts).reshape((-1,) + (1,) * (len(dims) - 1 - dim))
    return loudness


def normal_values(own_key, shape, scale, limit, cuts=(), held_as=jnp.bfloat16):
    gain = block_scale(own_key, shape, cuts, -0.22, 0.18) if cuts else 1.0
    values = jax.random.normal(own_key, shape, jnp.float32) * scale * gain
    return jnp.minimum(jnp.maximum(values, -limit), limit).astype(held_as)


def setup_inputs(seed: int = 0) -> dict:
    streams_of = jax.random.split(jax.random.key(seed), 12)
    return {
        "tokens": normal_values(streams_of[0], (NSEQ, SEQ_LEN, D), 1.0, 6.0, ((0, 4), (1, 8))),
        "doc_lengths": draw_doc_lengths(jax.random.fold_in(streams_of[11], 71), 0),
        "group_deal": jax.vmap(lambda own: jax.random.permutation(own, N_CTX))(jax.random.split(streams_of[2], NSEQ)).reshape((NSEQ, N_CTX)).astype(jnp.int32),
        "qkv_weight": normal_values(streams_of[3], (D, 3 * D), D ** -0.5, 0.21875, ((0, 4),)),
        "out_weight": normal_values(streams_of[4], (D, D), (max(1, D * 8 // SEQ_LEN)) ** -0.5, 2.5, ((0, 4),)),
        "up_weight": normal_values(streams_of[5], (D, FF), D ** -0.5, 0.21875, ((0, 4),)),
        "up_bias": normal_values(streams_of[6], (FF,), 0.5, 3.0, ((0, 4),)),
        "down_weight": normal_values(streams_of[7], (FF, D), FF ** -0.5, 0.109375, ((0, 4),)),
        "proj_weight": normal_values(streams_of[8], (D, E), D ** -0.5, 0.21875, ((0, 4),)),
        "vectors": draw_vectors(jax.random.fold_in(streams_of[11], 71), 0),
        "cotangent": normal_values(streams_of[10], (NSEQ, SEQ_LEN, E), 1.0, 6.0, ((0, 4), (1, 8))),
    }


NEG_FILL = -1e+30
NORM_EPS = 1e-06
ROOT_HALF = 0.7071067811865476
HIGHEST_MODE = lax.Precision.HIGHEST

@jax.custom_vjp
def low(v):
    return lax.optimization_barrier(v.astype(jnp.bfloat16)).astype(jnp.float32)

@jax.custom_vjp
def low_back(v):
    return v

def low_keep(v):
    return (low(v), None)

def low_pass(kept, grad):
    return (grad,)

def back_keep(v):
    return (v, None)

def back_low(kept, grad):
    return (low(grad),)
low.defvjp(low_keep, low_pass)
low_back.defvjp(back_keep, back_low)

def layer_norm(inputs, gain_row, shift_row):
    middle = lax.optimization_barrier(jnp.mean(inputs, axis=-1, keepdims=True))
    center = inputs - middle
    spread = lax.optimization_barrier(jnp.mean(center * center, axis=-1, keepdims=True))
    return center * lax.rsqrt(spread + NORM_EPS) * gain_row + shift_row

def matmul(left_side, right_side):
    return jnp.dot(left_side, right_side, precision=HIGHEST_MODE)

def one_sequence(params, hidden, valid_row):
    qkv_weight, out_weight, up_weight, up_bias, down_weight, proj_weight, vectors = params
    seq_span = hidden.shape[0]
    mixed = matmul(hidden, qkv_weight)
    queries = low(low_back((mixed[:, :D] + vectors[0]) * HEAD ** (-0.5)))
    keys_all = low(low_back(mixed[:, D:2 * D]))
    values_all = low(low_back(mixed[:, 2 * D:] + vectors[1]))
    key_heads = keys_all.reshape(seq_span, H, HEAD)
    value_heads = values_all.reshape(seq_span, H, HEAD)
    tile_width = 512 if seq_span % 512 == 0 else seq_span

    def attend(query_tile):
        scores = low_back(jnp.einsum('qhd,khd->hqk', query_tile, key_heads, precision=HIGHEST_MODE))
        scores = jnp.where(valid_row[None, None, :], scores, NEG_FILL)
        highest = lax.optimization_barrier(jnp.max(scores, axis=-1, keepdims=True))
        raised = jnp.exp(scores - highest)
        probs = low(raised / lax.optimization_barrier(jnp.sum(raised, axis=-1, keepdims=True)))
        return jnp.einsum('hqk,khd->qhd', probs, value_heads, precision=HIGHEST_MODE)
    attended = lax.map(jax.checkpoint(attend), queries.reshape(seq_span // tile_width, tile_width, H, HEAD))
    attended = low(low_back(attended.reshape(seq_span, D)))
    first_sum = hidden + (low_back(matmul(attended, out_weight)) + vectors[2])
    normed = layer_norm(first_sum, vectors[3], vectors[4])
    inner_sum = low_back(matmul(low(normed), up_weight)) + up_bias
    active = low(0.5 * inner_sum * (1.0 + lax.erf(inner_sum * ROOT_HALF)))
    second_sum = normed + (low_back(matmul(active, down_weight)) + vectors[5])
    final_sum = layer_norm(second_sum, vectors[6], vectors[7])
    project = low_back(matmul(low(final_sum), proj_weight))
    scaling = lax.rsqrt(lax.optimization_barrier(jnp.sum(project * project, axis=-1, keepdims=True)) + NORM_EPS)
    return project * scaling * valid_row[:, None].astype(project.dtype)

def reference(tokens, doc_lengths, group_deal, qkv_weight, out_weight, up_weight, up_bias, down_weight, proj_weight, vectors, cotangent):
    offsets = jnp.tile(jnp.arange(GROUP, dtype=jnp.int32), N_CTX)
    positions = jnp.repeat(group_deal.astype(jnp.int32), GROUP, axis=1) * GROUP + offsets[None, :]
    valid = positions < doc_lengths.astype(jnp.int32)[:, None]
    floats = tuple((member.astype(jnp.float32) for member in (tokens, qkv_weight, out_weight, up_weight, up_bias, down_weight, proj_weight, vectors)))

    def forward(hidden_all, *params):

        def per_sequence(paired):
            return one_sequence(params, paired[0], paired[1])
        return lax.map(jax.checkpoint(per_sequence), (hidden_all, valid))
    embedded, pullback = jax.vjp(forward, *floats)
    gradients = pullback(cotangent.astype(jnp.float32))
    return (embedded.astype(jnp.bfloat16), gradients[0], gradients[1], gradients[2], gradients[3], gradients[4], gradients[5], gradients[6], gradients[7])
```

```python
from functools import partial

import jax
import jax.numpy as jnp
from jax import lax
from jax.sharding import PartitionSpec as P

H = 12
HEAD = 64


NEG_FILL = -1e30
NORM_EPS = 1e-06
ROOT_HALF = 0.7071067811865476
DENSITY_SCALE = 0.3989422804014327


def norm_rows(inputs, gain_row, shift_row):
    middle = jnp.mean(inputs, axis=-1, keepdims=True)
    center = inputs - middle
    spread = jnp.mean(center * center, axis=-1, keepdims=True)
    scaled = lax.rsqrt(spread + NORM_EPS)
    unit_rows = center * scaled
    return (unit_rows * gain_row + shift_row, unit_rows, scaled)


def norm_back(grad_in, unit_rows, scaled, gain_row):
    gain_grad = jnp.sum(grad_in * unit_rows, axis=(0, 1))
    shift_grad = jnp.sum(grad_in, axis=(0, 1))
    inner_grad = grad_in * gain_row
    centered = inner_grad - jnp.mean(inner_grad, axis=-1, keepdims=True)
    result = scaled * (
        centered - unit_rows * jnp.mean(inner_grad * unit_rows, axis=-1, keepdims=True)
    )
    return (result, gain_grad, shift_grad)


def gelu_both(inner_sum):
    normal_cdf = 0.5 * (1.0 + lax.erf(inner_sum * ROOT_HALF))
    density = jnp.exp(-0.5 * inner_sum * inner_sum) * DENSITY_SCALE
    return (inner_sum * normal_cdf, normal_cdf + inner_sum * density)


def split_tiles(key_rows, value_rows, key_valid):
    key_count = key_rows.shape[0]
    tile_width = 512
    tile_count = key_count // tile_width
    return (
        key_rows.reshape(tile_count, tile_width, H, HEAD),
        value_rows.reshape(tile_count, tile_width, H, HEAD),
        key_valid.reshape(tile_count, tile_width),
    )


def masked_scores(queries, key_tile, mask_tile):
    products = jnp.einsum("qhd,khd->hqk", queries, key_tile, preferred_element_type=jnp.float32)
    return jnp.where(mask_tile[None, None, :], products, NEG_FILL)


def attend_forward(queries, key_rows, value_rows, key_valid):
    key_tiles, value_tiles, mask_tiles = split_tiles(key_rows, value_rows, key_valid)
    row_span = queries.shape[0]

    def stats_step(running, portion):
        highest, summed = running
        key_tile, mask_tile = portion
        scores = masked_scores(queries, key_tile, mask_tile)
        new_peak = jnp.maximum(highest, jnp.max(scores, axis=-1))
        raised = jnp.where(mask_tile[None, None, :], jnp.exp(scores - new_peak[:, :, None]), 0.0)
        return ((new_peak, summed * jnp.exp(highest - new_peak) + jnp.sum(raised, axis=-1)), None)

    start_peak = jnp.full((H, row_span), NEG_FILL, jnp.float32)
    start_sum = jnp.zeros((H, row_span), jnp.float32)
    (highest, summed), _ = lax.scan(stats_step, (start_peak, start_sum), (key_tiles, mask_tiles))
    logsum = highest + jnp.log(summed)

    def value_step(running, portion):
        key_tile, value_tile, mask_tile = portion
        scores = masked_scores(queries, key_tile, mask_tile)
        prob_low = jnp.where(
            mask_tile[None, None, :], jnp.exp(scores - logsum[:, :, None]), 0.0
        ).astype(jnp.bfloat16)
        return (
            running
            + jnp.einsum("hqk,khd->qhd", prob_low, value_tile, preferred_element_type=jnp.float32),
            None,
        )

    attended, _ = lax.scan(
        value_step,
        jnp.zeros((row_span, H, HEAD), jnp.float32),
        (key_tiles, value_tiles, mask_tiles),
    )
    return (attended, logsum)


def attend_backward(
    queries, key_rows, value_rows, key_valid, logsum, delta_rows, grad_heads, with_keys
):
    key_tiles, value_tiles, mask_tiles = split_tiles(key_rows, value_rows, key_valid)

    def back_step(running, portion):
        key_tile, value_tile, mask_tile = portion
        scores = masked_scores(queries, key_tile, mask_tile)
        prob_rows = jnp.where(mask_tile[None, None, :], jnp.exp(scores - logsum[:, :, None]), 0.0)
        prob_grad = jnp.einsum(
            "qhd,khd->hqk", grad_heads, value_tile, preferred_element_type=jnp.float32
        )
        score_low = (prob_rows * (prob_grad - delta_rows[:, :, None])).astype(jnp.bfloat16)
        running = running + jnp.einsum(
            "hqk,khd->qhd", score_low, key_tile, preferred_element_type=jnp.float32
        )
        value_part = jnp.einsum(
            "hqk,qhd->khd",
            prob_rows.astype(jnp.bfloat16),
            grad_heads,
            preferred_element_type=jnp.float32,
        )
        key_part = jnp.einsum(
            "hqk,qhd->khd", score_low, queries, preferred_element_type=jnp.float32
        )
        return (running, (key_part, value_part))

    start_grad = jnp.zeros(queries.shape, jnp.float32)
    query_grad, pieces = lax.scan(back_step, start_grad, (key_tiles, value_tiles, mask_tiles))
    key_count = key_rows.shape[0]
    return (
        query_grad,
        pieces[0].reshape(key_count, H * HEAD),
        pieces[1].reshape(key_count, H * HEAD),
    )


def general_body(
    tokens,
    doc_lengths,
    group_deal,
    qkv_weight,
    out_weight,
    up_weight,
    up_bias,
    down_weight,
    proj_weight,
    vectors,
    cotangent,
):
    gathered = (
        lax.all_gather(qkv_weight, "wa", axis=0, tiled=True),
        lax.all_gather(out_weight, "wa", axis=0, tiled=True),
        lax.all_gather(up_weight, "wa", axis=0, tiled=True),
        lax.all_gather(up_bias, "wa", axis=0, tiled=True),
        lax.all_gather(down_weight, "wa", axis=0, tiled=True),
        lax.all_gather(proj_weight, "wa", axis=0, tiled=True),
        lax.all_gather(vectors, "wa", axis=1, tiled=True),
    )
    qkv_full, out_full, up_full, bias_full, down_full, proj_full, vector_full = gathered
    seq_count, group_rows, model_width = tokens.shape
    ctx_count = lax.axis_size("ctx")
    seq_start = lax.axis_index("wa") * seq_count
    my_lengths = lax.dynamic_slice_in_dim(doc_lengths, seq_start, seq_count, 0)
    my_deal = lax.dynamic_slice_in_dim(group_deal, seq_start, seq_count, 0)
    offsets = jnp.tile(jnp.arange(group_rows, dtype=jnp.int32), ctx_count)
    positions = jnp.repeat(my_deal, group_rows, axis=1) * group_rows + offsets[None, :]
    key_valid = positions < my_lengths[:, None]
    query_valid = lax.dynamic_slice_in_dim(
        key_valid, lax.axis_index("ctx") * group_rows, group_rows, 1
    )
    row_mask = query_valid.astype(jnp.float32)[:, :, None]
    query_scale = HEAD ** (-0.5)
    mixed_rows = jnp.einsum("scd,de->sce", tokens, qkv_full, preferred_element_type=jnp.float32)
    queries = ((mixed_rows[:, :, :model_width] + vector_full[0]) * query_scale).astype(jnp.bfloat16)
    key_rows = mixed_rows[:, :, model_width : 2 * model_width].astype(jnp.bfloat16)
    value_rows = (mixed_rows[:, :, 2 * model_width :] + vector_full[1]).astype(jnp.bfloat16)
    all_keys, all_values = (
        lax.all_gather(key_rows, "ctx", axis=1, tiled=True),
        lax.all_gather(value_rows, "ctx", axis=1, tiled=True),
    )
    query_heads = queries.reshape(seq_count, group_rows, H, HEAD)
    attended, logsum = jax.vmap(attend_forward)(query_heads, all_keys, all_values, key_valid)
    attended_low = attended.reshape(seq_count, group_rows, model_width).astype(jnp.bfloat16)
    first_sum = tokens.astype(jnp.float32) + (
        jnp.einsum("scd,de->sce", attended_low, out_full, preferred_element_type=jnp.float32)
        + vector_full[2]
    )
    normed, unit_one, scale_one = norm_rows(first_sum, vector_full[3], vector_full[4])
    normed_low = normed.astype(jnp.bfloat16)
    inner_sum = (
        jnp.einsum("scd,df->scf", normed_low, up_full, preferred_element_type=jnp.float32)
        + bias_full
    )
    active, gelu_slope = gelu_both(inner_sum)
    active_low = active.astype(jnp.bfloat16)
    second_sum = normed + (
        jnp.einsum("scf,fd->scd", active_low, down_full, preferred_element_type=jnp.float32)
        + vector_full[5]
    )
    final_sum, unit_two, scale_two = norm_rows(second_sum, vector_full[6], vector_full[7])
    final_low = final_sum.astype(jnp.bfloat16)
    project = jnp.einsum("scd,de->sce", final_low, proj_full, preferred_element_type=jnp.float32)
    inverse = lax.rsqrt(jnp.sum(project * project, axis=-1, keepdims=True) + NORM_EPS)
    direction = project * inverse
    embeddings = (direction * row_mask).astype(jnp.bfloat16)
    upstream = cotangent.astype(jnp.float32) * row_mask
    project_grad = (
        inverse * (upstream - direction * jnp.sum(upstream * direction, axis=-1, keepdims=True))
    ).astype(jnp.bfloat16)
    proj_grad = jnp.einsum(
        "scd,sce->de", final_low, project_grad, preferred_element_type=jnp.float32
    )
    final_grad = jnp.einsum(
        "sce,de->scd", project_grad, proj_full, preferred_element_type=jnp.float32
    )
    second_grad, gain_two, shift_two = norm_back(final_grad, unit_two, scale_two, vector_full[6])
    down_low = second_grad.astype(jnp.bfloat16)
    down_grad = jnp.einsum("scf,scd->fd", active_low, down_low, preferred_element_type=jnp.float32)
    inner_grad = (
        jnp.einsum("scd,fd->scf", down_low, down_full, preferred_element_type=jnp.float32)
        * gelu_slope
    )
    bias_grad = jnp.sum(inner_grad, axis=(0, 1))
    inner_low = inner_grad.astype(jnp.bfloat16)
    up_grad = jnp.einsum("scd,scf->df", normed_low, inner_low, preferred_element_type=jnp.float32)
    normed_grad = second_grad + jnp.einsum(
        "scf,df->scd", inner_low, up_full, preferred_element_type=jnp.float32
    )
    first_grad, gain_one, shift_one = norm_back(normed_grad, unit_one, scale_one, vector_full[3])
    first_low = first_grad.astype(jnp.bfloat16)
    out_grad = jnp.einsum(
        "scd,sce->de", attended_low, first_low, preferred_element_type=jnp.float32
    )
    attended_grad = jnp.einsum(
        "sce,de->scd", first_low, out_full, preferred_element_type=jnp.float32
    ).astype(jnp.bfloat16)
    grad_heads = attended_grad.reshape(seq_count, group_rows, H, HEAD)
    delta_rows = jnp.sum(grad_heads.astype(jnp.float32) * attended, axis=-1)
    delta_heads = jnp.swapaxes(delta_rows, 1, 2)
    query_grad, key_terms, value_terms = jax.vmap(partial(attend_backward, with_keys=True))(
        query_heads, all_keys, all_values, key_valid, logsum, delta_heads, grad_heads
    )
    key_grad, value_grad = (
        lax.psum_scatter(
            key_terms.astype(jnp.bfloat16), "ctx", scatter_dimension=1, tiled=True
        ).astype(jnp.float32),
        lax.psum_scatter(
            value_terms.astype(jnp.bfloat16), "ctx", scatter_dimension=1, tiled=True
        ).astype(jnp.float32),
    )
    query_part = (
        query_grad.reshape(seq_count, group_rows, model_width).astype(jnp.bfloat16) * query_scale
    )
    value_part = value_grad.astype(jnp.bfloat16)
    mixed_grad = jnp.concatenate([query_part, key_grad.astype(jnp.bfloat16), value_part], axis=-1)
    qkv_grad = jnp.einsum("scd,sce->de", tokens, mixed_grad, preferred_element_type=jnp.float32)
    tokens_grad = first_grad + jnp.einsum(
        "sce,de->scd", mixed_grad, qkv_full, preferred_element_type=jnp.float32
    )
    vectors_grad = jnp.stack(
        [
            jnp.sum(query_part.astype(jnp.float32), axis=(0, 1)),
            jnp.sum(value_part.astype(jnp.float32), axis=(0, 1)),
            jnp.sum(first_grad, axis=(0, 1)),
            gain_one,
            shift_one,
            jnp.sum(second_grad, axis=(0, 1)),
            gain_two,
            shift_two,
        ],
        axis=0,
    )
    owned = (
        lax.psum_scatter(
            qkv_grad.astype(jnp.bfloat16), "wa", scatter_dimension=0, tiled=True
        ).astype(jnp.float32),
        lax.psum_scatter(
            out_grad.astype(jnp.bfloat16), "wa", scatter_dimension=0, tiled=True
        ).astype(jnp.float32),
        lax.psum_scatter(
            up_grad.astype(jnp.bfloat16), "wa", scatter_dimension=0, tiled=True
        ).astype(jnp.float32),
        lax.psum_scatter(
            bias_grad.astype(jnp.bfloat16), "wa", scatter_dimension=0, tiled=True
        ).astype(jnp.float32),
        lax.psum_scatter(
            down_grad.astype(jnp.bfloat16), "wa", scatter_dimension=0, tiled=True
        ).astype(jnp.float32),
        lax.psum_scatter(
            proj_grad.astype(jnp.bfloat16), "wa", scatter_dimension=0, tiled=True
        ).astype(jnp.float32),
        lax.psum_scatter(
            vectors_grad.astype(jnp.bfloat16), "wa", scatter_dimension=1, tiled=True
        ).astype(jnp.float32),
    )
    summed = (
        lax.psum(owned[0].astype(jnp.bfloat16), "ctx").astype(jnp.float32),
        lax.psum(owned[1].astype(jnp.bfloat16), "ctx").astype(jnp.float32),
        lax.psum(owned[2].astype(jnp.bfloat16), "ctx").astype(jnp.float32),
        lax.psum(owned[3].astype(jnp.bfloat16), "ctx").astype(jnp.float32),
        lax.psum(owned[4].astype(jnp.bfloat16), "ctx").astype(jnp.float32),
        lax.psum(owned[5].astype(jnp.bfloat16), "ctx").astype(jnp.float32),
        lax.psum(owned[6].astype(jnp.bfloat16), "ctx").astype(jnp.float32),
    )
    return (
        embeddings,
        tokens_grad,
        summed[0],
        summed[1],
        summed[2],
        summed[3],
        summed[4],
        summed[5],
        summed[6],
    )


PLANE = 8
LINE = 4
ORDER = (0, 4, 2, 6, 1, 5, 3, 7)
F32 = jnp.float32
BF16 = jnp.bfloat16


def plane_swap(array, bits):
    return lax.ppermute(array, "ctx", [(i, i ^ bits) for i in range(PLANE)])


def line_turn(array, step):
    return lax.ppermute(array, "wa", [(i, (i + step) % LINE) for i in range(LINE)])


def line_turns(array):
    return [line_turn(array, step) for step in range(1, LINE)]


def relay(from_x, from_y, core):
    passed = jnp.where(core == 0, from_y, from_x)
    pairs = [(i, i ^ 2 if i % 2 == 0 else i ^ 4) for i in range(PLANE)]
    return lax.ppermute(passed, "ctx", pairs)


def pick(array, index):
    return lax.dynamic_index_in_dim(array, index, 0, keepdims=False)


def dot(left, right, dims):
    return lax.dot_general(left, right, (dims, ((), ())), preferred_element_type=F32)


NN = ((1,), (0,))
NT = ((1,), (1,))
TN = ((0,), (0,))


def norm_forward(rows):
    middle = jnp.mean(rows, axis=-1, keepdims=True)
    center = rows - middle
    scaled = lax.rsqrt(jnp.mean(center * center, axis=-1, keepdims=True) + NORM_EPS)
    return center * scaled, scaled


def norm_reverse(grad, unit, scaled, gain):
    inner = grad * gain
    return scaled * (
        inner
        - jnp.mean(inner, axis=-1, keepdims=True)
        - unit * jnp.mean(inner * unit, axis=-1, keepdims=True)
    )


def plane_body(
    tokens,
    doc_lengths,
    group_deal,
    qkv_weight,
    out_weight,
    up_weight,
    up_bias,
    down_weight,
    proj_weight,
    vectors,
    cotangent,
):
    me = lax.axis_index("ctx")
    line = lax.axis_index("wa")
    y, core, group = me // 4, me % 2, me % 4
    seq_count, span, width = tokens.shape
    shard = width // LINE
    inner_shard = up_weight.shape[1] // LINE
    piece = inner_shard // PLANE
    half = shard // 2
    wide = H * HEAD // 4

    mine, other = pick(tokens, y), pick(tokens, 1 - y)
    got_y = plane_swap(other, 4)
    got_x = plane_swap(mine, 2)
    got_d = plane_swap(other, 6)
    near = jnp.stack([mine, got_y, got_x, got_d])
    far = plane_swap(near, 1)
    slots = jnp.concatenate([near, far]).reshape(PLANE * span, width)

    own_cols = jnp.concatenate(
        [
            lax.dynamic_slice(qkv_weight, (0, part * width + group * wide), (shard, wide))
            for part in range(3)
        ]
        + [vectors.T, up_bias.reshape(LINE, shard).T, jnp.zeros((shard, 64 - 12), BF16)],
        axis=1,
    )
    half_rows = lax.dynamic_slice(own_cols, (y * half, 0), (half, own_cols.shape[1]))
    line_halves = jnp.stack(line_turns(half_rows))
    other_halves = plane_swap(line_halves, 4)
    low_half = jnp.where(y == 0, line_halves, other_halves)
    high_half = jnp.where(y == 0, other_halves, line_halves)
    cols_by_turn = jnp.concatenate(
        [own_cols[None], jnp.concatenate([low_half, high_half], axis=1)]
    )

    def by_line(turned):
        return jnp.concatenate([pick(turned, (line - a) % LINE)[None] for a in range(LINE)])

    cols = by_line(cols_by_turn).reshape(width, -1)
    qkv_cols = cols[:, : 3 * wide]
    small = cols[:, 3 * wide :]
    vector_full = small[:, :8].T.astype(F32)
    bias_full = small[:, 8:12].reshape(LINE, shard, 4).transpose(0, 2, 1).reshape(-1)
    bias_parts = bias_full.reshape(LINE, PLANE, piece).transpose(1, 0, 2).reshape(PLANE, -1)

    up_own = jnp.concatenate(
        [
            lax.dynamic_slice(up_weight, (0, s * inner_shard + me * piece), (shard, piece))
            for s in range(LINE)
        ],
        axis=1,
    )
    eighth = shard // PLANE
    out_own = lax.dynamic_slice(out_weight, (me * eighth, 0), (eighth, width))
    first_own = jnp.concatenate([up_own, out_own[:, : width // 2], out_own[:, width // 2 :]])
    down_own = lax.dynamic_slice(down_weight, (me * piece, 0), (piece, width))
    proj_own = lax.dynamic_slice(proj_weight, (me * eighth, 0), (eighth, 128))
    second_own = jnp.concatenate(
        [down_own, proj_own.reshape(-1, width), jnp.zeros((12, width), BF16)]
    )

    def over_plane(turns):
        stacked = jnp.stack(turns)
        from_x = plane_swap(stacked, 2)
        from_y = plane_swap(stacked, 4)
        from_d = relay(from_x, from_y, core)
        close = [stacked, from_y, from_x, from_d]
        return close + [plane_swap(part, 1) for part in close]

    first_turns = line_turns(first_own)
    second_turns = line_turns(second_own)
    first_parts = over_plane(first_turns)
    second_parts = over_plane(second_turns)

    up_all = (
        up_weight.reshape(shard, LINE, PLANE, piece).transpose(2, 0, 1, 3).reshape(PLANE, shard, -1)
    )
    down_all = down_weight.reshape(PLANE, piece, width)
    ups, downs = [], []
    for place, bits in enumerate(ORDER):
        ups.append(
            by_line(
                jnp.concatenate([pick(up_all, me ^ bits)[None], first_parts[place][:, :shard]])
            ).reshape(width, -1)
        )
        downs.append(
            by_line(
                jnp.concatenate([pick(down_all, me ^ bits)[None], second_parts[place][:, :piece]])
            ).reshape(-1, width)
        )
    out_rel = jnp.stack(
        [
            jnp.concatenate([p[:, shard : shard + eighth], p[:, shard + eighth :]], axis=2)
            for p in first_parts
        ]
    )
    proj_rel = jnp.stack([p[:, piece : piece + 4].reshape(3, eighth, 128) for p in second_parts])

    def whole(own, rel):
        ordered = jnp.stack([pick(rel, jnp.asarray(inverse_order)[me ^ b]) for b in range(PLANE)], 1)
        turned = jnp.concatenate([own[None], ordered.reshape(3, own.shape[0], -1)])
        return by_line(turned).reshape(LINE * own.shape[0], -1)

    inverse_order = [ORDER.index(b) for b in range(PLANE)]
    out_full = whole(out_weight, out_rel)
    proj_full = whole(proj_weight, proj_rel)

    seq = line * seq_count + y
    length = pick(doc_lengths, seq)
    deal_row = pick(group_deal, seq)
    blocks = jnp.stack([pick(deal_row, me ^ bits) for bits in ORDER])
    valid = (blocks[:, None] * span + jnp.arange(span, dtype=jnp.int32)[None, :]) < length
    valid = valid.reshape(1, PLANE * span)

    mixed = dot(slots, qkv_cols, NN)
    scale = HEAD ** (-0.5)
    q_bias = lax.dynamic_slice(vector_full, (0, group * wide), (1, wide))
    v_bias = lax.dynamic_slice(vector_full, (1, group * wide), (1, wide))
    queries = ((mixed[:, :wide] + q_bias) * scale).astype(BF16)
    keys = mixed[:, wide : 2 * wide].astype(BF16)
    values = (mixed[:, 2 * wide :] + v_bias).astype(BF16)
    heads = wide // HEAD
    attended, probs_kept = [], []
    for h in range(heads):
        cut = slice(h * HEAD, (h + 1) * HEAD)
        scores = jnp.where(valid, dot(queries[:, cut], keys[:, cut], NT), NEG_FILL)
        raised = jnp.exp(scores - jnp.max(scores, axis=-1, keepdims=True))
        probs = raised / jnp.sum(raised, axis=-1, keepdims=True)
        probs_kept.append(probs)
        attended.append(dot(probs.astype(BF16), values[:, cut], NN))
    attended_f = jnp.concatenate(attended, axis=1)
    sent = attended_f.astype(BF16).reshape(4, 2 * span, wide)
    near_bits = (0, 2, 1, 3)
    attended_low = [sent[0]] + [plane_swap(sent[i], near_bits[i]) for i in (1, 2, 3)]

    own_slots = slots[: 2 * span].astype(F32)
    first_sum = own_slots + vector_full[2]
    out_groups = out_full.reshape(4, wide, width)
    for i, bits in enumerate(near_bits):
        first_sum = first_sum + dot(attended_low[i], pick(out_groups, group ^ bits), NN)
    unit_one, scale_one = norm_forward(first_sum)
    normed = unit_one * vector_full[3] + vector_full[4]
    normed_low = normed.astype(BF16)

    def gather_plane(array):
        from_y = plane_swap(array, 4)
        from_x = plane_swap(array, 2)
        from_d = plane_swap(array, 6)
        close = jnp.concatenate([array, from_y, from_x, from_d])
        return jnp.concatenate([close, plane_swap(close, 1)])

    normed_plane = gather_plane(normed_low)

    inner_sums, actives = [], []
    second_sum = normed + vector_full[5]
    for place, bits in enumerate(ORDER):
        inner = dot(normed_low, ups[place], NN) + pick(bias_parts, me ^ bits).astype(F32)
        active, slope = gelu_both(inner)
        inner_sums.append(slope)
        second_sum = second_sum + dot(active.astype(BF16), downs[place], NN)
    unit_two, scale_two = norm_forward(second_sum)
    final_low = (unit_two * vector_full[6] + vector_full[7]).astype(BF16)
    project = dot(final_low, proj_full, NN)
    inverse = lax.rsqrt(jnp.sum(project * project, axis=-1, keepdims=True) + NORM_EPS)
    direction = project * inverse
    cot_mine, cot_other = pick(cotangent, y), pick(cotangent, 1 - y)
    own_cot = jnp.concatenate([cot_mine, plane_swap(cot_other, 4)]).astype(F32)
    row_mask = valid[0, : 2 * span].astype(F32)[:, None]
    embedded = (direction * row_mask).astype(BF16)
    upstream = own_cot * row_mask
    project_grad = (
        inverse * (upstream - direction * jnp.sum(upstream * direction, axis=-1, keepdims=True))
    ).astype(BF16)
    embed_other = plane_swap(embedded[span:], 4)
    embeddings = jnp.where(
        y == 0,
        jnp.stack([embedded[:span], embed_other]),
        jnp.stack([embed_other, embedded[:span]]),
    )
    proj_part = dot(final_low, project_grad, TN)
    final_grad = dot(project_grad, proj_full, NT)
    second_grad = norm_reverse(final_grad, unit_two, scale_two, vector_full[6])
    down_low = second_grad.astype(BF16)
    down_plane = gather_plane(down_low)

    normed_grad = second_grad
    bias_part = jnp.zeros((PLANE, 4 * piece), F32)
    for place, bits in enumerate(ORDER):
        inner_grad = dot(down_low, downs[place], NT) * inner_sums[place]
        bias_part = lax.dynamic_update_slice(
            bias_part, jnp.sum(inner_grad, axis=0, keepdims=True), (me ^ bits, 0)
        )
        normed_grad = normed_grad + dot(inner_grad.astype(BF16), ups[place], NT)
    first_grad = norm_reverse(normed_grad, unit_one, scale_one, vector_full[3])
    first_low = first_grad.astype(BF16)
    attended_all = jnp.zeros((4, 2 * span, wide), BF16)
    for i, bits in enumerate(near_bits):
        attended_all = lax.dynamic_update_slice(
            attended_all, attended_low[i][None], (group ^ bits, 0, 0)
        )
    out_part = jnp.concatenate([dot(attended_all[g], first_low, TN) for g in range(4)])
    grad_sent = [
        dot(first_low, pick(out_groups, group ^ bits), NT).astype(BF16) for bits in near_bits
    ]
    attended_grad = jnp.concatenate(
        [grad_sent[0]] + [plane_swap(grad_sent[i], near_bits[i]) for i in (1, 2, 3)]
    )

    bias_rows = bias_part.reshape(PLANE, LINE, piece).transpose(1, 0, 2).reshape(LINE, 4, shard)
    bias_rows = bias_rows.transpose(0, 2, 1).reshape(width, 4)
    sums = jnp.stack(
        [
            jnp.sum(first_grad, axis=0),
            jnp.sum(normed_grad * unit_one, axis=0),
            jnp.sum(normed_grad, axis=0),
            jnp.sum(second_grad, axis=0),
            jnp.sum(final_grad * unit_two, axis=0),
            jnp.sum(final_grad, axis=0),
        ],
        axis=1,
    )
    rest = jnp.concatenate(
        [out_part, proj_part, sums, bias_rows, jnp.zeros((width, 128 - 10), F32)], axis=1
    ).astype(BF16)
    rest = lax.psum_scatter(rest, "wa", scatter_dimension=0, tiled=True)
    rest = lax.psum(rest, "ctx").astype(F32)
    out_grad = rest[:, :width]
    proj_grad = rest[:, width : width + 128]
    bias_grad = rest[:, width + 134 : width + 138].T.reshape(-1)
    late_rows = rest[:, width + 128 : width + 134].T

    inner = dot(normed_plane, ups[0], NN) + pick(bias_parts, me).astype(F32)
    active, slope = gelu_both(inner)
    inner_low = (dot(down_plane, downs[0], NT) * slope).astype(BF16)
    up_part = dot(normed_plane, inner_low, TN).astype(BF16).reshape(LINE, shard, -1)
    down_part = dot(active.astype(BF16), down_plane, TN).astype(BF16)
    down_part = down_part.reshape(LINE, piece, width)

    def sum_line(parts):
        total = pick(parts, line).astype(F32)
        for step in range(1, LINE):
            total = total + line_turn(pick(parts, (line + step) % LINE), step).astype(F32)
        return total.astype(BF16)

    def share_plane(array):
        from_x = plane_swap(array, 2)
        from_y = plane_swap(array, 4)
        from_d = plane_swap(array, 6)
        close = jnp.stack([array, from_y, from_x, from_d])
        both = jnp.concatenate([close, plane_swap(close, 1)])
        return jnp.stack([pick(both, jnp.asarray(inverse_order)[me ^ b]) for b in range(PLANE)])

    up_mine = share_plane(sum_line(up_part))
    down_mine = share_plane(sum_line(down_part))
    up_grad = (
        up_mine.reshape(PLANE, shard, LINE, piece)
        .transpose(1, 2, 0, 3)
        .reshape(shard, -1)
        .astype(F32)
    )
    down_grad = down_mine.reshape(-1, width).astype(F32)

    query_parts, key_parts, value_parts = [], [], []
    for h in range(heads):
        cut = slice(h * HEAD, (h + 1) * HEAD)
        probs = probs_kept[h]
        grad_h = attended_grad[:, cut]
        prob_grad = dot(grad_h, values[:, cut], NT)
        delta = jnp.sum(grad_h.astype(F32) * attended[h], axis=-1, keepdims=True)
        score_low = (probs * (prob_grad - delta)).astype(BF16)
        query_parts.append(dot(score_low, keys[:, cut], NN).astype(BF16) * BF16(scale))
        key_parts.append(dot(score_low, queries[:, cut], TN).astype(BF16))
        value_parts.append(dot(probs.astype(BF16), grad_h, TN).astype(BF16))
    mixed_grad = jnp.concatenate(query_parts + key_parts + value_parts, axis=1)
    qkv_part = dot(slots, mixed_grad, TN).astype(BF16).reshape(LINE, 2, half, 3 * wide)
    column_sums = jnp.sum(mixed_grad.astype(F32), axis=0).astype(BF16)
    extra = jnp.concatenate(
        [column_sums[None], jnp.zeros((15, 3 * wide), BF16)]
    )
    extra = jnp.broadcast_to(extra[None], (LINE, 16, 3 * wide))
    half_mine = jnp.concatenate([jnp.where(y == 0, qkv_part[:, 0], qkv_part[:, 1]), extra], axis=1)
    half_other = jnp.concatenate([jnp.where(y == 0, qkv_part[:, 1], qkv_part[:, 0]), extra], axis=1)
    half_sum = (half_mine.astype(F32) + plane_swap(half_other, 4).astype(F32)).astype(BF16)
    qkv_mine = share_plane(sum_line(half_sum))
    qkv_grad = (
        qkv_mine[:, :half]
        .reshape(2, 4, half, 3, wide)
        .transpose(0, 2, 3, 1, 4)
        .reshape(shard, 3 * width)
        .astype(F32)
    )
    group_sums = pick(qkv_mine[:4, half], line).astype(F32)
    early_rows = jnp.stack([group_sums[:wide], group_sums[2 * wide :]])
    vectors_grad = jnp.concatenate([early_rows, late_rows])

    token_part = dot(mixed_grad, qkv_cols, NT).reshape(PLANE, span, width)
    near_sum = token_part[:4] + plane_swap(token_part[4:].astype(BF16), 1).astype(F32)
    kept = near_sum[0] + first_grad[:span]
    passed = near_sum[1] + first_grad[span:]
    for_mine = kept + plane_swap(near_sum[2].astype(BF16), 2).astype(F32)
    for_other = plane_swap(passed.astype(BF16), 4).astype(F32) + plane_swap(
        near_sum[3].astype(BF16), 6
    ).astype(F32)
    tokens_grad = jnp.where(
        y == 0, jnp.stack([for_mine, for_other]), jnp.stack([for_other, for_mine])
    )
    return (
        embeddings,
        tokens_grad,
        qkv_grad,
        out_grad,
        up_grad,
        bias_grad,
        down_grad,
        proj_grad,
        vectors_grad,
    )


def body(*arrays):
    sequences, span, width = arrays[0].shape
    fits = (
        lax.axis_size("ctx") == PLANE
        and lax.axis_size("wa") == LINE
        and sequences == 2
        and span == 128
        and width == H * HEAD
    )
    return (plane_body if fits else general_body)(*arrays)


def solution(mesh):
    in_specs = (
        P("wa", "ctx", None),
        P(),
        P(),
        P("wa", None),
        P("wa", None),
        P("wa", None),
        P("wa"),
        P("wa", None),
        P("wa", None),
        P(None, "wa"),
        P("wa", "ctx", None),
    )
    out_specs = (
        P("wa", "ctx", None),
        P("wa", "ctx", None),
        P("wa", None),
        P("wa", None),
        P("wa", None),
        P("wa"),
        P("wa", None),
        P("wa", None),
        P(None, "wa"),
    )
    return jax.shard_map(body, mesh=mesh, in_specs=in_specs, out_specs=out_specs, check_vma=False)
```

```python
from functools import partial

import jax
import jax.numpy as jnp
from jax import lax
from jax.experimental import pallas as pl
from jax.experimental.pallas import tpu as pltpu
from jax.sharding import PartitionSpec as P

H = 12
HEAD = 64


NEG_FILL = -1e30
NORM_EPS = 1e-06
ROOT_HALF = 0.7071067811865476
DENSITY_SCALE = 0.3989422804014327


def norm_rows(inputs, gain_row, shift_row):
    middle = jnp.mean(inputs, axis=-1, keepdims=True)
    center = inputs - middle
    spread = jnp.mean(center * center, axis=-1, keepdims=True)
    scaled = lax.rsqrt(spread + NORM_EPS)
    unit_rows = center * scaled
    return (unit_rows * gain_row + shift_row, unit_rows, scaled)


def norm_back(grad_in, unit_rows, scaled, gain_row):
    gain_grad = jnp.sum(grad_in * unit_rows, axis=(0, 1))
    shift_grad = jnp.sum(grad_in, axis=(0, 1))
    inner_grad = grad_in * gain_row
    centered = inner_grad - jnp.mean(inner_grad, axis=-1, keepdims=True)
    result = scaled * (
        centered - unit_rows * jnp.mean(inner_grad * unit_rows, axis=-1, keepdims=True)
    )
    return (result, gain_grad, shift_grad)


def gelu_both(inner_sum):
    normal_cdf = 0.5 * (1.0 + lax.erf(inner_sum * ROOT_HALF))
    density = jnp.exp(-0.5 * inner_sum * inner_sum) * DENSITY_SCALE
    return (inner_sum * normal_cdf, normal_cdf + inner_sum * density)


def split_tiles(key_rows, value_rows, key_valid):
    key_count = key_rows.shape[0]
    tile_width = 512
    tile_count = key_count // tile_width
    return (
        key_rows.reshape(tile_count, tile_width, H, HEAD),
        value_rows.reshape(tile_count, tile_width, H, HEAD),
        key_valid.reshape(tile_count, tile_width),
    )


def masked_scores(queries, key_tile, mask_tile):
    products = jnp.einsum("qhd,khd->hqk", queries, key_tile, preferred_element_type=jnp.float32)
    return jnp.where(mask_tile[None, None, :], products, NEG_FILL)


def attend_forward(queries, key_rows, value_rows, key_valid):
    key_tiles, value_tiles, mask_tiles = split_tiles(key_rows, value_rows, key_valid)
    row_span = queries.shape[0]

    def stats_step(running, portion):
        highest, summed = running
        key_tile, mask_tile = portion
        scores = masked_scores(queries, key_tile, mask_tile)
        new_peak = jnp.maximum(highest, jnp.max(scores, axis=-1))
        raised = jnp.where(mask_tile[None, None, :], jnp.exp(scores - new_peak[:, :, None]), 0.0)
        return ((new_peak, summed * jnp.exp(highest - new_peak) + jnp.sum(raised, axis=-1)), None)

    start_peak = jnp.full((H, row_span), NEG_FILL, jnp.float32)
    start_sum = jnp.zeros((H, row_span), jnp.float32)
    (highest, summed), _ = lax.scan(stats_step, (start_peak, start_sum), (key_tiles, mask_tiles))
    logsum = highest + jnp.log(summed)

    def value_step(running, portion):
        key_tile, value_tile, mask_tile = portion
        scores = masked_scores(queries, key_tile, mask_tile)
        prob_low = jnp.where(
            mask_tile[None, None, :], jnp.exp(scores - logsum[:, :, None]), 0.0
        ).astype(jnp.bfloat16)
        return (
            running
            + jnp.einsum("hqk,khd->qhd", prob_low, value_tile, preferred_element_type=jnp.float32),
            None,
        )

    attended, _ = lax.scan(
        value_step,
        jnp.zeros((row_span, H, HEAD), jnp.float32),
        (key_tiles, value_tiles, mask_tiles),
    )
    return (attended, logsum)


def attend_backward(
    queries, key_rows, value_rows, key_valid, logsum, delta_rows, grad_heads, with_keys
):
    key_tiles, value_tiles, mask_tiles = split_tiles(key_rows, value_rows, key_valid)

    def back_step(running, portion):
        key_tile, value_tile, mask_tile = portion
        scores = masked_scores(queries, key_tile, mask_tile)
        prob_rows = jnp.where(mask_tile[None, None, :], jnp.exp(scores - logsum[:, :, None]), 0.0)
        prob_grad = jnp.einsum(
            "qhd,khd->hqk", grad_heads, value_tile, preferred_element_type=jnp.float32
        )
        score_low = (prob_rows * (prob_grad - delta_rows[:, :, None])).astype(jnp.bfloat16)
        running = running + jnp.einsum(
            "hqk,khd->qhd", score_low, key_tile, preferred_element_type=jnp.float32
        )
        value_part = jnp.einsum(
            "hqk,qhd->khd",
            prob_rows.astype(jnp.bfloat16),
            grad_heads,
            preferred_element_type=jnp.float32,
        )
        key_part = jnp.einsum(
            "hqk,qhd->khd", score_low, queries, preferred_element_type=jnp.float32
        )
        return (running, (key_part, value_part))

    start_grad = jnp.zeros(queries.shape, jnp.float32)
    query_grad, pieces = lax.scan(back_step, start_grad, (key_tiles, value_tiles, mask_tiles))
    key_count = key_rows.shape[0]
    return (
        query_grad,
        pieces[0].reshape(key_count, H * HEAD),
        pieces[1].reshape(key_count, H * HEAD),
    )


def general_body(
    tokens,
    doc_lengths,
    group_deal,
    qkv_weight,
    out_weight,
    up_weight,
    up_bias,
    down_weight,
    proj_weight,
    vectors,
    cotangent,
):
    gathered = (
        lax.all_gather(qkv_weight, "wa", axis=0, tiled=True),
        lax.all_gather(out_weight, "wa", axis=0, tiled=True),
        lax.all_gather(up_weight, "wa", axis=0, tiled=True),
        lax.all_gather(up_bias, "wa", axis=0, tiled=True),
        lax.all_gather(down_weight, "wa", axis=0, tiled=True),
        lax.all_gather(proj_weight, "wa", axis=0, tiled=True),
        lax.all_gather(vectors, "wa", axis=1, tiled=True),
    )
    qkv_full, out_full, up_full, bias_full, down_full, proj_full, vector_full = gathered
    seq_count, group_rows, model_width = tokens.shape
    ctx_count = lax.axis_size("ctx")
    seq_start = lax.axis_index("wa") * seq_count
    my_lengths = lax.dynamic_slice_in_dim(doc_lengths, seq_start, seq_count, 0)
    my_deal = lax.dynamic_slice_in_dim(group_deal, seq_start, seq_count, 0)
    offsets = jnp.tile(jnp.arange(group_rows, dtype=jnp.int32), ctx_count)
    positions = jnp.repeat(my_deal, group_rows, axis=1) * group_rows + offsets[None, :]
    key_valid = positions < my_lengths[:, None]
    query_valid = lax.dynamic_slice_in_dim(
        key_valid, lax.axis_index("ctx") * group_rows, group_rows, 1
    )
    row_mask = query_valid.astype(jnp.float32)[:, :, None]
    query_scale = HEAD ** (-0.5)
    mixed_rows = jnp.einsum("scd,de->sce", tokens, qkv_full, preferred_element_type=jnp.float32)
    queries = ((mixed_rows[:, :, :model_width] + vector_full[0]) * query_scale).astype(jnp.bfloat16)
    key_rows = mixed_rows[:, :, model_width : 2 * model_width].astype(jnp.bfloat16)
    value_rows = (mixed_rows[:, :, 2 * model_width :] + vector_full[1]).astype(jnp.bfloat16)
    all_keys, all_values = (
        lax.all_gather(key_rows, "ctx", axis=1, tiled=True),
        lax.all_gather(value_rows, "ctx", axis=1, tiled=True),
    )
    query_heads = queries.reshape(seq_count, group_rows, H, HEAD)
    attended, logsum = jax.vmap(attend_forward)(query_heads, all_keys, all_values, key_valid)
    attended_low = attended.reshape(seq_count, group_rows, model_width).astype(jnp.bfloat16)
    first_sum = tokens.astype(jnp.float32) + (
        jnp.einsum("scd,de->sce", attended_low, out_full, preferred_element_type=jnp.float32)
        + vector_full[2]
    )
    normed, unit_one, scale_one = norm_rows(first_sum, vector_full[3], vector_full[4])
    normed_low = normed.astype(jnp.bfloat16)
    inner_sum = (
        jnp.einsum("scd,df->scf", normed_low, up_full, preferred_element_type=jnp.float32)
        + bias_full
    )
    active, gelu_slope = gelu_both(inner_sum)
    active_low = active.astype(jnp.bfloat16)
    second_sum = normed + (
        jnp.einsum("scf,fd->scd", active_low, down_full, preferred_element_type=jnp.float32)
        + vector_full[5]
    )
    final_sum, unit_two, scale_two = norm_rows(second_sum, vector_full[6], vector_full[7])
    final_low = final_sum.astype(jnp.bfloat16)
    project = jnp.einsum("scd,de->sce", final_low, proj_full, preferred_element_type=jnp.float32)
    inverse = lax.rsqrt(jnp.sum(project * project, axis=-1, keepdims=True) + NORM_EPS)
    direction = project * inverse
    embeddings = (direction * row_mask).astype(jnp.bfloat16)
    upstream = cotangent.astype(jnp.float32) * row_mask
    project_grad = (
        inverse * (upstream - direction * jnp.sum(upstream * direction, axis=-1, keepdims=True))
    ).astype(jnp.bfloat16)
    proj_grad = jnp.einsum(
        "scd,sce->de", final_low, project_grad, preferred_element_type=jnp.float32
    )
    final_grad = jnp.einsum(
        "sce,de->scd", project_grad, proj_full, preferred_element_type=jnp.float32
    )
    second_grad, gain_two, shift_two = norm_back(final_grad, unit_two, scale_two, vector_full[6])
    down_low = second_grad.astype(jnp.bfloat16)
    down_grad = jnp.einsum("scf,scd->fd", active_low, down_low, preferred_element_type=jnp.float32)
    inner_grad = (
        jnp.einsum("scd,fd->scf", down_low, down_full, preferred_element_type=jnp.float32)
        * gelu_slope
    )
    bias_grad = jnp.sum(inner_grad, axis=(0, 1))
    inner_low = inner_grad.astype(jnp.bfloat16)
    up_grad = jnp.einsum("scd,scf->df", normed_low, inner_low, preferred_element_type=jnp.float32)
    normed_grad = second_grad + jnp.einsum(
        "scf,df->scd", inner_low, up_full, preferred_element_type=jnp.float32
    )
    first_grad, gain_one, shift_one = norm_back(normed_grad, unit_one, scale_one, vector_full[3])
    first_low = first_grad.astype(jnp.bfloat16)
    out_grad = jnp.einsum(
        "scd,sce->de", attended_low, first_low, preferred_element_type=jnp.float32
    )
    attended_grad = jnp.einsum(
        "sce,de->scd", first_low, out_full, preferred_element_type=jnp.float32
    ).astype(jnp.bfloat16)
    grad_heads = attended_grad.reshape(seq_count, group_rows, H, HEAD)
    delta_rows = jnp.sum(grad_heads.astype(jnp.float32) * attended, axis=-1)
    delta_heads = jnp.swapaxes(delta_rows, 1, 2)
    query_grad, key_terms, value_terms = jax.vmap(partial(attend_backward, with_keys=True))(
        query_heads, all_keys, all_values, key_valid, logsum, delta_heads, grad_heads
    )
    key_grad, value_grad = (
        lax.psum_scatter(
            key_terms.astype(jnp.bfloat16), "ctx", scatter_dimension=1, tiled=True
        ).astype(jnp.float32),
        lax.psum_scatter(
            value_terms.astype(jnp.bfloat16), "ctx", scatter_dimension=1, tiled=True
        ).astype(jnp.float32),
    )
    query_part = (
        query_grad.reshape(seq_count, group_rows, model_width).astype(jnp.bfloat16) * query_scale
    )
    value_part = value_grad.astype(jnp.bfloat16)
    mixed_grad = jnp.concatenate([query_part, key_grad.astype(jnp.bfloat16), value_part], axis=-1)
    qkv_grad = jnp.einsum("scd,sce->de", tokens, mixed_grad, preferred_element_type=jnp.float32)
    tokens_grad = first_grad + jnp.einsum(
        "sce,de->scd", mixed_grad, qkv_full, preferred_element_type=jnp.float32
    )
    vectors_grad = jnp.stack(
        [
            jnp.sum(query_part.astype(jnp.float32), axis=(0, 1)),
            jnp.sum(value_part.astype(jnp.float32), axis=(0, 1)),
            jnp.sum(first_grad, axis=(0, 1)),
            gain_one,
            shift_one,
            jnp.sum(second_grad, axis=(0, 1)),
            gain_two,
            shift_two,
        ],
        axis=0,
    )
    owned = (
        lax.psum_scatter(
            qkv_grad.astype(jnp.bfloat16), "wa", scatter_dimension=0, tiled=True
        ).astype(jnp.float32),
        lax.psum_scatter(
            out_grad.astype(jnp.bfloat16), "wa", scatter_dimension=0, tiled=True
        ).astype(jnp.float32),
        lax.psum_scatter(
            up_grad.astype(jnp.bfloat16), "wa", scatter_dimension=0, tiled=True
        ).astype(jnp.float32),
        lax.psum_scatter(
            bias_grad.astype(jnp.bfloat16), "wa", scatter_dimension=0, tiled=True
        ).astype(jnp.float32),
        lax.psum_scatter(
            down_grad.astype(jnp.bfloat16), "wa", scatter_dimension=0, tiled=True
        ).astype(jnp.float32),
        lax.psum_scatter(
            proj_grad.astype(jnp.bfloat16), "wa", scatter_dimension=0, tiled=True
        ).astype(jnp.float32),
        lax.psum_scatter(
            vectors_grad.astype(jnp.bfloat16), "wa", scatter_dimension=1, tiled=True
        ).astype(jnp.float32),
    )
    summed = (
        lax.psum(owned[0].astype(jnp.bfloat16), "ctx").astype(jnp.float32),
        lax.psum(owned[1].astype(jnp.bfloat16), "ctx").astype(jnp.float32),
        lax.psum(owned[2].astype(jnp.bfloat16), "ctx").astype(jnp.float32),
        lax.psum(owned[3].astype(jnp.bfloat16), "ctx").astype(jnp.float32),
        lax.psum(owned[4].astype(jnp.bfloat16), "ctx").astype(jnp.float32),
        lax.psum(owned[5].astype(jnp.bfloat16), "ctx").astype(jnp.float32),
        lax.psum(owned[6].astype(jnp.bfloat16), "ctx").astype(jnp.float32),
    )
    return (
        embeddings,
        tokens_grad,
        summed[0],
        summed[1],
        summed[2],
        summed[3],
        summed[4],
        summed[5],
        summed[6],
    )


PLANE = 8
LINE = 4
SPAN = 128
OWN = 2 * SPAN
WIDTH = H * HEAD
INNER = 4 * WIDTH
SHARD = WIDTH // LINE
HALF = SHARD // 2
PIECE = INNER // LINE // PLANE
SLICE = LINE * PIECE
HEADS = 3
WIDE = HEADS * HEAD
PAD = 256
SLOTS = PLANE * SPAN
BLOCK = SHARD // 4
FIRST = SHARD + BLOCK
SIDE = PIECE + 16
PARTS = FIRST + 2 * SIDE
QUARTER = HALF // 2
COLS = HALF + QUARTER
EMBED = 128
ORDER = (0, 4, 2, 6, 1, 5, 3, 7)
NEAR = (0, 2, 1, 3)
F32 = jnp.float32
BF16 = jnp.bfloat16

NN = ((1,), (0,))
NT = ((1,), (1,))
TN = ((0,), (0,))


def dot(left, right, dims):
    return lax.dot_general(left, right, (dims, ((), ())), preferred_element_type=F32)


def plane_swap(array, bits):
    return lax.ppermute(array, "ctx", [(i, i ^ bits) for i in range(PLANE)])


def line_turn(array, step):
    return lax.ppermute(array, "wa", [(i, (i + step) % LINE) for i in range(LINE)])


def line_turns(array):
    return [line_turn(array, step) for step in range(1, LINE)]


def relay(from_x, from_y, core):
    passed = jnp.where(core == 0, from_y, from_x)
    pairs = [(i, i ^ 2 if i % 2 == 0 else i ^ 4) for i in range(PLANE)]
    return lax.ppermute(passed, "ctx", pairs)


def pick(array, index):
    return lax.dynamic_index_in_dim(array, index, 0, keepdims=False)


COST = {'cut': 3, 'vectors': 1, 'attend': 12, 'out': 3, 'middle': 17, 'slice_grad': 9, 'attend_back': 18, 'rest_shard': 4, 'qkv_shard': 2, 'attend_tail': 6, 'cut_qkv': 1, 'cut_rest': 2}
VM = pl.BlockSpec(memory_space=pltpu.VMEM)
SM = pl.BlockSpec(memory_space=pltpu.SMEM)
HB = pl.BlockSpec(memory_space=pl.ANY)
BIG = 56


def call(kernel, inputs, spaces, outputs, scratch=(), mebibytes=32, name=None):
    shapes = [jax.ShapeDtypeStruct(shape, kind) for shape, kind in outputs]
    return pl.pallas_call(
        kernel,
        out_shape=shapes,
        in_specs=list(spaces),
        out_specs=[VM] * len(shapes),
        scratch_shapes=list(scratch),
        compiler_params=pltpu.CompilerParams(vmem_limit_bytes=mebibytes << 20),
        cost_estimate=pl.CostEstimate(flops=int(COST[name] * 1e+09), bytes_accessed=1, transcendentals=0),
        name=name,
    )(*inputs)


def place_of(scal):
    return scal[0], scal[1]


def shard_of_turn(line, turn):
    return lax.rem(line - turn + LINE, LINE)


def turn_ahead(line, turn):
    return lax.rem(line + turn, LINE)


def norm_forward(rows):
    middle = jnp.mean(rows, axis=-1, keepdims=True)
    center = rows - middle
    scaled = lax.rsqrt(jnp.mean(center * center, axis=-1, keepdims=True) + NORM_EPS)
    return center * scaled, scaled


def norm_reverse(grad, unit, scaled, gain):
    inner = grad * gain
    return scaled * (
        inner
        - jnp.mean(inner, axis=-1, keepdims=True)
        - unit * jnp.mean(inner * unit, axis=-1, keepdims=True)
    )


def cut_qkv_kernel(scal, vectors, bias, qkv, cols_ref, half_ref, held, sem):
    copy = pltpu.make_async_copy(qkv, held, sem)
    copy.start()
    me, line = place_of(scal)
    rows = [vectors[...].astype(F32)]
    rows += [bias[:, a * SHARD : (a + 1) * SHARD].astype(F32) for a in range(LINE)]
    rows = jnp.concatenate(rows + [jnp.zeros((4, SHARD), F32)])
    half_ref[COLS:, :SHARD] = rows.astype(BF16)
    half_ref[COLS:, SHARD:] = jnp.zeros((16, SLICE - SHARD), BF16)
    copy.wait()
    for g in range(4):

        @pl.when(lax.rem(me, 4) == g)
        def _():
            for part in range(3):
                start = part * WIDTH + g * WIDE
                cols_ref[:, part * WIDE : (part + 1) * WIDE] = held[:, start : start + WIDE]

    base = lax.div(me, 4) * HALF
    rows = cols_ref[pl.ds(pl.multiple_of(base, 16), HALF), :]
    half_ref[:HALF, :] = rows[:, :SLICE]
    for side in range(2):
        half_ref[HALF:COLS, side * WIDE : (side + 1) * WIDE] = rows[
            side * QUARTER : (side + 1) * QUARTER, SLICE:
        ]


def cut_rest_kernel(
    scal, proj, up, down, out, earlier,
    ups_ref, own_ref,
    up_held, down_held, out_held, sems,
):
    del earlier
    me, line = place_of(scal)
    core = lax.rem(me, 2)
    copies = [
        pltpu.make_async_copy(up, up_held, sems.at[0]),
        pltpu.make_async_copy(
            down.at[pl.ds(pl.multiple_of(me * PIECE, 16), PIECE)], down_held, sems.at[1]
        ),
        pltpu.make_async_copy(
            out.at[pl.ds(pl.multiple_of(lax.div(me, 2) * BLOCK, 16), BLOCK)], out_held, sems.at[2]
        ),
    ]
    for copy in copies:
        copy.start()
    for side in range(2):
        start = FIRST + side * SIDE + PIECE
        for t in range(3):
            own_ref[start : start + 16, t * EMBED : (t + 1) * EMBED] = proj[
                pl.ds(pl.multiple_of(core * HALF + 16 * (3 * side + t), 16), 16), :
            ]
    copies[0].wait()
    for k in range(PLANE):
        for s in range(LINE):
            start = s * PLANE * PIECE + k * PIECE
            ups_ref[k, :, s * PIECE : (s + 1) * PIECE] = up_held[:, start : start + PIECE]
    own_ref[:SHARD] = ups_ref[me]
    copies[1].wait()
    for side in range(2):
        start = FIRST + side * SIDE
        own_ref[start : start + PIECE] = down_held[:, side * SLICE : (side + 1) * SLICE]
    copies[2].wait()
    own_ref[SHARD:FIRST] = out_held[:, pl.ds(pl.multiple_of(core * SLICE, 128), SLICE)]


def vectors_kernel(scal, own, halves, full_ref, bias_ref, ends_ref, held):
    me, line = place_of(scal)
    held[line] = own[COLS:, :SHARD].astype(F32)
    for turn in range(1, LINE):
        held[shard_of_turn(line, turn)] = halves[turn - 1, COLS:, :SHARD].astype(F32)
    for a in range(LINE):
        full_ref[:, a * SHARD : (a + 1) * SHARD] = held[a, :8, :]
        for k in range(PLANE):
            start = (k % 2) * PIECE
            bias_ref[k : k + 1, a * PIECE : (a + 1) * PIECE] = held[
                a, 8 + k // 2 : 9 + k // 2, start : start + PIECE
            ]
    ends_ref[...] = jnp.zeros((8, PAD), F32)
    ends_ref[:, :WIDE] = held[lax.rem(me, 4), :8, :]


def slots_left(scal, lengths, deal, place):
    me, line = place_of(scal)
    seq = 2 * line + lax.div(me, 4)
    return lengths[seq] - deal[seq, me ^ ORDER[place]] * SPAN


def fill_mask(scal, lengths, deal, mask):
    rows = lax.broadcasted_iota(jnp.int32, (SPAN, SPAN), 0)
    for place in range(PLANE):
        limit = slots_left(scal, lengths, deal, place)
        mask[place * SPAN : (place + 1) * SPAN, :] = jnp.where(rows < limit, 0.0, NEG_FILL)


def head_lanes(h):
    lanes = lax.broadcasted_iota(jnp.int32, (OWN, 128), 1)
    return (lanes >= HEAD) if h % 2 else (lanes < HEAD)


def attend_kernel(
    scal, lengths, deal, ends, own_cols, halves, others, near, far,
    q_ref, k_ref, v_ref, w_ref, own_ref, core_ref, x_ref, lse_ref,
    raw, mask, v_turned, o_turned, att,
):
    me, line = place_of(scal)
    y = lax.div(me, 4)
    raw[pl.ds(pl.multiple_of(line * SHARD, 16), SHARD), :] = own_cols[...]
    for turn in range(1, LINE):
        base = shard_of_turn(line, turn) * SHARD
        for source, side in ((halves, y), (others, 1 - y)):
            start = base + side * HALF
            at = pl.ds(pl.multiple_of(start, 16), HALF)
            raw[at, :SLICE] = source[turn - 1, :HALF, :]
            for i in range(2):
                at = pl.ds(pl.multiple_of(start + i * QUARTER, 16), QUARTER)
                raw[at, SLICE:] = source[turn - 1, HALF:COLS, i * WIDE : (i + 1) * WIDE]
    fill_mask(scal, lengths, deal, mask)
    for part in range(3):
        w_ref[:, part * PAD : part * PAD + WIDE] = raw[:, part * WIDE : (part + 1) * WIDE]
        w_ref[:, part * PAD + WIDE : (part + 1) * PAD] = jnp.zeros((WIDTH, PAD - WIDE), BF16)
    for t in range(4):
        source = (near, far)[t // 2]
        rows = source[(t % 2) * OWN : (t % 2 + 1) * OWN, :]
        mixed = dot(rows, w_ref[...], NN)
        at = slice(t * OWN, (t + 1) * OWN)
        q_ref[at, :] = ((mixed[:, :PAD] + ends[0:1, :]) * (HEAD ** (-0.5))).astype(BF16)
        k_ref[at, :] = mixed[:, PAD : 2 * PAD].astype(BF16)
        values = mixed[:, 2 * PAD :] + ends[1:2, :]
        v_ref[at, :] = values.astype(BF16)
        v_turned[:, at] = values.T.astype(BF16)

    o_turned[WIDE:, :] = jnp.zeros((PAD - WIDE, OWN), F32)

    def tile(t, carry):
        at = pl.ds(pl.multiple_of(t * OWN, OWN), OWN)
        for h in range(HEADS):
            cut = slice((h // 2) * 128, (h // 2 + 1) * 128)
            q_tile = jnp.where(head_lanes(h), q_ref[at, cut], jnp.zeros((), BF16))
            scores = dot(k_ref[:, cut], q_tile, NT)
            scores = scores + jnp.concatenate([mask[...], mask[...]], axis=1)
            peak = jnp.max(scores, axis=0, keepdims=True)
            raised = jnp.exp(scores - peak)
            total = jnp.sum(raised, axis=0, keepdims=True)
            rows = slice(h * HEAD, (h + 1) * HEAD)
            o_turned[rows, :] = dot(v_turned[rows, :], raised.astype(BF16), NN) * (1.0 / total)
            lse_ref[t, h : h + 1, :] = peak + jnp.log(total)
        att[t] = o_turned[...].T.astype(BF16)
        return carry

    lax.fori_loop(0, 4, tile, 0)
    own_ref[...] = att[0]
    core_ref[...] = att[2]
    x_ref[0] = att[1]
    x_ref[1] = att[3]


def attend_back_kernel(
    scal, lengths, deal, q_ref, k_ref, v_ref, lse, weights, near, far, first_grad, g0, g1, g2, g3,
    mine_ref, other_ref, near_ref, far_ref,
    q_held, k_held, v_held, w_held, near_held, far_held, first_held, grads,
    mask, k_turned, q_turned, mixed, key_sum, value_sum, part, sems,
):
    sources = (k_ref, q_ref, v_ref, g0, g1.at[0], g2, g3, weights, near, far, first_grad)
    targets = (k_held, q_held, v_held, grads.at[0], grads.at[1], grads.at[2], grads.at[3])
    targets += (w_held, near_held, far_held, first_held)
    copies = [
        pltpu.make_async_copy(source, target, sems.at[i])
        for i, (source, target) in enumerate(zip(sources, targets, strict=True))
    ]
    for copy in copies:
        copy.start()
    fill_mask(scal, lengths, deal, mask)
    copies[0].wait()
    for t in range(4):
        at = slice(t * OWN, (t + 1) * OWN)
        k_turned[:, at] = k_held[at, :].astype(F32).T.astype(BF16)
    key_sum[...] = jnp.zeros_like(key_sum)
    value_sum[...] = jnp.zeros_like(value_sum)
    q_turned[WIDE:, :] = jnp.zeros((PAD - WIDE, OWN), F32)
    for copy in copies[1:7]:
        copy.wait()

    def tile(t, carry):
        at = pl.ds(pl.multiple_of(t * OWN, OWN), OWN)
        for h in range(HEADS):
            cut = slice((h // 2) * 128, (h // 2 + 1) * 128)
            rows = slice(h * HEAD, (h + 1) * HEAD)
            q_tile = jnp.where(head_lanes(h), q_held[at, cut], jnp.zeros((), BF16))
            g_tile = jnp.where(head_lanes(h), grads[t, :, cut], jnp.zeros((), BF16))
            scores = dot(k_held[:, cut], q_tile, NT)
            scores = scores + jnp.concatenate([mask[...], mask[...]], axis=1)
            probs = jnp.exp(scores - lse[t, h : h + 1, :])
            prob_grad = dot(v_held[:, cut], g_tile, NT)
            delta = jnp.sum(probs * prob_grad, axis=0, keepdims=True)
            score_low = (probs * (prob_grad - delta)).astype(BF16)
            q_turned[rows, :] = dot(k_turned[rows, :], score_low, NN)
            key_sum[:, cut] += dot(score_low, q_tile, NN)
            value_sum[:, cut] += dot(probs.astype(BF16), g_tile, NN)
        low = q_turned[...].T.astype(BF16)
        mixed[at, :PAD] = (low.astype(F32) * (HEAD ** (-0.5))).astype(BF16)
        return carry

    lax.fori_loop(0, 4, tile, 0)
    mixed[:, PAD : 2 * PAD] = key_sum[...].astype(BF16)
    mixed[:, 2 * PAD :] = value_sum[...].astype(BF16)

    me, line = place_of(scal)
    y = lax.div(me, 4)
    for copy in copies[7:]:
        copy.wait()
    for i in range(3):
        cut = slice(i * 256, (i + 1) * 256)
        part[cut, :] = (
            dot(near_held[:, cut], mixed[: 2 * OWN, :], TN) + dot(far_held[:, cut], mixed[2 * OWN :, :], TN)
        ).astype(BF16)
    sums = jnp.sum(mixed[...].astype(F32), axis=0, keepdims=True)
    sums = jnp.concatenate([sums, jnp.zeros((15, 3 * PAD), F32)]).astype(BF16)
    for turn in range(LINE):
        base = turn_ahead(line, turn) * SHARD
        for target, side in ((mine_ref, y), (other_ref, 1 - y)):
            rows = part[pl.ds(pl.multiple_of(base + side * HALF, 16), HALF), :]
            for p in range(3):
                to = slice(p * WIDE, (p + 1) * WIDE)
                target[turn, :HALF, to] = rows[:, p * PAD : p * PAD + WIDE]
                target[turn, HALF:, to] = sums[:, p * PAD : p * PAD + WIDE]
    for t in range(4):
        at = slice(t * OWN, (t + 1) * OWN)
        token_part = dot(mixed[at, :], w_held[...], NT)
        if t == 0:
            near_ref[at, :] = token_part + first_held[...]
        elif t == 1:
            near_ref[at, :] = token_part
        else:
            far_ref[(t - 2) * OWN : (t - 1) * OWN, :] = token_part.astype(BF16)


def out_kernel(
    scal, near, full, out_shard, a0, a1, a2, a3, p0, p1, p2, p3, p4, p5, p6, p7,
    normed_ref, low_ref, unit_ref, scale_ref, out_ref,
    sem,
):
    me, line = place_of(scal)
    group = lax.rem(me, 4)
    pieces = (p0, p1, p2, p3, p4, p5, p6, p7)
    copies = []
    for place, bits in enumerate(ORDER):
        k = me ^ bits
        rows = pl.ds(pl.multiple_of(lax.div(k, 2) * BLOCK, 16), BLOCK)
        lanes = pl.ds(pl.multiple_of(lax.rem(k, 2) * SLICE, 128), SLICE)
        for turn in range(1, LINE):
            copies.append(
                pltpu.make_async_copy(
                    pieces[place].at[turn - 1, pl.ds(SHARD, BLOCK)],
                    out_ref.at[shard_of_turn(line, turn), rows, lanes],
                    sem,
                )
            )
    for copy in copies:
        copy.start()
    for z in range(LINE):
        out_ref[z, SHARD:, :] = jnp.zeros((PAD - SHARD, WIDTH), BF16)
    out_ref[line, :SHARD, :] = out_shard[...]
    rows = near[:OWN, :].astype(F32) + full[2:3, :]
    filled = out_ref.at[pl.ds(0, LINE - 1), pl.ds(0, SHARD)]
    pltpu.make_async_copy(filled, filled, sem).wait()
    for i, source in enumerate((a0[...], a1[0], a2[...], a3[...])):
        rows = rows + dot(source, out_ref[group ^ NEAR[i]], NN)
    unit, scaled = norm_forward(rows)
    normed = unit * full[3:4, :] + full[4:5, :]
    normed_ref[...] = normed
    low_ref[...] = normed.astype(BF16)
    unit_ref[...] = unit
    scale_ref[...] = jnp.broadcast_to(scaled, (OWN, 128))


def weight_copies(ups, down, parts, up_own, down_own, held, sems):
    copies = [
        pltpu.make_async_copy(ups, up_own, sems.at[PLANE]),
        pltpu.make_async_copy(down, down_own, sems.at[PLANE + 1]),
    ]
    for place in range(PLANE):
        copies.append(pltpu.make_async_copy(parts[place], held.at[place], sems.at[place]))
    return copies


def place_up(scal, place, up_own, held, up_all):
    me, line = place_of(scal)
    at = pl.ds(pl.multiple_of(line * SHARD, 16), SHARD)
    up_all[place, at, :] = up_own[me ^ ORDER[place]]
    for turn in range(1, LINE):
        at = pl.ds(pl.multiple_of(shard_of_turn(line, turn) * SHARD, 16), SHARD)
        up_all[place, at, :] = held[place, turn - 1, :SHARD, :]


def place_down(scal, place, down_own, held, down_all):
    me, line = place_of(scal)
    at = pl.ds(pl.multiple_of(line * PIECE, 16), PIECE)
    start = pl.multiple_of((me ^ ORDER[place]) * PIECE, 16)
    down_all[place, at, :] = down_own[pl.ds(start, PIECE), :]
    for turn in range(1, LINE):
        at = pl.ds(pl.multiple_of(shard_of_turn(line, turn) * PIECE, 16), PIECE)
        for side in range(2):
            start = FIRST + side * SIDE
            down_all[place, at, side * SLICE : (side + 1) * SLICE] = held[
                place, turn - 1, start : start + PIECE, :
            ]


def middle_kernel(
    scal, lengths, deal, normed, normed_low, unit_one, scale_one, full, bias, proj_shard,
    cot_mine, cot_other, out_all, a0, a1, a2, a3, ups, down, p0, p1, p2, p3, p4, p5, p6, p7,
    embed_ref, low_ref, first_ref, own_ref, core_ref, x_ref, mine_ref, other_ref,
    up_own, down_own, held, up_all, down_all, proj_all, slopes, proj_part, bias_sum, out_part, sems,
):
    copies = weight_copies(
        ups, down, (p0, p1, p2, p3, p4, p5, p6, p7), up_own, down_own, held, sems
    )
    for copy in copies:
        copy.start()
    me, line = place_of(scal)
    core, group = lax.rem(me, 2), lax.rem(me, 4)
    proj_all[pl.ds(pl.multiple_of(line * SHARD, 16), SHARD), :] = proj_shard[...]

    second_sum = normed[...] + full[5:6, :]
    copies[0].wait()
    copies[1].wait()
    for place, bits in enumerate(ORDER):
        copies[2 + place].wait()
        place_up(scal, place, up_own, held, up_all)
        place_down(scal, place, down_own, held, down_all)
        inner = dot(normed_low[...], up_all[place], NN) + bias[pl.ds(me ^ bits, 1), :]
        active, slope = gelu_both(inner)
        slopes[place] = slope
        second_sum = second_sum + dot(active.astype(BF16), down_all[place], NN)
    unit, scaled = norm_forward(second_sum)
    final_low = (unit * full[6:7, :] + full[7:8, :]).astype(BF16)
    for place in (0, 4):
        half = core if place == 0 else 1 - core
        for turn in range(1, LINE):
            base = shard_of_turn(line, turn) * SHARD + half * HALF
            for t in range(6):
                start = FIRST + (t // 3) * SIDE + PIECE
                proj_all[pl.ds(pl.multiple_of(base + 16 * t, 16), 16), :] = held[
                    place, turn - 1, start : start + 16, (t % 3) * EMBED : (t % 3 + 1) * EMBED
                ]
    project = dot(final_low, proj_all[...], NN)
    inverse = lax.rsqrt(jnp.sum(project * project, axis=-1, keepdims=True) + NORM_EPS)
    direction = project * inverse
    rows = lax.broadcasted_iota(jnp.int32, (SPAN, EMBED), 0)
    keep = jnp.concatenate(
        [
            jnp.where(rows < slots_left(scal, lengths, deal, i), 1.0, 0.0).astype(F32)
            for i in range(2)
        ]
    )
    embed_ref[...] = (direction * keep).astype(BF16)
    upstream = jnp.concatenate([cot_mine[...], cot_other[...]]).astype(F32) * keep
    project_grad = (
        inverse * (upstream - direction * jnp.sum(upstream * direction, axis=-1, keepdims=True))
    ).astype(BF16)
    proj_part[...] = dot(final_low, project_grad, TN).astype(BF16)
    final_grad = dot(project_grad, proj_all[...], NT)
    second_grad = norm_reverse(final_grad, unit, scaled, full[6:7, :])
    down_low = second_grad.astype(BF16)
    low_ref[...] = down_low

    normed_grad = second_grad
    for place, bits in enumerate(ORDER):
        inner_grad = dot(down_low, down_all[place], NT) * slopes[place]
        bias_sum[pl.ds(me ^ bits, 1), :] = jnp.sum(inner_grad, axis=0, keepdims=True)
        normed_grad = normed_grad + dot(inner_grad.astype(BF16), up_all[place], NT)
    first_grad = norm_reverse(normed_grad, unit_one[...], scale_one[:, :1], full[3:4, :])
    first_ref[...] = first_grad
    first_low = first_grad.astype(BF16)
    for i, target in enumerate((own_ref, x_ref.at[0], core_ref, x_ref.at[1])):
        target[...] = dot(first_low, out_all[group ^ NEAR[i]], NT).astype(BF16)
    small = jnp.concatenate(
        [
            jnp.sum(first_grad, axis=0, keepdims=True),
            jnp.sum(normed_grad * unit_one[...], axis=0, keepdims=True),
            jnp.sum(normed_grad, axis=0, keepdims=True),
            jnp.sum(second_grad, axis=0, keepdims=True),
            jnp.sum(final_grad * unit, axis=0, keepdims=True),
            jnp.sum(final_grad, axis=0, keepdims=True),
            jnp.zeros((2, WIDTH), F32),
        ]
    )
    tail = jnp.concatenate([bias_sum[...], jnp.zeros((8, WIDTH - SLICE), F32)], axis=1)
    small = jnp.concatenate([small, tail]).astype(BF16)
    for i, source in enumerate((a0[...], a1[0], a2[...], a3[...])):
        z = group ^ NEAR[i]
        turn = lax.rem(z - line + LINE, LINE)
        out_part[i] = dot(source, first_low, TN).astype(BF16)
        for target, half in ((mine_ref, core), (other_ref, 1 - core)):
            base = half * HALF
            target[turn, :HALF, :] = out_part[i, pl.ds(pl.multiple_of(base, 16), HALF), :]
            for t in range(6):
                target[turn, HALF : HALF + 16, t * EMBED : (t + 1) * EMBED] = proj_part[
                    pl.ds(pl.multiple_of(z * SHARD + base + 16 * t, 16), 16), :
                ]
            target[turn, HALF + 16 :, :] = small


def slice_grad_kernel(
    scal, bias, own, turns, core_turns, ups, down, n0, n1, n2, n3, d0, d1, d2, d3,
    mine_ref, other_ref,
    own_held, held, ups_held, down_held, slots, up_rows, up_turned, down_rows, up_sum, down_sum,
    up_back,
    sems,
):
    me, line = place_of(scal)
    start = pl.multiple_of((me ^ 1) * PIECE, 16)
    copies = [
        pltpu.make_async_copy(own, own_held, sems.at[0]),
        pltpu.make_async_copy(turns, held.at[0], sems.at[1]),
        pltpu.make_async_copy(core_turns, held.at[1], sems.at[2]),
        pltpu.make_async_copy(ups.at[me ^ 1], ups_held, sems.at[3]),
        pltpu.make_async_copy(down.at[pl.ds(start, PIECE)], down_held, sems.at[4]),
    ]
    for j, source in enumerate((n0, d0, n1, d1, n2, d2, n3, d3)):
        copies.append(pltpu.make_async_copy(source, slots.at[j], sems.at[5 + j]))
    for copy in copies:
        copy.start()
    for copy in copies[:5]:
        copy.wait()
    for i, target in enumerate((other_ref, mine_ref)):
        core = 1 - i
        for turn in range(LINE):
            z = shard_of_turn(line, turn)
            if turn:
                rows = held[core, turn - 1, :SHARD, :]
            else:
                rows = ups_held[...] if core else own_held[:SHARD, :]
            up_rows[core, pl.ds(pl.multiple_of(z * SHARD, 16), SHARD), :] = rows.astype(F32)
            at = pl.ds(pl.multiple_of(z * PIECE, 16), PIECE)
            if turn == 0 and core:
                down_rows[core, at, :] = down_held[...]
                continue
            for side in range(2):
                start = FIRST + side * SIDE
                if turn:
                    rows = held[core, turn - 1, start : start + PIECE, :]
                else:
                    rows = own_held[start : start + PIECE, :]
                down_rows[core, at, side * SLICE : (side + 1) * SLICE] = rows
        up_turned[core] = up_rows[core].T.astype(BF16)
        bias_rows = jnp.broadcast_to(bias[pl.ds(me ^ core, 1), :], (128, SLICE)).T
        bias_rows = jnp.concatenate([bias_rows, bias_rows], axis=1)
        for j in range(4):
            if i == 0:
                copies[5 + 2 * j].wait()
                copies[6 + 2 * j].wait()
            normed, low = slots[2 * j], slots[2 * j + 1]
            inner = dot(up_turned[core], normed, NT) + bias_rows
            active, slope = gelu_both(inner)
            inner_low = (dot(down_rows[core], low, NT) * slope).astype(BF16)
            up_part = dot(inner_low, normed, NN)
            down_part = dot(active.astype(BF16), low, NN)
            if j == 0:
                up_sum[core] = up_part
                down_sum[core] = down_part
            else:
                up_sum[core] += up_part
                down_sum[core] += down_part
        up_back[core] = up_sum[core].T
        for turn in range(LINE):
            z = turn_ahead(line, turn)
            for side in range(2):
                at = pl.ds(pl.multiple_of(z * SHARD + side * HALF, 16), HALF)
                target[turn, :HALF, side * SLICE : (side + 1) * SLICE] = up_back[
                    core, at, :
                ].astype(BF16)
            at = pl.ds(pl.multiple_of(z * PIECE, 16), PIECE)
            target[turn, HALF:, :] = down_sum[core, at, :].astype(BF16)


def rest_shard_kernel(
    scal, p0, p1, p2, p3, p4, p5, p6, p7,
    up_ref, down_ref, out_ref, proj_ref, rows_ref, bias_ref, held,
):
    me, line = place_of(scal)
    for source, bits in zip((p0, p1, p2, p3, p4, p5, p6, p7), ORDER, strict=True):
        held[me ^ bits] = source[...]
    for k in range(PLANE):
        core, x, y = k % 2, (k // 2) % 2, k // 4
        for side in range(2):
            rows = held[k, :HALF, side * SLICE : (side + 1) * SLICE].astype(F32)
            for s in range(LINE):
                start = s * PLANE * PIECE + k * PIECE
                up_ref[side * HALF : (side + 1) * HALF, start : start + PIECE] = rows[
                    :, s * PIECE : (s + 1) * PIECE
                ]
        down_ref[k * PIECE : (k + 1) * PIECE, :] = held[k, HALF : 2 * HALF, :].astype(F32)
        tail = held[k, 2 * HALF :, :].astype(F32)
        block = 2 * x + y
        if block < 3:
            start = core * HALF + 32 * block
            out_ref[start : start + 32, :] = tail
        else:
            for t in range(6):
                start = core * HALF + 16 * t
                proj_ref[start : start + 16, :] = tail[:16, t * EMBED : (t + 1) * EMBED]
            if core == 0:
                small = tail[16:, :]
    for z in range(LINE):

        @pl.when(line == z)
        def _():
            rows_ref[...] = small[:8, z * SHARD : (z + 1) * SHARD]
            bias_ref[...] = small[8:, z * PIECE : (z + 1) * PIECE]


def qkv_shard_kernel(scal, late, p0, p1, p2, p3, p4, p5, p6, p7, qkv_ref, rows_ref, held):
    me, line = place_of(scal)
    for source, bits in zip((p0, p1, p2, p3, p4, p5, p6, p7), ORDER, strict=True):
        held[me ^ bits] = source[...]
    for k in range(PLANE):
        y, g = k // 4, k % 4
        for part in range(3):
            start = part * WIDTH + g * WIDE
            qkv_ref[y * HALF : (y + 1) * HALF, start : start + WIDE] = held[
                k, :HALF, part * WIDE : (part + 1) * WIDE
            ].astype(F32)
    sums = held[line, HALF:, :].astype(F32)
    rows_ref[...] = jnp.concatenate(
        [sums[:1, :WIDE], sums[:1, 2 * WIDE : 3 * WIDE], late[:6, :]]
    )


def gather_side(array):
    return [array, plane_swap(array, 4), plane_swap(array, 2), plane_swap(array, 6)]


def gather_plane(array):
    close = gather_side(array)
    return close + [plane_swap(part, 1) for part in close]


def sum_turns(parts):
    total = parts[0].astype(F32)
    for turn in range(1, LINE):
        total = total + line_turn(parts[turn], turn).astype(F32)
    return total.astype(BF16)


def swap_groups(own, from_x, for_core):
    return own, from_x, plane_swap(for_core, 1), plane_swap(from_x[1], 1)


def plane_body(
    tokens,
    doc_lengths,
    group_deal,
    qkv_weight,
    out_weight,
    up_weight,
    up_bias,
    down_weight,
    proj_weight,
    vectors,
    cotangent,
):
    me = lax.axis_index("ctx").astype(jnp.int32)
    line = lax.axis_index("wa").astype(jnp.int32)
    y, x, core = me // 4, (me // 2) % 2, me % 2
    scal = jnp.stack([me, line])
    spots = (scal, doc_lengths, group_deal)

    own_cols, half_cols = call(
        cut_qkv_kernel,
        (scal, vectors, up_bias.reshape(1, -1), qkv_weight),
        (SM, VM, VM, HB),
        [((SHARD, 3 * WIDE), BF16), ((COLS + 16, SLICE), BF16)],
        [pltpu.VMEM((SHARD, 3 * WIDTH), BF16), pltpu.SemaphoreType.DMA],
        mebibytes=BIG,
        name="cut_qkv",
    )
    half_turns = line_turns(half_cols)
    ups, own_parts = call(
        cut_rest_kernel,
        (scal, proj_weight, up_weight, down_weight, out_weight, half_cols),
        (SM, VM, HB, HB, HB, HB),
        [((PLANE, SHARD, SLICE), BF16), ((PARTS, SLICE), BF16)],
        [
            pltpu.VMEM((SHARD, INNER), BF16),
            pltpu.VMEM((PIECE, WIDTH), BF16),
            pltpu.VMEM((BLOCK, WIDTH), BF16),
            pltpu.SemaphoreType.DMA((3,)),
        ],
        mebibytes=BIG,
        name="cut_rest",
    )
    mine, other = pick(tokens, y), pick(tokens, 1 - y)
    got_y = plane_swap(other, 4)
    got_x = plane_swap(mine, 2)
    got_d = plane_swap(other, 6)
    near = jnp.concatenate([mine, got_y, got_x, got_d])
    far = plane_swap(near, 1)
    halves = jnp.stack(half_turns)
    others = plane_swap(halves, 4)

    full, bias, ends = call(
        vectors_kernel,
        (scal, half_cols, halves),
        (SM, VM, VM),
        [((8, WIDTH), F32), ((PLANE, SLICE), F32), ((8, PAD), F32)],
        [pltpu.VMEM((LINE, 16, SHARD), F32)],
        name="vectors",
    )

    queries, keys, values, weights, att_own, att_core, att_x, lse = call(
        attend_kernel,
        (*spots, ends, own_cols, halves, others, near, far),
        (SM, SM, SM, *[VM] * 6),
        [
            ((SLOTS, PAD), BF16),
            ((SLOTS, PAD), BF16),
            ((SLOTS, PAD), BF16),
            ((WIDTH, 3 * PAD), BF16),
            ((OWN, PAD), BF16),
            ((OWN, PAD), BF16),
            ((2, OWN, PAD), BF16),
            ((4, 8, OWN), F32),
        ],
        [
            pltpu.VMEM((WIDTH, 3 * WIDE), BF16),
            pltpu.VMEM((SLOTS, SPAN), F32),
            pltpu.VMEM((PAD, SLOTS), BF16),
            pltpu.VMEM((PAD, OWN), F32),
            pltpu.VMEM((4, OWN, PAD), BF16),
        ],
        name="attend",
    )
    att_x = plane_swap(att_x, 2)

    turns = line_turns(own_parts)
    *turns, att_core = lax.optimization_barrier((*turns, att_core))
    turns = jnp.stack(turns)
    from_x = plane_swap(turns, 2)
    from_y = plane_swap(turns, 4)
    from_d = relay(from_x, from_y, core)
    parts = [turns, from_y, from_x, from_d]
    parts += [plane_swap(part, 1) for part in parts]
    groups = swap_groups(att_own, att_x, att_core)

    normed, normed_low, unit, scale, out_all = call(
        out_kernel,
        (scal, near, full, out_weight, *groups, *parts),
        (SM, VM, VM, VM, *[VM] * 4, *[HB] * 8),
        [
            ((OWN, WIDTH), F32),
            ((OWN, WIDTH), BF16),
            ((OWN, WIDTH), F32),
            ((OWN, 128), F32),
            ((LINE, PAD, WIDTH), BF16),
        ],
        [pltpu.SemaphoreType.DMA],
        name="out",
    )
    normed_side = gather_side(normed_low)
    cot_mine, cot_other = pick(cotangent, y), plane_swap(pick(cotangent, 1 - y), 4)
    embedded, down_low, first_grad, grad_own, grad_core, grad_x, rest_mine, rest_other = call(
        middle_kernel,
        (*spots, normed, normed_low, unit, scale, full, bias, proj_weight, cot_mine, cot_other)
        + (out_all, *groups, ups, down_weight, *parts),
        (SM, SM, SM, *[VM] * 14, *[HB] * 10),
        [
            ((OWN, EMBED), BF16),
            ((OWN, WIDTH), BF16),
            ((OWN, WIDTH), F32),
            *[((OWN, PAD), BF16)] * 2,
            ((2, OWN, PAD), BF16),
            *[((LINE, SPAN, WIDTH), BF16)] * 2,
        ],
        [
            pltpu.VMEM((PLANE, SHARD, SLICE), BF16),
            pltpu.VMEM((WIDTH, WIDTH), BF16),
            pltpu.VMEM((PLANE, LINE - 1, PARTS, SLICE), BF16),
            pltpu.VMEM((PLANE, WIDTH, SLICE), BF16),
            pltpu.VMEM((PLANE, SLICE, WIDTH), BF16),
            pltpu.VMEM((WIDTH, EMBED), BF16),
            pltpu.VMEM((PLANE, OWN, SLICE), F32),
            pltpu.VMEM((WIDTH, EMBED), BF16),
            pltpu.VMEM((PLANE, SLICE), F32),
            pltpu.VMEM((4, PAD, WIDTH), BF16),
            pltpu.SemaphoreType.DMA((PLANE + 2,)),
        ],
        mebibytes=48,
        name="middle",
    )
    *normed_side, down_low, embedded, grad_core, grad_x, rest_other = lax.optimization_barrier(
        (*normed_side, down_low, embedded, grad_core, grad_x, rest_other)
    )
    down_side = gather_side(down_low)
    embed_other = plane_swap(embedded[SPAN:], 4)
    embeddings = jnp.where(
        y == 0,
        jnp.stack([embedded[:SPAN], embed_other]),
        jnp.stack([embed_other, embedded[:SPAN]]),
    )

    grad_x = plane_swap(grad_x, 2)
    grads = swap_groups(grad_own, grad_x, grad_core)

    qkv_mine, qkv_other, token_near, token_far = call(
        attend_back_kernel,
        (*spots, queries, keys, values, lse, weights, near, far, first_grad, *grads),
        (SM, SM, SM, HB, HB, HB, VM, *[HB] * 8),
        [
            *[((LINE, HALF + 16, 3 * WIDE), BF16)] * 2,
            ((2 * OWN, WIDTH), F32),
            ((2 * OWN, WIDTH), BF16),
        ],
        [
            *[pltpu.VMEM((SLOTS, PAD), BF16)] * 3,
            pltpu.VMEM((WIDTH, 3 * PAD), BF16),
            *[pltpu.VMEM((2 * OWN, WIDTH), BF16)] * 2,
            pltpu.VMEM((OWN, WIDTH), F32),
            pltpu.VMEM((4, OWN, PAD), BF16),
            pltpu.VMEM((SLOTS, SPAN), F32),
            pltpu.VMEM((PAD, SLOTS), BF16),
            pltpu.VMEM((PAD, OWN), F32),
            pltpu.VMEM((SLOTS, 3 * PAD), BF16),
            pltpu.VMEM((SLOTS, PAD), F32),
            pltpu.VMEM((SLOTS, PAD), F32),
            pltpu.VMEM((WIDTH, 3 * PAD), BF16),
            pltpu.SemaphoreType.DMA((11,)),
        ],
        mebibytes=BIG,
        name="attend_back",
    )

    rest = rest_mine.astype(F32) + plane_swap(rest_other, 1).astype(F32)
    rest = rest.astype(BF16).reshape(LINE, 2, 64, WIDTH)
    kept = lax.dynamic_index_in_dim(rest, x, 1, keepdims=False)
    sent = lax.dynamic_index_in_dim(rest, 1 - x, 1, keepdims=False)
    sent = plane_swap(sent, 2)
    sent, token_far = lax.optimization_barrier((sent, token_far))
    rest = (kept.astype(F32) + sent.astype(F32)).astype(BF16)
    rest = rest.reshape(LINE, 2, 32, WIDTH)
    kept = lax.dynamic_index_in_dim(rest, y, 1, keepdims=False)
    sent = lax.dynamic_index_in_dim(rest, 1 - y, 1, keepdims=False)
    rest = (kept.astype(F32) + plane_swap(sent, 4).astype(F32)).astype(BF16)

    *down_side, token_near = lax.optimization_barrier((*down_side, token_near))
    slices_mine, slices_other = call(
        slice_grad_kernel,
        (scal, bias, own_parts, turns, parts[4], ups, down_weight, *normed_side, *down_side),
        (SM, VM, *[HB] * 13),
        [((LINE, 2 * HALF, WIDTH), BF16)] * 2,
        [
            pltpu.VMEM((PARTS, SLICE), BF16),
            pltpu.VMEM((2, LINE - 1, PARTS, SLICE), BF16),
            pltpu.VMEM((SHARD, SLICE), BF16),
            pltpu.VMEM((PIECE, WIDTH), BF16),
            pltpu.VMEM((PLANE, OWN, WIDTH), BF16),
            pltpu.VMEM((2, WIDTH, SLICE), F32),
            *[pltpu.VMEM((2, SLICE, WIDTH), BF16)] * 2,
            *[pltpu.VMEM((2, SLICE, WIDTH), F32)] * 2,
            pltpu.VMEM((2, WIDTH, SLICE), F32),
            pltpu.SemaphoreType.DMA((13,)),
        ],
        mebibytes=BIG,
        name="slice_grad",
    )
    slices_other = plane_swap(slices_other, 1)
    shard_parts = []
    for turn in range(LINE):
        total = slices_mine[turn].astype(F32) + slices_other[turn].astype(F32)
        shard_parts.append(jnp.concatenate([total.astype(BF16), rest[turn]]))
    shard_part = sum_turns(shard_parts)
    up_grad, down_grad, out_grad, proj_grad, late_rows, bias_rows = call(
        rest_shard_kernel,
        (scal, *gather_plane(shard_part)),
        (SM, *[VM] * 8),
        [
            ((SHARD, INNER), F32),
            ((WIDTH, WIDTH), F32),
            ((SHARD, WIDTH), F32),
            ((SHARD, EMBED), F32),
            ((8, SHARD), F32),
            ((PLANE, PIECE), F32),
        ],
        [pltpu.VMEM((PLANE, 2 * HALF + 32, WIDTH), BF16)],
        name="rest_shard",
    )
    bias_grad = bias_rows.reshape(-1)

    qkv_other = plane_swap(qkv_other, 4)
    qkv_sums = [
        (qkv_mine[turn].astype(F32) + qkv_other[turn].astype(F32)).astype(BF16)
        for turn in range(LINE)
    ]
    qkv_part = sum_turns(qkv_sums)
    qkv_grad, vectors_grad = call(
        qkv_shard_kernel,
        (scal, late_rows, *gather_plane(qkv_part)),
        (SM, *[VM] * 9),
        [((SHARD, 3 * WIDTH), F32), ((8, SHARD), F32)],
        [pltpu.VMEM((PLANE, HALF + 16, 3 * WIDE), BF16)],
        name="qkv_shard",
    )

    near_sum = (token_near + plane_swap(token_far, 1).astype(F32)).reshape(4, SPAN, WIDTH)
    to_y, to_x, to_d = (near_sum[i].astype(BF16) for i in (1, 2, 3))
    for_mine = near_sum[0] + plane_swap(to_x, 2).astype(F32)
    for_other = plane_swap(to_y, 4).astype(F32) + plane_swap(to_d, 6).astype(F32)
    tokens_grad = jnp.where(
        y == 0, jnp.stack([for_mine, for_other]), jnp.stack([for_other, for_mine])
    )
    return (
        embeddings,
        tokens_grad,
        qkv_grad,
        out_grad,
        up_grad,
        bias_grad,
        down_grad,
        proj_grad,
        vectors_grad,
    )


def body(*arrays):
    sequences, span, width = arrays[0].shape
    fits = (
        lax.axis_size("ctx") == PLANE
        and lax.axis_size("wa") == LINE
        and sequences == 2
        and span == SPAN
        and width == WIDTH
    )
    return (plane_body if fits else general_body)(*arrays)


def solution(mesh):
    in_specs = (
        P("wa", "ctx", None),
        P(),
        P(),
        P("wa", None),
        P("wa", None),
        P("wa", None),
        P("wa"),
        P("wa", None),
        P("wa", None),
        P(None, "wa"),
        P("wa", "ctx", None),
    )
    out_specs = (
        P("wa", "ctx", None),
        P("wa", "ctx", None),
        P("wa", None),
        P("wa", None),
        P("wa", None),
        P("wa"),
        P("wa", None),
        P("wa", None),
        P(None, "wa"),
    )
    return jax.shard_map(body, mesh=mesh, in_specs=in_specs, out_specs=out_specs, check_vma=False)
```

```python
from functools import partial

import jax
import jax.numpy as jnp
from jax import lax
from jax.experimental import pallas as pl
from jax.experimental.pallas import tpu as pltpu
from jax.sharding import PartitionSpec as P

H = 12
HEAD = 64


NEG_FILL = -1e30
NORM_EPS = 1e-06
ROOT_HALF = 0.7071067811865476
DENSITY_SCALE = 0.3989422804014327


def norm_rows(inputs, gain_row, shift_row):
    middle = jnp.mean(inputs, axis=-1, keepdims=True)
    center = inputs - middle
    spread = jnp.mean(center * center, axis=-1, keepdims=True)
    scaled = lax.rsqrt(spread + NORM_EPS)
    unit_rows = center * scaled
    return (unit_rows * gain_row + shift_row, unit_rows, scaled)


def norm_back(grad_in, unit_rows, scaled, gain_row):
    gain_grad = jnp.sum(grad_in * unit_rows, axis=(0, 1))
    shift_grad = jnp.sum(grad_in, axis=(0, 1))
    inner_grad = grad_in * gain_row
    centered = inner_grad - jnp.mean(inner_grad, axis=-1, keepdims=True)
    result = scaled * (
        centered - unit_rows * jnp.mean(inner_grad * unit_rows, axis=-1, keepdims=True)
    )
    return (result, gain_grad, shift_grad)


def gelu_both(inner_sum):
    normal_cdf = 0.5 * (1.0 + lax.erf(inner_sum * ROOT_HALF))
    density = jnp.exp(-0.5 * inner_sum * inner_sum) * DENSITY_SCALE
    return (inner_sum * normal_cdf, normal_cdf + inner_sum * density)


def split_tiles(key_rows, value_rows, key_valid):
    key_count = key_rows.shape[0]
    tile_width = 512
    tile_count = key_count // tile_width
    return (
        key_rows.reshape(tile_count, tile_width, H, HEAD),
        value_rows.reshape(tile_count, tile_width, H, HEAD),
        key_valid.reshape(tile_count, tile_width),
    )


def masked_scores(queries, key_tile, mask_tile):
    products = jnp.einsum("qhd,khd->hqk", queries, key_tile, preferred_element_type=jnp.float32)
    return jnp.where(mask_tile[None, None, :], products, NEG_FILL)


def attend_forward(queries, key_rows, value_rows, key_valid):
    key_tiles, value_tiles, mask_tiles = split_tiles(key_rows, value_rows, key_valid)
    row_span = queries.shape[0]

    def stats_step(running, portion):
        highest, summed = running
        key_tile, mask_tile = portion
        scores = masked_scores(queries, key_tile, mask_tile)
        new_peak = jnp.maximum(highest, jnp.max(scores, axis=-1))
        raised = jnp.where(mask_tile[None, None, :], jnp.exp(scores - new_peak[:, :, None]), 0.0)
        return ((new_peak, summed * jnp.exp(highest - new_peak) + jnp.sum(raised, axis=-1)), None)

    start_peak = jnp.full((H, row_span), NEG_FILL, jnp.float32)
    start_sum = jnp.zeros((H, row_span), jnp.float32)
    (highest, summed), _ = lax.scan(stats_step, (start_peak, start_sum), (key_tiles, mask_tiles))
    logsum = highest + jnp.log(summed)

    def value_step(running, portion):
        key_tile, value_tile, mask_tile = portion
        scores = masked_scores(queries, key_tile, mask_tile)
        prob_low = jnp.where(
            mask_tile[None, None, :], jnp.exp(scores - logsum[:, :, None]), 0.0
        ).astype(jnp.bfloat16)
        return (
            running
            + jnp.einsum("hqk,khd->qhd", prob_low, value_tile, preferred_element_type=jnp.float32),
            None,
        )

    attended, _ = lax.scan(
        value_step,
        jnp.zeros((row_span, H, HEAD), jnp.float32),
        (key_tiles, value_tiles, mask_tiles),
    )
    return (attended, logsum)


def attend_backward(
    queries, key_rows, value_rows, key_valid, logsum, delta_rows, grad_heads, with_keys
):
    key_tiles, value_tiles, mask_tiles = split_tiles(key_rows, value_rows, key_valid)

    def back_step(running, portion):
        key_tile, value_tile, mask_tile = portion
        scores = masked_scores(queries, key_tile, mask_tile)
        prob_rows = jnp.where(mask_tile[None, None, :], jnp.exp(scores - logsum[:, :, None]), 0.0)
        prob_grad = jnp.einsum(
            "qhd,khd->hqk", grad_heads, value_tile, preferred_element_type=jnp.float32
        )
        score_low = (prob_rows * (prob_grad - delta_rows[:, :, None])).astype(jnp.bfloat16)
        running = running + jnp.einsum(
            "hqk,khd->qhd", score_low, key_tile, preferred_element_type=jnp.float32
        )
        value_part = jnp.einsum(
            "hqk,qhd->khd",
            prob_rows.astype(jnp.bfloat16),
            grad_heads,
            preferred_element_type=jnp.float32,
        )
        key_part = jnp.einsum(
            "hqk,qhd->khd", score_low, queries, preferred_element_type=jnp.float32
        )
        return (running, (key_part, value_part))

    start_grad = jnp.zeros(queries.shape, jnp.float32)
    query_grad, pieces = lax.scan(back_step, start_grad, (key_tiles, value_tiles, mask_tiles))
    key_count = key_rows.shape[0]
    return (
        query_grad,
        pieces[0].reshape(key_count, H * HEAD),
        pieces[1].reshape(key_count, H * HEAD),
    )


def general_body(
    tokens,
    doc_lengths,
    group_deal,
    qkv_weight,
    out_weight,
    up_weight,
    up_bias,
    down_weight,
    proj_weight,
    vectors,
    cotangent,
):
    gathered = (
        lax.all_gather(qkv_weight, "wa", axis=0, tiled=True),
        lax.all_gather(out_weight, "wa", axis=0, tiled=True),
        lax.all_gather(up_weight, "wa", axis=0, tiled=True),
        lax.all_gather(up_bias, "wa", axis=0, tiled=True),
        lax.all_gather(down_weight, "wa", axis=0, tiled=True),
        lax.all_gather(proj_weight, "wa", axis=0, tiled=True),
        lax.all_gather(vectors, "wa", axis=1, tiled=True),
    )
    qkv_full, out_full, up_full, bias_full, down_full, proj_full, vector_full = gathered
    seq_count, group_rows, model_width = tokens.shape
    ctx_count = lax.axis_size("ctx")
    seq_start = lax.axis_index("wa") * seq_count
    my_lengths = lax.dynamic_slice_in_dim(doc_lengths, seq_start, seq_count, 0)
    my_deal = lax.dynamic_slice_in_dim(group_deal, seq_start, seq_count, 0)
    offsets = jnp.tile(jnp.arange(group_rows, dtype=jnp.int32), ctx_count)
    positions = jnp.repeat(my_deal, group_rows, axis=1) * group_rows + offsets[None, :]
    key_valid = positions < my_lengths[:, None]
    query_valid = lax.dynamic_slice_in_dim(
        key_valid, lax.axis_index("ctx") * group_rows, group_rows, 1
    )
    row_mask = query_valid.astype(jnp.float32)[:, :, None]
    query_scale = HEAD ** (-0.5)
    mixed_rows = jnp.einsum("scd,de->sce", tokens, qkv_full, preferred_element_type=jnp.float32)
    queries = ((mixed_rows[:, :, :model_width] + vector_full[0]) * query_scale).astype(jnp.bfloat16)
    key_rows = mixed_rows[:, :, model_width : 2 * model_width].astype(jnp.bfloat16)
    value_rows = (mixed_rows[:, :, 2 * model_width :] + vector_full[1]).astype(jnp.bfloat16)
    all_keys, all_values = (
        lax.all_gather(key_rows, "ctx", axis=1, tiled=True),
        lax.all_gather(value_rows, "ctx", axis=1, tiled=True),
    )
    query_heads = queries.reshape(seq_count, group_rows, H, HEAD)
    attended, logsum = jax.vmap(attend_forward)(query_heads, all_keys, all_values, key_valid)
    attended_low = attended.reshape(seq_count, group_rows, model_width).astype(jnp.bfloat16)
    first_sum = tokens.astype(jnp.float32) + (
        jnp.einsum("scd,de->sce", attended_low, out_full, preferred_element_type=jnp.float32)
        + vector_full[2]
    )
    normed, unit_one, scale_one = norm_rows(first_sum, vector_full[3], vector_full[4])
    normed_low = normed.astype(jnp.bfloat16)
    inner_sum = (
        jnp.einsum("scd,df->scf", normed_low, up_full, preferred_element_type=jnp.float32)
        + bias_full
    )
    active, gelu_slope = gelu_both(inner_sum)
    active_low = active.astype(jnp.bfloat16)
    second_sum = normed + (
        jnp.einsum("scf,fd->scd", active_low, down_full, preferred_element_type=jnp.float32)
        + vector_full[5]
    )
    final_sum, unit_two, scale_two = norm_rows(second_sum, vector_full[6], vector_full[7])
    final_low = final_sum.astype(jnp.bfloat16)
    project = jnp.einsum("scd,de->sce", final_low, proj_full, preferred_element_type=jnp.float32)
    inverse = lax.rsqrt(jnp.sum(project * project, axis=-1, keepdims=True) + NORM_EPS)
    direction = project * inverse
    embeddings = (direction * row_mask).astype(jnp.bfloat16)
    upstream = cotangent.astype(jnp.float32) * row_mask
    project_grad = (
        inverse * (upstream - direction * jnp.sum(upstream * direction, axis=-1, keepdims=True))
    ).astype(jnp.bfloat16)
    proj_grad = jnp.einsum(
        "scd,sce->de", final_low, project_grad, preferred_element_type=jnp.float32
    )
    final_grad = jnp.einsum(
        "sce,de->scd", project_grad, proj_full, preferred_element_type=jnp.float32
    )
    second_grad, gain_two, shift_two = norm_back(final_grad, unit_two, scale_two, vector_full[6])
    down_low = second_grad.astype(jnp.bfloat16)
    down_grad = jnp.einsum("scf,scd->fd", active_low, down_low, preferred_element_type=jnp.float32)
    inner_grad = (
        jnp.einsum("scd,fd->scf", down_low, down_full, preferred_element_type=jnp.float32)
        * gelu_slope
    )
    bias_grad = jnp.sum(inner_grad, axis=(0, 1))
    inner_low = inner_grad.astype(jnp.bfloat16)
    up_grad = jnp.einsum("scd,scf->df", normed_low, inner_low, preferred_element_type=jnp.float32)
    normed_grad = second_grad + jnp.einsum(
        "scf,df->scd", inner_low, up_full, preferred_element_type=jnp.float32
    )
    first_grad, gain_one, shift_one = norm_back(normed_grad, unit_one, scale_one, vector_full[3])
    first_low = first_grad.astype(jnp.bfloat16)
    out_grad = jnp.einsum(
        "scd,sce->de", attended_low, first_low, preferred_element_type=jnp.float32
    )
    attended_grad = jnp.einsum(
        "sce,de->scd", first_low, out_full, preferred_element_type=jnp.float32
    ).astype(jnp.bfloat16)
    grad_heads = attended_grad.reshape(seq_count, group_rows, H, HEAD)
    delta_rows = jnp.sum(grad_heads.astype(jnp.float32) * attended, axis=-1)
    delta_heads = jnp.swapaxes(delta_rows, 1, 2)
    query_grad, key_terms, value_terms = jax.vmap(partial(attend_backward, with_keys=True))(
        query_heads, all_keys, all_values, key_valid, logsum, delta_heads, grad_heads
    )
    key_grad, value_grad = (
        lax.psum_scatter(
            key_terms.astype(jnp.bfloat16), "ctx", scatter_dimension=1, tiled=True
        ).astype(jnp.float32),
        lax.psum_scatter(
            value_terms.astype(jnp.bfloat16), "ctx", scatter_dimension=1, tiled=True
        ).astype(jnp.float32),
    )
    query_part = (
        query_grad.reshape(seq_count, group_rows, model_width).astype(jnp.bfloat16) * query_scale
    )
    value_part = value_grad.astype(jnp.bfloat16)
    mixed_grad = jnp.concatenate([query_part, key_grad.astype(jnp.bfloat16), value_part], axis=-1)
    qkv_grad = jnp.einsum("scd,sce->de", tokens, mixed_grad, preferred_element_type=jnp.float32)
    tokens_grad = first_grad + jnp.einsum(
        "sce,de->scd", mixed_grad, qkv_full, preferred_element_type=jnp.float32
    )
    vectors_grad = jnp.stack(
        [
            jnp.sum(query_part.astype(jnp.float32), axis=(0, 1)),
            jnp.sum(value_part.astype(jnp.float32), axis=(0, 1)),
            jnp.sum(first_grad, axis=(0, 1)),
            gain_one,
            shift_one,
            jnp.sum(second_grad, axis=(0, 1)),
            gain_two,
            shift_two,
        ],
        axis=0,
    )
    owned = (
        lax.psum_scatter(
            qkv_grad.astype(jnp.bfloat16), "wa", scatter_dimension=0, tiled=True
        ).astype(jnp.float32),
        lax.psum_scatter(
            out_grad.astype(jnp.bfloat16), "wa", scatter_dimension=0, tiled=True
        ).astype(jnp.float32),
        lax.psum_scatter(
            up_grad.astype(jnp.bfloat16), "wa", scatter_dimension=0, tiled=True
        ).astype(jnp.float32),
        lax.psum_scatter(
            bias_grad.astype(jnp.bfloat16), "wa", scatter_dimension=0, tiled=True
        ).astype(jnp.float32),
        lax.psum_scatter(
            down_grad.astype(jnp.bfloat16), "wa", scatter_dimension=0, tiled=True
        ).astype(jnp.float32),
        lax.psum_scatter(
            proj_grad.astype(jnp.bfloat16), "wa", scatter_dimension=0, tiled=True
        ).astype(jnp.float32),
        lax.psum_scatter(
            vectors_grad.astype(jnp.bfloat16), "wa", scatter_dimension=1, tiled=True
        ).astype(jnp.float32),
    )
    summed = (
        lax.psum(owned[0].astype(jnp.bfloat16), "ctx").astype(jnp.float32),
        lax.psum(owned[1].astype(jnp.bfloat16), "ctx").astype(jnp.float32),
        lax.psum(owned[2].astype(jnp.bfloat16), "ctx").astype(jnp.float32),
        lax.psum(owned[3].astype(jnp.bfloat16), "ctx").astype(jnp.float32),
        lax.psum(owned[4].astype(jnp.bfloat16), "ctx").astype(jnp.float32),
        lax.psum(owned[5].astype(jnp.bfloat16), "ctx").astype(jnp.float32),
        lax.psum(owned[6].astype(jnp.bfloat16), "ctx").astype(jnp.float32),
    )
    return (
        embeddings,
        tokens_grad,
        summed[0],
        summed[1],
        summed[2],
        summed[3],
        summed[4],
        summed[5],
        summed[6],
    )


PLANE = 8
LINE = 4
SPAN = 128
OWN = 2 * SPAN
WIDTH = H * HEAD
INNER = 4 * WIDTH
SHARD = WIDTH // LINE
HALF = SHARD // 2
PIECE = INNER // LINE // PLANE
SLICE = LINE * PIECE
HEADS = 3
WIDE = HEADS * HEAD
PAD = 256
SLOTS = PLANE * SPAN
BLOCK = SHARD // 4
FIRST = SHARD + BLOCK
SIDE = PIECE + 16
PARTS = FIRST + 2 * SIDE
QUARTER = HALF // 2
COLS = HALF + QUARTER
EMBED = 128
ORDER = (0, 4, 2, 6, 1, 5, 3, 7)
NEAR = (0, 2, 1, 3)
F32 = jnp.float32
BF16 = jnp.bfloat16

NN = ((1,), (0,))
NT = ((1,), (1,))
TN = ((0,), (0,))


def dot(left, right, dims):
    return lax.dot_general(left, right, (dims, ((), ())), preferred_element_type=F32)


def plane_swap(array, bits):
    return lax.ppermute(array, "ctx", [(i, i ^ bits) for i in range(PLANE)])


def line_turn(array, step):
    return lax.ppermute(array, "wa", [(i, (i + step) % LINE) for i in range(LINE)])


def line_turns(array):
    return [line_turn(array, step) for step in range(1, LINE)]


def relay(from_x, from_y, core):
    passed = jnp.where(core == 0, from_y, from_x)
    pairs = [(i, i ^ 2 if i % 2 == 0 else i ^ 4) for i in range(PLANE)]
    return lax.ppermute(passed, "ctx", pairs)


def pick(array, index):
    return lax.dynamic_index_in_dim(array, index, 0, keepdims=False)


COST = {'cut': 3, 'vectors': 1, 'attend': 12, 'out': 3, 'middle': 17, 'attend_back': 18, 'rest_shard': 4, 'qkv_shard': 2, 'slice_other': 6, 'slice_mine': 6}
VM = pl.BlockSpec(memory_space=pltpu.VMEM)
SM = pl.BlockSpec(memory_space=pltpu.SMEM)
HB = pl.BlockSpec(memory_space=pl.ANY)
BIG = 56


def call(kernel, inputs, spaces, outputs, scratch=(), mebibytes=32, name=None, own=()):
    shapes = [jax.ShapeDtypeStruct(shape, kind) for shape, kind in outputs]
    return pl.pallas_call(
        kernel,
        out_shape=shapes,
        in_specs=list(spaces),
        out_specs=[HB if i in own else VM for i in range(len(shapes))],
        scratch_shapes=list(scratch),
        compiler_params=pltpu.CompilerParams(vmem_limit_bytes=mebibytes << 20),
        cost_estimate=pl.CostEstimate(flops=int(COST[name] * 1e9), bytes_accessed=1, transcendentals=0),
        name=name,
    )(*inputs)


def place_of(scal):
    return scal[0], scal[1]


def shard_of_turn(line, turn):
    return lax.rem(line - turn + LINE, LINE)


def turn_ahead(line, turn):
    return lax.rem(line + turn, LINE)


def norm_forward(rows):
    middle = jnp.mean(rows, axis=-1, keepdims=True)
    center = rows - middle
    scaled = lax.rsqrt(jnp.mean(center * center, axis=-1, keepdims=True) + NORM_EPS)
    return center * scaled, scaled


def norm_reverse(grad, unit, scaled, gain):
    inner = grad * gain
    return scaled * (
        inner
        - jnp.mean(inner, axis=-1, keepdims=True)
        - unit * jnp.mean(inner * unit, axis=-1, keepdims=True)
    )


def cut_kernel(
    scal, vectors, bias, proj, qkv, up, down, out,
    cols_ref, ups_ref, own_ref,
    qkv_held, up_held, down_held, out_held, sems,
):
    me, line = place_of(scal)
    core = lax.rem(me, 2)
    copies = [
        pltpu.make_async_copy(qkv, qkv_held, sems.at[0]),
        pltpu.make_async_copy(up, up_held, sems.at[1]),
        pltpu.make_async_copy(
            down.at[pl.ds(pl.multiple_of(me * PIECE, 16), PIECE)], down_held, sems.at[2]
        ),
        pltpu.make_async_copy(
            out.at[pl.ds(pl.multiple_of(lax.div(me, 2) * BLOCK, 16), BLOCK)], out_held, sems.at[3]
        ),
    ]
    for copy in copies:
        copy.start()
    rows = [vectors[...].astype(F32)]
    rows += [bias[:, a * SHARD : (a + 1) * SHARD].astype(F32) for a in range(LINE)]
    rows = jnp.concatenate(rows + [jnp.zeros((4, SHARD), F32)])
    own_ref[PARTS + COLS :, :SHARD] = rows.astype(BF16)
    own_ref[PARTS + COLS :, SHARD:] = jnp.zeros((16, SLICE - SHARD), BF16)
    for side in range(2):
        start = FIRST + side * SIDE + PIECE
        for t in range(3):
            own_ref[start : start + 16, t * EMBED : (t + 1) * EMBED] = proj[
                pl.ds(pl.multiple_of(core * HALF + 16 * (3 * side + t), 16), 16), :
            ]
    copies[0].wait()
    for g in range(4):

        @pl.when(lax.rem(me, 4) == g)
        def _():
            for part in range(3):
                start = part * WIDTH + g * WIDE
                cols_ref[:, part * WIDE : (part + 1) * WIDE] = qkv_held[:, start : start + WIDE]

    base = lax.div(me, 4) * HALF
    rows = cols_ref[pl.ds(pl.multiple_of(base, 16), HALF), :]
    own_ref[PARTS : PARTS + HALF, :] = rows[:, :SLICE]
    for side in range(2):
        own_ref[PARTS + HALF : PARTS + COLS, side * WIDE : (side + 1) * WIDE] = rows[
            side * QUARTER : (side + 1) * QUARTER, SLICE:
        ]
    copies[1].wait()
    for k in range(PLANE):
        for s in range(LINE):
            start = s * PLANE * PIECE + k * PIECE
            ups_ref[k, :, s * PIECE : (s + 1) * PIECE] = up_held[:, start : start + PIECE]
    own_ref[:SHARD] = ups_ref[me]
    copies[2].wait()
    for side in range(2):
        start = FIRST + side * SIDE
        own_ref[start : start + PIECE] = down_held[:, side * SLICE : (side + 1) * SLICE]
    copies[3].wait()
    own_ref[SHARD:FIRST] = out_held[:, pl.ds(pl.multiple_of(core * SLICE, 128), SLICE)]


def vectors_kernel(scal, own, halves, full_ref, bias_ref, ends_ref, held):
    me, line = place_of(scal)
    held[line] = own[PARTS + COLS :, :SHARD].astype(F32)
    for turn in range(1, LINE):
        held[shard_of_turn(line, turn)] = halves[turn - 1, COLS:, :SHARD].astype(F32)
    for a in range(LINE):
        full_ref[:, a * SHARD : (a + 1) * SHARD] = held[a, :8, :]
        for k in range(PLANE):
            start = (k % 2) * PIECE
            bias_ref[k : k + 1, a * PIECE : (a + 1) * PIECE] = held[
                a, 8 + k // 2 : 9 + k // 2, start : start + PIECE
            ]
    ends_ref[...] = jnp.zeros((8, PAD), F32)
    ends_ref[:, :WIDE] = held[lax.rem(me, 4), :8, :]


def slots_left(scal, lengths, deal, place):
    me, line = place_of(scal)
    seq = 2 * line + lax.div(me, 4)
    return lengths[seq] - deal[seq, me ^ ORDER[place]] * SPAN


def fill_mask(scal, lengths, deal, mask):
    rows = lax.broadcasted_iota(jnp.int32, (SPAN, SPAN), 0)
    for place in range(PLANE):
        limit = slots_left(scal, lengths, deal, place)
        mask[place * SPAN : (place + 1) * SPAN, :] = jnp.where(rows < limit, 0.0, NEG_FILL)


def head_lanes(h):
    lanes = lax.broadcasted_iota(jnp.int32, (OWN, 128), 1)
    return (lanes >= HEAD) if h % 2 else (lanes < HEAD)


def attend_kernel(
    scal, lengths, deal, ends, own_cols, halves, others, near, far,
    q_out, k_out, v_out, w_out, own_ref, core_ref, x_ref, lse_ref,
    raw, mask, v_turned, o_turned, att, q_ref, k_ref, v_ref, w_ref, sems,
):
    me, line = place_of(scal)
    y = lax.div(me, 4)
    raw[pl.ds(pl.multiple_of(line * SHARD, 16), SHARD), :] = own_cols[...]
    for turn in range(1, LINE):
        base = shard_of_turn(line, turn) * SHARD
        for source, side in ((halves, y), (others, 1 - y)):
            start = base + side * HALF
            at = pl.ds(pl.multiple_of(start, 16), HALF)
            raw[at, :SLICE] = source[turn - 1, :HALF, :]
            for i in range(2):
                at = pl.ds(pl.multiple_of(start + i * QUARTER, 16), QUARTER)
                raw[at, SLICE:] = source[turn - 1, HALF:COLS, i * WIDE : (i + 1) * WIDE]
    fill_mask(scal, lengths, deal, mask)
    for part in range(3):
        w_ref[:, part * PAD : part * PAD + WIDE] = raw[:, part * WIDE : (part + 1) * WIDE]
        w_ref[:, part * PAD + WIDE : (part + 1) * PAD] = jnp.zeros((WIDTH, PAD - WIDE), BF16)
    for t in range(4):
        source = (near, far)[t // 2]
        rows = source[(t % 2) * OWN : (t % 2 + 1) * OWN, :]
        mixed = dot(rows, w_ref[...], NN)
        at = slice(t * OWN, (t + 1) * OWN)
        q_ref[at, :] = ((mixed[:, :PAD] + ends[0:1, :]) * (HEAD ** (-0.5))).astype(BF16)
        k_ref[at, :] = mixed[:, PAD : 2 * PAD].astype(BF16)
        values = mixed[:, 2 * PAD :] + ends[1:2, :]
        v_ref[at, :] = values.astype(BF16)
        v_turned[:, at] = values.T.astype(BF16)

    copies = [
        pltpu.make_async_copy(source, target, sems.at[i])
        for i, (source, target) in enumerate(
            ((q_ref, q_out), (k_ref, k_out), (v_ref, v_out), (w_ref, w_out))
        )
    ]
    for copy in copies:
        copy.start()
    o_turned[WIDE:, :] = jnp.zeros((PAD - WIDE, OWN), F32)

    def tile(t, carry):
        at = pl.ds(pl.multiple_of(t * OWN, OWN), OWN)
        for h in range(HEADS):
            cut = slice((h // 2) * 128, (h // 2 + 1) * 128)
            q_tile = jnp.where(head_lanes(h), q_ref[at, cut], jnp.zeros((), BF16))
            scores = dot(k_ref[:, cut], q_tile, NT)
            scores = scores + jnp.concatenate([mask[...], mask[...]], axis=1)
            peak = jnp.max(scores, axis=0, keepdims=True)
            raised = jnp.exp(scores - peak)
            total = jnp.sum(raised, axis=0, keepdims=True)
            rows = slice(h * HEAD, (h + 1) * HEAD)
            o_turned[rows, :] = dot(v_turned[rows, :], raised.astype(BF16), NN) * (1.0 / total)
            lse_ref[t, h : h + 1, :] = peak + jnp.log(total)
        att[t] = o_turned[...].T.astype(BF16)
        return carry

    lax.fori_loop(0, 4, tile, 0)
    own_ref[...] = att[0]
    core_ref[...] = att[2]
    x_ref[0] = att[1]
    x_ref[1] = att[3]
    for copy in copies:
        copy.wait()


def attend_back_kernel(
    scal, lengths, deal, q_ref, k_ref, v_ref, lse, weights, near, far, first_grad, g0, g1, g2, g3,
    mine_out, other_out, near_out, far_out,
    mine_ref, other_ref, near_ref, far_ref,
    q_held, k_held, v_held, w_held, near_held, far_held, first_held, grads,
    mask, k_turned, q_turned, mixed, key_sum, value_sum, part, sems,
):
    sources = (k_ref, q_ref, v_ref, g0, g1.at[0], g2, g3, weights, near, far, first_grad)
    targets = (k_held, q_held, v_held, grads.at[0], grads.at[1], grads.at[2], grads.at[3])
    targets += (w_held, near_held, far_held, first_held)
    copies = [
        pltpu.make_async_copy(source, target, sems.at[i])
        for i, (source, target) in enumerate(zip(sources, targets, strict=True))
    ]
    for copy in copies:
        copy.start()
    fill_mask(scal, lengths, deal, mask)
    copies[0].wait()
    for t in range(4):
        at = slice(t * OWN, (t + 1) * OWN)
        k_turned[:, at] = k_held[at, :].astype(F32).T.astype(BF16)
    key_sum[...] = jnp.zeros_like(key_sum)
    value_sum[...] = jnp.zeros_like(value_sum)
    q_turned[WIDE:, :] = jnp.zeros((PAD - WIDE, OWN), F32)
    for copy in copies[1:7]:
        copy.wait()

    def tile(t, carry):
        at = pl.ds(pl.multiple_of(t * OWN, OWN), OWN)
        for h in range(HEADS):
            cut = slice((h // 2) * 128, (h // 2 + 1) * 128)
            rows = slice(h * HEAD, (h + 1) * HEAD)
            q_tile = jnp.where(head_lanes(h), q_held[at, cut], jnp.zeros((), BF16))
            g_tile = jnp.where(head_lanes(h), grads[t, :, cut], jnp.zeros((), BF16))
            scores = dot(k_held[:, cut], q_tile, NT)
            scores = scores + jnp.concatenate([mask[...], mask[...]], axis=1)
            probs = jnp.exp(scores - lse[t, h : h + 1, :])
            prob_grad = dot(v_held[:, cut], g_tile, NT)
            delta = jnp.sum(probs * prob_grad, axis=0, keepdims=True)
            score_low = (probs * (prob_grad - delta)).astype(BF16)
            q_turned[rows, :] = dot(k_turned[rows, :], score_low, NN)
            key_sum[:, cut] += dot(score_low, q_tile, NN)
            value_sum[:, cut] += dot(probs.astype(BF16), g_tile, NN)
        low = q_turned[...].T.astype(BF16)
        mixed[at, :PAD] = (low.astype(F32) * (HEAD ** (-0.5))).astype(BF16)
        return carry

    lax.fori_loop(0, 4, tile, 0)
    mixed[:, PAD : 2 * PAD] = key_sum[...].astype(BF16)
    mixed[:, 2 * PAD :] = value_sum[...].astype(BF16)

    me, line = place_of(scal)
    y = lax.div(me, 4)
    for copy in copies[7:]:
        copy.wait()
    for i in range(3):
        cut = slice(i * 256, (i + 1) * 256)
        part[cut, :] = (
            dot(near_held[:, cut], mixed[: 2 * OWN, :], TN) + dot(far_held[:, cut], mixed[2 * OWN :, :], TN)
        ).astype(BF16)
    sums = jnp.sum(mixed[...].astype(F32), axis=0, keepdims=True)
    sums = jnp.concatenate([sums, jnp.zeros((15, 3 * PAD), F32)]).astype(BF16)
    for turn in range(LINE):
        base = turn_ahead(line, turn) * SHARD
        for target, side in ((mine_ref, y), (other_ref, 1 - y)):
            rows = part[pl.ds(pl.multiple_of(base + side * HALF, 16), HALF), :]
            for p in range(3):
                to = slice(p * WIDE, (p + 1) * WIDE)
                target[turn, :HALF, to] = rows[:, p * PAD : p * PAD + WIDE]
                target[turn, HALF:, to] = sums[:, p * PAD : p * PAD + WIDE]
    outs = [
        pltpu.make_async_copy(source, target, sems.at[11 + i])
        for i, (source, target) in enumerate(
            (
                (other_ref, other_out),
                (mine_ref, mine_out),
                (far_ref, far_out),
                (near_ref, near_out),
            )
        )
    ]
    outs[0].start()
    outs[1].start()
    for t in (2, 3, 0, 1):
        at = slice(t * OWN, (t + 1) * OWN)
        token_part = dot(mixed[at, :], w_held[...], NT)
        if t == 0:
            near_ref[at, :] = token_part + first_held[...]
        elif t == 1:
            near_ref[at, :] = token_part
        else:
            far_ref[(t - 2) * OWN : (t - 1) * OWN, :] = token_part.astype(BF16)
        if t == 3:
            outs[2].start()
    outs[3].start()
    for copy in outs:
        copy.wait()


def out_kernel(
    scal, near, full, out_shard, a0, a1, a2, a3, p0, p1, p2, p3, p4, p5, p6, p7,
    sum_ref, low_ref,
    out_ref, sem,
):
    me, line = place_of(scal)
    group = lax.rem(me, 4)
    pieces = (p0, p1, p2, p3, p4, p5, p6, p7)
    copies = []
    for place, bits in enumerate(ORDER):
        k = me ^ bits
        rows = pl.ds(pl.multiple_of(lax.div(k, 2) * BLOCK, 16), BLOCK)
        lanes = pl.ds(pl.multiple_of(lax.rem(k, 2) * SLICE, 128), SLICE)
        for turn in range(1, LINE):
            copies.append(
                pltpu.make_async_copy(
                    pieces[place].at[turn - 1, pl.ds(SHARD, BLOCK)],
                    out_ref.at[shard_of_turn(line, turn), rows, lanes],
                    sem,
                )
            )
    for copy in copies:
        copy.start()
    for z in range(LINE):
        out_ref[z, SHARD:, :] = jnp.zeros((PAD - SHARD, WIDTH), BF16)
    out_ref[line, :SHARD, :] = out_shard[...]
    rows = near[:OWN, :].astype(F32) + full[2:3, :]
    filled = out_ref.at[pl.ds(0, LINE - 1), pl.ds(0, SHARD)]
    pltpu.make_async_copy(filled, filled, sem).wait()
    for i, source in enumerate((a0[...], a1[0], a2[...], a3[...])):
        rows = rows + dot(source, out_ref[group ^ NEAR[i]], NN)
    sum_ref[...] = rows
    unit, _ = norm_forward(rows)
    low_ref[...] = (unit * full[3:4, :] + full[4:5, :]).astype(BF16)


def weight_copies(ups, down, parts, up_own, down_own, held, sems):
    copies = [
        pltpu.make_async_copy(ups, up_own, sems.at[PLANE]),
        pltpu.make_async_copy(down, down_own, sems.at[PLANE + 1]),
    ]
    for place in range(PLANE):
        copies.append(pltpu.make_async_copy(parts[place], held.at[place], sems.at[place]))
    return copies


def place_up(scal, place, up_own, held, up_all):
    me, line = place_of(scal)
    at = pl.ds(pl.multiple_of(line * SHARD, 16), SHARD)
    up_all[place, at, :] = up_own[me ^ ORDER[place]]
    for turn in range(1, LINE):
        at = pl.ds(pl.multiple_of(shard_of_turn(line, turn) * SHARD, 16), SHARD)
        up_all[place, at, :] = held[place, turn - 1, :SHARD, :]


def place_down(scal, place, down_own, held, down_all):
    me, line = place_of(scal)
    at = pl.ds(pl.multiple_of(line * PIECE, 16), PIECE)
    start = pl.multiple_of((me ^ ORDER[place]) * PIECE, 16)
    down_all[place, at, :] = down_own[pl.ds(start, PIECE), :]
    for turn in range(1, LINE):
        at = pl.ds(pl.multiple_of(shard_of_turn(line, turn) * PIECE, 16), PIECE)
        for side in range(2):
            start = FIRST + side * SIDE
            down_all[place, at, side * SLICE : (side + 1) * SLICE] = held[
                place, turn - 1, start : start + PIECE, :
            ]


def place_out(scal, place, held, out_all):
    me, line = place_of(scal)
    k = me ^ ORDER[place]
    rows = pl.ds(pl.multiple_of(lax.div(k, 2) * BLOCK, 16), BLOCK)
    lanes = pl.ds(pl.multiple_of(lax.rem(k, 2) * SLICE, 128), SLICE)
    for turn in range(1, LINE):
        out_all[shard_of_turn(line, turn), rows, lanes] = held[place, turn - 1, SHARD:FIRST, :]


def middle_kernel(
    scal, lengths, deal, first_sum, full, bias, proj_shard, out_shard, cot_mine, cot_other, a0, a1, a2, a3, ups, down, p0, p1, p2, p3, p4, p5, p6, p7,
    embed_ref, low_out, first_out, own_out, core_out, x_out, mine_out, other_out,
    low_ref, first_ref, own_ref, core_ref, x_ref, mine_ref, other_ref,
    up_own, down_own, held, up_all, down_all, out_all, proj_all, slopes, proj_part, bias_sum, out_part, sems,
):
    copies = weight_copies(
        ups, down, (p0, p1, p2, p3, p4, p5, p6, p7), up_own, down_own, held, sems
    )
    for copy in copies:
        copy.start()
    me, line = place_of(scal)
    core, group = lax.rem(me, 2), lax.rem(me, 4)
    proj_all[pl.ds(pl.multiple_of(line * SHARD, 16), SHARD), :] = proj_shard[...]

    unit_one, scale_one = norm_forward(first_sum[...])
    normed = unit_one * full[3:4, :] + full[4:5, :]
    normed_low = normed.astype(BF16)
    second_sum = normed + full[5:6, :]
    for z in range(LINE):
        out_all[z, SHARD:, :] = jnp.zeros((PAD - SHARD, WIDTH), BF16)
    out_all[line, :SHARD, :] = out_shard[...]
    copies[0].wait()
    copies[1].wait()
    for place, bits in enumerate(ORDER):
        copies[2 + place].wait()
        place_up(scal, place, up_own, held, up_all)
        place_down(scal, place, down_own, held, down_all)
        place_out(scal, place, held, out_all)
        inner = dot(normed_low, up_all[place], NN) + bias[pl.ds(me ^ bits, 1), :]
        active, slope = gelu_both(inner)
        slopes[place] = slope
        second_sum = second_sum + dot(active.astype(BF16), down_all[place], NN)
    unit, scaled = norm_forward(second_sum)
    final_low = (unit * full[6:7, :] + full[7:8, :]).astype(BF16)
    for place in (0, 4):
        half = core if place == 0 else 1 - core
        for turn in range(1, LINE):
            base = shard_of_turn(line, turn) * SHARD + half * HALF
            for t in range(6):
                start = FIRST + (t // 3) * SIDE + PIECE
                proj_all[pl.ds(pl.multiple_of(base + 16 * t, 16), 16), :] = held[
                    place, turn - 1, start : start + 16, (t % 3) * EMBED : (t % 3 + 1) * EMBED
                ]
    project = dot(final_low, proj_all[...], NN)
    inverse = lax.rsqrt(jnp.sum(project * project, axis=-1, keepdims=True) + NORM_EPS)
    direction = project * inverse
    rows = lax.broadcasted_iota(jnp.int32, (SPAN, EMBED), 0)
    keep = jnp.concatenate(
        [
            jnp.where(rows < slots_left(scal, lengths, deal, i), 1.0, 0.0).astype(F32)
            for i in range(2)
        ]
    )
    embed_ref[...] = (direction * keep).astype(BF16)
    upstream = jnp.concatenate([cot_mine[...], cot_other[...]]).astype(F32) * keep
    project_grad = (
        inverse * (upstream - direction * jnp.sum(upstream * direction, axis=-1, keepdims=True))
    ).astype(BF16)
    proj_part[...] = dot(final_low, project_grad, TN).astype(BF16)
    final_grad = dot(project_grad, proj_all[...], NT)
    second_grad = norm_reverse(final_grad, unit, scaled, full[6:7, :])
    down_low = second_grad.astype(BF16)
    low_ref[...] = down_low
    outs = [
        pltpu.make_async_copy(source, target, sems.at[PLANE + 2 + i])
        for i, (source, target) in enumerate(
            (
                (low_ref, low_out),
                (x_ref, x_out),
                (core_ref, core_out),
                (own_ref, own_out),
                (first_ref, first_out),
                (other_ref, other_out),
                (mine_ref, mine_out),
            )
        )
    ]
    outs[0].start()

    normed_grad = second_grad
    for place, bits in enumerate(ORDER):
        inner_grad = dot(down_low, down_all[place], NT) * slopes[place]
        bias_sum[pl.ds(me ^ bits, 1), :] = jnp.sum(inner_grad, axis=0, keepdims=True)
        normed_grad = normed_grad + dot(inner_grad.astype(BF16), up_all[place], NT)
    first_grad = norm_reverse(normed_grad, unit_one, scale_one, full[3:4, :])
    first_ref[...] = first_grad
    first_low = first_grad.astype(BF16)
    for i, target in enumerate((own_ref, x_ref.at[0], core_ref, x_ref.at[1])):
        target[...] = dot(first_low, out_all[group ^ NEAR[i]], NT).astype(BF16)
    for copy in outs[1:5]:
        copy.start()
    small = jnp.concatenate(
        [
            jnp.sum(first_grad, axis=0, keepdims=True),
            jnp.sum(normed_grad * unit_one, axis=0, keepdims=True),
            jnp.sum(normed_grad, axis=0, keepdims=True),
            jnp.sum(second_grad, axis=0, keepdims=True),
            jnp.sum(final_grad * unit, axis=0, keepdims=True),
            jnp.sum(final_grad, axis=0, keepdims=True),
            jnp.zeros((2, WIDTH), F32),
        ]
    )
    tail = jnp.concatenate([bias_sum[...], jnp.zeros((8, WIDTH - SLICE), F32)], axis=1)
    small = jnp.concatenate([small, tail]).astype(BF16)
    for i, source in enumerate((a0[...], a1[0], a2[...], a3[...])):
        z = group ^ NEAR[i]
        turn = lax.rem(z - line + LINE, LINE)
        out_part[i] = dot(source, first_low, TN).astype(BF16)
        for target, half in ((mine_ref, core), (other_ref, 1 - core)):
            base = half * HALF
            target[turn, :HALF, :] = out_part[i, pl.ds(pl.multiple_of(base, 16), HALF), :]
            for t in range(6):
                target[turn, HALF : HALF + 16, t * EMBED : (t + 1) * EMBED] = proj_part[
                    pl.ds(pl.multiple_of(z * SHARD + base + 16 * t, 16), 16), :
                ]
            target[turn, HALF + 16 :, :] = small
    outs[5].start()
    outs[6].start()
    for copy in outs:
        copy.wait()


def slice_grad_kernel(
    other, scal, bias, turns, ups, down, n0, n1, n2, n3, d0, d1, d2, d3,
    part_ref,
    held, ups_held, down_held, slots, up_rows, up_turned, down_rows, up_sum, down_sum, up_back,
    sems,
):
    me, line = place_of(scal)
    k = me ^ 1 if other else me
    copies = [
        pltpu.make_async_copy(turns, held, sems.at[0]),
        pltpu.make_async_copy(ups.at[k], ups_held, sems.at[1]),
        pltpu.make_async_copy(
            down.at[pl.ds(pl.multiple_of(k * PIECE, 16), PIECE)], down_held, sems.at[2]
        ),
    ]
    for j, source in enumerate((n0, d0, n1, d1, n2, d2, n3, d3)):
        copies.append(pltpu.make_async_copy(source, slots.at[j], sems.at[3 + j]))
    for copy in copies:
        copy.start()
    for copy in copies[:3]:
        copy.wait()
    for turn in range(LINE):
        z = shard_of_turn(line, turn)
        rows = held[turn - 1, :SHARD, :] if turn else ups_held[...]
        up_rows[pl.ds(pl.multiple_of(z * SHARD, 16), SHARD), :] = rows.astype(F32)
        at = pl.ds(pl.multiple_of(z * PIECE, 16), PIECE)
        if turn == 0:
            down_rows[at, :] = down_held[...]
            continue
        for side in range(2):
            start = FIRST + side * SIDE
            down_rows[at, side * SLICE : (side + 1) * SLICE] = held[
                turn - 1, start : start + PIECE, :
            ]
    up_turned[...] = up_rows[...].T.astype(BF16)
    bias_rows = jnp.broadcast_to(bias[pl.ds(k, 1), :], (128, SLICE)).T
    bias_rows = jnp.concatenate([bias_rows, bias_rows], axis=1)
    for j in range(4):
        copies[3 + 2 * j].wait()
        copies[4 + 2 * j].wait()
        normed, low = slots[2 * j], slots[2 * j + 1]
        inner = dot(up_turned[...], normed, NT) + bias_rows
        active, slope = gelu_both(inner)
        inner_low = (dot(down_rows[...], low, NT) * slope).astype(BF16)
        up_part = dot(inner_low, normed, NN)
        down_part = dot(active.astype(BF16), low, NN)
        if j == 0:
            up_sum[...] = up_part
            down_sum[...] = down_part
        else:
            up_sum[...] += up_part
            down_sum[...] += down_part
    up_back[...] = up_sum[...].T
    for turn in range(LINE):
        z = turn_ahead(line, turn)
        for side in range(2):
            at = pl.ds(pl.multiple_of(z * SHARD + side * HALF, 16), HALF)
            part_ref[turn, :HALF, side * SLICE : (side + 1) * SLICE] = up_back[at, :].astype(BF16)
        at = pl.ds(pl.multiple_of(z * PIECE, 16), PIECE)
        part_ref[turn, HALF:, :] = down_sum[at, :].astype(BF16)


def hold_parts(me, close, far, held):
    for place in range(4):
        held[me ^ ORDER[place]] = close[place][...]
        held[me ^ ORDER[place + 4]] = far[place]


def rest_shard_kernel(
    scal, p0, p1, p2, p3, far,
    up_ref, down_ref, out_ref, proj_ref, rows_ref, bias_ref, held,
):
    me, line = place_of(scal)
    hold_parts(me, (p0, p1, p2, p3), far, held)
    for k in range(PLANE):
        core, x, y = k % 2, (k // 2) % 2, k // 4
        for side in range(2):
            rows = held[k, :HALF, side * SLICE : (side + 1) * SLICE].astype(F32)
            for s in range(LINE):
                start = s * PLANE * PIECE + k * PIECE
                up_ref[side * HALF : (side + 1) * HALF, start : start + PIECE] = rows[
                    :, s * PIECE : (s + 1) * PIECE
                ]
        down_ref[k * PIECE : (k + 1) * PIECE, :] = held[k, HALF : 2 * HALF, :].astype(F32)
        tail = held[k, 2 * HALF :, :].astype(F32)
        block = 2 * x + y
        if block < 3:
            start = core * HALF + 32 * block
            out_ref[start : start + 32, :] = tail
        else:
            for t in range(6):
                start = core * HALF + 16 * t
                proj_ref[start : start + 16, :] = tail[:16, t * EMBED : (t + 1) * EMBED]
            if core == 0:
                small = tail[16:, :]
    for z in range(LINE):

        @pl.when(line == z)
        def _():
            rows_ref[...] = small[:8, z * SHARD : (z + 1) * SHARD]
            bias_ref[...] = small[8:, z * PIECE : (z + 1) * PIECE]


def qkv_shard_kernel(scal, late, p0, p1, p2, p3, far, qkv_ref, rows_ref, held):
    me, line = place_of(scal)
    hold_parts(me, (p0, p1, p2, p3), far, held)
    for k in range(PLANE):
        y, g = k // 4, k % 4
        for part in range(3):
            start = part * WIDTH + g * WIDE
            qkv_ref[y * HALF : (y + 1) * HALF, start : start + WIDE] = held[
                k, :HALF, part * WIDE : (part + 1) * WIDE
            ].astype(F32)
    sums = held[line, HALF:, :].astype(F32)
    rows_ref[...] = jnp.concatenate(
        [sums[:1, :WIDE], sums[:1, 2 * WIDE : 3 * WIDE], late[:6, :]]
    )


def gather_side(array):
    return [array, plane_swap(array, 4), plane_swap(array, 2), plane_swap(array, 6)]


def gather_plane(array):
    close = gather_side(array)
    return close + [plane_swap(jnp.stack(close), 1)]


def turn_parts(parts):
    return [parts[0]] + [line_turn(parts[turn], turn) for turn in range(1, LINE)]


def sum_parts(parts):
    total = parts[0].astype(F32)
    for part in parts[1:]:
        total = total + part.astype(F32)
    return total.astype(BF16)


def swap_groups(own, from_x, for_core):
    return own, from_x, plane_swap(for_core, 1), plane_swap(from_x[1], 1)


def plane_body(
    tokens,
    doc_lengths,
    group_deal,
    qkv_weight,
    out_weight,
    up_weight,
    up_bias,
    down_weight,
    proj_weight,
    vectors,
    cotangent,
):
    me = lax.axis_index("ctx").astype(jnp.int32)
    line = lax.axis_index("wa").astype(jnp.int32)
    y, x, core = me // 4, (me // 2) % 2, me % 2
    scal = jnp.stack([me, line])
    spots = (scal, doc_lengths, group_deal)

    own_cols, ups, own_parts = call(
        cut_kernel,
        (scal, vectors, up_bias.reshape(1, -1), proj_weight)
        + (qkv_weight, up_weight, down_weight, out_weight),
        (SM, VM, VM, VM, HB, HB, HB, HB),
        [
            ((SHARD, 3 * WIDE), BF16),
            ((PLANE, SHARD, SLICE), BF16),
            ((PARTS + COLS + 16, SLICE), BF16),
        ],
        [
            pltpu.VMEM((SHARD, 3 * WIDTH), BF16),
            pltpu.VMEM((SHARD, INNER), BF16),
            pltpu.VMEM((PIECE, WIDTH), BF16),
            pltpu.VMEM((BLOCK, WIDTH), BF16),
            pltpu.SemaphoreType.DMA((4,)),
        ],
        mebibytes=BIG,
        name="cut",
    )
    line_parts = line_turns(own_parts)
    tokens, own_parts = lax.optimization_barrier((tokens, own_parts))
    mine, other = pick(tokens, y), pick(tokens, 1 - y)
    got = [plane_swap(other, 4), plane_swap(mine, 2), plane_swap(other, 6)]
    *line_parts, got_y, got_x, got_d = lax.optimization_barrier((*line_parts, *got))
    near = jnp.concatenate([mine, got_y, got_x, got_d])
    far = plane_swap(near, 1)
    cot_mine, cot_other = pick(cotangent, y), plane_swap(pick(cotangent, 1 - y), 4)
    far, cot_other = lax.optimization_barrier((far, cot_other))
    halves = jnp.stack([part[PARTS:] for part in line_parts])
    others = plane_swap(halves, 4)
    turns = jnp.stack([part[:PARTS] for part in line_parts])
    from_x = plane_swap(turns, 2)
    from_y = plane_swap(turns, 4)

    full, bias, ends = call(
        vectors_kernel,
        (scal, own_parts, halves),
        (SM, VM, VM),
        [((8, WIDTH), F32), ((PLANE, SLICE), F32), ((8, PAD), F32)],
        [pltpu.VMEM((LINE, 16, SHARD), F32)],
        name="vectors",
    )

    queries, keys, values, weights, att_own, att_core, att_x, lse = call(
        attend_kernel,
        (*spots, ends, own_cols, halves, others, near, far),
        (SM, SM, SM, *[VM] * 6),
        [
            ((SLOTS, PAD), BF16),
            ((SLOTS, PAD), BF16),
            ((SLOTS, PAD), BF16),
            ((WIDTH, 3 * PAD), BF16),
            ((OWN, PAD), BF16),
            ((OWN, PAD), BF16),
            ((2, OWN, PAD), BF16),
            ((4, 8, OWN), F32),
        ],
        [
            pltpu.VMEM((WIDTH, 3 * WIDE), BF16),
            pltpu.VMEM((SLOTS, SPAN), F32),
            pltpu.VMEM((PAD, SLOTS), BF16),
            pltpu.VMEM((PAD, OWN), F32),
            pltpu.VMEM((4, OWN, PAD), BF16),
            *[pltpu.VMEM((SLOTS, PAD), BF16)] * 3,
            pltpu.VMEM((WIDTH, 3 * PAD), BF16),
            pltpu.SemaphoreType.DMA((4,)),
        ],
        mebibytes=BIG,
        own=(0, 1, 2, 3),
        name="attend",
    )
    att_x = plane_swap(att_x, 2)
    from_x, from_y, att_x = lax.optimization_barrier((from_x, from_y, att_x))
    from_d = relay(from_x, from_y, core)
    parts = [turns, from_y, from_x, from_d]
    parts += [plane_swap(part, 1) for part in parts]
    groups = swap_groups(att_own, att_x, att_core)

    first_sum, normed_low = call(
        out_kernel,
        (scal, near, full, out_weight, *groups, *parts),
        (SM, VM, VM, VM, *[VM] * 4, *[HB] * 8),
        [
            ((OWN, WIDTH), F32),
            ((OWN, WIDTH), BF16),
        ],
        [pltpu.VMEM((LINE, PAD, WIDTH), BF16), pltpu.SemaphoreType.DMA],
        name="out",
    )
    normed_side = gather_side(normed_low)
    embedded, down_low, first_grad, grad_own, grad_core, grad_x, rest_mine, rest_other = call(
        middle_kernel,
        (*spots, first_sum, full, bias, proj_weight, out_weight, cot_mine, cot_other)
        + (*groups, ups, down_weight, *parts),
        (SM, SM, SM, *[VM] * 11, *[HB] * 10),
        [
            ((OWN, EMBED), BF16),
            ((OWN, WIDTH), BF16),
            ((OWN, WIDTH), F32),
            *[((OWN, PAD), BF16)] * 2,
            ((2, OWN, PAD), BF16),
            *[((LINE, SPAN, WIDTH), BF16)] * 2,
        ],
        [
            pltpu.VMEM((OWN, WIDTH), BF16),
            pltpu.VMEM((OWN, WIDTH), F32),
            *[pltpu.VMEM((OWN, PAD), BF16)] * 2,
            pltpu.VMEM((2, OWN, PAD), BF16),
            *[pltpu.VMEM((LINE, SPAN, WIDTH), BF16)] * 2,
            pltpu.VMEM((PLANE, SHARD, SLICE), BF16),
            pltpu.VMEM((WIDTH, WIDTH), BF16),
            pltpu.VMEM((PLANE, LINE - 1, PARTS, SLICE), BF16),
            pltpu.VMEM((PLANE, WIDTH, SLICE), BF16),
            pltpu.VMEM((PLANE, SLICE, WIDTH), BF16),
            pltpu.VMEM((LINE, PAD, WIDTH), BF16),
            pltpu.VMEM((WIDTH, EMBED), BF16),
            pltpu.VMEM((PLANE, OWN, SLICE), F32),
            pltpu.VMEM((WIDTH, EMBED), BF16),
            pltpu.VMEM((PLANE, SLICE), F32),
            pltpu.VMEM((4, PAD, WIDTH), BF16),
            pltpu.SemaphoreType.DMA((PLANE + 9,)),
        ],
        mebibytes=BIG,
        own=(1, 2, 3, 4, 5, 6, 7),
        name="middle",
    )
    *normed_side, down_low, embedded, grad_core, grad_x, rest_other = lax.optimization_barrier(
        (*normed_side, down_low, embedded, grad_core, grad_x, rest_other)
    )
    down_side = gather_side(down_low)
    embed_other = plane_swap(embedded[SPAN:], 4)
    embeddings = jnp.where(
        y == 0,
        jnp.stack([embedded[:SPAN], embed_other]),
        jnp.stack([embed_other, embedded[:SPAN]]),
    )

    grad_x = plane_swap(grad_x, 2)
    grads = swap_groups(grad_own, grad_x, grad_core)

    rest = rest_mine.astype(F32) + plane_swap(rest_other, 1).astype(F32)
    rest = rest.astype(BF16).reshape(LINE, 2, 64, WIDTH)
    rest_kept = lax.dynamic_index_in_dim(rest, x, 1, keepdims=False)
    rest_sent = lax.dynamic_index_in_dim(rest, 1 - x, 1, keepdims=False)
    rest_sent, first_grad = lax.optimization_barrier((rest_sent, first_grad))
    rest_sent = plane_swap(rest_sent, 2)

    qkv_mine, qkv_other, token_near, token_far = call(
        attend_back_kernel,
        (*spots, queries, keys, values, lse, weights, near, far, first_grad, *grads),
        (SM, SM, SM, HB, HB, HB, VM, *[HB] * 8),
        [
            *[((LINE, HALF + 16, 3 * WIDE), BF16)] * 2,
            ((2 * OWN, WIDTH), F32),
            ((2 * OWN, WIDTH), BF16),
        ],
        [
            *[pltpu.VMEM((LINE, HALF + 16, 3 * WIDE), BF16)] * 2,
            pltpu.VMEM((2 * OWN, WIDTH), F32),
            pltpu.VMEM((2 * OWN, WIDTH), BF16),
            *[pltpu.VMEM((SLOTS, PAD), BF16)] * 3,
            pltpu.VMEM((WIDTH, 3 * PAD), BF16),
            *[pltpu.VMEM((2 * OWN, WIDTH), BF16)] * 2,
            pltpu.VMEM((OWN, WIDTH), F32),
            pltpu.VMEM((4, OWN, PAD), BF16),
            pltpu.VMEM((SLOTS, SPAN), F32),
            pltpu.VMEM((PAD, SLOTS), BF16),
            pltpu.VMEM((PAD, OWN), F32),
            pltpu.VMEM((SLOTS, 3 * PAD), BF16),
            pltpu.VMEM((SLOTS, PAD), F32),
            pltpu.VMEM((SLOTS, PAD), F32),
            pltpu.VMEM((WIDTH, 3 * PAD), BF16),
            pltpu.SemaphoreType.DMA((15,)),
        ],
        mebibytes=BIG,
        own=(0, 1, 2, 3),
        name="attend_back",
    )

    rest = (rest_kept.astype(F32) + rest_sent.astype(F32)).astype(BF16)
    rest = rest.reshape(LINE, 2, 32, WIDTH)
    rest_kept = lax.dynamic_index_in_dim(rest, y, 1, keepdims=False)
    rest_sent = lax.dynamic_index_in_dim(rest, 1 - y, 1, keepdims=False)
    rest_sent = plane_swap(rest_sent, 4)

    *down_side, token_near = lax.optimization_barrier((*down_side, token_near))

    def slice_grad(turns, ups, down, name):
        (parts,) = call(
            partial(slice_grad_kernel, name == "slice_other"),
            (scal, bias, turns, ups, down, *normed_side, *down_side),
            (SM, VM, *[HB] * 11),
            [((LINE, 2 * HALF, WIDTH), BF16)],
            [
                pltpu.VMEM((LINE - 1, PARTS, SLICE), BF16),
                pltpu.VMEM((SHARD, SLICE), BF16),
                pltpu.VMEM((PIECE, WIDTH), BF16),
                pltpu.VMEM((PLANE, OWN, WIDTH), BF16),
                pltpu.VMEM((WIDTH, SLICE), F32),
                *[pltpu.VMEM((SLICE, WIDTH), BF16)] * 2,
                *[pltpu.VMEM((SLICE, WIDTH), F32)] * 2,
                pltpu.VMEM((WIDTH, SLICE), F32),
                pltpu.SemaphoreType.DMA((11,)),
            ],
            mebibytes=BIG,
            name=name,
        )
        return parts

    slices_other = slice_grad(parts[4], ups, down_weight, "slice_other")
    *down_side, slices_other = lax.optimization_barrier((*down_side, slices_other))
    slices_mine = slice_grad(turns, ups, down_weight, "slice_mine")
    slices_other = plane_swap(slices_other, 1)
    slices_mine, rest_sent = lax.optimization_barrier((slices_mine, rest_sent))
    rest = (rest_kept.astype(F32) + rest_sent.astype(F32)).astype(BF16)
    shard_parts = []
    for turn in range(LINE):
        total = slices_mine[turn].astype(F32) + slices_other[turn].astype(F32)
        shard_parts.append(jnp.concatenate([total.astype(BF16), rest[turn]]))
    shard_part = sum_parts(turn_parts(shard_parts))

    qkv_other = plane_swap(qkv_other, 4)
    qkv_parts = [
        (qkv_mine[turn].astype(F32) + qkv_other[turn].astype(F32)).astype(BF16)
        for turn in range(LINE)
    ]
    qkv_part = sum_parts(turn_parts(qkv_parts))

    near_sum = (token_near + plane_swap(token_far, 1).astype(F32)).reshape(4, SPAN, WIDTH)
    pair = near_sum[:2] + plane_swap(near_sum[2:].astype(BF16), 2).astype(F32)
    for_other = plane_swap(pair[1].astype(BF16), 4)
    for_mine, for_other = pair[0], for_other.astype(F32)
    tokens_grad = jnp.where(
        y == 0, jnp.stack([for_mine, for_other]), jnp.stack([for_other, for_mine])
    )
    up_grad, down_grad, out_grad, proj_grad, late_rows, bias_rows = call(
        rest_shard_kernel,
        (scal, *gather_plane(shard_part)),
        (SM, *[VM] * 5),
        [
            ((SHARD, INNER), F32),
            ((WIDTH, WIDTH), F32),
            ((SHARD, WIDTH), F32),
            ((SHARD, EMBED), F32),
            ((8, SHARD), F32),
            ((PLANE, PIECE), F32),
        ],
        [pltpu.VMEM((PLANE, 2 * HALF + 32, WIDTH), BF16)],
        name="rest_shard",
    )
    bias_grad = bias_rows.reshape(-1)
    qkv_grad, vectors_grad = call(
        qkv_shard_kernel,
        (scal, late_rows, *gather_plane(qkv_part)),
        (SM, *[VM] * 6),
        [((SHARD, 3 * WIDTH), F32), ((8, SHARD), F32)],
        [pltpu.VMEM((PLANE, HALF + 16, 3 * WIDE), BF16)],
        name="qkv_shard",
    )
    return (
        embeddings,
        tokens_grad,
        qkv_grad,
        out_grad,
        up_grad,
        bias_grad,
        down_grad,
        proj_grad,
        vectors_grad,
    )


def body(*arrays):
    sequences, span, width = arrays[0].shape
    fits = (
        lax.axis_size("ctx") == PLANE
        and lax.axis_size("wa") == LINE
        and sequences == 2
        and span == SPAN
        and width == WIDTH
    )
    return (plane_body if fits else general_body)(*arrays)


def solution(mesh):
    in_specs = (
        P("wa", "ctx", None),
        P(),
        P(),
        P("wa", None),
        P("wa", None),
        P("wa", None),
        P("wa"),
        P("wa", None),
        P("wa", None),
        P(None, "wa"),
        P("wa", "ctx", None),
    )
    out_specs = (
        P("wa", "ctx", None),
        P("wa", "ctx", None),
        P("wa", None),
        P("wa", None),
        P("wa", None),
        P("wa"),
        P("wa", None),
        P("wa", None),
        P(None, "wa"),
    )
    return jax.shard_map(body, mesh=mesh, in_specs=in_specs, out_specs=out_specs, check_vma=False)
```

```python
from functools import partial

import jax
import jax.numpy as jnp
from jax import lax
from jax.experimental import pallas as pl
from jax.experimental.pallas import tpu as pltpu
from jax.sharding import PartitionSpec as P

H = 12
HEAD = 64


NEG_FILL = -1e30
NORM_EPS = 1e-06
ROOT_HALF = 0.7071067811865476
DENSITY_SCALE = 0.3989422804014327


def norm_rows(inputs, gain_row, shift_row):
    middle = jnp.mean(inputs, axis=-1, keepdims=True)
    center = inputs - middle
    spread = jnp.mean(center * center, axis=-1, keepdims=True)
    scaled = lax.rsqrt(spread + NORM_EPS)
    unit_rows = center * scaled
    return (unit_rows * gain_row + shift_row, unit_rows, scaled)


def norm_back(grad_in, unit_rows, scaled, gain_row):
    gain_grad = jnp.sum(grad_in * unit_rows, axis=(0, 1))
    shift_grad = jnp.sum(grad_in, axis=(0, 1))
    inner_grad = grad_in * gain_row
    centered = inner_grad - jnp.mean(inner_grad, axis=-1, keepdims=True)
    result = scaled * (
        centered - unit_rows * jnp.mean(inner_grad * unit_rows, axis=-1, keepdims=True)
    )
    return (result, gain_grad, shift_grad)


def gelu_both(inner_sum):
    normal_cdf = 0.5 * (1.0 + lax.erf(inner_sum * ROOT_HALF))
    density = jnp.exp(-0.5 * inner_sum * inner_sum) * DENSITY_SCALE
    return (inner_sum * normal_cdf, normal_cdf + inner_sum * density)


def split_tiles(key_rows, value_rows, key_valid):
    key_count = key_rows.shape[0]
    tile_width = 512
    tile_count = key_count // tile_width
    return (
        key_rows.reshape(tile_count, tile_width, H, HEAD),
        value_rows.reshape(tile_count, tile_width, H, HEAD),
        key_valid.reshape(tile_count, tile_width),
    )


def masked_scores(queries, key_tile, mask_tile):
    products = jnp.einsum("qhd,khd->hqk", queries, key_tile, preferred_element_type=jnp.float32)
    return jnp.where(mask_tile[None, None, :], products, NEG_FILL)


def attend_forward(queries, key_rows, value_rows, key_valid):
    key_tiles, value_tiles, mask_tiles = split_tiles(key_rows, value_rows, key_valid)
    row_span = queries.shape[0]

    def stats_step(running, portion):
        highest, summed = running
        key_tile, mask_tile = portion
        scores = masked_scores(queries, key_tile, mask_tile)
        new_peak = jnp.maximum(highest, jnp.max(scores, axis=-1))
        raised = jnp.where(mask_tile[None, None, :], jnp.exp(scores - new_peak[:, :, None]), 0.0)
        return ((new_peak, summed * jnp.exp(highest - new_peak) + jnp.sum(raised, axis=-1)), None)

    start_peak = jnp.full((H, row_span), NEG_FILL, jnp.float32)
    start_sum = jnp.zeros((H, row_span), jnp.float32)
    (highest, summed), _ = lax.scan(stats_step, (start_peak, start_sum), (key_tiles, mask_tiles))
    logsum = highest + jnp.log(summed)

    def value_step(running, portion):
        key_tile, value_tile, mask_tile = portion
        scores = masked_scores(queries, key_tile, mask_tile)
        prob_low = jnp.where(
            mask_tile[None, None, :], jnp.exp(scores - logsum[:, :, None]), 0.0
        ).astype(jnp.bfloat16)
        return (
            running
            + jnp.einsum("hqk,khd->qhd", prob_low, value_tile, preferred_element_type=jnp.float32),
            None,
        )

    attended, _ = lax.scan(
        value_step,
        jnp.zeros((row_span, H, HEAD), jnp.float32),
        (key_tiles, value_tiles, mask_tiles),
    )
    return (attended, logsum)


def attend_backward(
    queries, key_rows, value_rows, key_valid, logsum, delta_rows, grad_heads, with_keys
):
    key_tiles, value_tiles, mask_tiles = split_tiles(key_rows, value_rows, key_valid)

    def back_step(running, portion):
        key_tile, value_tile, mask_tile = portion
        scores = masked_scores(queries, key_tile, mask_tile)
        prob_rows = jnp.where(mask_tile[None, None, :], jnp.exp(scores - logsum[:, :, None]), 0.0)
        prob_grad = jnp.einsum(
            "qhd,khd->hqk", grad_heads, value_tile, preferred_element_type=jnp.float32
        )
        score_low = (prob_rows * (prob_grad - delta_rows[:, :, None])).astype(jnp.bfloat16)
        running = running + jnp.einsum(
            "hqk,khd->qhd", score_low, key_tile, preferred_element_type=jnp.float32
        )
        value_part = jnp.einsum(
            "hqk,qhd->khd",
            prob_rows.astype(jnp.bfloat16),
            grad_heads,
            preferred_element_type=jnp.float32,
        )
        key_part = jnp.einsum(
            "hqk,qhd->khd", score_low, queries, preferred_element_type=jnp.float32
        )
        return (running, (key_part, value_part))

    start_grad = jnp.zeros(queries.shape, jnp.float32)
    query_grad, pieces = lax.scan(back_step, start_grad, (key_tiles, value_tiles, mask_tiles))
    key_count = key_rows.shape[0]
    return (
        query_grad,
        pieces[0].reshape(key_count, H * HEAD),
        pieces[1].reshape(key_count, H * HEAD),
    )


def general_body(
    tokens,
    doc_lengths,
    group_deal,
    qkv_weight,
    out_weight,
    up_weight,
    up_bias,
    down_weight,
    proj_weight,
    vectors,
    cotangent,
):
    gathered = (
        lax.all_gather(qkv_weight, "wa", axis=0, tiled=True),
        lax.all_gather(out_weight, "wa", axis=0, tiled=True),
        lax.all_gather(up_weight, "wa", axis=0, tiled=True),
        lax.all_gather(up_bias, "wa", axis=0, tiled=True),
        lax.all_gather(down_weight, "wa", axis=0, tiled=True),
        lax.all_gather(proj_weight, "wa", axis=0, tiled=True),
        lax.all_gather(vectors, "wa", axis=1, tiled=True),
    )
    qkv_full, out_full, up_full, bias_full, down_full, proj_full, vector_full = gathered
    seq_count, group_rows, model_width = tokens.shape
    ctx_count = lax.axis_size("ctx")
    seq_start = lax.axis_index("wa") * seq_count
    my_lengths = lax.dynamic_slice_in_dim(doc_lengths, seq_start, seq_count, 0)
    my_deal = lax.dynamic_slice_in_dim(group_deal, seq_start, seq_count, 0)
    offsets = jnp.tile(jnp.arange(group_rows, dtype=jnp.int32), ctx_count)
    positions = jnp.repeat(my_deal, group_rows, axis=1) * group_rows + offsets[None, :]
    key_valid = positions < my_lengths[:, None]
    query_valid = lax.dynamic_slice_in_dim(
        key_valid, lax.axis_index("ctx") * group_rows, group_rows, 1
    )
    row_mask = query_valid.astype(jnp.float32)[:, :, None]
    query_scale = HEAD ** (-0.5)
    mixed_rows = jnp.einsum("scd,de->sce", tokens, qkv_full, preferred_element_type=jnp.float32)
    queries = ((mixed_rows[:, :, :model_width] + vector_full[0]) * query_scale).astype(jnp.bfloat16)
    key_rows = mixed_rows[:, :, model_width : 2 * model_width].astype(jnp.bfloat16)
    value_rows = (mixed_rows[:, :, 2 * model_width :] + vector_full[1]).astype(jnp.bfloat16)
    all_keys, all_values = (
        lax.all_gather(key_rows, "ctx", axis=1, tiled=True),
        lax.all_gather(value_rows, "ctx", axis=1, tiled=True),
    )
    query_heads = queries.reshape(seq_count, group_rows, H, HEAD)
    attended, logsum = jax.vmap(attend_forward)(query_heads, all_keys, all_values, key_valid)
    attended_low = attended.reshape(seq_count, group_rows, model_width).astype(jnp.bfloat16)
    first_sum = tokens.astype(jnp.float32) + (
        jnp.einsum("scd,de->sce", attended_low, out_full, preferred_element_type=jnp.float32)
        + vector_full[2]
    )
    normed, unit_one, scale_one = norm_rows(first_sum, vector_full[3], vector_full[4])
    normed_low = normed.astype(jnp.bfloat16)
    inner_sum = (
        jnp.einsum("scd,df->scf", normed_low, up_full, preferred_element_type=jnp.float32)
        + bias_full
    )
    active, gelu_slope = gelu_both(inner_sum)
    active_low = active.astype(jnp.bfloat16)
    second_sum = normed + (
        jnp.einsum("scf,fd->scd", active_low, down_full, preferred_element_type=jnp.float32)
        + vector_full[5]
    )
    final_sum, unit_two, scale_two = norm_rows(second_sum, vector_full[6], vector_full[7])
    final_low = final_sum.astype(jnp.bfloat16)
    project = jnp.einsum("scd,de->sce", final_low, proj_full, preferred_element_type=jnp.float32)
    inverse = lax.rsqrt(jnp.sum(project * project, axis=-1, keepdims=True) + NORM_EPS)
    direction = project * inverse
    embeddings = (direction * row_mask).astype(jnp.bfloat16)
    upstream = cotangent.astype(jnp.float32) * row_mask
    project_grad = (
        inverse * (upstream - direction * jnp.sum(upstream * direction, axis=-1, keepdims=True))
    ).astype(jnp.bfloat16)
    proj_grad = jnp.einsum(
        "scd,sce->de", final_low, project_grad, preferred_element_type=jnp.float32
    )
    final_grad = jnp.einsum(
        "sce,de->scd", project_grad, proj_full, preferred_element_type=jnp.float32
    )
    second_grad, gain_two, shift_two = norm_back(final_grad, unit_two, scale_two, vector_full[6])
    down_low = second_grad.astype(jnp.bfloat16)
    down_grad = jnp.einsum("scf,scd->fd", active_low, down_low, preferred_element_type=jnp.float32)
    inner_grad = (
        jnp.einsum("scd,fd->scf", down_low, down_full, preferred_element_type=jnp.float32)
        * gelu_slope
    )
    bias_grad = jnp.sum(inner_grad, axis=(0, 1))
    inner_low = inner_grad.astype(jnp.bfloat16)
    up_grad = jnp.einsum("scd,scf->df", normed_low, inner_low, preferred_element_type=jnp.float32)
    normed_grad = second_grad + jnp.einsum(
        "scf,df->scd", inner_low, up_full, preferred_element_type=jnp.float32
    )
    first_grad, gain_one, shift_one = norm_back(normed_grad, unit_one, scale_one, vector_full[3])
    first_low = first_grad.astype(jnp.bfloat16)
    out_grad = jnp.einsum(
        "scd,sce->de", attended_low, first_low, preferred_element_type=jnp.float32
    )
    attended_grad = jnp.einsum(
        "sce,de->scd", first_low, out_full, preferred_element_type=jnp.float32
    ).astype(jnp.bfloat16)
    grad_heads = attended_grad.reshape(seq_count, group_rows, H, HEAD)
    delta_rows = jnp.sum(grad_heads.astype(jnp.float32) * attended, axis=-1)
    delta_heads = jnp.swapaxes(delta_rows, 1, 2)
    query_grad, key_terms, value_terms = jax.vmap(partial(attend_backward, with_keys=True))(
        query_heads, all_keys, all_values, key_valid, logsum, delta_heads, grad_heads
    )
    key_grad, value_grad = (
        lax.psum_scatter(
            key_terms.astype(jnp.bfloat16), "ctx", scatter_dimension=1, tiled=True
        ).astype(jnp.float32),
        lax.psum_scatter(
            value_terms.astype(jnp.bfloat16), "ctx", scatter_dimension=1, tiled=True
        ).astype(jnp.float32),
    )
    query_part = (
        query_grad.reshape(seq_count, group_rows, model_width).astype(jnp.bfloat16) * query_scale
    )
    value_part = value_grad.astype(jnp.bfloat16)
    mixed_grad = jnp.concatenate([query_part, key_grad.astype(jnp.bfloat16), value_part], axis=-1)
    qkv_grad = jnp.einsum("scd,sce->de", tokens, mixed_grad, preferred_element_type=jnp.float32)
    tokens_grad = first_grad + jnp.einsum(
        "sce,de->scd", mixed_grad, qkv_full, preferred_element_type=jnp.float32
    )
    vectors_grad = jnp.stack(
        [
            jnp.sum(query_part.astype(jnp.float32), axis=(0, 1)),
            jnp.sum(value_part.astype(jnp.float32), axis=(0, 1)),
            jnp.sum(first_grad, axis=(0, 1)),
            gain_one,
            shift_one,
            jnp.sum(second_grad, axis=(0, 1)),
            gain_two,
            shift_two,
        ],
        axis=0,
    )
    owned = (
        lax.psum_scatter(
            qkv_grad.astype(jnp.bfloat16), "wa", scatter_dimension=0, tiled=True
        ).astype(jnp.float32),
        lax.psum_scatter(
            out_grad.astype(jnp.bfloat16), "wa", scatter_dimension=0, tiled=True
        ).astype(jnp.float32),
        lax.psum_scatter(
            up_grad.astype(jnp.bfloat16), "wa", scatter_dimension=0, tiled=True
        ).astype(jnp.float32),
        lax.psum_scatter(
            bias_grad.astype(jnp.bfloat16), "wa", scatter_dimension=0, tiled=True
        ).astype(jnp.float32),
        lax.psum_scatter(
            down_grad.astype(jnp.bfloat16), "wa", scatter_dimension=0, tiled=True
        ).astype(jnp.float32),
        lax.psum_scatter(
            proj_grad.astype(jnp.bfloat16), "wa", scatter_dimension=0, tiled=True
        ).astype(jnp.float32),
        lax.psum_scatter(
            vectors_grad.astype(jnp.bfloat16), "wa", scatter_dimension=1, tiled=True
        ).astype(jnp.float32),
    )
    summed = (
        lax.psum(owned[0].astype(jnp.bfloat16), "ctx").astype(jnp.float32),
        lax.psum(owned[1].astype(jnp.bfloat16), "ctx").astype(jnp.float32),
        lax.psum(owned[2].astype(jnp.bfloat16), "ctx").astype(jnp.float32),
        lax.psum(owned[3].astype(jnp.bfloat16), "ctx").astype(jnp.float32),
        lax.psum(owned[4].astype(jnp.bfloat16), "ctx").astype(jnp.float32),
        lax.psum(owned[5].astype(jnp.bfloat16), "ctx").astype(jnp.float32),
        lax.psum(owned[6].astype(jnp.bfloat16), "ctx").astype(jnp.float32),
    )
    return (
        embeddings,
        tokens_grad,
        summed[0],
        summed[1],
        summed[2],
        summed[3],
        summed[4],
        summed[5],
        summed[6],
    )


PLANE = 8
LINE = 4
SPAN = 128
OWN = 2 * SPAN
WIDTH = H * HEAD
INNER = 4 * WIDTH
SHARD = WIDTH // LINE
HALF = SHARD // 2
PIECE = INNER // LINE // PLANE
SLICE = LINE * PIECE
HEADS = 3
WIDE = HEADS * HEAD
PAD = 256
SLOTS = PLANE * SPAN
BLOCK = SHARD // 4
FIRST = SHARD + BLOCK
SIDE = PIECE + 16
PARTS = FIRST + 2 * SIDE
QUARTER = HALF // 2
COLS = HALF + QUARTER
EMBED = 128
ORDER = (0, 4, 2, 6, 1, 5, 3, 7)
NEAR = (0, 2, 1, 3)
F32 = jnp.float32
BF16 = jnp.bfloat16

NN = ((1,), (0,))
NT = ((1,), (1,))
TN = ((0,), (0,))


def dot(left, right, dims):
    return lax.dot_general(left, right, (dims, ((), ())), preferred_element_type=F32)


def plane_swap(array, bits):
    return lax.ppermute(array, "ctx", [(i, i ^ bits) for i in range(PLANE)])


def line_turn(array, step):
    return lax.ppermute(array, "wa", [(i, (i + step) % LINE) for i in range(LINE)])


def line_turns(array):
    return [line_turn(array, step) for step in range(1, LINE)]


def relay(from_x, from_y, core):
    passed = jnp.where(core == 0, from_y, from_x)
    pairs = [(i, i ^ 2 if i % 2 == 0 else i ^ 4) for i in range(PLANE)]
    return lax.ppermute(passed, "ctx", pairs)


def pick(array, index):
    return lax.dynamic_index_in_dim(array, index, 0, keepdims=False)


COST = {'cut': 3, 'vectors': 1, 'attend': 12, 'out': 3, 'middle': 17, 'attend_back': 18, 'rest_shard': 4, 'qkv_shard': 2, 'slice_other': 3.0, 'slice_mine': 3.0}
VM = pl.BlockSpec(memory_space=pltpu.VMEM)
SM = pl.BlockSpec(memory_space=pltpu.SMEM)
HB = pl.BlockSpec(memory_space=pl.ANY)
BIG = 56


def call(kernel, inputs, spaces, outputs, scratch=(), mebibytes=32, name=None, own=()):
    shapes = [jax.ShapeDtypeStruct(shape, kind) for shape, kind in outputs]
    return pl.pallas_call(
        kernel,
        out_shape=shapes,
        in_specs=list(spaces),
        out_specs=[HB if i in own else VM for i in range(len(shapes))],
        scratch_shapes=list(scratch),
        compiler_params=pltpu.CompilerParams(vmem_limit_bytes=mebibytes << 20),
        cost_estimate=pl.CostEstimate(flops=int(COST[name] * 1e9), bytes_accessed=1, transcendentals=0),
        name=name,
    )(*inputs)


def place_of(scal):
    return scal[0], scal[1]


def shard_of_turn(line, turn):
    return lax.rem(line - turn + LINE, LINE)


def turn_ahead(line, turn):
    return lax.rem(line + turn, LINE)


def norm_forward(rows):
    middle = jnp.mean(rows, axis=-1, keepdims=True)
    center = rows - middle
    scaled = lax.rsqrt(jnp.mean(center * center, axis=-1, keepdims=True) + NORM_EPS)
    return center * scaled, scaled


def norm_reverse(grad, unit, scaled, gain):
    inner = grad * gain
    return scaled * (
        inner
        - jnp.mean(inner, axis=-1, keepdims=True)
        - unit * jnp.mean(inner * unit, axis=-1, keepdims=True)
    )


def cut_kernel(
    scal, vectors, bias, proj, qkv, up, down, out,
    cols_ref, ups_ref, own_ref,
    qkv_held, up_held, down_held, out_held, sems,
):
    me, line = place_of(scal)
    core = lax.rem(me, 2)
    copies = [
        pltpu.make_async_copy(qkv, qkv_held, sems.at[0]),
        pltpu.make_async_copy(up, up_held, sems.at[1]),
        pltpu.make_async_copy(
            down.at[pl.ds(pl.multiple_of(me * PIECE, 16), PIECE)], down_held, sems.at[2]
        ),
        pltpu.make_async_copy(
            out.at[pl.ds(pl.multiple_of(lax.div(me, 2) * BLOCK, 16), BLOCK)], out_held, sems.at[3]
        ),
    ]
    for copy in copies:
        copy.start()
    rows = [vectors[...].astype(F32)]
    rows += [bias[:, a * SHARD : (a + 1) * SHARD].astype(F32) for a in range(LINE)]
    rows = jnp.concatenate(rows + [jnp.zeros((4, SHARD), F32)])
    own_ref[PARTS + COLS :, :SHARD] = rows.astype(BF16)
    own_ref[PARTS + COLS :, SHARD:] = jnp.zeros((16, SLICE - SHARD), BF16)
    for side in range(2):
        start = FIRST + side * SIDE + PIECE
        for t in range(3):
            own_ref[start : start + 16, t * EMBED : (t + 1) * EMBED] = proj[
                pl.ds(pl.multiple_of(core * HALF + 16 * (3 * side + t), 16), 16), :
            ]
    copies[0].wait()
    for g in range(4):

        @pl.when(lax.rem(me, 4) == g)
        def _():
            for part in range(3):
                start = part * WIDTH + g * WIDE
                cols_ref[:, part * WIDE : (part + 1) * WIDE] = qkv_held[:, start : start + WIDE]

    base = lax.div(me, 4) * HALF
    rows = cols_ref[pl.ds(pl.multiple_of(base, 16), HALF), :]
    own_ref[PARTS : PARTS + HALF, :] = rows[:, :SLICE]
    for side in range(2):
        own_ref[PARTS + HALF : PARTS + COLS, side * WIDE : (side + 1) * WIDE] = rows[
            side * QUARTER : (side + 1) * QUARTER, SLICE:
        ]
    copies[1].wait()
    for k in range(PLANE):
        for s in range(LINE):
            start = s * PLANE * PIECE + k * PIECE
            ups_ref[k, :, s * PIECE : (s + 1) * PIECE] = up_held[:, start : start + PIECE]
    own_ref[:SHARD] = ups_ref[me]
    copies[2].wait()
    for side in range(2):
        start = FIRST + side * SIDE
        own_ref[start : start + PIECE] = down_held[:, side * SLICE : (side + 1) * SLICE]
    copies[3].wait()
    own_ref[SHARD:FIRST] = out_held[:, pl.ds(pl.multiple_of(core * SLICE, 128), SLICE)]


def vectors_kernel(scal, own, halves, full_ref, bias_ref, ends_ref, held):
    me, line = place_of(scal)
    held[line] = own[PARTS + COLS :, :SHARD].astype(F32)
    for turn in range(1, LINE):
        held[shard_of_turn(line, turn)] = halves[turn - 1, COLS:, :SHARD].astype(F32)
    for a in range(LINE):
        full_ref[:, a * SHARD : (a + 1) * SHARD] = held[a, :8, :]
        for k in range(PLANE):
            start = (k % 2) * PIECE
            bias_ref[k : k + 1, a * PIECE : (a + 1) * PIECE] = held[
                a, 8 + k // 2 : 9 + k // 2, start : start + PIECE
            ]
    ends_ref[...] = jnp.zeros((8, PAD), F32)
    ends_ref[:, :WIDE] = held[lax.rem(me, 4), :8, :]


def slots_left(scal, lengths, deal, place):
    me, line = place_of(scal)
    seq = 2 * line + lax.div(me, 4)
    return lengths[seq] - deal[seq, me ^ ORDER[place]] * SPAN


def fill_mask(scal, lengths, deal, mask):
    rows = lax.broadcasted_iota(jnp.int32, (SPAN, SPAN), 0)
    for place in range(PLANE):
        limit = slots_left(scal, lengths, deal, place)
        mask[place * SPAN : (place + 1) * SPAN, :] = jnp.where(rows < limit, 0.0, NEG_FILL)


def head_lanes(h):
    lanes = lax.broadcasted_iota(jnp.int32, (OWN, 128), 1)
    return (lanes >= HEAD) if h % 2 else (lanes < HEAD)


def attend_kernel(
    scal, lengths, deal, ends, own_cols, halves, others, near, far,
    q_out, k_out, v_out, w_out, own_ref, core_ref, x_ref, lse_ref,
    raw, mask, v_turned, o_turned, att, q_ref, k_ref, v_ref, w_ref, sems,
):
    me, line = place_of(scal)
    y = lax.div(me, 4)
    raw[pl.ds(pl.multiple_of(line * SHARD, 16), SHARD), :] = own_cols[...]
    for turn in range(1, LINE):
        base = shard_of_turn(line, turn) * SHARD
        for source, side in ((halves, y), (others, 1 - y)):
            start = base + side * HALF
            at = pl.ds(pl.multiple_of(start, 16), HALF)
            raw[at, :SLICE] = source[turn - 1, :HALF, :]
            for i in range(2):
                at = pl.ds(pl.multiple_of(start + i * QUARTER, 16), QUARTER)
                raw[at, SLICE:] = source[turn - 1, HALF:COLS, i * WIDE : (i + 1) * WIDE]
    fill_mask(scal, lengths, deal, mask)
    for part in range(3):
        w_ref[:, part * PAD : part * PAD + WIDE] = raw[:, part * WIDE : (part + 1) * WIDE]
        w_ref[:, part * PAD + WIDE : (part + 1) * PAD] = jnp.zeros((WIDTH, PAD - WIDE), BF16)
    for t in range(4):
        source = (near, far)[t // 2]
        rows = source[(t % 2) * OWN : (t % 2 + 1) * OWN, :]
        mixed = dot(rows, w_ref[...], NN)
        at = slice(t * OWN, (t + 1) * OWN)
        q_ref[at, :] = ((mixed[:, :PAD] + ends[0:1, :]) * (HEAD ** (-0.5))).astype(BF16)
        k_ref[at, :] = mixed[:, PAD : 2 * PAD].astype(BF16)
        values = mixed[:, 2 * PAD :] + ends[1:2, :]
        v_ref[at, :] = values.astype(BF16)
        v_turned[:, at] = values.T.astype(BF16)

    copies = [
        pltpu.make_async_copy(source, target, sems.at[i])
        for i, (source, target) in enumerate(
            ((q_ref, q_out), (k_ref, k_out), (v_ref, v_out), (w_ref, w_out))
        )
    ]
    for copy in copies:
        copy.start()
    o_turned[WIDE:, :] = jnp.zeros((PAD - WIDE, OWN), F32)

    def tile(t, carry):
        at = pl.ds(pl.multiple_of(t * OWN, OWN), OWN)
        for h in range(HEADS):
            cut = slice((h // 2) * 128, (h // 2 + 1) * 128)
            q_tile = jnp.where(head_lanes(h), q_ref[at, cut], jnp.zeros((), BF16))
            scores = dot(k_ref[:, cut], q_tile, NT)
            scores = scores + jnp.concatenate([mask[...], mask[...]], axis=1)
            peak = jnp.max(scores, axis=0, keepdims=True)
            raised = jnp.exp(scores - peak)
            total = jnp.sum(raised, axis=0, keepdims=True)
            rows = slice(h * HEAD, (h + 1) * HEAD)
            o_turned[rows, :] = dot(v_turned[rows, :], raised.astype(BF16), NN) * (1.0 / total)
            lse_ref[t, h : h + 1, :] = peak + jnp.log(total)
        att[t] = o_turned[...].T.astype(BF16)
        return carry

    lax.fori_loop(0, 4, tile, 0)
    own_ref[...] = att[0]
    core_ref[...] = att[2]
    x_ref[0] = att[1]
    x_ref[1] = att[3]
    for copy in copies:
        copy.wait()


def attend_back_kernel(
    scal, lengths, deal, q_ref, k_ref, v_ref, lse, weights, near, far, first_grad, g0, g1, g2, g3,
    mine_out, other_out, near_out, far_out,
    mine_ref, other_ref, near_ref, far_ref,
    q_held, k_held, v_held, w_held, near_held, far_held, first_held, grads,
    mask, k_turned, q_turned, mixed, key_sum, value_sum, part, sems,
):
    sources = (k_ref, q_ref, v_ref, g0, g1.at[0], g2, g3, weights, near, far, first_grad)
    targets = (k_held, q_held, v_held, grads.at[0], grads.at[1], grads.at[2], grads.at[3])
    targets += (w_held, near_held, far_held, first_held)
    copies = [
        pltpu.make_async_copy(source, target, sems.at[i])
        for i, (source, target) in enumerate(zip(sources, targets, strict=True))
    ]
    for copy in copies:
        copy.start()
    fill_mask(scal, lengths, deal, mask)
    copies[0].wait()
    for t in range(4):
        at = slice(t * OWN, (t + 1) * OWN)
        k_turned[:, at] = k_held[at, :].astype(F32).T.astype(BF16)
    key_sum[...] = jnp.zeros_like(key_sum)
    value_sum[...] = jnp.zeros_like(value_sum)
    q_turned[WIDE:, :] = jnp.zeros((PAD - WIDE, OWN), F32)
    for copy in copies[1:7]:
        copy.wait()

    def tile(t, carry):
        at = pl.ds(pl.multiple_of(t * OWN, OWN), OWN)
        for h in range(HEADS):
            cut = slice((h // 2) * 128, (h // 2 + 1) * 128)
            rows = slice(h * HEAD, (h + 1) * HEAD)
            q_tile = jnp.where(head_lanes(h), q_held[at, cut], jnp.zeros((), BF16))
            g_tile = jnp.where(head_lanes(h), grads[t, :, cut], jnp.zeros((), BF16))
            scores = dot(k_held[:, cut], q_tile, NT)
            scores = scores + jnp.concatenate([mask[...], mask[...]], axis=1)
            probs = jnp.exp(scores - lse[t, h : h + 1, :])
            prob_grad = dot(v_held[:, cut], g_tile, NT)
            delta = jnp.sum(probs * prob_grad, axis=0, keepdims=True)
            score_low = (probs * (prob_grad - delta)).astype(BF16)
            q_turned[rows, :] = dot(k_turned[rows, :], score_low, NN)
            key_sum[:, cut] += dot(score_low, q_tile, NN)
            value_sum[:, cut] += dot(probs.astype(BF16), g_tile, NN)
        low = q_turned[...].T.astype(BF16)
        mixed[at, :PAD] = (low.astype(F32) * (HEAD ** (-0.5))).astype(BF16)
        return carry

    lax.fori_loop(0, 4, tile, 0)
    mixed[:, PAD : 2 * PAD] = key_sum[...].astype(BF16)
    mixed[:, 2 * PAD :] = value_sum[...].astype(BF16)

    me, line = place_of(scal)
    y = lax.div(me, 4)
    for copy in copies[7:]:
        copy.wait()
    for i in range(3):
        cut = slice(i * 256, (i + 1) * 256)
        part[cut, :] = (
            dot(near_held[:, cut], mixed[: 2 * OWN, :], TN) + dot(far_held[:, cut], mixed[2 * OWN :, :], TN)
        ).astype(BF16)
    sums = jnp.sum(mixed[...].astype(F32), axis=0, keepdims=True)
    sums = jnp.concatenate([sums, jnp.zeros((15, 3 * PAD), F32)]).astype(BF16)
    for turn in range(LINE):
        base = turn_ahead(line, turn) * SHARD
        for target, side in ((mine_ref, y), (other_ref, 1 - y)):
            rows = part[pl.ds(pl.multiple_of(base + side * HALF, 16), HALF), :]
            for p in range(3):
                to = slice(p * WIDE, (p + 1) * WIDE)
                target[turn, :HALF, to] = rows[:, p * PAD : p * PAD + WIDE]
                target[turn, HALF:, to] = sums[:, p * PAD : p * PAD + WIDE]
    outs = [
        pltpu.make_async_copy(source, target, sems.at[11 + i])
        for i, (source, target) in enumerate(
            (
                (other_ref, other_out),
                (mine_ref, mine_out),
                (far_ref, far_out),
                (near_ref, near_out),
            )
        )
    ]
    outs[0].start()
    outs[1].start()
    for t in (2, 3, 0, 1):
        at = slice(t * OWN, (t + 1) * OWN)
        token_part = dot(mixed[at, :], w_held[...], NT)
        if t == 0:
            near_ref[at, :] = token_part + first_held[...]
        elif t == 1:
            near_ref[at, :] = token_part
        else:
            far_ref[(t - 2) * OWN : (t - 1) * OWN, :] = token_part.astype(BF16)
        if t == 3:
            outs[2].start()
    outs[3].start()
    for copy in outs:
        copy.wait()


def out_kernel(
    scal, near, full, out_shard, a0, a1, a2, a3, p0, p1, p2, p3, p4, p5, p6, p7,
    sum_ref, low_ref,
    out_ref, sem,
):
    me, line = place_of(scal)
    group = lax.rem(me, 4)
    pieces = (p0, p1, p2, p3, p4, p5, p6, p7)
    copies = []
    for place, bits in enumerate(ORDER):
        k = me ^ bits
        rows = pl.ds(pl.multiple_of(lax.div(k, 2) * BLOCK, 16), BLOCK)
        lanes = pl.ds(pl.multiple_of(lax.rem(k, 2) * SLICE, 128), SLICE)
        for turn in range(1, LINE):
            copies.append(
                pltpu.make_async_copy(
                    pieces[place].at[turn - 1, pl.ds(SHARD, BLOCK)],
                    out_ref.at[shard_of_turn(line, turn), rows, lanes],
                    sem,
                )
            )
    for copy in copies:
        copy.start()
    for z in range(LINE):
        out_ref[z, SHARD:, :] = jnp.zeros((PAD - SHARD, WIDTH), BF16)
    out_ref[line, :SHARD, :] = out_shard[...]
    rows = near[:OWN, :].astype(F32) + full[2:3, :]
    filled = out_ref.at[pl.ds(0, LINE - 1), pl.ds(0, SHARD)]
    pltpu.make_async_copy(filled, filled, sem).wait()
    for i, source in enumerate((a0[...], a1[0], a2[...], a3[...])):
        rows = rows + dot(source, out_ref[group ^ NEAR[i]], NN)
    sum_ref[...] = rows
    unit, _ = norm_forward(rows)
    low_ref[...] = (unit * full[3:4, :] + full[4:5, :]).astype(BF16)


def place_up(scal, place, up_own, held, up_all):
    me, line = place_of(scal)
    at = pl.ds(pl.multiple_of(line * SHARD, 16), SHARD)
    up_all[place, at, :] = up_own[me ^ ORDER[place]]
    for turn in range(1, LINE):
        at = pl.ds(pl.multiple_of(shard_of_turn(line, turn) * SHARD, 16), SHARD)
        up_all[place, at, :] = held[place][turn - 1, :SHARD, :]


def place_down(scal, place, down_own, held, down_all):
    me, line = place_of(scal)
    at = pl.ds(pl.multiple_of(line * PIECE, 16), PIECE)
    start = pl.multiple_of((me ^ ORDER[place]) * PIECE, 16)
    down_all[place, at, :] = down_own[pl.ds(start, PIECE), :]
    for turn in range(1, LINE):
        at = pl.ds(pl.multiple_of(shard_of_turn(line, turn) * PIECE, 16), PIECE)
        for side in range(2):
            start = FIRST + side * SIDE
            down_all[place, at, side * SLICE : (side + 1) * SLICE] = held[place][
                turn - 1, start : start + PIECE, :
            ]


def place_out(scal, place, held, out_all):
    me, line = place_of(scal)
    k = me ^ ORDER[place]
    rows = pl.ds(pl.multiple_of(lax.div(k, 2) * BLOCK, 16), BLOCK)
    lanes = pl.ds(pl.multiple_of(lax.rem(k, 2) * SLICE, 128), SLICE)
    for turn in range(1, LINE):
        out_all[shard_of_turn(line, turn), rows, lanes] = held[place][turn - 1, SHARD:FIRST, :]


def middle_kernel(
    scal, lengths, deal, first_sum, full, bias, proj_shard, out_shard, cot_mine, cot_other, a0, a1, a2, a3, ups, down, p0, p1, p2, p3, p4, p5, p6, p7,
    embed_ref, low_out, first_out, own_out, core_out, x_out, mine_out, other_out,
    low_ref, first_ref, own_ref, core_ref, x_ref, mine_ref, other_ref,
    up_all, down_all, out_all, proj_all, slopes, proj_part, bias_sum, out_part, sems,
):
    held = (p0, p1, p2, p3, p4, p5, p6, p7)
    up_own, down_own = ups, down
    me, line = place_of(scal)
    core, group = lax.rem(me, 2), lax.rem(me, 4)
    proj_all[pl.ds(pl.multiple_of(line * SHARD, 16), SHARD), :] = proj_shard[...]

    unit_one, scale_one = norm_forward(first_sum[...])
    normed = unit_one * full[3:4, :] + full[4:5, :]
    normed_low = normed.astype(BF16)
    second_sum = normed + full[5:6, :]
    for z in range(LINE):
        out_all[z, SHARD:, :] = jnp.zeros((PAD - SHARD, WIDTH), BF16)
    out_all[line, :SHARD, :] = out_shard[...]
    for place, bits in enumerate(ORDER):
        place_up(scal, place, up_own, held, up_all)
        place_down(scal, place, down_own, held, down_all)
        place_out(scal, place, held, out_all)
        inner = dot(normed_low, up_all[place], NN) + bias[pl.ds(me ^ bits, 1), :]
        active, slope = gelu_both(inner)
        slopes[place] = slope
        second_sum = second_sum + dot(active.astype(BF16), down_all[place], NN)
    unit, scaled = norm_forward(second_sum)
    final_low = (unit * full[6:7, :] + full[7:8, :]).astype(BF16)
    for place in (0, 4):
        half = core if place == 0 else 1 - core
        for turn in range(1, LINE):
            base = shard_of_turn(line, turn) * SHARD + half * HALF
            for t in range(6):
                start = FIRST + (t // 3) * SIDE + PIECE
                proj_all[pl.ds(pl.multiple_of(base + 16 * t, 16), 16), :] = held[place][
                    turn - 1, start : start + 16, (t % 3) * EMBED : (t % 3 + 1) * EMBED
                ]
    project = dot(final_low, proj_all[...], NN)
    inverse = lax.rsqrt(jnp.sum(project * project, axis=-1, keepdims=True) + NORM_EPS)
    direction = project * inverse
    rows = lax.broadcasted_iota(jnp.int32, (SPAN, EMBED), 0)
    keep = jnp.concatenate(
        [
            jnp.where(rows < slots_left(scal, lengths, deal, i), 1.0, 0.0).astype(F32)
            for i in range(2)
        ]
    )
    embed_ref[...] = (direction * keep).astype(BF16)
    upstream = jnp.concatenate([cot_mine[...], cot_other[...]]).astype(F32) * keep
    project_grad = (
        inverse * (upstream - direction * jnp.sum(upstream * direction, axis=-1, keepdims=True))
    ).astype(BF16)
    proj_part[...] = dot(final_low, project_grad, TN).astype(BF16)
    final_grad = dot(project_grad, proj_all[...], NT)
    second_grad = norm_reverse(final_grad, unit, scaled, full[6:7, :])
    down_low = second_grad.astype(BF16)
    low_ref[...] = down_low
    outs = [
        pltpu.make_async_copy(source, target, sems.at[i])
        for i, (source, target) in enumerate(
            (
                (low_ref, low_out),
                (x_ref, x_out),
                (core_ref, core_out),
                (own_ref, own_out),
                (first_ref, first_out),
                (other_ref, other_out),
                (mine_ref, mine_out),
            )
        )
    ]
    outs[0].start()

    normed_grad = second_grad
    for place, bits in enumerate(ORDER):
        inner_grad = dot(down_low, down_all[place], NT) * slopes[place]
        bias_sum[pl.ds(me ^ bits, 1), :] = jnp.sum(inner_grad, axis=0, keepdims=True)
        normed_grad = normed_grad + dot(inner_grad.astype(BF16), up_all[place], NT)
    first_grad = norm_reverse(normed_grad, unit_one, scale_one, full[3:4, :])
    first_ref[...] = first_grad
    first_low = first_grad.astype(BF16)
    for i, target in enumerate((own_ref, x_ref.at[0], core_ref, x_ref.at[1])):
        target[...] = dot(first_low, out_all[group ^ NEAR[i]], NT).astype(BF16)
    for copy in outs[1:5]:
        copy.start()
    small = jnp.concatenate(
        [
            jnp.sum(first_grad, axis=0, keepdims=True),
            jnp.sum(normed_grad * unit_one, axis=0, keepdims=True),
            jnp.sum(normed_grad, axis=0, keepdims=True),
            jnp.sum(second_grad, axis=0, keepdims=True),
            jnp.sum(final_grad * unit, axis=0, keepdims=True),
            jnp.sum(final_grad, axis=0, keepdims=True),
            jnp.zeros((2, WIDTH), F32),
        ]
    )
    tail = jnp.concatenate([bias_sum[...], jnp.zeros((8, WIDTH - SLICE), F32)], axis=1)
    small = jnp.concatenate([small, tail]).astype(BF16)
    for i, source in enumerate((a0[...], a1[0], a2[...], a3[...])):
        z = group ^ NEAR[i]
        turn = lax.rem(z - line + LINE, LINE)
        out_part[i] = dot(source, first_low, TN).astype(BF16)
        for target, half in ((mine_ref, core), (other_ref, 1 - core)):
            base = half * HALF
            target[turn, :HALF, :] = out_part[i, pl.ds(pl.multiple_of(base, 16), HALF), :]
            for t in range(6):
                target[turn, HALF : HALF + 16, t * EMBED : (t + 1) * EMBED] = proj_part[
                    pl.ds(pl.multiple_of(z * SHARD + base + 16 * t, 16), 16), :
                ]
            target[turn, HALF + 16 :, :] = small
    outs[5].start()
    outs[6].start()
    for copy in outs:
        copy.wait()


def slice_grad_kernel(
    other, scal, bias, turns, ups, down, n0, n1, n2, n3, d0, d1, d2, d3,
    part_ref,
    held, ups_held, down_held, slots, up_rows, up_turned, down_rows, up_sum, down_sum, up_back,
    sems,
):
    me, line = place_of(scal)
    k = me ^ 1 if other else me
    copies = [
        pltpu.make_async_copy(turns, held, sems.at[0]),
        pltpu.make_async_copy(ups.at[k], ups_held, sems.at[1]),
        pltpu.make_async_copy(
            down.at[pl.ds(pl.multiple_of(k * PIECE, 16), PIECE)], down_held, sems.at[2]
        ),
    ]
    for j, source in enumerate((n0, d0, n1, d1, n2, d2, n3, d3)):
        copies.append(pltpu.make_async_copy(source, slots.at[j], sems.at[3 + j]))
    for copy in copies:
        copy.start()
    for copy in copies[:3]:
        copy.wait()
    for turn in range(LINE):
        z = shard_of_turn(line, turn)
        rows = held[turn - 1, :SHARD, :] if turn else ups_held[...]
        up_rows[pl.ds(pl.multiple_of(z * SHARD, 16), SHARD), :] = rows.astype(F32)
        at = pl.ds(pl.multiple_of(z * PIECE, 16), PIECE)
        if turn == 0:
            down_rows[at, :] = down_held[...]
            continue
        for side in range(2):
            start = FIRST + side * SIDE
            down_rows[at, side * SLICE : (side + 1) * SLICE] = held[
                turn - 1, start : start + PIECE, :
            ]
    up_turned[...] = up_rows[...].T.astype(BF16)
    bias_rows = jnp.broadcast_to(bias[pl.ds(k, 1), :], (128, SLICE)).T
    bias_rows = jnp.concatenate([bias_rows, bias_rows], axis=1)
    for j in range(4):
        copies[3 + 2 * j].wait()
        copies[4 + 2 * j].wait()
        normed, low = slots[2 * j], slots[2 * j + 1]
        inner = dot(up_turned[...], normed, NT) + bias_rows
        active, slope = gelu_both(inner)
        inner_low = (dot(down_rows[...], low, NT) * slope).astype(BF16)
        up_part = dot(inner_low, normed, NN)
        down_part = dot(active.astype(BF16), low, NN)
        if j == 0:
            up_sum[...] = up_part
            down_sum[...] = down_part
        else:
            up_sum[...] += up_part
            down_sum[...] += down_part
    up_back[...] = up_sum[...].T
    for turn in range(LINE):
        z = turn_ahead(line, turn)
        for side in range(2):
            at = pl.ds(pl.multiple_of(z * SHARD + side * HALF, 16), HALF)
            part_ref[turn, :HALF, side * SLICE : (side + 1) * SLICE] = up_back[at, :].astype(BF16)
        at = pl.ds(pl.multiple_of(z * PIECE, 16), PIECE)
        part_ref[turn, HALF:, :] = down_sum[at, :].astype(BF16)


def hold_parts(me, close, far, held):
    for place in range(4):
        held[me ^ ORDER[place]] = close[place][...]
        held[me ^ ORDER[place + 4]] = far[place]


def rest_shard_kernel(
    scal, p0, p1, p2, p3, far,
    up_ref, down_ref, out_ref, proj_ref, rows_ref, bias_ref, held,
):
    me, line = place_of(scal)
    hold_parts(me, (p0, p1, p2, p3), far, held)
    for k in range(PLANE):
        core, x, y = k % 2, (k // 2) % 2, k // 4
        for side in range(2):
            rows = held[k, :HALF, side * SLICE : (side + 1) * SLICE].astype(F32)
            for s in range(LINE):
                start = s * PLANE * PIECE + k * PIECE
                up_ref[side * HALF : (side + 1) * HALF, start : start + PIECE] = rows[
                    :, s * PIECE : (s + 1) * PIECE
                ]
        down_ref[k * PIECE : (k + 1) * PIECE, :] = held[k, HALF : 2 * HALF, :].astype(F32)
        tail = held[k, 2 * HALF :, :].astype(F32)
        block = 2 * x + y
        if block < 3:
            start = core * HALF + 32 * block
            out_ref[start : start + 32, :] = tail
        else:
            for t in range(6):
                start = core * HALF + 16 * t
                proj_ref[start : start + 16, :] = tail[:16, t * EMBED : (t + 1) * EMBED]
            if core == 0:
                small = tail[16:, :]
    for z in range(LINE):

        @pl.when(line == z)
        def _():
            rows_ref[...] = small[:8, z * SHARD : (z + 1) * SHARD]
            bias_ref[...] = small[8:, z * PIECE : (z + 1) * PIECE]


def qkv_shard_kernel(scal, late, p0, p1, p2, p3, far, qkv_ref, rows_ref, held):
    me, line = place_of(scal)
    hold_parts(me, (p0, p1, p2, p3), far, held)
    for k in range(PLANE):
        y, g = k // 4, k % 4
        for part in range(3):
            start = part * WIDTH + g * WIDE
            qkv_ref[y * HALF : (y + 1) * HALF, start : start + WIDE] = held[
                k, :HALF, part * WIDE : (part + 1) * WIDE
            ].astype(F32)
    sums = held[line, HALF:, :].astype(F32)
    rows_ref[...] = jnp.concatenate(
        [sums[:1, :WIDE], sums[:1, 2 * WIDE : 3 * WIDE], late[:6, :]]
    )


def gather_side(array):
    return [array, plane_swap(array, 4), plane_swap(array, 2), plane_swap(array, 6)]


def gather_plane(array):
    close = gather_side(array)
    return close + [plane_swap(jnp.stack(close), 1)]


def turn_parts(parts):
    return [parts[0]] + [line_turn(parts[turn], turn) for turn in range(1, LINE)]


def sum_parts(parts):
    total = parts[0].astype(F32)
    for part in parts[1:]:
        total = total + part.astype(F32)
    return total.astype(BF16)


def swap_groups(own, from_x, for_core):
    return own, from_x, plane_swap(for_core, 1), plane_swap(from_x[1], 1)


def plane_body(
    tokens,
    doc_lengths,
    group_deal,
    qkv_weight,
    out_weight,
    up_weight,
    up_bias,
    down_weight,
    proj_weight,
    vectors,
    cotangent,
):
    me = lax.axis_index("ctx").astype(jnp.int32)
    line = lax.axis_index("wa").astype(jnp.int32)
    y, x, core = me // 4, (me // 2) % 2, me % 2
    scal = jnp.stack([me, line])
    spots = (scal, doc_lengths, group_deal)

    own_cols, ups, own_parts = call(
        cut_kernel,
        (scal, vectors, up_bias.reshape(1, -1), proj_weight)
        + (qkv_weight, up_weight, down_weight, out_weight),
        (SM, VM, VM, VM, HB, HB, HB, HB),
        [
            ((SHARD, 3 * WIDE), BF16),
            ((PLANE, SHARD, SLICE), BF16),
            ((PARTS + COLS + 16, SLICE), BF16),
        ],
        [
            pltpu.VMEM((SHARD, 3 * WIDTH), BF16),
            pltpu.VMEM((SHARD, INNER), BF16),
            pltpu.VMEM((PIECE, WIDTH), BF16),
            pltpu.VMEM((BLOCK, WIDTH), BF16),
            pltpu.SemaphoreType.DMA((4,)),
        ],
        mebibytes=BIG,
        name="cut",
    )
    line_parts = line_turns(own_parts)
    tokens, own_parts = lax.optimization_barrier((tokens, own_parts))
    mine, other = pick(tokens, y), pick(tokens, 1 - y)
    got = [plane_swap(other, 4), plane_swap(mine, 2), plane_swap(other, 6)]
    *line_parts, got_y, got_x, got_d = lax.optimization_barrier((*line_parts, *got))
    near = jnp.concatenate([mine, got_y, got_x, got_d])
    far = plane_swap(near, 1)
    cot_mine, cot_other = pick(cotangent, y), plane_swap(pick(cotangent, 1 - y), 4)
    far, cot_other = lax.optimization_barrier((far, cot_other))
    halves = jnp.stack([part[PARTS:] for part in line_parts])
    others = plane_swap(halves, 4)
    turns = jnp.stack([part[:PARTS] for part in line_parts])
    from_x = plane_swap(turns, 2)
    from_y = plane_swap(turns, 4)

    full, bias, ends = call(
        vectors_kernel,
        (scal, own_parts, halves),
        (SM, VM, VM),
        [((8, WIDTH), F32), ((PLANE, SLICE), F32), ((8, PAD), F32)],
        [pltpu.VMEM((LINE, 16, SHARD), F32)],
        name="vectors",
    )

    queries, keys, values, weights, att_own, att_core, att_x, lse = call(
        attend_kernel,
        (*spots, ends, own_cols, halves, others, near, far),
        (SM, SM, SM, *[VM] * 6),
        [
            ((SLOTS, PAD), BF16),
            ((SLOTS, PAD), BF16),
            ((SLOTS, PAD), BF16),
            ((WIDTH, 3 * PAD), BF16),
            ((OWN, PAD), BF16),
            ((OWN, PAD), BF16),
            ((2, OWN, PAD), BF16),
            ((4, 8, OWN), F32),
        ],
        [
            pltpu.VMEM((WIDTH, 3 * WIDE), BF16),
            pltpu.VMEM((SLOTS, SPAN), F32),
            pltpu.VMEM((PAD, SLOTS), BF16),
            pltpu.VMEM((PAD, OWN), F32),
            pltpu.VMEM((4, OWN, PAD), BF16),
            *[pltpu.VMEM((SLOTS, PAD), BF16)] * 3,
            pltpu.VMEM((WIDTH, 3 * PAD), BF16),
            pltpu.SemaphoreType.DMA((4,)),
        ],
        mebibytes=BIG,
        own=(0, 1, 2, 3),
        name="attend",
    )
    att_x = plane_swap(att_x, 2)
    from_x, from_y, att_x = lax.optimization_barrier((from_x, from_y, att_x))
    from_d = relay(from_x, from_y, core)
    parts = [turns, from_y, from_x, from_d]
    parts += [plane_swap(part, 1) for part in parts]
    groups = swap_groups(att_own, att_x, att_core)

    first_sum, normed_low = call(
        out_kernel,
        (scal, near, full, out_weight, *groups, *parts),
        (SM, VM, VM, VM, *[VM] * 4, *[HB] * 8),
        [
            ((OWN, WIDTH), F32),
            ((OWN, WIDTH), BF16),
        ],
        [pltpu.VMEM((LINE, PAD, WIDTH), BF16), pltpu.SemaphoreType.DMA],
        name="out",
    )
    normed_side = gather_side(normed_low)
    embedded, down_low, first_grad, grad_own, grad_core, grad_x, rest_mine, rest_other = call(
        middle_kernel,
        (*spots, first_sum, full, bias, proj_weight, out_weight, cot_mine, cot_other)
        + (*groups, ups, down_weight, *parts),
        (SM, SM, SM, *[VM] * 21),
        [
            ((OWN, EMBED), BF16),
            ((OWN, WIDTH), BF16),
            ((OWN, WIDTH), F32),
            *[((OWN, PAD), BF16)] * 2,
            ((2, OWN, PAD), BF16),
            *[((LINE, SPAN, WIDTH), BF16)] * 2,
        ],
        [
            pltpu.VMEM((OWN, WIDTH), BF16),
            pltpu.VMEM((OWN, WIDTH), F32),
            *[pltpu.VMEM((OWN, PAD), BF16)] * 2,
            pltpu.VMEM((2, OWN, PAD), BF16),
            *[pltpu.VMEM((LINE, SPAN, WIDTH), BF16)] * 2,
            pltpu.VMEM((PLANE, WIDTH, SLICE), BF16),
            pltpu.VMEM((PLANE, SLICE, WIDTH), BF16),
            pltpu.VMEM((LINE, PAD, WIDTH), BF16),
            pltpu.VMEM((WIDTH, EMBED), BF16),
            pltpu.VMEM((PLANE, OWN, SLICE), F32),
            pltpu.VMEM((WIDTH, EMBED), BF16),
            pltpu.VMEM((PLANE, SLICE), F32),
            pltpu.VMEM((4, PAD, WIDTH), BF16),
            pltpu.SemaphoreType.DMA((7,)),
        ],
        mebibytes=48,
        own=(1, 2, 3, 4, 5, 6, 7),
        name="middle",
    )
    *normed_side, down_low, embedded, grad_core, grad_x, rest_other = lax.optimization_barrier(
        (*normed_side, down_low, embedded, grad_core, grad_x, rest_other)
    )
    down_side = gather_side(down_low)
    embed_other = plane_swap(embedded[SPAN:], 4)
    embeddings = jnp.where(
        y == 0,
        jnp.stack([embedded[:SPAN], embed_other]),
        jnp.stack([embed_other, embedded[:SPAN]]),
    )

    grad_x = plane_swap(grad_x, 2)
    grads = swap_groups(grad_own, grad_x, grad_core)

    rest = rest_mine.astype(F32) + plane_swap(rest_other, 1).astype(F32)
    rest = rest.astype(BF16).reshape(LINE, 2, 64, WIDTH)
    rest_kept = lax.dynamic_index_in_dim(rest, x, 1, keepdims=False)
    rest_sent = lax.dynamic_index_in_dim(rest, 1 - x, 1, keepdims=False)
    rest_sent, first_grad = lax.optimization_barrier((rest_sent, first_grad))
    rest_sent = plane_swap(rest_sent, 2)

    qkv_mine, qkv_other, token_near, token_far = call(
        attend_back_kernel,
        (*spots, queries, keys, values, lse, weights, near, far, first_grad, *grads),
        (SM, SM, SM, HB, HB, HB, VM, *[HB] * 8),
        [
            *[((LINE, HALF + 16, 3 * WIDE), BF16)] * 2,
            ((2 * OWN, WIDTH), F32),
            ((2 * OWN, WIDTH), BF16),
        ],
        [
            *[pltpu.VMEM((LINE, HALF + 16, 3 * WIDE), BF16)] * 2,
            pltpu.VMEM((2 * OWN, WIDTH), F32),
            pltpu.VMEM((2 * OWN, WIDTH), BF16),
            *[pltpu.VMEM((SLOTS, PAD), BF16)] * 3,
            pltpu.VMEM((WIDTH, 3 * PAD), BF16),
            *[pltpu.VMEM((2 * OWN, WIDTH), BF16)] * 2,
            pltpu.VMEM((OWN, WIDTH), F32),
            pltpu.VMEM((4, OWN, PAD), BF16),
            pltpu.VMEM((SLOTS, SPAN), F32),
            pltpu.VMEM((PAD, SLOTS), BF16),
            pltpu.VMEM((PAD, OWN), F32),
            pltpu.VMEM((SLOTS, 3 * PAD), BF16),
            pltpu.VMEM((SLOTS, PAD), F32),
            pltpu.VMEM((SLOTS, PAD), F32),
            pltpu.VMEM((WIDTH, 3 * PAD), BF16),
            pltpu.SemaphoreType.DMA((15,)),
        ],
        mebibytes=BIG,
        own=(0, 1, 2, 3),
        name="attend_back",
    )

    rest = (rest_kept.astype(F32) + rest_sent.astype(F32)).astype(BF16)
    rest = rest.reshape(LINE, 2, 32, WIDTH)
    rest_kept = lax.dynamic_index_in_dim(rest, y, 1, keepdims=False)
    rest_sent = lax.dynamic_index_in_dim(rest, 1 - y, 1, keepdims=False)
    rest_sent = plane_swap(rest_sent, 4)

    *down_side, token_near = lax.optimization_barrier((*down_side, token_near))

    def slice_grad(turns, ups, down, name):
        (parts,) = call(
            partial(slice_grad_kernel, name == "slice_other"),
            (scal, bias, turns, ups, down, *normed_side, *down_side),
            (SM, VM, *[HB] * 11),
            [((LINE, 2 * HALF, WIDTH), BF16)],
            [
                pltpu.VMEM((LINE - 1, PARTS, SLICE), BF16),
                pltpu.VMEM((SHARD, SLICE), BF16),
                pltpu.VMEM((PIECE, WIDTH), BF16),
                pltpu.VMEM((PLANE, OWN, WIDTH), BF16),
                pltpu.VMEM((WIDTH, SLICE), F32),
                *[pltpu.VMEM((SLICE, WIDTH), BF16)] * 2,
                *[pltpu.VMEM((SLICE, WIDTH), F32)] * 2,
                pltpu.VMEM((WIDTH, SLICE), F32),
                pltpu.SemaphoreType.DMA((11,)),
            ],
            mebibytes=BIG,
            name=name,
        )
        return parts

    slices_other = slice_grad(parts[4], ups, down_weight, "slice_other")
    *down_side, slices_other = lax.optimization_barrier((*down_side, slices_other))
    slices_mine = slice_grad(turns, ups, down_weight, "slice_mine")
    slices_other = plane_swap(slices_other, 1)
    slices_mine, rest_sent = lax.optimization_barrier((slices_mine, rest_sent))
    rest = (rest_kept.astype(F32) + rest_sent.astype(F32)).astype(BF16)
    shard_parts = []
    for turn in range(LINE):
        total = slices_mine[turn].astype(F32) + slices_other[turn].astype(F32)
        shard_parts.append(jnp.concatenate([total.astype(BF16), rest[turn]]))
    shard_part = sum_parts(turn_parts(shard_parts))

    qkv_other = plane_swap(qkv_other, 4)
    qkv_parts = [
        (qkv_mine[turn].astype(F32) + qkv_other[turn].astype(F32)).astype(BF16)
        for turn in range(LINE)
    ]
    qkv_part = sum_parts(turn_parts(qkv_parts))

    near_sum = (token_near + plane_swap(token_far, 1).astype(F32)).reshape(4, SPAN, WIDTH)
    pair = near_sum[:2] + plane_swap(near_sum[2:].astype(BF16), 2).astype(F32)
    for_other = plane_swap(pair[1].astype(BF16), 4)
    for_mine, for_other = pair[0], for_other.astype(F32)
    tokens_grad = jnp.where(
        y == 0, jnp.stack([for_mine, for_other]), jnp.stack([for_other, for_mine])
    )
    up_grad, down_grad, out_grad, proj_grad, late_rows, bias_rows = call(
        rest_shard_kernel,
        (scal, *gather_plane(shard_part)),
        (SM, *[VM] * 5),
        [
            ((SHARD, INNER), F32),
            ((WIDTH, WIDTH), F32),
            ((SHARD, WIDTH), F32),
            ((SHARD, EMBED), F32),
            ((8, SHARD), F32),
            ((PLANE, PIECE), F32),
        ],
        [pltpu.VMEM((PLANE, 2 * HALF + 32, WIDTH), BF16)],
        name="rest_shard",
    )
    bias_grad = bias_rows.reshape(-1)
    qkv_grad, vectors_grad = call(
        qkv_shard_kernel,
        (scal, late_rows, *gather_plane(qkv_part)),
        (SM, *[VM] * 6),
        [((SHARD, 3 * WIDTH), F32), ((8, SHARD), F32)],
        [pltpu.VMEM((PLANE, HALF + 16, 3 * WIDE), BF16)],
        name="qkv_shard",
    )
    return (
        embeddings,
        tokens_grad,
        qkv_grad,
        out_grad,
        up_grad,
        bias_grad,
        down_grad,
        proj_grad,
        vectors_grad,
    )


def body(*arrays):
    sequences, span, width = arrays[0].shape
    fits = (
        lax.axis_size("ctx") == PLANE
        and lax.axis_size("wa") == LINE
        and sequences == 2
        and span == SPAN
        and width == WIDTH
    )
    return (plane_body if fits else general_body)(*arrays)


def solution(mesh):
    in_specs = (
        P("wa", "ctx", None),
        P(),
        P(),
        P("wa", None),
        P("wa", None),
        P("wa", None),
        P("wa"),
        P("wa", None),
        P("wa", None),
        P(None, "wa"),
        P("wa", "ctx", None),
    )
    out_specs = (
        P("wa", "ctx", None),
        P("wa", "ctx", None),
        P("wa", None),
        P("wa", None),
        P("wa", None),
        P("wa"),
        P("wa", None),
        P("wa", None),
        P(None, "wa"),
    )
    return jax.shard_map(body, mesh=mesh, in_specs=in_specs, out_specs=out_specs, check_vma=False)
```

```python
from functools import partial

import jax
import jax.numpy as jnp
from jax import lax
from jax.experimental import pallas as pl
from jax.experimental.pallas import tpu as pltpu
from jax.sharding import PartitionSpec as P

H = 12
HEAD = 64


NEG_FILL = -1e30
NORM_EPS = 1e-06
ROOT_HALF = 0.7071067811865476
DENSITY_SCALE = 0.3989422804014327


def norm_rows(inputs, gain_row, shift_row):
    middle = jnp.mean(inputs, axis=-1, keepdims=True)
    center = inputs - middle
    spread = jnp.mean(center * center, axis=-1, keepdims=True)
    scaled = lax.rsqrt(spread + NORM_EPS)
    unit_rows = center * scaled
    return (unit_rows * gain_row + shift_row, unit_rows, scaled)


def norm_back(grad_in, unit_rows, scaled, gain_row):
    gain_grad = jnp.sum(grad_in * unit_rows, axis=(0, 1))
    shift_grad = jnp.sum(grad_in, axis=(0, 1))
    inner_grad = grad_in * gain_row
    centered = inner_grad - jnp.mean(inner_grad, axis=-1, keepdims=True)
    result = scaled * (
        centered - unit_rows * jnp.mean(inner_grad * unit_rows, axis=-1, keepdims=True)
    )
    return (result, gain_grad, shift_grad)


def gelu_both(inner_sum):
    normal_cdf = 0.5 * (1.0 + lax.erf(inner_sum * ROOT_HALF))
    density = jnp.exp(-0.5 * inner_sum * inner_sum) * DENSITY_SCALE
    return (inner_sum * normal_cdf, normal_cdf + inner_sum * density)


def split_tiles(key_rows, value_rows, key_valid):
    key_count = key_rows.shape[0]
    tile_width = 512
    tile_count = key_count // tile_width
    return (
        key_rows.reshape(tile_count, tile_width, H, HEAD),
        value_rows.reshape(tile_count, tile_width, H, HEAD),
        key_valid.reshape(tile_count, tile_width),
    )


def masked_scores(queries, key_tile, mask_tile):
    products = jnp.einsum("qhd,khd->hqk", queries, key_tile, preferred_element_type=jnp.float32)
    return jnp.where(mask_tile[None, None, :], products, NEG_FILL)


def attend_forward(queries, key_rows, value_rows, key_valid):
    key_tiles, value_tiles, mask_tiles = split_tiles(key_rows, value_rows, key_valid)
    row_span = queries.shape[0]

    def stats_step(running, portion):
        highest, summed = running
        key_tile, mask_tile = portion
        scores = masked_scores(queries, key_tile, mask_tile)
        new_peak = jnp.maximum(highest, jnp.max(scores, axis=-1))
        raised = jnp.where(mask_tile[None, None, :], jnp.exp(scores - new_peak[:, :, None]), 0.0)
        return ((new_peak, summed * jnp.exp(highest - new_peak) + jnp.sum(raised, axis=-1)), None)

    start_peak = jnp.full((H, row_span), NEG_FILL, jnp.float32)
    start_sum = jnp.zeros((H, row_span), jnp.float32)
    (highest, summed), _ = lax.scan(stats_step, (start_peak, start_sum), (key_tiles, mask_tiles))
    logsum = highest + jnp.log(summed)

    def value_step(running, portion):
        key_tile, value_tile, mask_tile = portion
        scores = masked_scores(queries, key_tile, mask_tile)
        prob_low = jnp.where(
            mask_tile[None, None, :], jnp.exp(scores - logsum[:, :, None]), 0.0
        ).astype(jnp.bfloat16)
        return (
            running
            + jnp.einsum("hqk,khd->qhd", prob_low, value_tile, preferred_element_type=jnp.float32),
            None,
        )

    attended, _ = lax.scan(
        value_step,
        jnp.zeros((row_span, H, HEAD), jnp.float32),
        (key_tiles, value_tiles, mask_tiles),
    )
    return (attended, logsum)


def attend_backward(
    queries, key_rows, value_rows, key_valid, logsum, delta_rows, grad_heads, with_keys
):
    key_tiles, value_tiles, mask_tiles = split_tiles(key_rows, value_rows, key_valid)

    def back_step(running, portion):
        key_tile, value_tile, mask_tile = portion
        scores = masked_scores(queries, key_tile, mask_tile)
        prob_rows = jnp.where(mask_tile[None, None, :], jnp.exp(scores - logsum[:, :, None]), 0.0)
        prob_grad = jnp.einsum(
            "qhd,khd->hqk", grad_heads, value_tile, preferred_element_type=jnp.float32
        )
        score_low = (prob_rows * (prob_grad - delta_rows[:, :, None])).astype(jnp.bfloat16)
        running = running + jnp.einsum(
            "hqk,khd->qhd", score_low, key_tile, preferred_element_type=jnp.float32
        )
        value_part = jnp.einsum(
            "hqk,qhd->khd",
            prob_rows.astype(jnp.bfloat16),
            grad_heads,
            preferred_element_type=jnp.float32,
        )
        key_part = jnp.einsum(
            "hqk,qhd->khd", score_low, queries, preferred_element_type=jnp.float32
        )
        return (running, (key_part, value_part))

    start_grad = jnp.zeros(queries.shape, jnp.float32)
    query_grad, pieces = lax.scan(back_step, start_grad, (key_tiles, value_tiles, mask_tiles))
    key_count = key_rows.shape[0]
    return (
        query_grad,
        pieces[0].reshape(key_count, H * HEAD),
        pieces[1].reshape(key_count, H * HEAD),
    )


def general_body(
    tokens,
    doc_lengths,
    group_deal,
    qkv_weight,
    out_weight,
    up_weight,
    up_bias,
    down_weight,
    proj_weight,
    vectors,
    cotangent,
):
    gathered = (
        lax.all_gather(qkv_weight, "wa", axis=0, tiled=True),
        lax.all_gather(out_weight, "wa", axis=0, tiled=True),
        lax.all_gather(up_weight, "wa", axis=0, tiled=True),
        lax.all_gather(up_bias, "wa", axis=0, tiled=True),
        lax.all_gather(down_weight, "wa", axis=0, tiled=True),
        lax.all_gather(proj_weight, "wa", axis=0, tiled=True),
        lax.all_gather(vectors, "wa", axis=1, tiled=True),
    )
    qkv_full, out_full, up_full, bias_full, down_full, proj_full, vector_full = gathered
    seq_count, group_rows, model_width = tokens.shape
    ctx_count = lax.axis_size("ctx")
    seq_start = lax.axis_index("wa") * seq_count
    my_lengths = lax.dynamic_slice_in_dim(doc_lengths, seq_start, seq_count, 0)
    my_deal = lax.dynamic_slice_in_dim(group_deal, seq_start, seq_count, 0)
    offsets = jnp.tile(jnp.arange(group_rows, dtype=jnp.int32), ctx_count)
    positions = jnp.repeat(my_deal, group_rows, axis=1) * group_rows + offsets[None, :]
    key_valid = positions < my_lengths[:, None]
    query_valid = lax.dynamic_slice_in_dim(
        key_valid, lax.axis_index("ctx") * group_rows, group_rows, 1
    )
    row_mask = query_valid.astype(jnp.float32)[:, :, None]
    query_scale = HEAD ** (-0.5)
    mixed_rows = jnp.einsum("scd,de->sce", tokens, qkv_full, preferred_element_type=jnp.float32)
    queries = ((mixed_rows[:, :, :model_width] + vector_full[0]) * query_scale).astype(jnp.bfloat16)
    key_rows = mixed_rows[:, :, model_width : 2 * model_width].astype(jnp.bfloat16)
    value_rows = (mixed_rows[:, :, 2 * model_width :] + vector_full[1]).astype(jnp.bfloat16)
    all_keys, all_values = (
        lax.all_gather(key_rows, "ctx", axis=1, tiled=True),
        lax.all_gather(value_rows, "ctx", axis=1, tiled=True),
    )
    query_heads = queries.reshape(seq_count, group_rows, H, HEAD)
    attended, logsum = jax.vmap(attend_forward)(query_heads, all_keys, all_values, key_valid)
    attended_low = attended.reshape(seq_count, group_rows, model_width).astype(jnp.bfloat16)
    first_sum = tokens.astype(jnp.float32) + (
        jnp.einsum("scd,de->sce", attended_low, out_full, preferred_element_type=jnp.float32)
        + vector_full[2]
    )
    normed, unit_one, scale_one = norm_rows(first_sum, vector_full[3], vector_full[4])
    normed_low = normed.astype(jnp.bfloat16)
    inner_sum = (
        jnp.einsum("scd,df->scf", normed_low, up_full, preferred_element_type=jnp.float32)
        + bias_full
    )
    active, gelu_slope = gelu_both(inner_sum)
    active_low = active.astype(jnp.bfloat16)
    second_sum = normed + (
        jnp.einsum("scf,fd->scd", active_low, down_full, preferred_element_type=jnp.float32)
        + vector_full[5]
    )
    final_sum, unit_two, scale_two = norm_rows(second_sum, vector_full[6], vector_full[7])
    final_low = final_sum.astype(jnp.bfloat16)
    project = jnp.einsum("scd,de->sce", final_low, proj_full, preferred_element_type=jnp.float32)
    inverse = lax.rsqrt(jnp.sum(project * project, axis=-1, keepdims=True) + NORM_EPS)
    direction = project * inverse
    embeddings = (direction * row_mask).astype(jnp.bfloat16)
    upstream = cotangent.astype(jnp.float32) * row_mask
    project_grad = (
        inverse * (upstream - direction * jnp.sum(upstream * direction, axis=-1, keepdims=True))
    ).astype(jnp.bfloat16)
    proj_grad = jnp.einsum(
        "scd,sce->de", final_low, project_grad, preferred_element_type=jnp.float32
    )
    final_grad = jnp.einsum(
        "sce,de->scd", project_grad, proj_full, preferred_element_type=jnp.float32
    )
    second_grad, gain_two, shift_two = norm_back(final_grad, unit_two, scale_two, vector_full[6])
    down_low = second_grad.astype(jnp.bfloat16)
    down_grad = jnp.einsum("scf,scd->fd", active_low, down_low, preferred_element_type=jnp.float32)
    inner_grad = (
        jnp.einsum("scd,fd->scf", down_low, down_full, preferred_element_type=jnp.float32)
        * gelu_slope
    )
    bias_grad = jnp.sum(inner_grad, axis=(0, 1))
    inner_low = inner_grad.astype(jnp.bfloat16)
    up_grad = jnp.einsum("scd,scf->df", normed_low, inner_low, preferred_element_type=jnp.float32)
    normed_grad = second_grad + jnp.einsum(
        "scf,df->scd", inner_low, up_full, preferred_element_type=jnp.float32
    )
    first_grad, gain_one, shift_one = norm_back(normed_grad, unit_one, scale_one, vector_full[3])
    first_low = first_grad.astype(jnp.bfloat16)
    out_grad = jnp.einsum(
        "scd,sce->de", attended_low, first_low, preferred_element_type=jnp.float32
    )
    attended_grad = jnp.einsum(
        "sce,de->scd", first_low, out_full, preferred_element_type=jnp.float32
    ).astype(jnp.bfloat16)
    grad_heads = attended_grad.reshape(seq_count, group_rows, H, HEAD)
    delta_rows = jnp.sum(grad_heads.astype(jnp.float32) * attended, axis=-1)
    delta_heads = jnp.swapaxes(delta_rows, 1, 2)
    query_grad, key_terms, value_terms = jax.vmap(partial(attend_backward, with_keys=True))(
        query_heads, all_keys, all_values, key_valid, logsum, delta_heads, grad_heads
    )
    key_grad, value_grad = (
        lax.psum_scatter(
            key_terms.astype(jnp.bfloat16), "ctx", scatter_dimension=1, tiled=True
        ).astype(jnp.float32),
        lax.psum_scatter(
            value_terms.astype(jnp.bfloat16), "ctx", scatter_dimension=1, tiled=True
        ).astype(jnp.float32),
    )
    query_part = (
        query_grad.reshape(seq_count, group_rows, model_width).astype(jnp.bfloat16) * query_scale
    )
    value_part = value_grad.astype(jnp.bfloat16)
    mixed_grad = jnp.concatenate([query_part, key_grad.astype(jnp.bfloat16), value_part], axis=-1)
    qkv_grad = jnp.einsum("scd,sce->de", tokens, mixed_grad, preferred_element_type=jnp.float32)
    tokens_grad = first_grad + jnp.einsum(
        "sce,de->scd", mixed_grad, qkv_full, preferred_element_type=jnp.float32
    )
    vectors_grad = jnp.stack(
        [
            jnp.sum(query_part.astype(jnp.float32), axis=(0, 1)),
            jnp.sum(value_part.astype(jnp.float32), axis=(0, 1)),
            jnp.sum(first_grad, axis=(0, 1)),
            gain_one,
            shift_one,
            jnp.sum(second_grad, axis=(0, 1)),
            gain_two,
            shift_two,
        ],
        axis=0,
    )
    owned = (
        lax.psum_scatter(
            qkv_grad.astype(jnp.bfloat16), "wa", scatter_dimension=0, tiled=True
        ).astype(jnp.float32),
        lax.psum_scatter(
            out_grad.astype(jnp.bfloat16), "wa", scatter_dimension=0, tiled=True
        ).astype(jnp.float32),
        lax.psum_scatter(
            up_grad.astype(jnp.bfloat16), "wa", scatter_dimension=0, tiled=True
        ).astype(jnp.float32),
        lax.psum_scatter(
            bias_grad.astype(jnp.bfloat16), "wa", scatter_dimension=0, tiled=True
        ).astype(jnp.float32),
        lax.psum_scatter(
            down_grad.astype(jnp.bfloat16), "wa", scatter_dimension=0, tiled=True
        ).astype(jnp.float32),
        lax.psum_scatter(
            proj_grad.astype(jnp.bfloat16), "wa", scatter_dimension=0, tiled=True
        ).astype(jnp.float32),
        lax.psum_scatter(
            vectors_grad.astype(jnp.bfloat16), "wa", scatter_dimension=1, tiled=True
        ).astype(jnp.float32),
    )
    summed = (
        lax.psum(owned[0].astype(jnp.bfloat16), "ctx").astype(jnp.float32),
        lax.psum(owned[1].astype(jnp.bfloat16), "ctx").astype(jnp.float32),
        lax.psum(owned[2].astype(jnp.bfloat16), "ctx").astype(jnp.float32),
        lax.psum(owned[3].astype(jnp.bfloat16), "ctx").astype(jnp.float32),
        lax.psum(owned[4].astype(jnp.bfloat16), "ctx").astype(jnp.float32),
        lax.psum(owned[5].astype(jnp.bfloat16), "ctx").astype(jnp.float32),
        lax.psum(owned[6].astype(jnp.bfloat16), "ctx").astype(jnp.float32),
    )
    return (
        embeddings,
        tokens_grad,
        summed[0],
        summed[1],
        summed[2],
        summed[3],
        summed[4],
        summed[5],
        summed[6],
    )


PLANE = 8
LINE = 4
SPAN = 128
OWN = 2 * SPAN
WIDTH = H * HEAD
INNER = 4 * WIDTH
SHARD = WIDTH // LINE
HALF = SHARD // 2
PIECE = INNER // LINE // PLANE
SLICE = LINE * PIECE
HEADS = 3
WIDE = HEADS * HEAD
PAD = 256
SLOTS = PLANE * SPAN
BLOCK = SHARD // 4
FIRST = SHARD + BLOCK
SIDE = PIECE
PARTS = FIRST + 2 * SIDE
QUARTER = HALF // 2
COLS = HALF + QUARTER
EMBED = 128
ORDER = (0, 4, 2, 6, 1, 5, 3, 7)
NEAR = (0, 2, 1, 3)
F32 = jnp.float32
BF16 = jnp.bfloat16

NN = ((1,), (0,))
NT = ((1,), (1,))
TN = ((0,), (0,))


def dot(left, right, dims):
    return lax.dot_general(left, right, (dims, ((), ())), preferred_element_type=F32)


def plane_swap(array, bits):
    return lax.ppermute(array, "ctx", [(i, i ^ bits) for i in range(PLANE)])


def line_turn(array, step):
    return lax.ppermute(array, "wa", [(i, (i + step) % LINE) for i in range(LINE)])


def line_turns(array):
    return [line_turn(array, step) for step in range(1, LINE)]


def relay(from_x, from_y, core):
    passed = jnp.where(core == 0, from_y, from_x)
    pairs = [(i, i ^ 2 if i % 2 == 0 else i ^ 4) for i in range(PLANE)]
    return lax.ppermute(passed, "ctx", pairs)


def pick(array, index):
    return lax.dynamic_index_in_dim(array, index, 0, keepdims=False)


COST = {'cut': 3, 'vectors': 1, 'attend': 12, 'out': 3, 'middle': 17, 'attend_back': 18, 'rest_shard': 4, 'qkv_shard': 2, 'slice_other': 3.0, 'slice_mine': 3.0}
VM = pl.BlockSpec(memory_space=pltpu.VMEM)
SM = pl.BlockSpec(memory_space=pltpu.SMEM)
HB = pl.BlockSpec(memory_space=pl.ANY)
BIG = 56


def call(kernel, inputs, spaces, outputs, scratch=(), mebibytes=32, name=None, own=()):
    shapes = [jax.ShapeDtypeStruct(shape, kind) for shape, kind in outputs]
    return pl.pallas_call(
        kernel,
        out_shape=shapes,
        in_specs=list(spaces),
        out_specs=[HB if i in own else VM for i in range(len(shapes))],
        scratch_shapes=list(scratch),
        compiler_params=pltpu.CompilerParams(vmem_limit_bytes=mebibytes << 20),
        cost_estimate=pl.CostEstimate(flops=int(COST[name] * 1e9), bytes_accessed=1, transcendentals=0),
        name=name,
    )(*inputs)


def place_of(scal):
    return scal[0], scal[1]


def shard_of_turn(line, turn):
    return lax.rem(line - turn + LINE, LINE)


def turn_ahead(line, turn):
    return lax.rem(line + turn, LINE)


def norm_forward(rows):
    middle = jnp.mean(rows, axis=-1, keepdims=True)
    center = rows - middle
    scaled = lax.rsqrt(jnp.mean(center * center, axis=-1, keepdims=True) + NORM_EPS)
    return center * scaled, scaled


def norm_reverse(grad, unit, scaled, gain):
    inner = grad * gain
    return scaled * (
        inner
        - jnp.mean(inner, axis=-1, keepdims=True)
        - unit * jnp.mean(inner * unit, axis=-1, keepdims=True)
    )


def cut_kernel(
    scal, vectors, bias, proj, qkv, up, down, out,
    cols_ref, ups_ref, own_ref,
    qkv_held, up_held, down_held, out_held, sems,
):
    me, line = place_of(scal)
    core = lax.rem(me, 2)
    copies = [
        pltpu.make_async_copy(qkv, qkv_held, sems.at[0]),
        pltpu.make_async_copy(up, up_held, sems.at[1]),
        pltpu.make_async_copy(
            down.at[pl.ds(pl.multiple_of(me * PIECE, 16), PIECE)], down_held, sems.at[2]
        ),
        pltpu.make_async_copy(
            out.at[pl.ds(pl.multiple_of(lax.div(me, 2) * BLOCK, 16), BLOCK)], out_held, sems.at[3]
        ),
    ]
    for copy in copies:
        copy.start()
    rows = [vectors[...].astype(F32)]
    rows += [bias[:, a * SHARD : (a + 1) * SHARD].astype(F32) for a in range(LINE)]
    rows = jnp.concatenate(rows + [jnp.zeros((4, SHARD), F32)])
    own_ref[PARTS + COLS : PARTS + COLS + 16, :SHARD] = rows.astype(BF16)
    own_ref[PARTS + COLS : PARTS + COLS + 16, SHARD:] = jnp.zeros((16, SLICE - SHARD), BF16)
    for side in range(2):
        start = PARTS + COLS + 16 * (1 + side)
        for t in range(3):
            own_ref[start : start + 16, t * EMBED : (t + 1) * EMBED] = proj[
                pl.ds(pl.multiple_of(core * HALF + 16 * (3 * side + t), 16), 16), :
            ]
    copies[0].wait()
    for g in range(4):

        @pl.when(lax.rem(me, 4) == g)
        def _():
            for part in range(3):
                start = part * WIDTH + g * WIDE
                cols_ref[:, part * WIDE : (part + 1) * WIDE] = qkv_held[:, start : start + WIDE]

    base = lax.div(me, 4) * HALF
    rows = cols_ref[pl.ds(pl.multiple_of(base, 16), HALF), :]
    own_ref[PARTS : PARTS + HALF, :] = rows[:, :SLICE]
    for side in range(2):
        own_ref[PARTS + HALF : PARTS + COLS, side * WIDE : (side + 1) * WIDE] = rows[
            side * QUARTER : (side + 1) * QUARTER, SLICE:
        ]
    copies[1].wait()
    for k in range(PLANE):
        for s in range(LINE):
            start = s * PLANE * PIECE + k * PIECE
            ups_ref[k, :, s * PIECE : (s + 1) * PIECE] = up_held[:, start : start + PIECE]
    own_ref[:SHARD] = ups_ref[me]
    copies[2].wait()
    for side in range(2):
        start = FIRST + side * SIDE
        own_ref[start : start + PIECE] = down_held[:, side * SLICE : (side + 1) * SLICE]
    copies[3].wait()
    own_ref[SHARD:FIRST] = out_held[:, pl.ds(pl.multiple_of(core * SLICE, 128), SLICE)]


def vectors_kernel(scal, own, halves, full_ref, bias_ref, ends_ref, held):
    me, line = place_of(scal)
    held[line] = own[PARTS + COLS : PARTS + COLS + 16, :SHARD].astype(F32)
    for turn in range(1, LINE):
        held[shard_of_turn(line, turn)] = halves[turn - 1, COLS:, :SHARD].astype(F32)
    for a in range(LINE):
        full_ref[:, a * SHARD : (a + 1) * SHARD] = held[a, :8, :]
        for k in range(PLANE):
            start = (k % 2) * PIECE
            bias_ref[k : k + 1, a * PIECE : (a + 1) * PIECE] = held[
                a, 8 + k // 2 : 9 + k // 2, start : start + PIECE
            ]
    ends_ref[...] = jnp.zeros((8, PAD), F32)
    ends_ref[:, :WIDE] = held[lax.rem(me, 4), :8, :]


def slots_left(scal, lengths, deal, place):
    me, line = place_of(scal)
    seq = 2 * line + lax.div(me, 4)
    return lengths[seq] - deal[seq, me ^ ORDER[place]] * SPAN


def fill_mask(scal, lengths, deal, mask):
    rows = lax.broadcasted_iota(jnp.int32, (SPAN, SPAN), 0)
    for place in range(PLANE):
        limit = slots_left(scal, lengths, deal, place)
        mask[place * SPAN : (place + 1) * SPAN, :] = jnp.where(rows < limit, 0.0, NEG_FILL)


def head_lanes(h):
    lanes = lax.broadcasted_iota(jnp.int32, (OWN, 128), 1)
    return (lanes >= HEAD) if h % 2 else (lanes < HEAD)


def attend_kernel(
    scal, lengths, deal, ends, own_cols, halves, others, near, far,
    q_out, k_out, v_out, w_out, own_ref, core_ref, x_ref, lse_ref,
    raw, mask, v_turned, o_turned, att, q_ref, k_ref, v_ref, w_ref, sems,
):
    me, line = place_of(scal)
    y = lax.div(me, 4)
    raw[pl.ds(pl.multiple_of(line * SHARD, 16), SHARD), :] = own_cols[...]
    for turn in range(1, LINE):
        base = shard_of_turn(line, turn) * SHARD
        for source, side in ((halves, y), (others, 1 - y)):
            start = base + side * HALF
            at = pl.ds(pl.multiple_of(start, 16), HALF)
            raw[at, :SLICE] = source[turn - 1, :HALF, :]
            for i in range(2):
                at = pl.ds(pl.multiple_of(start + i * QUARTER, 16), QUARTER)
                raw[at, SLICE:] = source[turn - 1, HALF:COLS, i * WIDE : (i + 1) * WIDE]
    fill_mask(scal, lengths, deal, mask)
    for part in range(3):
        w_ref[:, part * PAD : part * PAD + WIDE] = raw[:, part * WIDE : (part + 1) * WIDE]
        w_ref[:, part * PAD + WIDE : (part + 1) * PAD] = jnp.zeros((WIDTH, PAD - WIDE), BF16)
    for t in range(4):
        source = (near, far)[t // 2]
        rows = source[(t % 2) * OWN : (t % 2 + 1) * OWN, :]
        mixed = dot(rows, w_ref[...], NN)
        at = slice(t * OWN, (t + 1) * OWN)
        q_ref[at, :] = ((mixed[:, :PAD] + ends[0:1, :]) * (HEAD ** (-0.5))).astype(BF16)
        k_ref[at, :] = mixed[:, PAD : 2 * PAD].astype(BF16)
        values = mixed[:, 2 * PAD :] + ends[1:2, :]
        v_ref[at, :] = values.astype(BF16)
        v_turned[:, at] = values.T.astype(BF16)

    copies = [
        pltpu.make_async_copy(source, target, sems.at[i])
        for i, (source, target) in enumerate(
            ((q_ref, q_out), (k_ref, k_out), (v_ref, v_out), (w_ref, w_out))
        )
    ]
    for copy in copies:
        copy.start()
    o_turned[WIDE:, :] = jnp.zeros((PAD - WIDE, OWN), F32)

    def tile(t, carry):
        at = pl.ds(pl.multiple_of(t * OWN, OWN), OWN)
        for h in range(HEADS):
            cut = slice((h // 2) * 128, (h // 2 + 1) * 128)
            q_tile = jnp.where(head_lanes(h), q_ref[at, cut], jnp.zeros((), BF16))
            scores = dot(k_ref[:, cut], q_tile, NT)
            scores = scores + jnp.concatenate([mask[...], mask[...]], axis=1)
            peak = jnp.max(scores, axis=0, keepdims=True)
            raised = jnp.exp(scores - peak)
            total = jnp.sum(raised, axis=0, keepdims=True)
            rows = slice(h * HEAD, (h + 1) * HEAD)
            o_turned[rows, :] = dot(v_turned[rows, :], raised.astype(BF16), NN) * (1.0 / total)
            lse_ref[t, h : h + 1, :] = peak + jnp.log(total)
        att[t] = o_turned[...].T.astype(BF16)
        return carry

    lax.fori_loop(0, 4, tile, 0)
    own_ref[...] = att[0]
    core_ref[...] = att[2]
    x_ref[0] = att[1]
    x_ref[1] = att[3]
    for copy in copies:
        copy.wait()


def attend_back_kernel(
    scal, lengths, deal, q_ref, k_ref, v_ref, lse, weights, near, far, first_grad, g0, g1, g2, g3,
    mine_out, other_out, near_out, far_out,
    mine_ref, other_ref, near_ref, far_ref,
    q_held, k_held, v_held, w_held, near_held, far_held, first_held, grads,
    mask, k_turned, q_turned, mixed, key_sum, value_sum, part, sems,
):
    sources = (k_ref, q_ref, v_ref, g0, g1.at[0], g2, g3, weights, near, far, first_grad)
    targets = (k_held, q_held, v_held, grads.at[0], grads.at[1], grads.at[2], grads.at[3])
    targets += (w_held, near_held, far_held, first_held)
    copies = [
        pltpu.make_async_copy(source, target, sems.at[i])
        for i, (source, target) in enumerate(zip(sources, targets, strict=True))
    ]
    for copy in copies:
        copy.start()
    fill_mask(scal, lengths, deal, mask)
    copies[0].wait()
    for t in range(4):
        at = slice(t * OWN, (t + 1) * OWN)
        k_turned[:, at] = k_held[at, :].astype(F32).T.astype(BF16)
    key_sum[...] = jnp.zeros_like(key_sum)
    value_sum[...] = jnp.zeros_like(value_sum)
    q_turned[WIDE:, :] = jnp.zeros((PAD - WIDE, OWN), F32)
    for copy in copies[1:7]:
        copy.wait()

    def tile(t, carry):
        at = pl.ds(pl.multiple_of(t * OWN, OWN), OWN)
        for h in range(HEADS):
            cut = slice((h // 2) * 128, (h // 2 + 1) * 128)
            rows = slice(h * HEAD, (h + 1) * HEAD)
            q_tile = jnp.where(head_lanes(h), q_held[at, cut], jnp.zeros((), BF16))
            g_tile = jnp.where(head_lanes(h), grads[t, :, cut], jnp.zeros((), BF16))
            scores = dot(k_held[:, cut], q_tile, NT)
            scores = scores + jnp.concatenate([mask[...], mask[...]], axis=1)
            probs = jnp.exp(scores - lse[t, h : h + 1, :])
            prob_grad = dot(v_held[:, cut], g_tile, NT)
            delta = jnp.sum(probs * prob_grad, axis=0, keepdims=True)
            score_low = (probs * (prob_grad - delta)).astype(BF16)
            q_turned[rows, :] = dot(k_turned[rows, :], score_low, NN)
            key_sum[:, cut] += dot(score_low, q_tile, NN)
            value_sum[:, cut] += dot(probs.astype(BF16), g_tile, NN)
        low = q_turned[...].T.astype(BF16)
        mixed[at, :PAD] = (low.astype(F32) * (HEAD ** (-0.5))).astype(BF16)
        return carry

    lax.fori_loop(0, 4, tile, 0)
    mixed[:, PAD : 2 * PAD] = key_sum[...].astype(BF16)
    mixed[:, 2 * PAD :] = value_sum[...].astype(BF16)

    me, line = place_of(scal)
    y = lax.div(me, 4)
    for copy in copies[7:]:
        copy.wait()
    for i in range(3):
        cut = slice(i * 256, (i + 1) * 256)
        part[cut, :] = (
            dot(near_held[:, cut], mixed[: 2 * OWN, :], TN) + dot(far_held[:, cut], mixed[2 * OWN :, :], TN)
        ).astype(BF16)
    sums = jnp.sum(mixed[...].astype(F32), axis=0, keepdims=True)
    sums = jnp.concatenate([sums, jnp.zeros((15, 3 * PAD), F32)]).astype(BF16)
    for turn in range(LINE):
        base = turn_ahead(line, turn) * SHARD
        for target, side in ((mine_ref, y), (other_ref, 1 - y)):
            rows = part[pl.ds(pl.multiple_of(base + side * HALF, 16), HALF), :]
            for p in range(3):
                to = slice(p * WIDE, (p + 1) * WIDE)
                target[turn, :HALF, to] = rows[:, p * PAD : p * PAD + WIDE]
                target[turn, HALF:, to] = sums[:, p * PAD : p * PAD + WIDE]
    outs = [
        pltpu.make_async_copy(source, target, sems.at[11 + i])
        for i, (source, target) in enumerate(
            (
                (other_ref, other_out),
                (mine_ref, mine_out),
                (far_ref, far_out),
                (near_ref, near_out),
            )
        )
    ]
    outs[0].start()
    outs[1].start()
    for t in (2, 3, 0, 1):
        at = slice(t * OWN, (t + 1) * OWN)
        token_part = dot(mixed[at, :], w_held[...], NT)
        if t == 0:
            near_ref[at, :] = token_part + first_held[...]
        elif t == 1:
            near_ref[at, :] = token_part
        else:
            far_ref[(t - 2) * OWN : (t - 1) * OWN, :] = token_part.astype(BF16)
        if t == 3:
            outs[2].start()
    outs[3].start()
    for copy in outs:
        copy.wait()


def out_kernel(
    scal, near, full, out_shard, a0, a1, a2, a3, p0, p1, p2, p3, p4, p5, p6, p7,
    sum_ref, low_ref,
    out_ref, sem,
):
    me, line = place_of(scal)
    group = lax.rem(me, 4)
    pieces = (p0, p1, p2, p3, p4, p5, p6, p7)
    copies = []
    for place, bits in enumerate(ORDER):
        k = me ^ bits
        rows = pl.ds(pl.multiple_of(lax.div(k, 2) * BLOCK, 16), BLOCK)
        lanes = pl.ds(pl.multiple_of(lax.rem(k, 2) * SLICE, 128), SLICE)
        for turn in range(1, LINE):
            copies.append(
                pltpu.make_async_copy(
                    pieces[place].at[turn - 1, pl.ds(SHARD, BLOCK)],
                    out_ref.at[shard_of_turn(line, turn), rows, lanes],
                    sem,
                )
            )
    for copy in copies:
        copy.start()
    for z in range(LINE):
        out_ref[z, SHARD:, :] = jnp.zeros((PAD - SHARD, WIDTH), BF16)
    out_ref[line, :SHARD, :] = out_shard[...]
    rows = near[:OWN, :].astype(F32) + full[2:3, :]
    filled = out_ref.at[pl.ds(0, LINE - 1), pl.ds(0, SHARD)]
    pltpu.make_async_copy(filled, filled, sem).wait()
    for i, source in enumerate((a0[...], a1[0], a2[...], a3[...])):
        rows = rows + dot(source, out_ref[group ^ NEAR[i]], NN)
    sum_ref[...] = rows
    unit, _ = norm_forward(rows)
    low_ref[...] = (unit * full[3:4, :] + full[4:5, :]).astype(BF16)


def place_up(scal, place, up_own, held, up_all):
    me, line = place_of(scal)
    at = pl.ds(pl.multiple_of(line * SHARD, 16), SHARD)
    up_all[place, at, :] = up_own[me ^ ORDER[place]]
    for turn in range(1, LINE):
        at = pl.ds(pl.multiple_of(shard_of_turn(line, turn) * SHARD, 16), SHARD)
        up_all[place, at, :] = held[place][turn - 1, :SHARD, :]


def place_down(scal, place, down_own, held, down_all):
    me, line = place_of(scal)
    at = pl.ds(pl.multiple_of(line * PIECE, 16), PIECE)
    start = pl.multiple_of((me ^ ORDER[place]) * PIECE, 16)
    down_all[place, at, :] = down_own[pl.ds(start, PIECE), :]
    for turn in range(1, LINE):
        at = pl.ds(pl.multiple_of(shard_of_turn(line, turn) * PIECE, 16), PIECE)
        for side in range(2):
            start = FIRST + side * SIDE
            down_all[place, at, side * SLICE : (side + 1) * SLICE] = held[place][
                turn - 1, start : start + PIECE, :
            ]


def place_out(scal, place, held, out_all):
    me, line = place_of(scal)
    k = me ^ ORDER[place]
    rows = pl.ds(pl.multiple_of(lax.div(k, 2) * BLOCK, 16), BLOCK)
    lanes = pl.ds(pl.multiple_of(lax.rem(k, 2) * SLICE, 128), SLICE)
    for turn in range(1, LINE):
        out_all[shard_of_turn(line, turn), rows, lanes] = held[place][turn - 1, SHARD:FIRST, :]


def middle_kernel(
    scal, lengths, deal, first_sum, full, bias, proj_shard, out_shard, cot_mine, cot_other,
    proj_near, proj_far, a0, a1, a2, a3, ups, down, p0, p1, p2, p3, p4, p5, p6, p7,
    embed_ref, low_out, first_out, own_out, core_out, x_out, mine_out, other_out,
    low_ref, first_ref, own_ref, core_ref, x_ref, mine_ref, other_ref,
    up_all, down_all, out_all, proj_all, slopes, proj_part, bias_sum, out_part, sems,
):
    held = (p0, p1, p2, p3, p4, p5, p6, p7)
    up_own, down_own = ups, down
    me, line = place_of(scal)
    core, group = lax.rem(me, 2), lax.rem(me, 4)
    proj_all[pl.ds(pl.multiple_of(line * SHARD, 16), SHARD), :] = proj_shard[...]

    unit_one, scale_one = norm_forward(first_sum[...])
    normed = unit_one * full[3:4, :] + full[4:5, :]
    normed_low = normed.astype(BF16)
    second_sum = normed + full[5:6, :]
    for z in range(LINE):
        out_all[z, SHARD:, :] = jnp.zeros((PAD - SHARD, WIDTH), BF16)
    out_all[line, :SHARD, :] = out_shard[...]
    for place, bits in enumerate(ORDER):
        place_up(scal, place, up_own, held, up_all)
        place_down(scal, place, down_own, held, down_all)
        place_out(scal, place, held, out_all)
        inner = dot(normed_low, up_all[place], NN) + bias[pl.ds(me ^ bits, 1), :]
        active, slope = gelu_both(inner)
        slopes[place] = slope
        second_sum = second_sum + dot(active.astype(BF16), down_all[place], NN)
    unit, scaled = norm_forward(second_sum)
    final_low = (unit * full[6:7, :] + full[7:8, :]).astype(BF16)
    for half, source in ((core, proj_near), (1 - core, proj_far)):
        for turn in range(1, LINE):
            base = shard_of_turn(line, turn) * SHARD + half * HALF
            for t in range(6):
                start = 16 * (t // 3)
                proj_all[pl.ds(pl.multiple_of(base + 16 * t, 16), 16), :] = source[
                    turn - 1, start : start + 16, (t % 3) * EMBED : (t % 3 + 1) * EMBED
                ]
    project = dot(final_low, proj_all[...], NN)
    inverse = lax.rsqrt(jnp.sum(project * project, axis=-1, keepdims=True) + NORM_EPS)
    direction = project * inverse
    rows = lax.broadcasted_iota(jnp.int32, (SPAN, EMBED), 0)
    keep = jnp.concatenate(
        [
            jnp.where(rows < slots_left(scal, lengths, deal, i), 1.0, 0.0).astype(F32)
            for i in range(2)
        ]
    )
    embed_ref[...] = (direction * keep).astype(BF16)
    upstream = jnp.concatenate([cot_mine[...], cot_other[...]]).astype(F32) * keep
    project_grad = (
        inverse * (upstream - direction * jnp.sum(upstream * direction, axis=-1, keepdims=True))
    ).astype(BF16)
    proj_part[...] = dot(final_low, project_grad, TN).astype(BF16)
    final_grad = dot(project_grad, proj_all[...], NT)
    second_grad = norm_reverse(final_grad, unit, scaled, full[6:7, :])
    down_low = second_grad.astype(BF16)
    low_ref[...] = down_low
    outs = [
        pltpu.make_async_copy(source, target, sems.at[i])
        for i, (source, target) in enumerate(
            (
                (low_ref, low_out),
                (x_ref, x_out),
                (core_ref, core_out),
                (own_ref, own_out),
                (first_ref, first_out),
                (other_ref, other_out),
                (mine_ref, mine_out),
            )
        )
    ]
    outs[0].start()

    normed_grad = second_grad
    for place, bits in enumerate(ORDER):
        inner_grad = dot(down_low, down_all[place], NT) * slopes[place]
        bias_sum[pl.ds(me ^ bits, 1), :] = jnp.sum(inner_grad, axis=0, keepdims=True)
        normed_grad = normed_grad + dot(inner_grad.astype(BF16), up_all[place], NT)
    first_grad = norm_reverse(normed_grad, unit_one, scale_one, full[3:4, :])
    first_ref[...] = first_grad
    first_low = first_grad.astype(BF16)
    for i, target in enumerate((own_ref, x_ref.at[0], core_ref, x_ref.at[1])):
        target[...] = dot(first_low, out_all[group ^ NEAR[i]], NT).astype(BF16)
    for copy in outs[1:5]:
        copy.start()
    small = jnp.concatenate(
        [
            jnp.sum(first_grad, axis=0, keepdims=True),
            jnp.sum(normed_grad * unit_one, axis=0, keepdims=True),
            jnp.sum(normed_grad, axis=0, keepdims=True),
            jnp.sum(second_grad, axis=0, keepdims=True),
            jnp.sum(final_grad * unit, axis=0, keepdims=True),
            jnp.sum(final_grad, axis=0, keepdims=True),
            jnp.zeros((2, WIDTH), F32),
        ]
    )
    tail = jnp.concatenate([bias_sum[...], jnp.zeros((8, WIDTH - SLICE), F32)], axis=1)
    small = jnp.concatenate([small, tail]).astype(BF16)
    for i, source in enumerate((a0[...], a1[0], a2[...], a3[...])):
        z = group ^ NEAR[i]
        turn = lax.rem(z - line + LINE, LINE)
        out_part[i] = dot(source, first_low, TN).astype(BF16)
        for target, half in ((mine_ref, core), (other_ref, 1 - core)):
            base = half * HALF
            target[turn, :HALF, :] = out_part[i, pl.ds(pl.multiple_of(base, 16), HALF), :]
            for t in range(6):
                target[turn, HALF : HALF + 16, t * EMBED : (t + 1) * EMBED] = proj_part[
                    pl.ds(pl.multiple_of(z * SHARD + base + 16 * t, 16), 16), :
                ]
            target[turn, HALF + 16 :, :] = small
    outs[5].start()
    outs[6].start()
    for copy in outs:
        copy.wait()


def slice_grad_kernel(
    other, scal, bias, turns, ups, down, n0, n1, n2, n3, d0, d1, d2, d3,
    part_ref,
    held, ups_held, down_held, slots, up_rows, up_turned, down_rows, up_sum, down_sum, up_back,
    sems,
):
    me, line = place_of(scal)
    k = me ^ 1 if other else me
    copies = [
        pltpu.make_async_copy(turns, held, sems.at[0]),
        pltpu.make_async_copy(ups.at[k], ups_held, sems.at[1]),
        pltpu.make_async_copy(
            down.at[pl.ds(pl.multiple_of(k * PIECE, 16), PIECE)], down_held, sems.at[2]
        ),
    ]
    for j, source in enumerate((n0, d0, n1, d1, n2, d2, n3, d3)):
        copies.append(pltpu.make_async_copy(source, slots.at[j], sems.at[3 + j]))
    for copy in copies:
        copy.start()
    for copy in copies[:3]:
        copy.wait()
    for turn in range(LINE):
        z = shard_of_turn(line, turn)
        rows = held[turn - 1, :SHARD, :] if turn else ups_held[...]
        up_rows[pl.ds(pl.multiple_of(z * SHARD, 16), SHARD), :] = rows.astype(F32)
        at = pl.ds(pl.multiple_of(z * PIECE, 16), PIECE)
        if turn == 0:
            down_rows[at, :] = down_held[...]
            continue
        for side in range(2):
            start = FIRST + side * SIDE
            down_rows[at, side * SLICE : (side + 1) * SLICE] = held[
                turn - 1, start : start + PIECE, :
            ]
    up_turned[...] = up_rows[...].T.astype(BF16)
    bias_rows = jnp.broadcast_to(bias[pl.ds(k, 1), :], (128, SLICE)).T
    bias_rows = jnp.concatenate([bias_rows, bias_rows], axis=1)
    for j in range(4):
        copies[3 + 2 * j].wait()
        copies[4 + 2 * j].wait()
        normed, low = slots[2 * j], slots[2 * j + 1]
        inner = dot(up_turned[...], normed, NT) + bias_rows
        active, slope = gelu_both(inner)
        inner_low = (dot(down_rows[...], low, NT) * slope).astype(BF16)
        up_part = dot(inner_low, normed, NN)
        down_part = dot(active.astype(BF16), low, NN)
        if j == 0:
            up_sum[...] = up_part
            down_sum[...] = down_part
        else:
            up_sum[...] += up_part
            down_sum[...] += down_part
    up_back[...] = up_sum[...].T
    for turn in range(LINE):
        z = turn_ahead(line, turn)
        for side in range(2):
            at = pl.ds(pl.multiple_of(z * SHARD + side * HALF, 16), HALF)
            part_ref[turn, :HALF, side * SLICE : (side + 1) * SLICE] = up_back[at, :].astype(BF16)
        at = pl.ds(pl.multiple_of(z * PIECE, 16), PIECE)
        part_ref[turn, HALF:, :] = down_sum[at, :].astype(BF16)


def hold_parts(me, close, far, held):
    for place in range(4):
        held[me ^ ORDER[place]] = close[place][...]
        held[me ^ ORDER[place + 4]] = far[place]


def rest_shard_kernel(
    scal, p0, p1, p2, p3, far,
    up_ref, down_ref, out_ref, proj_ref, rows_ref, bias_ref, held,
):
    me, line = place_of(scal)
    hold_parts(me, (p0, p1, p2, p3), far, held)
    for k in range(PLANE):
        core, x, y = k % 2, (k // 2) % 2, k // 4
        for side in range(2):
            rows = held[k, :HALF, side * SLICE : (side + 1) * SLICE].astype(F32)
            for s in range(LINE):
                start = s * PLANE * PIECE + k * PIECE
                up_ref[side * HALF : (side + 1) * HALF, start : start + PIECE] = rows[
                    :, s * PIECE : (s + 1) * PIECE
                ]
        down_ref[k * PIECE : (k + 1) * PIECE, :] = held[k, HALF : 2 * HALF, :].astype(F32)
        tail = held[k, 2 * HALF :, :].astype(F32)
        block = 2 * x + y
        if block < 3:
            start = core * HALF + 32 * block
            out_ref[start : start + 32, :] = tail
        else:
            for t in range(6):
                start = core * HALF + 16 * t
                proj_ref[start : start + 16, :] = tail[:16, t * EMBED : (t + 1) * EMBED]
            if core == 0:
                small = tail[16:, :]
    for z in range(LINE):

        @pl.when(line == z)
        def _():
            rows_ref[...] = small[:8, z * SHARD : (z + 1) * SHARD]
            bias_ref[...] = small[8:, z * PIECE : (z + 1) * PIECE]


def qkv_shard_kernel(scal, late, p0, p1, p2, p3, far, qkv_ref, rows_ref, held):
    me, line = place_of(scal)
    hold_parts(me, (p0, p1, p2, p3), far, held)
    for k in range(PLANE):
        y, g = k // 4, k % 4
        for part in range(3):
            start = part * WIDTH + g * WIDE
            qkv_ref[y * HALF : (y + 1) * HALF, start : start + WIDE] = held[
                k, :HALF, part * WIDE : (part + 1) * WIDE
            ].astype(F32)
    sums = held[line, HALF:, :].astype(F32)
    rows_ref[...] = jnp.concatenate(
        [sums[:1, :WIDE], sums[:1, 2 * WIDE : 3 * WIDE], late[:6, :]]
    )


def gather_side(array):
    return [array, plane_swap(array, 4), plane_swap(array, 2), plane_swap(array, 6)]


def gather_plane(array):
    close = gather_side(array)
    return close + [plane_swap(jnp.stack(close), 1)]


def turn_parts(parts):
    return [parts[0]] + [line_turn(parts[turn], turn) for turn in range(1, LINE)]


def sum_parts(parts):
    total = parts[0].astype(F32)
    for part in parts[1:]:
        total = total + part.astype(F32)
    return total.astype(BF16)


def swap_groups(own, from_x, for_core):
    return own, from_x, plane_swap(for_core, 1), plane_swap(from_x[1], 1)


def plane_body(
    tokens,
    doc_lengths,
    group_deal,
    qkv_weight,
    out_weight,
    up_weight,
    up_bias,
    down_weight,
    proj_weight,
    vectors,
    cotangent,
):
    me = lax.axis_index("ctx").astype(jnp.int32)
    line = lax.axis_index("wa").astype(jnp.int32)
    y, x, core = me // 4, (me // 2) % 2, me % 2
    scal = jnp.stack([me, line])
    spots = (scal, doc_lengths, group_deal)

    own_cols, ups, own_parts = call(
        cut_kernel,
        (scal, vectors, up_bias.reshape(1, -1), proj_weight)
        + (qkv_weight, up_weight, down_weight, out_weight),
        (SM, VM, VM, VM, HB, HB, HB, HB),
        [
            ((SHARD, 3 * WIDE), BF16),
            ((PLANE, SHARD, SLICE), BF16),
            ((PARTS + COLS + 48, SLICE), BF16),
        ],
        [
            pltpu.VMEM((SHARD, 3 * WIDTH), BF16),
            pltpu.VMEM((SHARD, INNER), BF16),
            pltpu.VMEM((PIECE, WIDTH), BF16),
            pltpu.VMEM((BLOCK, WIDTH), BF16),
            pltpu.SemaphoreType.DMA((4,)),
        ],
        mebibytes=BIG,
        name="cut",
    )
    line_parts = line_turns(own_parts)
    tokens, own_parts = lax.optimization_barrier((tokens, own_parts))
    mine, other = pick(tokens, y), pick(tokens, 1 - y)
    got = [plane_swap(other, 4), plane_swap(mine, 2), plane_swap(other, 6)]
    *line_parts, got_y, got_x, got_d = lax.optimization_barrier((*line_parts, *got))
    near = jnp.concatenate([mine, got_y, got_x, got_d])
    far = plane_swap(near, 1)
    cot_mine, cot_other = pick(cotangent, y), plane_swap(pick(cotangent, 1 - y), 4)
    far, cot_other = lax.optimization_barrier((far, cot_other))
    halves = jnp.stack([part[PARTS : PARTS + COLS + 16] for part in line_parts])
    proj_near = jnp.stack([part[PARTS + COLS + 16 :] for part in line_parts])
    proj_far = plane_swap(proj_near, 1)
    others = plane_swap(halves, 4)
    turns = jnp.stack([part[:PARTS] for part in line_parts])
    from_x = plane_swap(turns, 2)
    from_y = plane_swap(turns, 4)

    full, bias, ends = call(
        vectors_kernel,
        (scal, own_parts, halves),
        (SM, VM, VM),
        [((8, WIDTH), F32), ((PLANE, SLICE), F32), ((8, PAD), F32)],
        [pltpu.VMEM((LINE, 16, SHARD), F32)],
        name="vectors",
    )

    queries, keys, values, weights, att_own, att_core, att_x, lse = call(
        attend_kernel,
        (*spots, ends, own_cols, halves, others, near, far),
        (SM, SM, SM, *[VM] * 6),
        [
            ((SLOTS, PAD), BF16),
            ((SLOTS, PAD), BF16),
            ((SLOTS, PAD), BF16),
            ((WIDTH, 3 * PAD), BF16),
            ((OWN, PAD), BF16),
            ((OWN, PAD), BF16),
            ((2, OWN, PAD), BF16),
            ((4, 8, OWN), F32),
        ],
        [
            pltpu.VMEM((WIDTH, 3 * WIDE), BF16),
            pltpu.VMEM((SLOTS, SPAN), F32),
            pltpu.VMEM((PAD, SLOTS), BF16),
            pltpu.VMEM((PAD, OWN), F32),
            pltpu.VMEM((4, OWN, PAD), BF16),
            *[pltpu.VMEM((SLOTS, PAD), BF16)] * 3,
            pltpu.VMEM((WIDTH, 3 * PAD), BF16),
            pltpu.SemaphoreType.DMA((4,)),
        ],
        mebibytes=BIG,
        own=(0, 1, 2, 3),
        name="attend",
    )
    att_x = plane_swap(att_x, 2)
    from_x, from_y, att_x = lax.optimization_barrier((from_x, from_y, att_x))
    from_d = relay(from_x, from_y, core)
    groups = list(swap_groups(att_own, att_x, att_core))
    from_d, groups[2], groups[3] = lax.optimization_barrier((from_d, groups[2], groups[3]))
    parts = [turns, from_y, from_x, from_d]
    parts += [plane_swap(part, 1) for part in parts]

    first_sum, normed_low = call(
        out_kernel,
        (scal, near, full, out_weight, *groups, *parts),
        (SM, VM, VM, VM, *[VM] * 4, *[HB] * 8),
        [
            ((OWN, WIDTH), F32),
            ((OWN, WIDTH), BF16),
        ],
        [pltpu.VMEM((LINE, PAD, WIDTH), BF16), pltpu.SemaphoreType.DMA],
        name="out",
    )
    normed_side = gather_side(normed_low)
    embedded, down_low, first_grad, grad_own, grad_core, grad_x, rest_mine, rest_other = call(
        middle_kernel,
        (*spots, first_sum, full, bias, proj_weight, out_weight, cot_mine, cot_other)
        + (proj_near, proj_far, *groups, ups, down_weight, *parts),
        (SM, SM, SM, *[VM] * 23),
        [
            ((OWN, EMBED), BF16),
            ((OWN, WIDTH), BF16),
            ((OWN, WIDTH), F32),
            *[((OWN, PAD), BF16)] * 2,
            ((2, OWN, PAD), BF16),
            *[((LINE, SPAN, WIDTH), BF16)] * 2,
        ],
        [
            pltpu.VMEM((OWN, WIDTH), BF16),
            pltpu.VMEM((OWN, WIDTH), F32),
            *[pltpu.VMEM((OWN, PAD), BF16)] * 2,
            pltpu.VMEM((2, OWN, PAD), BF16),
            *[pltpu.VMEM((LINE, SPAN, WIDTH), BF16)] * 2,
            pltpu.VMEM((PLANE, WIDTH, SLICE), BF16),
            pltpu.VMEM((PLANE, SLICE, WIDTH), BF16),
            pltpu.VMEM((LINE, PAD, WIDTH), BF16),
            pltpu.VMEM((WIDTH, EMBED), BF16),
            pltpu.VMEM((PLANE, OWN, SLICE), F32),
            pltpu.VMEM((WIDTH, EMBED), BF16),
            pltpu.VMEM((PLANE, SLICE), F32),
            pltpu.VMEM((4, PAD, WIDTH), BF16),
            pltpu.SemaphoreType.DMA((7,)),
        ],
        mebibytes=48,
        own=(1, 2, 3, 4, 5, 6, 7),
        name="middle",
    )
    *normed_side, down_low, embedded, grad_core, grad_x, rest_other = lax.optimization_barrier(
        (*normed_side, down_low, embedded, grad_core, grad_x, rest_other)
    )
    down_side = gather_side(down_low)
    embed_other = plane_swap(embedded[SPAN:], 4)
    embeddings = jnp.where(
        y == 0,
        jnp.stack([embedded[:SPAN], embed_other]),
        jnp.stack([embed_other, embedded[:SPAN]]),
    )

    grad_x = plane_swap(grad_x, 2)
    grads = swap_groups(grad_own, grad_x, grad_core)

    rest = rest_mine.astype(F32) + plane_swap(rest_other, 1).astype(F32)
    rest = rest.astype(BF16).reshape(LINE, 2, 64, WIDTH)
    rest_kept = lax.dynamic_index_in_dim(rest, x, 1, keepdims=False)
    rest_sent = lax.dynamic_index_in_dim(rest, 1 - x, 1, keepdims=False)
    rest_sent, first_grad = lax.optimization_barrier((rest_sent, first_grad))
    rest_sent = plane_swap(rest_sent, 2)

    qkv_mine, qkv_other, token_near, token_far = call(
        attend_back_kernel,
        (*spots, queries, keys, values, lse, weights, near, far, first_grad, *grads),
        (SM, SM, SM, HB, HB, HB, VM, *[HB] * 8),
        [
            *[((LINE, HALF + 16, 3 * WIDE), BF16)] * 2,
            ((2 * OWN, WIDTH), F32),
            ((2 * OWN, WIDTH), BF16),
        ],
        [
            *[pltpu.VMEM((LINE, HALF + 16, 3 * WIDE), BF16)] * 2,
            pltpu.VMEM((2 * OWN, WIDTH), F32),
            pltpu.VMEM((2 * OWN, WIDTH), BF16),
            *[pltpu.VMEM((SLOTS, PAD), BF16)] * 3,
            pltpu.VMEM((WIDTH, 3 * PAD), BF16),
            *[pltpu.VMEM((2 * OWN, WIDTH), BF16)] * 2,
            pltpu.VMEM((OWN, WIDTH), F32),
            pltpu.VMEM((4, OWN, PAD), BF16),
            pltpu.VMEM((SLOTS, SPAN), F32),
            pltpu.VMEM((PAD, SLOTS), BF16),
            pltpu.VMEM((PAD, OWN), F32),
            pltpu.VMEM((SLOTS, 3 * PAD), BF16),
            pltpu.VMEM((SLOTS, PAD), F32),
            pltpu.VMEM((SLOTS, PAD), F32),
            pltpu.VMEM((WIDTH, 3 * PAD), BF16),
            pltpu.SemaphoreType.DMA((15,)),
        ],
        mebibytes=BIG,
        own=(0, 1, 2, 3),
        name="attend_back",
    )

    rest = (rest_kept.astype(F32) + rest_sent.astype(F32)).astype(BF16)
    rest = rest.reshape(LINE, 2, 32, WIDTH)
    rest_kept = lax.dynamic_index_in_dim(rest, y, 1, keepdims=False)
    rest_sent = lax.dynamic_index_in_dim(rest, 1 - y, 1, keepdims=False)
    rest_sent = plane_swap(rest_sent, 4)

    *down_side, token_near = lax.optimization_barrier((*down_side, token_near))

    def slice_grad(turns, ups, down, name):
        (parts,) = call(
            partial(slice_grad_kernel, name == "slice_other"),
            (scal, bias, turns, ups, down, *normed_side, *down_side),
            (SM, VM, *[HB] * 11),
            [((LINE, 2 * HALF, WIDTH), BF16)],
            [
                pltpu.VMEM((LINE - 1, PARTS, SLICE), BF16),
                pltpu.VMEM((SHARD, SLICE), BF16),
                pltpu.VMEM((PIECE, WIDTH), BF16),
                pltpu.VMEM((PLANE, OWN, WIDTH), BF16),
                pltpu.VMEM((WIDTH, SLICE), F32),
                *[pltpu.VMEM((SLICE, WIDTH), BF16)] * 2,
                *[pltpu.VMEM((SLICE, WIDTH), F32)] * 2,
                pltpu.VMEM((WIDTH, SLICE), F32),
                pltpu.SemaphoreType.DMA((11,)),
            ],
            mebibytes=BIG,
            name=name,
        )
        return parts

    slices_other = slice_grad(parts[4], ups, down_weight, "slice_other")
    *down_side, slices_other = lax.optimization_barrier((*down_side, slices_other))
    slices_mine = slice_grad(turns, ups, down_weight, "slice_mine")
    slices_other = plane_swap(slices_other, 1)
    slices_mine, rest_sent = lax.optimization_barrier((slices_mine, rest_sent))
    rest = (rest_kept.astype(F32) + rest_sent.astype(F32)).astype(BF16)
    shard_parts = []
    for turn in range(LINE):
        total = slices_mine[turn].astype(F32) + slices_other[turn].astype(F32)
        shard_parts.append(jnp.concatenate([total.astype(BF16), rest[turn]]))
    shard_part = sum_parts(turn_parts(shard_parts))

    qkv_other = plane_swap(qkv_other, 4)
    qkv_parts = [
        (qkv_mine[turn].astype(F32) + qkv_other[turn].astype(F32)).astype(BF16)
        for turn in range(LINE)
    ]
    qkv_part = sum_parts(turn_parts(qkv_parts))

    near_sum = (token_near + plane_swap(token_far, 1).astype(F32)).reshape(4, SPAN, WIDTH)
    pair = near_sum[:2] + plane_swap(near_sum[2:].astype(BF16), 2).astype(F32)
    for_other = plane_swap(pair[1].astype(BF16), 4)
    for_mine, for_other = pair[0], for_other.astype(F32)
    tokens_grad = jnp.where(
        y == 0, jnp.stack([for_mine, for_other]), jnp.stack([for_other, for_mine])
    )
    up_grad, down_grad, out_grad, proj_grad, late_rows, bias_rows = call(
        rest_shard_kernel,
        (scal, *gather_plane(shard_part)),
        (SM, *[VM] * 5),
        [
            ((SHARD, INNER), F32),
            ((WIDTH, WIDTH), F32),
            ((SHARD, WIDTH), F32),
            ((SHARD, EMBED), F32),
            ((8, SHARD), F32),
            ((PLANE, PIECE), F32),
        ],
        [pltpu.VMEM((PLANE, 2 * HALF + 32, WIDTH), BF16)],
        name="rest_shard",
    )
    bias_grad = bias_rows.reshape(-1)
    qkv_grad, vectors_grad = call(
        qkv_shard_kernel,
        (scal, late_rows, *gather_plane(qkv_part)),
        (SM, *[VM] * 6),
        [((SHARD, 3 * WIDTH), F32), ((8, SHARD), F32)],
        [pltpu.VMEM((PLANE, HALF + 16, 3 * WIDE), BF16)],
        name="qkv_shard",
    )
    return (
        embeddings,
        tokens_grad,
        qkv_grad,
        out_grad,
        up_grad,
        bias_grad,
        down_grad,
        proj_grad,
        vectors_grad,
    )


def body(*arrays):
    sequences, span, width = arrays[0].shape
    fits = (
        lax.axis_size("ctx") == PLANE
        and lax.axis_size("wa") == LINE
        and sequences == 2
        and span == SPAN
        and width == WIDTH
    )
    return (plane_body if fits else general_body)(*arrays)


def solution(mesh):
    in_specs = (
        P("wa", "ctx", None),
        P(),
        P(),
        P("wa", None),
        P("wa", None),
        P("wa", None),
        P("wa"),
        P("wa", None),
        P("wa", None),
        P(None, "wa"),
        P("wa", "ctx", None),
    )
    out_specs = (
        P("wa", "ctx", None),
        P("wa", "ctx", None),
        P("wa", None),
        P("wa", None),
        P("wa", None),
        P("wa"),
        P("wa", None),
        P("wa", None),
        P(None, "wa"),
    )
    return jax.shard_map(body, mesh=mesh, in_specs=in_specs, out_specs=out_specs, check_vma=False)
```

```python
from functools import partial

import jax
import jax.numpy as jnp
from jax import lax
from jax.experimental import pallas as pl
from jax.experimental.pallas import tpu as pltpu
from jax.sharding import PartitionSpec as P

H = 12
HEAD = 64


NEG_FILL = -1e30
NORM_EPS = 1e-06
ROOT_HALF = 0.7071067811865476
DENSITY_SCALE = 0.3989422804014327


def norm_rows(inputs, gain_row, shift_row):
    middle = jnp.mean(inputs, axis=-1, keepdims=True)
    center = inputs - middle
    spread = jnp.mean(center * center, axis=-1, keepdims=True)
    scaled = lax.rsqrt(spread + NORM_EPS)
    unit_rows = center * scaled
    return (unit_rows * gain_row + shift_row, unit_rows, scaled)


def norm_back(grad_in, unit_rows, scaled, gain_row):
    gain_grad = jnp.sum(grad_in * unit_rows, axis=(0, 1))
    shift_grad = jnp.sum(grad_in, axis=(0, 1))
    inner_grad = grad_in * gain_row
    centered = inner_grad - jnp.mean(inner_grad, axis=-1, keepdims=True)
    result = scaled * (
        centered - unit_rows * jnp.mean(inner_grad * unit_rows, axis=-1, keepdims=True)
    )
    return (result, gain_grad, shift_grad)


def gelu_both(inner_sum):
    normal_cdf = 0.5 * (1.0 + lax.erf(inner_sum * ROOT_HALF))
    density = jnp.exp(-0.5 * inner_sum * inner_sum) * DENSITY_SCALE
    return (inner_sum * normal_cdf, normal_cdf + inner_sum * density)


def split_tiles(key_rows, value_rows, key_valid):
    key_count = key_rows.shape[0]
    tile_width = 512
    tile_count = key_count // tile_width
    return (
        key_rows.reshape(tile_count, tile_width, H, HEAD),
        value_rows.reshape(tile_count, tile_width, H, HEAD),
        key_valid.reshape(tile_count, tile_width),
    )


def masked_scores(queries, key_tile, mask_tile):
    products = jnp.einsum("qhd,khd->hqk", queries, key_tile, preferred_element_type=jnp.float32)
    return jnp.where(mask_tile[None, None, :], products, NEG_FILL)


def attend_forward(queries, key_rows, value_rows, key_valid):
    key_tiles, value_tiles, mask_tiles = split_tiles(key_rows, value_rows, key_valid)
    row_span = queries.shape[0]

    def stats_step(running, portion):
        highest, summed = running
        key_tile, mask_tile = portion
        scores = masked_scores(queries, key_tile, mask_tile)
        new_peak = jnp.maximum(highest, jnp.max(scores, axis=-1))
        raised = jnp.where(mask_tile[None, None, :], jnp.exp(scores - new_peak[:, :, None]), 0.0)
        return ((new_peak, summed * jnp.exp(highest - new_peak) + jnp.sum(raised, axis=-1)), None)

    start_peak = jnp.full((H, row_span), NEG_FILL, jnp.float32)
    start_sum = jnp.zeros((H, row_span), jnp.float32)
    (highest, summed), _ = lax.scan(stats_step, (start_peak, start_sum), (key_tiles, mask_tiles))
    logsum = highest + jnp.log(summed)

    def value_step(running, portion):
        key_tile, value_tile, mask_tile = portion
        scores = masked_scores(queries, key_tile, mask_tile)
        prob_low = jnp.where(
            mask_tile[None, None, :], jnp.exp(scores - logsum[:, :, None]), 0.0
        ).astype(jnp.bfloat16)
        return (
            running
            + jnp.einsum("hqk,khd->qhd", prob_low, value_tile, preferred_element_type=jnp.float32),
            None,
        )

    attended, _ = lax.scan(
        value_step,
        jnp.zeros((row_span, H, HEAD), jnp.float32),
        (key_tiles, value_tiles, mask_tiles),
    )
    return (attended, logsum)


def attend_backward(
    queries, key_rows, value_rows, key_valid, logsum, delta_rows, grad_heads, with_keys
):
    key_tiles, value_tiles, mask_tiles = split_tiles(key_rows, value_rows, key_valid)

    def back_step(running, portion):
        key_tile, value_tile, mask_tile = portion
        scores = masked_scores(queries, key_tile, mask_tile)
        prob_rows = jnp.where(mask_tile[None, None, :], jnp.exp(scores - logsum[:, :, None]), 0.0)
        prob_grad = jnp.einsum(
            "qhd,khd->hqk", grad_heads, value_tile, preferred_element_type=jnp.float32
        )
        score_low = (prob_rows * (prob_grad - delta_rows[:, :, None])).astype(jnp.bfloat16)
        running = running + jnp.einsum(
            "hqk,khd->qhd", score_low, key_tile, preferred_element_type=jnp.float32
        )
        value_part = jnp.einsum(
            "hqk,qhd->khd",
            prob_rows.astype(jnp.bfloat16),
            grad_heads,
            preferred_element_type=jnp.float32,
        )
        key_part = jnp.einsum(
            "hqk,qhd->khd", score_low, queries, preferred_element_type=jnp.float32
        )
        return (running, (key_part, value_part))

    start_grad = jnp.zeros(queries.shape, jnp.float32)
    query_grad, pieces = lax.scan(back_step, start_grad, (key_tiles, value_tiles, mask_tiles))
    key_count = key_rows.shape[0]
    return (
        query_grad,
        pieces[0].reshape(key_count, H * HEAD),
        pieces[1].reshape(key_count, H * HEAD),
    )


def general_body(
    tokens,
    doc_lengths,
    group_deal,
    qkv_weight,
    out_weight,
    up_weight,
    up_bias,
    down_weight,
    proj_weight,
    vectors,
    cotangent,
):
    gathered = (
        lax.all_gather(qkv_weight, "wa", axis=0, tiled=True),
        lax.all_gather(out_weight, "wa", axis=0, tiled=True),
        lax.all_gather(up_weight, "wa", axis=0, tiled=True),
        lax.all_gather(up_bias, "wa", axis=0, tiled=True),
        lax.all_gather(down_weight, "wa", axis=0, tiled=True),
        lax.all_gather(proj_weight, "wa", axis=0, tiled=True),
        lax.all_gather(vectors, "wa", axis=1, tiled=True),
    )
    qkv_full, out_full, up_full, bias_full, down_full, proj_full, vector_full = gathered
    seq_count, group_rows, model_width = tokens.shape
    ctx_count = lax.axis_size("ctx")
    seq_start = lax.axis_index("wa") * seq_count
    my_lengths = lax.dynamic_slice_in_dim(doc_lengths, seq_start, seq_count, 0)
    my_deal = lax.dynamic_slice_in_dim(group_deal, seq_start, seq_count, 0)
    offsets = jnp.tile(jnp.arange(group_rows, dtype=jnp.int32), ctx_count)
    positions = jnp.repeat(my_deal, group_rows, axis=1) * group_rows + offsets[None, :]
    key_valid = positions < my_lengths[:, None]
    query_valid = lax.dynamic_slice_in_dim(
        key_valid, lax.axis_index("ctx") * group_rows, group_rows, 1
    )
    row_mask = query_valid.astype(jnp.float32)[:, :, None]
    query_scale = HEAD ** (-0.5)
    mixed_rows = jnp.einsum("scd,de->sce", tokens, qkv_full, preferred_element_type=jnp.float32)
    queries = ((mixed_rows[:, :, :model_width] + vector_full[0]) * query_scale).astype(jnp.bfloat16)
    key_rows = mixed_rows[:, :, model_width : 2 * model_width].astype(jnp.bfloat16)
    value_rows = (mixed_rows[:, :, 2 * model_width :] + vector_full[1]).astype(jnp.bfloat16)
    all_keys, all_values = (
        lax.all_gather(key_rows, "ctx", axis=1, tiled=True),
        lax.all_gather(value_rows, "ctx", axis=1, tiled=True),
    )
    query_heads = queries.reshape(seq_count, group_rows, H, HEAD)
    attended, logsum = jax.vmap(attend_forward)(query_heads, all_keys, all_values, key_valid)
    attended_low = attended.reshape(seq_count, group_rows, model_width).astype(jnp.bfloat16)
    first_sum = tokens.astype(jnp.float32) + (
        jnp.einsum("scd,de->sce", attended_low, out_full, preferred_element_type=jnp.float32)
        + vector_full[2]
    )
    normed, unit_one, scale_one = norm_rows(first_sum, vector_full[3], vector_full[4])
    normed_low = normed.astype(jnp.bfloat16)
    inner_sum = (
        jnp.einsum("scd,df->scf", normed_low, up_full, preferred_element_type=jnp.float32)
        + bias_full
    )
    active, gelu_slope = gelu_both(inner_sum)
    active_low = active.astype(jnp.bfloat16)
    second_sum = normed + (
        jnp.einsum("scf,fd->scd", active_low, down_full, preferred_element_type=jnp.float32)
        + vector_full[5]
    )
    final_sum, unit_two, scale_two = norm_rows(second_sum, vector_full[6], vector_full[7])
    final_low = final_sum.astype(jnp.bfloat16)
    project = jnp.einsum("scd,de->sce", final_low, proj_full, preferred_element_type=jnp.float32)
    inverse = lax.rsqrt(jnp.sum(project * project, axis=-1, keepdims=True) + NORM_EPS)
    direction = project * inverse
    embeddings = (direction * row_mask).astype(jnp.bfloat16)
    upstream = cotangent.astype(jnp.float32) * row_mask
    project_grad = (
        inverse * (upstream - direction * jnp.sum(upstream * direction, axis=-1, keepdims=True))
    ).astype(jnp.bfloat16)
    proj_grad = jnp.einsum(
        "scd,sce->de", final_low, project_grad, preferred_element_type=jnp.float32
    )
    final_grad = jnp.einsum(
        "sce,de->scd", project_grad, proj_full, preferred_element_type=jnp.float32
    )
    second_grad, gain_two, shift_two = norm_back(final_grad, unit_two, scale_two, vector_full[6])
    down_low = second_grad.astype(jnp.bfloat16)
    down_grad = jnp.einsum("scf,scd->fd", active_low, down_low, preferred_element_type=jnp.float32)
    inner_grad = (
        jnp.einsum("scd,fd->scf", down_low, down_full, preferred_element_type=jnp.float32)
        * gelu_slope
    )
    bias_grad = jnp.sum(inner_grad, axis=(0, 1))
    inner_low = inner_grad.astype(jnp.bfloat16)
    up_grad = jnp.einsum("scd,scf->df", normed_low, inner_low, preferred_element_type=jnp.float32)
    normed_grad = second_grad + jnp.einsum(
        "scf,df->scd", inner_low, up_full, preferred_element_type=jnp.float32
    )
    first_grad, gain_one, shift_one = norm_back(normed_grad, unit_one, scale_one, vector_full[3])
    first_low = first_grad.astype(jnp.bfloat16)
    out_grad = jnp.einsum(
        "scd,sce->de", attended_low, first_low, preferred_element_type=jnp.float32
    )
    attended_grad = jnp.einsum(
        "sce,de->scd", first_low, out_full, preferred_element_type=jnp.float32
    ).astype(jnp.bfloat16)
    grad_heads = attended_grad.reshape(seq_count, group_rows, H, HEAD)
    delta_rows = jnp.sum(grad_heads.astype(jnp.float32) * attended, axis=-1)
    delta_heads = jnp.swapaxes(delta_rows, 1, 2)
    query_grad, key_terms, value_terms = jax.vmap(partial(attend_backward, with_keys=True))(
        query_heads, all_keys, all_values, key_valid, logsum, delta_heads, grad_heads
    )
    key_grad, value_grad = (
        lax.psum_scatter(
            key_terms.astype(jnp.bfloat16), "ctx", scatter_dimension=1, tiled=True
        ).astype(jnp.float32),
        lax.psum_scatter(
            value_terms.astype(jnp.bfloat16), "ctx", scatter_dimension=1, tiled=True
        ).astype(jnp.float32),
    )
    query_part = (
        query_grad.reshape(seq_count, group_rows, model_width).astype(jnp.bfloat16) * query_scale
    )
    value_part = value_grad.astype(jnp.bfloat16)
    mixed_grad = jnp.concatenate([query_part, key_grad.astype(jnp.bfloat16), value_part], axis=-1)
    qkv_grad = jnp.einsum("scd,sce->de", tokens, mixed_grad, preferred_element_type=jnp.float32)
    tokens_grad = first_grad + jnp.einsum(
        "sce,de->scd", mixed_grad, qkv_full, preferred_element_type=jnp.float32
    )
    vectors_grad = jnp.stack(
        [
            jnp.sum(query_part.astype(jnp.float32), axis=(0, 1)),
            jnp.sum(value_part.astype(jnp.float32), axis=(0, 1)),
            jnp.sum(first_grad, axis=(0, 1)),
            gain_one,
            shift_one,
            jnp.sum(second_grad, axis=(0, 1)),
            gain_two,
            shift_two,
        ],
        axis=0,
    )
    owned = (
        lax.psum_scatter(
            qkv_grad.astype(jnp.bfloat16), "wa", scatter_dimension=0, tiled=True
        ).astype(jnp.float32),
        lax.psum_scatter(
            out_grad.astype(jnp.bfloat16), "wa", scatter_dimension=0, tiled=True
        ).astype(jnp.float32),
        lax.psum_scatter(
            up_grad.astype(jnp.bfloat16), "wa", scatter_dimension=0, tiled=True
        ).astype(jnp.float32),
        lax.psum_scatter(
            bias_grad.astype(jnp.bfloat16), "wa", scatter_dimension=0, tiled=True
        ).astype(jnp.float32),
        lax.psum_scatter(
            down_grad.astype(jnp.bfloat16), "wa", scatter_dimension=0, tiled=True
        ).astype(jnp.float32),
        lax.psum_scatter(
            proj_grad.astype(jnp.bfloat16), "wa", scatter_dimension=0, tiled=True
        ).astype(jnp.float32),
        lax.psum_scatter(
            vectors_grad.astype(jnp.bfloat16), "wa", scatter_dimension=1, tiled=True
        ).astype(jnp.float32),
    )
    summed = (
        lax.psum(owned[0].astype(jnp.bfloat16), "ctx").astype(jnp.float32),
        lax.psum(owned[1].astype(jnp.bfloat16), "ctx").astype(jnp.float32),
        lax.psum(owned[2].astype(jnp.bfloat16), "ctx").astype(jnp.float32),
        lax.psum(owned[3].astype(jnp.bfloat16), "ctx").astype(jnp.float32),
        lax.psum(owned[4].astype(jnp.bfloat16), "ctx").astype(jnp.float32),
        lax.psum(owned[5].astype(jnp.bfloat16), "ctx").astype(jnp.float32),
        lax.psum(owned[6].astype(jnp.bfloat16), "ctx").astype(jnp.float32),
    )
    return (
        embeddings,
        tokens_grad,
        summed[0],
        summed[1],
        summed[2],
        summed[3],
        summed[4],
        summed[5],
        summed[6],
    )


PLANE = 8
LINE = 4
SPAN = 128
OWN = 2 * SPAN
WIDTH = H * HEAD
INNER = 4 * WIDTH
SHARD = WIDTH // LINE
HALF = SHARD // 2
PIECE = INNER // LINE // PLANE
SLICE = LINE * PIECE
HEADS = 3
WIDE = HEADS * HEAD
PAD = 256
SLOTS = PLANE * SPAN
BLOCK = SHARD // 4
FIRST = SHARD + BLOCK
SIDE = PIECE
PARTS = FIRST + 2 * SIDE
QUARTER = HALF // 2
COLS = HALF + QUARTER
EMBED = 128
ORDER = (0, 4, 2, 6, 1, 5, 3, 7)
NEAR = (0, 2, 1, 3)
F32 = jnp.float32
BF16 = jnp.bfloat16

NN = ((1,), (0,))
NT = ((1,), (1,))
TN = ((0,), (0,))


def dot(left, right, dims):
    return lax.dot_general(left, right, (dims, ((), ())), preferred_element_type=F32)


def plane_swap(array, bits):
    return lax.ppermute(array, "ctx", [(i, i ^ bits) for i in range(PLANE)])


def line_turn(array, step):
    return lax.ppermute(array, "wa", [(i, (i + step) % LINE) for i in range(LINE)])


def line_turns(array):
    return [line_turn(array, step) for step in range(1, LINE)]


def relay(from_x, from_y, core):
    passed = jnp.where(core == 0, from_y, from_x)
    pairs = [(i, i ^ 2 if i % 2 == 0 else i ^ 4) for i in range(PLANE)]
    return lax.ppermute(passed, "ctx", pairs)


def pick(array, index):
    return lax.dynamic_index_in_dim(array, index, 0, keepdims=False)


COST = {'cut': 3, 'vectors': 1, 'attend': 12, 'out': 3, 'middle': 17, 'attend_back': 18, 'rest_shard': 4, 'qkv_shard': 2, 'slice_other': 3.0, 'slice_mine': 3.0}
VM = pl.BlockSpec(memory_space=pltpu.VMEM)
SM = pl.BlockSpec(memory_space=pltpu.SMEM)
HB = pl.BlockSpec(memory_space=pl.ANY)
BIG = 56


def call(kernel, inputs, spaces, outputs, scratch=(), mebibytes=32, name=None, own=()):
    shapes = [jax.ShapeDtypeStruct(shape, kind) for shape, kind in outputs]
    return pl.pallas_call(
        kernel,
        out_shape=shapes,
        in_specs=list(spaces),
        out_specs=[HB if i in own else VM for i in range(len(shapes))],
        scratch_shapes=list(scratch),
        compiler_params=pltpu.CompilerParams(vmem_limit_bytes=mebibytes << 20),
        cost_estimate=pl.CostEstimate(flops=int(COST[name] * 1e9), bytes_accessed=1, transcendentals=0),
        name=name,
    )(*inputs)


def place_of(scal):
    return scal[0], scal[1]


def shard_of_turn(line, turn):
    return lax.rem(line - turn + LINE, LINE)


def turn_ahead(line, turn):
    return lax.rem(line + turn, LINE)


def norm_forward(rows):
    middle = jnp.mean(rows, axis=-1, keepdims=True)
    center = rows - middle
    scaled = lax.rsqrt(jnp.mean(center * center, axis=-1, keepdims=True) + NORM_EPS)
    return center * scaled, scaled


def norm_reverse(grad, unit, scaled, gain):
    inner = grad * gain
    return scaled * (
        inner
        - jnp.mean(inner, axis=-1, keepdims=True)
        - unit * jnp.mean(inner * unit, axis=-1, keepdims=True)
    )


def cut_kernel(
    scal, vectors, bias, proj, qkv, up, down, out,
    cols_ref, ups_ref, own_ref,
    qkv_held, up_held, down_held, out_held, sems,
):
    me, line = place_of(scal)
    core = lax.rem(me, 2)
    copies = [
        pltpu.make_async_copy(qkv, qkv_held, sems.at[0]),
        pltpu.make_async_copy(up, up_held, sems.at[1]),
        pltpu.make_async_copy(
            down.at[pl.ds(pl.multiple_of(me * PIECE, 16), PIECE)], down_held, sems.at[2]
        ),
        pltpu.make_async_copy(
            out.at[pl.ds(pl.multiple_of(lax.div(me, 2) * BLOCK, 16), BLOCK)], out_held, sems.at[3]
        ),
    ]
    for copy in copies:
        copy.start()
    rows = [vectors[...].astype(F32)]
    rows += [bias[:, a * SHARD : (a + 1) * SHARD].astype(F32) for a in range(LINE)]
    rows = jnp.concatenate(rows + [jnp.zeros((4, SHARD), F32)])
    own_ref[PARTS + COLS : PARTS + COLS + 16, :SHARD] = rows.astype(BF16)
    own_ref[PARTS + COLS : PARTS + COLS + 16, SHARD:] = jnp.zeros((16, SLICE - SHARD), BF16)
    for side in range(2):
        start = PARTS + COLS + 16 * (1 + side)
        for t in range(3):
            own_ref[start : start + 16, t * EMBED : (t + 1) * EMBED] = proj[
                pl.ds(pl.multiple_of(core * HALF + 16 * (3 * side + t), 16), 16), :
            ]
    copies[0].wait()
    for g in range(4):

        @pl.when(lax.rem(me, 4) == g)
        def _():
            for part in range(3):
                start = part * WIDTH + g * WIDE
                cols_ref[:, part * WIDE : (part + 1) * WIDE] = qkv_held[:, start : start + WIDE]

    base = lax.div(me, 4) * HALF
    rows = cols_ref[pl.ds(pl.multiple_of(base, 16), HALF), :]
    own_ref[PARTS : PARTS + HALF, :] = rows[:, :SLICE]
    for side in range(2):
        own_ref[PARTS + HALF : PARTS + COLS, side * WIDE : (side + 1) * WIDE] = rows[
            side * QUARTER : (side + 1) * QUARTER, SLICE:
        ]
    copies[1].wait()
    for k in range(PLANE):
        for s in range(LINE):
            start = s * PLANE * PIECE + k * PIECE
            ups_ref[k, :, s * PIECE : (s + 1) * PIECE] = up_held[:, start : start + PIECE]
    own_ref[:SHARD] = ups_ref[me]
    copies[2].wait()
    for side in range(2):
        start = FIRST + side * SIDE
        own_ref[start : start + PIECE] = down_held[:, side * SLICE : (side + 1) * SLICE]
    copies[3].wait()
    own_ref[SHARD:FIRST] = out_held[:, pl.ds(pl.multiple_of(core * SLICE, 128), SLICE)]


def vectors_kernel(scal, own, halves, full_ref, bias_ref, ends_ref, held):
    me, line = place_of(scal)
    held[line] = own[PARTS + COLS : PARTS + COLS + 16, :SHARD].astype(F32)
    for turn in range(1, LINE):
        held[shard_of_turn(line, turn)] = halves[turn - 1, COLS:, :SHARD].astype(F32)
    for a in range(LINE):
        full_ref[:, a * SHARD : (a + 1) * SHARD] = held[a, :8, :]
        for k in range(PLANE):
            start = (k % 2) * PIECE
            bias_ref[k : k + 1, a * PIECE : (a + 1) * PIECE] = held[
                a, 8 + k // 2 : 9 + k // 2, start : start + PIECE
            ]
    ends_ref[...] = jnp.zeros((8, PAD), F32)
    ends_ref[:, :WIDE] = held[lax.rem(me, 4), :8, :]


def slots_left(scal, lengths, deal, place):
    me, line = place_of(scal)
    seq = 2 * line + lax.div(me, 4)
    return lengths[seq] - deal[seq, me ^ ORDER[place]] * SPAN


def fill_mask(scal, lengths, deal, mask):
    rows = lax.broadcasted_iota(jnp.int32, (SPAN, SPAN), 0)
    for place in range(PLANE):
        limit = slots_left(scal, lengths, deal, place)
        mask[place * SPAN : (place + 1) * SPAN, :] = jnp.where(rows < limit, 0.0, NEG_FILL)


def head_lanes(h):
    lanes = lax.broadcasted_iota(jnp.int32, (OWN, 128), 1)
    return (lanes >= HEAD) if h % 2 else (lanes < HEAD)


def attend_kernel(
    scal, lengths, deal, ends, own_cols, halves, others, near, far,
    q_out, k_out, v_out, w_out, own_ref, core_ref, x_ref, lse_ref,
    raw, mask, v_turned, o_turned, att, q_ref, k_ref, v_ref, w_ref, sems,
):
    me, line = place_of(scal)
    y = lax.div(me, 4)
    raw[pl.ds(pl.multiple_of(line * SHARD, 16), SHARD), :] = own_cols[...]
    for turn in range(1, LINE):
        base = shard_of_turn(line, turn) * SHARD
        for source, side in ((halves, y), (others, 1 - y)):
            start = base + side * HALF
            at = pl.ds(pl.multiple_of(start, 16), HALF)
            raw[at, :SLICE] = source[turn - 1, :HALF, :]
            for i in range(2):
                at = pl.ds(pl.multiple_of(start + i * QUARTER, 16), QUARTER)
                raw[at, SLICE:] = source[turn - 1, HALF:COLS, i * WIDE : (i + 1) * WIDE]
    fill_mask(scal, lengths, deal, mask)
    for part in range(3):
        w_ref[:, part * PAD : part * PAD + WIDE] = raw[:, part * WIDE : (part + 1) * WIDE]
        w_ref[:, part * PAD + WIDE : (part + 1) * PAD] = jnp.zeros((WIDTH, PAD - WIDE), BF16)
    for t in range(4):
        source = (near, far)[t // 2]
        rows = source[(t % 2) * OWN : (t % 2 + 1) * OWN, :]
        mixed = dot(rows, w_ref[...], NN)
        at = slice(t * OWN, (t + 1) * OWN)
        q_ref[at, :] = ((mixed[:, :PAD] + ends[0:1, :]) * (HEAD ** (-0.5))).astype(BF16)
        k_ref[at, :] = mixed[:, PAD : 2 * PAD].astype(BF16)
        values = mixed[:, 2 * PAD :] + ends[1:2, :]
        v_ref[at, :] = values.astype(BF16)
        v_turned[:, at] = values.T.astype(BF16)

    copies = [
        pltpu.make_async_copy(source, target, sems.at[i])
        for i, (source, target) in enumerate(
            ((q_ref, q_out), (k_ref, k_out), (v_ref, v_out), (w_ref, w_out))
        )
    ]
    for copy in copies:
        copy.start()
    o_turned[WIDE:, :] = jnp.zeros((PAD - WIDE, OWN), F32)

    def tile(t, carry):
        at = pl.ds(pl.multiple_of(t * OWN, OWN), OWN)
        for h in range(HEADS):
            cut = slice((h // 2) * 128, (h // 2 + 1) * 128)
            q_tile = jnp.where(head_lanes(h), q_ref[at, cut], jnp.zeros((), BF16))
            scores = dot(k_ref[:, cut], q_tile, NT)
            scores = scores + jnp.concatenate([mask[...], mask[...]], axis=1)
            peak = jnp.max(scores, axis=0, keepdims=True)
            raised = jnp.exp(scores - peak)
            total = jnp.sum(raised, axis=0, keepdims=True)
            rows = slice(h * HEAD, (h + 1) * HEAD)
            o_turned[rows, :] = dot(v_turned[rows, :], raised.astype(BF16), NN) * (1.0 / total)
            lse_ref[t, h : h + 1, :] = peak + jnp.log(total)
        att[t] = o_turned[...].T.astype(BF16)
        return carry

    lax.fori_loop(0, 4, tile, 0)
    own_ref[...] = att[0]
    core_ref[...] = att[2]
    x_ref[0] = att[1]
    x_ref[1] = att[3]
    for copy in copies:
        copy.wait()


def attend_back_kernel(
    scal, lengths, deal, q_ref, k_ref, v_ref, lse, weights, near, far, first_grad, g0, g1, g2, g3,
    mine_out, other_out, near_out, far_out,
    mine_ref, other_ref, near_ref, far_ref,
    q_held, k_held, v_held, w_held, near_held, far_held, first_held, grads,
    mask, k_turned, q_turned, mixed, key_sum, value_sum, part, sems,
):
    sources = (k_ref, q_ref, v_ref, g0, g1.at[0], g2, g3, weights, near, far, first_grad)
    targets = (k_held, q_held, v_held, grads.at[0], grads.at[1], grads.at[2], grads.at[3])
    targets += (w_held, near_held, far_held, first_held)
    copies = [
        pltpu.make_async_copy(source, target, sems.at[i])
        for i, (source, target) in enumerate(zip(sources, targets, strict=True))
    ]
    for copy in copies:
        copy.start()
    fill_mask(scal, lengths, deal, mask)
    copies[0].wait()
    for t in range(4):
        at = slice(t * OWN, (t + 1) * OWN)
        k_turned[:, at] = k_held[at, :].astype(F32).T.astype(BF16)
    key_sum[...] = jnp.zeros_like(key_sum)
    value_sum[...] = jnp.zeros_like(value_sum)
    q_turned[WIDE:, :] = jnp.zeros((PAD - WIDE, OWN), F32)
    for copy in copies[1:7]:
        copy.wait()

    def tile(t, carry):
        at = pl.ds(pl.multiple_of(t * OWN, OWN), OWN)
        for h in range(HEADS):
            cut = slice((h // 2) * 128, (h // 2 + 1) * 128)
            rows = slice(h * HEAD, (h + 1) * HEAD)
            q_tile = jnp.where(head_lanes(h), q_held[at, cut], jnp.zeros((), BF16))
            g_tile = jnp.where(head_lanes(h), grads[t, :, cut], jnp.zeros((), BF16))
            scores = dot(k_held[:, cut], q_tile, NT)
            scores = scores + jnp.concatenate([mask[...], mask[...]], axis=1)
            probs = jnp.exp(scores - lse[t, h : h + 1, :])
            prob_grad = dot(v_held[:, cut], g_tile, NT)
            delta = jnp.sum(probs * prob_grad, axis=0, keepdims=True)
            score_low = (probs * (prob_grad - delta)).astype(BF16)
            q_turned[rows, :] = dot(k_turned[rows, :], score_low, NN)
            key_sum[:, cut] += dot(score_low, q_tile, NN)
            value_sum[:, cut] += dot(probs.astype(BF16), g_tile, NN)
        low = q_turned[...].T.astype(BF16)
        mixed[at, :PAD] = (low.astype(F32) * (HEAD ** (-0.5))).astype(BF16)
        return carry

    lax.fori_loop(0, 4, tile, 0)
    mixed[:, PAD : 2 * PAD] = key_sum[...].astype(BF16)
    mixed[:, 2 * PAD :] = value_sum[...].astype(BF16)

    me, line = place_of(scal)
    y = lax.div(me, 4)
    for copy in copies[7:]:
        copy.wait()
    for i in range(3):
        cut = slice(i * 256, (i + 1) * 256)
        part[cut, :] = (
            dot(near_held[:, cut], mixed[: 2 * OWN, :], TN) + dot(far_held[:, cut], mixed[2 * OWN :, :], TN)
        ).astype(BF16)
    sums = jnp.sum(mixed[...].astype(F32), axis=0, keepdims=True)
    sums = jnp.concatenate([sums, jnp.zeros((15, 3 * PAD), F32)]).astype(BF16)
    for turn in range(LINE):
        base = turn_ahead(line, turn) * SHARD
        for target, side in ((mine_ref, y), (other_ref, 1 - y)):
            rows = part[pl.ds(pl.multiple_of(base + side * HALF, 16), HALF), :]
            for p in range(3):
                to = slice(p * WIDE, (p + 1) * WIDE)
                target[turn, :HALF, to] = rows[:, p * PAD : p * PAD + WIDE]
                target[turn, HALF:, to] = sums[:, p * PAD : p * PAD + WIDE]
    outs = [
        pltpu.make_async_copy(source, target, sems.at[11 + i])
        for i, (source, target) in enumerate(
            (
                (other_ref, other_out),
                (mine_ref, mine_out),
                (far_ref, far_out),
                (near_ref, near_out),
            )
        )
    ]
    outs[0].start()
    outs[1].start()
    for t in (2, 3, 0, 1):
        at = slice(t * OWN, (t + 1) * OWN)
        token_part = dot(mixed[at, :], w_held[...], NT)
        if t == 0:
            near_ref[at, :] = (token_part + first_held[...]).astype(BF16)
        elif t == 1:
            near_ref[at, :] = token_part.astype(BF16)
        else:
            far_ref[(t - 2) * OWN : (t - 1) * OWN, :] = token_part.astype(BF16)
        if t == 3:
            outs[2].start()
    outs[3].start()
    for copy in outs:
        copy.wait()


def out_kernel(
    scal, near, full, out_shard, a0, a1, a2, a3, p0, p1, p2, p3, p4, p5, p6, p7,
    sum_ref, low_ref,
    out_ref, sem,
):
    me, line = place_of(scal)
    group = lax.rem(me, 4)
    pieces = (p0, p1, p2, p3, p4, p5, p6, p7)
    copies = []
    for place, bits in enumerate(ORDER):
        k = me ^ bits
        rows = pl.ds(pl.multiple_of(lax.div(k, 2) * BLOCK, 16), BLOCK)
        lanes = pl.ds(pl.multiple_of(lax.rem(k, 2) * SLICE, 128), SLICE)
        for turn in range(1, LINE):
            copies.append(
                pltpu.make_async_copy(
                    pieces[place].at[turn - 1, pl.ds(SHARD, BLOCK)],
                    out_ref.at[shard_of_turn(line, turn), rows, lanes],
                    sem,
                )
            )
    for copy in copies:
        copy.start()
    for z in range(LINE):
        out_ref[z, SHARD:, :] = jnp.zeros((PAD - SHARD, WIDTH), BF16)
    out_ref[line, :SHARD, :] = out_shard[...]
    rows = near[:OWN, :].astype(F32) + full[2:3, :]
    filled = out_ref.at[pl.ds(0, LINE - 1), pl.ds(0, SHARD)]
    pltpu.make_async_copy(filled, filled, sem).wait()
    for i, source in enumerate((a0[...], a1[0], a2[...], a3[...])):
        rows = rows + dot(source, out_ref[group ^ NEAR[i]], NN)
    sum_ref[...] = rows
    unit, _ = norm_forward(rows)
    low_ref[...] = (unit * full[3:4, :] + full[4:5, :]).astype(BF16)


def place_up(scal, place, up_own, held, up_all):
    me, line = place_of(scal)
    at = pl.ds(pl.multiple_of(line * SHARD, 16), SHARD)
    up_all[place, at, :] = up_own[me ^ ORDER[place]]
    for turn in range(1, LINE):
        at = pl.ds(pl.multiple_of(shard_of_turn(line, turn) * SHARD, 16), SHARD)
        up_all[place, at, :] = held[place][turn - 1, :SHARD, :]


def place_down(scal, place, down_own, held, down_all):
    me, line = place_of(scal)
    at = pl.ds(pl.multiple_of(line * PIECE, 16), PIECE)
    start = pl.multiple_of((me ^ ORDER[place]) * PIECE, 16)
    down_all[place, at, :] = down_own[pl.ds(start, PIECE), :]
    for turn in range(1, LINE):
        at = pl.ds(pl.multiple_of(shard_of_turn(line, turn) * PIECE, 16), PIECE)
        for side in range(2):
            start = FIRST + side * SIDE
            down_all[place, at, side * SLICE : (side + 1) * SLICE] = held[place][
                turn - 1, start : start + PIECE, :
            ]


def place_out(scal, place, held, out_all):
    me, line = place_of(scal)
    k = me ^ ORDER[place]
    rows = pl.ds(pl.multiple_of(lax.div(k, 2) * BLOCK, 16), BLOCK)
    lanes = pl.ds(pl.multiple_of(lax.rem(k, 2) * SLICE, 128), SLICE)
    for turn in range(1, LINE):
        out_all[shard_of_turn(line, turn), rows, lanes] = held[place][turn - 1, SHARD:FIRST, :]


def middle_kernel(
    scal, lengths, deal, first_sum, full, bias, proj_shard, out_shard, cot_mine, cot_other,
    proj_near, proj_far, a0, a1, a2, a3, ups, down, p0, p1, p2, p3, p4, p5, p6, p7,
    embed_ref, low_out, first_out, own_out, core_out, x_out, mine_out, other_out,
    low_ref, first_ref, own_ref, core_ref, x_ref, mine_ref, other_ref,
    up_all, down_all, out_all, proj_all, slopes, proj_part, bias_sum, out_part, sems,
):
    held = (p0, p1, p2, p3, p4, p5, p6, p7)
    up_own, down_own = ups, down
    me, line = place_of(scal)
    core, group = lax.rem(me, 2), lax.rem(me, 4)
    proj_all[pl.ds(pl.multiple_of(line * SHARD, 16), SHARD), :] = proj_shard[...]

    unit_one, scale_one = norm_forward(first_sum[...])
    normed = unit_one * full[3:4, :] + full[4:5, :]
    normed_low = normed.astype(BF16)
    second_sum = normed + full[5:6, :]
    for z in range(LINE):
        out_all[z, SHARD:, :] = jnp.zeros((PAD - SHARD, WIDTH), BF16)
    out_all[line, :SHARD, :] = out_shard[...]
    for place, bits in enumerate(ORDER):
        place_up(scal, place, up_own, held, up_all)
        place_down(scal, place, down_own, held, down_all)
        place_out(scal, place, held, out_all)
        inner = dot(normed_low, up_all[place], NN) + bias[pl.ds(me ^ bits, 1), :]
        active, slope = gelu_both(inner)
        slopes[place] = slope
        second_sum = second_sum + dot(active.astype(BF16), down_all[place], NN)
    unit, scaled = norm_forward(second_sum)
    final_low = (unit * full[6:7, :] + full[7:8, :]).astype(BF16)
    for half, source in ((core, proj_near), (1 - core, proj_far)):
        for turn in range(1, LINE):
            base = shard_of_turn(line, turn) * SHARD + half * HALF
            for t in range(6):
                start = 16 * (t // 3)
                proj_all[pl.ds(pl.multiple_of(base + 16 * t, 16), 16), :] = source[
                    turn - 1, start : start + 16, (t % 3) * EMBED : (t % 3 + 1) * EMBED
                ]
    project = dot(final_low, proj_all[...], NN)
    inverse = lax.rsqrt(jnp.sum(project * project, axis=-1, keepdims=True) + NORM_EPS)
    direction = project * inverse
    rows = lax.broadcasted_iota(jnp.int32, (SPAN, EMBED), 0)
    keep = jnp.concatenate(
        [
            jnp.where(rows < slots_left(scal, lengths, deal, i), 1.0, 0.0).astype(F32)
            for i in range(2)
        ]
    )
    embed_ref[...] = (direction * keep).astype(BF16)
    upstream = jnp.concatenate([cot_mine[...], cot_other[...]]).astype(F32) * keep
    project_grad = (
        inverse * (upstream - direction * jnp.sum(upstream * direction, axis=-1, keepdims=True))
    ).astype(BF16)
    proj_part[...] = dot(final_low, project_grad, TN).astype(BF16)
    final_grad = dot(project_grad, proj_all[...], NT)
    second_grad = norm_reverse(final_grad, unit, scaled, full[6:7, :])
    down_low = second_grad.astype(BF16)
    low_ref[...] = down_low
    outs = [
        pltpu.make_async_copy(source, target, sems.at[i])
        for i, (source, target) in enumerate(
            (
                (low_ref, low_out),
                (x_ref, x_out),
                (core_ref, core_out),
                (own_ref, own_out),
                (first_ref, first_out),
                (other_ref, other_out),
                (mine_ref, mine_out),
            )
        )
    ]
    outs[0].start()

    normed_grad = second_grad
    for place, bits in enumerate(ORDER):
        inner_grad = dot(down_low, down_all[place], NT) * slopes[place]
        bias_sum[pl.ds(me ^ bits, 1), :] = jnp.sum(inner_grad, axis=0, keepdims=True)
        normed_grad = normed_grad + dot(inner_grad.astype(BF16), up_all[place], NT)
    first_grad = norm_reverse(normed_grad, unit_one, scale_one, full[3:4, :])
    first_ref[...] = first_grad
    first_low = first_grad.astype(BF16)
    for i, target in enumerate((own_ref, x_ref.at[0], core_ref, x_ref.at[1])):
        target[...] = dot(first_low, out_all[group ^ NEAR[i]], NT).astype(BF16)
    for copy in outs[1:5]:
        copy.start()
    small = jnp.concatenate(
        [
            jnp.sum(first_grad, axis=0, keepdims=True),
            jnp.sum(normed_grad * unit_one, axis=0, keepdims=True),
            jnp.sum(normed_grad, axis=0, keepdims=True),
            jnp.sum(second_grad, axis=0, keepdims=True),
            jnp.sum(final_grad * unit, axis=0, keepdims=True),
            jnp.sum(final_grad, axis=0, keepdims=True),
            jnp.zeros((2, WIDTH), F32),
        ]
    )
    tail = jnp.concatenate([bias_sum[...], jnp.zeros((8, WIDTH - SLICE), F32)], axis=1)
    small = jnp.concatenate([small, tail]).astype(BF16)
    for i, source in enumerate((a0[...], a1[0], a2[...], a3[...])):
        z = group ^ NEAR[i]
        turn = lax.rem(z - line + LINE, LINE)
        out_part[i] = dot(source, first_low, TN).astype(BF16)
        for target, half in ((mine_ref, core), (other_ref, 1 - core)):
            base = half * HALF
            target[turn, :HALF, :] = out_part[i, pl.ds(pl.multiple_of(base, 16), HALF), :]
            for t in range(6):
                target[turn, HALF : HALF + 16, t * EMBED : (t + 1) * EMBED] = proj_part[
                    pl.ds(pl.multiple_of(z * SHARD + base + 16 * t, 16), 16), :
                ]
            target[turn, HALF + 16 :, :] = small
    outs[5].start()
    outs[6].start()
    for copy in outs:
        copy.wait()


def slice_grad_kernel(
    other, scal, bias, turns, ups, down, n0, n1, n2, n3, d0, d1, d2, d3,
    part_ref,
    held, ups_held, down_held, slots, up_rows, up_turned, down_rows, up_sum, down_sum, up_back,
    sems,
):
    me, line = place_of(scal)
    k = me ^ 1 if other else me
    copies = [
        pltpu.make_async_copy(turns, held, sems.at[0]),
        pltpu.make_async_copy(ups.at[k], ups_held, sems.at[1]),
        pltpu.make_async_copy(
            down.at[pl.ds(pl.multiple_of(k * PIECE, 16), PIECE)], down_held, sems.at[2]
        ),
    ]
    for j, source in enumerate((n0, d0, n1, d1, n2, d2, n3, d3)):
        copies.append(pltpu.make_async_copy(source, slots.at[j], sems.at[3 + j]))
    for copy in copies:
        copy.start()
    for copy in copies[:3]:
        copy.wait()
    for turn in range(LINE):
        z = shard_of_turn(line, turn)
        rows = held[turn - 1, :SHARD, :] if turn else ups_held[...]
        up_rows[pl.ds(pl.multiple_of(z * SHARD, 16), SHARD), :] = rows.astype(F32)
        at = pl.ds(pl.multiple_of(z * PIECE, 16), PIECE)
        if turn == 0:
            down_rows[at, :] = down_held[...]
            continue
        for side in range(2):
            start = FIRST + side * SIDE
            down_rows[at, side * SLICE : (side + 1) * SLICE] = held[
                turn - 1, start : start + PIECE, :
            ]
    up_turned[...] = up_rows[...].T.astype(BF16)
    bias_rows = jnp.broadcast_to(bias[pl.ds(k, 1), :], (128, SLICE)).T
    bias_rows = jnp.concatenate([bias_rows, bias_rows], axis=1)
    for j in range(4):
        copies[3 + 2 * j].wait()
        copies[4 + 2 * j].wait()
        normed, low = slots[2 * j], slots[2 * j + 1]
        inner = dot(up_turned[...], normed, NT) + bias_rows
        active, slope = gelu_both(inner)
        inner_low = (dot(down_rows[...], low, NT) * slope).astype(BF16)
        up_part = dot(inner_low, normed, NN)
        down_part = dot(active.astype(BF16), low, NN)
        if j == 0:
            up_sum[...] = up_part
            down_sum[...] = down_part
        else:
            up_sum[...] += up_part
            down_sum[...] += down_part
    up_back[...] = up_sum[...].T
    for turn in range(LINE):
        z = turn_ahead(line, turn)
        for side in range(2):
            at = pl.ds(pl.multiple_of(z * SHARD + side * HALF, 16), HALF)
            part_ref[turn, :HALF, side * SLICE : (side + 1) * SLICE] = up_back[at, :].astype(BF16)
        at = pl.ds(pl.multiple_of(z * PIECE, 16), PIECE)
        part_ref[turn, HALF:, :] = down_sum[at, :].astype(BF16)


def hold_parts(me, close, far, held):
    for place in range(4):
        held[me ^ ORDER[place]] = close[place][...]
        held[me ^ ORDER[place + 4]] = far[place]


def rest_shard_kernel(
    scal, p0, p1, p2, p3, far,
    up_ref, down_ref, out_ref, proj_ref, rows_ref, bias_ref, held,
):
    me, line = place_of(scal)
    hold_parts(me, (p0, p1, p2, p3), far, held)
    for k in range(PLANE):
        core, x, y = k % 2, (k // 2) % 2, k // 4
        for side in range(2):
            rows = held[k, :HALF, side * SLICE : (side + 1) * SLICE].astype(F32)
            for s in range(LINE):
                start = s * PLANE * PIECE + k * PIECE
                up_ref[side * HALF : (side + 1) * HALF, start : start + PIECE] = rows[
                    :, s * PIECE : (s + 1) * PIECE
                ]
        down_ref[k * PIECE : (k + 1) * PIECE, :] = held[k, HALF : 2 * HALF, :].astype(F32)
        tail = held[k, 2 * HALF :, :].astype(F32)
        block = 2 * x + y
        if block < 3:
            start = core * HALF + 32 * block
            out_ref[start : start + 32, :] = tail
        else:
            for t in range(6):
                start = core * HALF + 16 * t
                proj_ref[start : start + 16, :] = tail[:16, t * EMBED : (t + 1) * EMBED]
            if core == 0:
                small = tail[16:, :]
    for z in range(LINE):

        @pl.when(line == z)
        def _():
            rows_ref[...] = small[:8, z * SHARD : (z + 1) * SHARD]
            bias_ref[...] = small[8:, z * PIECE : (z + 1) * PIECE]


def qkv_shard_kernel(scal, late, p0, p1, p2, p3, far, qkv_ref, rows_ref, held):
    me, line = place_of(scal)
    hold_parts(me, (p0, p1, p2, p3), far, held)
    for k in range(PLANE):
        y, g = k // 4, k % 4
        for part in range(3):
            start = part * WIDTH + g * WIDE
            qkv_ref[y * HALF : (y + 1) * HALF, start : start + WIDE] = held[
                k, :HALF, part * WIDE : (part + 1) * WIDE
            ].astype(F32)
    sums = held[line, HALF:, :].astype(F32)
    rows_ref[...] = jnp.concatenate(
        [sums[:1, :WIDE], sums[:1, 2 * WIDE : 3 * WIDE], late[:6, :]]
    )


def gather_side(array):
    return [array, plane_swap(array, 4), plane_swap(array, 2), plane_swap(array, 6)]


def gather_plane(array):
    close = gather_side(array)
    return close + [plane_swap(jnp.stack(close), 1)]


def turn_parts(parts):
    return [parts[0]] + [line_turn(parts[turn], turn) for turn in range(1, LINE)]


def sum_parts(parts):
    total = parts[0].astype(F32)
    for part in parts[1:]:
        total = total + part.astype(F32)
    return total.astype(BF16)


def swap_groups(own, from_x, for_core):
    return own, from_x, plane_swap(for_core, 1), plane_swap(from_x[1], 1)


def plane_body(
    tokens,
    doc_lengths,
    group_deal,
    qkv_weight,
    out_weight,
    up_weight,
    up_bias,
    down_weight,
    proj_weight,
    vectors,
    cotangent,
):
    me = lax.axis_index("ctx").astype(jnp.int32)
    line = lax.axis_index("wa").astype(jnp.int32)
    y, x, core = me // 4, (me // 2) % 2, me % 2
    scal = jnp.stack([me, line])
    spots = (scal, doc_lengths, group_deal)

    own_cols, ups, own_parts = call(
        cut_kernel,
        (scal, vectors, up_bias.reshape(1, -1), proj_weight)
        + (qkv_weight, up_weight, down_weight, out_weight),
        (SM, VM, VM, VM, HB, HB, HB, HB),
        [
            ((SHARD, 3 * WIDE), BF16),
            ((PLANE, SHARD, SLICE), BF16),
            ((PARTS + COLS + 48, SLICE), BF16),
        ],
        [
            pltpu.VMEM((SHARD, 3 * WIDTH), BF16),
            pltpu.VMEM((SHARD, INNER), BF16),
            pltpu.VMEM((PIECE, WIDTH), BF16),
            pltpu.VMEM((BLOCK, WIDTH), BF16),
            pltpu.SemaphoreType.DMA((4,)),
        ],
        mebibytes=BIG,
        name="cut",
    )
    line_parts = line_turns(own_parts)
    tokens, own_parts = lax.optimization_barrier((tokens, own_parts))
    mine, other = pick(tokens, y), pick(tokens, 1 - y)
    got = [plane_swap(other, 4), plane_swap(mine, 2), plane_swap(other, 6)]
    *line_parts, got_y, got_x, got_d = lax.optimization_barrier((*line_parts, *got))
    near = jnp.concatenate([mine, got_y, got_x, got_d])
    far = plane_swap(near, 1)
    cot_mine, cot_other = pick(cotangent, y), plane_swap(pick(cotangent, 1 - y), 4)
    far, cot_other = lax.optimization_barrier((far, cot_other))
    halves = jnp.stack([part[PARTS : PARTS + COLS + 16] for part in line_parts])
    proj_near = jnp.stack([part[PARTS + COLS + 16 :] for part in line_parts])
    proj_far = plane_swap(proj_near, 1)
    others = plane_swap(halves, 4)
    turns = jnp.stack([part[:PARTS] for part in line_parts])
    from_x = plane_swap(turns, 2)
    from_y = plane_swap(turns, 4)

    full, bias, ends = call(
        vectors_kernel,
        (scal, own_parts, halves),
        (SM, VM, VM),
        [((8, WIDTH), F32), ((PLANE, SLICE), F32), ((8, PAD), F32)],
        [pltpu.VMEM((LINE, 16, SHARD), F32)],
        name="vectors",
    )

    queries, keys, values, weights, att_own, att_core, att_x, lse = call(
        attend_kernel,
        (*spots, ends, own_cols, halves, others, near, far),
        (SM, SM, SM, *[VM] * 6),
        [
            ((SLOTS, PAD), BF16),
            ((SLOTS, PAD), BF16),
            ((SLOTS, PAD), BF16),
            ((WIDTH, 3 * PAD), BF16),
            ((OWN, PAD), BF16),
            ((OWN, PAD), BF16),
            ((2, OWN, PAD), BF16),
            ((4, 8, OWN), F32),
        ],
        [
            pltpu.VMEM((WIDTH, 3 * WIDE), BF16),
            pltpu.VMEM((SLOTS, SPAN), F32),
            pltpu.VMEM((PAD, SLOTS), BF16),
            pltpu.VMEM((PAD, OWN), F32),
            pltpu.VMEM((4, OWN, PAD), BF16),
            *[pltpu.VMEM((SLOTS, PAD), BF16)] * 3,
            pltpu.VMEM((WIDTH, 3 * PAD), BF16),
            pltpu.SemaphoreType.DMA((4,)),
        ],
        mebibytes=BIG,
        own=(0, 1, 2, 3),
        name="attend",
    )
    att_x = plane_swap(att_x, 2)
    from_x, from_y, att_x = lax.optimization_barrier((from_x, from_y, att_x))
    from_d = relay(from_x, from_y, core)
    groups = list(swap_groups(att_own, att_x, att_core))
    from_d, groups[2], groups[3] = lax.optimization_barrier((from_d, groups[2], groups[3]))
    parts = [turns, from_y, from_x, from_d]
    parts += [plane_swap(part, 1) for part in parts]

    first_sum, normed_low = call(
        out_kernel,
        (scal, near, full, out_weight, *groups, *parts),
        (SM, VM, VM, VM, *[VM] * 4, *[HB] * 8),
        [
            ((OWN, WIDTH), F32),
            ((OWN, WIDTH), BF16),
        ],
        [pltpu.VMEM((LINE, PAD, WIDTH), BF16), pltpu.SemaphoreType.DMA],
        name="out",
    )
    normed_side = gather_side(normed_low)
    embedded, down_low, first_grad, grad_own, grad_core, grad_x, rest_mine, rest_other = call(
        middle_kernel,
        (*spots, first_sum, full, bias, proj_weight, out_weight, cot_mine, cot_other)
        + (proj_near, proj_far, *groups, ups, down_weight, *parts),
        (SM, SM, SM, *[VM] * 23),
        [
            ((OWN, EMBED), BF16),
            ((OWN, WIDTH), BF16),
            ((OWN, WIDTH), F32),
            *[((OWN, PAD), BF16)] * 2,
            ((2, OWN, PAD), BF16),
            *[((LINE, SPAN, WIDTH), BF16)] * 2,
        ],
        [
            pltpu.VMEM((OWN, WIDTH), BF16),
            pltpu.VMEM((OWN, WIDTH), F32),
            *[pltpu.VMEM((OWN, PAD), BF16)] * 2,
            pltpu.VMEM((2, OWN, PAD), BF16),
            *[pltpu.VMEM((LINE, SPAN, WIDTH), BF16)] * 2,
            pltpu.VMEM((PLANE, WIDTH, SLICE), BF16),
            pltpu.VMEM((PLANE, SLICE, WIDTH), BF16),
            pltpu.VMEM((LINE, PAD, WIDTH), BF16),
            pltpu.VMEM((WIDTH, EMBED), BF16),
            pltpu.VMEM((PLANE, OWN, SLICE), F32),
            pltpu.VMEM((WIDTH, EMBED), BF16),
            pltpu.VMEM((PLANE, SLICE), F32),
            pltpu.VMEM((4, PAD, WIDTH), BF16),
            pltpu.SemaphoreType.DMA((7,)),
        ],
        mebibytes=48,
        own=(1, 2, 3, 4, 5, 6, 7),
        name="middle",
    )
    *normed_side, down_low, embedded, grad_core, grad_x, rest_other = lax.optimization_barrier(
        (*normed_side, down_low, embedded, grad_core, grad_x, rest_other)
    )
    down_side = gather_side(down_low)
    embed_other = plane_swap(embedded[SPAN:], 4)
    embeddings = jnp.where(
        y == 0,
        jnp.stack([embedded[:SPAN], embed_other]),
        jnp.stack([embed_other, embedded[:SPAN]]),
    )

    grad_x = plane_swap(grad_x, 2)
    grads = swap_groups(grad_own, grad_x, grad_core)

    rest = rest_mine.astype(F32) + plane_swap(rest_other, 1).astype(F32)
    rest = rest.astype(BF16).reshape(LINE, 2, 64, WIDTH)
    rest_kept = lax.dynamic_index_in_dim(rest, x, 1, keepdims=False)
    rest_sent = lax.dynamic_index_in_dim(rest, 1 - x, 1, keepdims=False)
    rest_sent, first_grad = lax.optimization_barrier((rest_sent, first_grad))
    rest_sent = plane_swap(rest_sent, 2)

    qkv_mine, qkv_other, token_near, token_far = call(
        attend_back_kernel,
        (*spots, queries, keys, values, lse, weights, near, far, first_grad, *grads),
        (SM, SM, SM, HB, HB, HB, VM, *[HB] * 8),
        [
            *[((LINE, HALF + 16, 3 * WIDE), BF16)] * 2,
            *[((2 * OWN, WIDTH), BF16)] * 2,
        ],
        [
            *[pltpu.VMEM((LINE, HALF + 16, 3 * WIDE), BF16)] * 2,
            *[pltpu.VMEM((2 * OWN, WIDTH), BF16)] * 2,
            *[pltpu.VMEM((SLOTS, PAD), BF16)] * 3,
            pltpu.VMEM((WIDTH, 3 * PAD), BF16),
            *[pltpu.VMEM((2 * OWN, WIDTH), BF16)] * 2,
            pltpu.VMEM((OWN, WIDTH), F32),
            pltpu.VMEM((4, OWN, PAD), BF16),
            pltpu.VMEM((SLOTS, SPAN), F32),
            pltpu.VMEM((PAD, SLOTS), BF16),
            pltpu.VMEM((PAD, OWN), F32),
            pltpu.VMEM((SLOTS, 3 * PAD), BF16),
            pltpu.VMEM((SLOTS, PAD), F32),
            pltpu.VMEM((SLOTS, PAD), F32),
            pltpu.VMEM((WIDTH, 3 * PAD), BF16),
            pltpu.SemaphoreType.DMA((15,)),
        ],
        mebibytes=BIG,
        own=(0, 1, 2, 3),
        name="attend_back",
    )

    rest = (rest_kept.astype(F32) + rest_sent.astype(F32)).astype(BF16)
    rest = rest.reshape(LINE, 2, 32, WIDTH)
    rest_kept = lax.dynamic_index_in_dim(rest, y, 1, keepdims=False)
    rest_sent = lax.dynamic_index_in_dim(rest, 1 - y, 1, keepdims=False)
    rest_sent = plane_swap(rest_sent, 4)

    *down_side, token_near = lax.optimization_barrier((*down_side, token_near))

    def slice_grad(turns, ups, down, name):
        (parts,) = call(
            partial(slice_grad_kernel, name == "slice_other"),
            (scal, bias, turns, ups, down, *normed_side, *down_side),
            (SM, VM, *[HB] * 11),
            [((LINE, 2 * HALF, WIDTH), BF16)],
            [
                pltpu.VMEM((LINE - 1, PARTS, SLICE), BF16),
                pltpu.VMEM((SHARD, SLICE), BF16),
                pltpu.VMEM((PIECE, WIDTH), BF16),
                pltpu.VMEM((PLANE, OWN, WIDTH), BF16),
                pltpu.VMEM((WIDTH, SLICE), F32),
                *[pltpu.VMEM((SLICE, WIDTH), BF16)] * 2,
                *[pltpu.VMEM((SLICE, WIDTH), F32)] * 2,
                pltpu.VMEM((WIDTH, SLICE), F32),
                pltpu.SemaphoreType.DMA((11,)),
            ],
            mebibytes=BIG,
            name=name,
        )
        return parts

    slices_other = slice_grad(parts[4], ups, down_weight, "slice_other")
    *down_side, slices_other = lax.optimization_barrier((*down_side, slices_other))
    slices_mine = slice_grad(turns, ups, down_weight, "slice_mine")
    slices_other = plane_swap(slices_other, 1)
    slices_mine, rest_sent = lax.optimization_barrier((slices_mine, rest_sent))
    rest = (rest_kept.astype(F32) + rest_sent.astype(F32)).astype(BF16)
    shard_parts = []
    for turn in range(LINE):
        total = slices_mine[turn].astype(F32) + slices_other[turn].astype(F32)
        shard_parts.append(jnp.concatenate([total.astype(BF16), rest[turn]]))
    shard_part = sum_parts(turn_parts(shard_parts))

    qkv_other = plane_swap(qkv_other, 4)
    qkv_parts = [
        (qkv_mine[turn].astype(F32) + qkv_other[turn].astype(F32)).astype(BF16)
        for turn in range(LINE)
    ]
    qkv_part = sum_parts(turn_parts(qkv_parts))

    near_sum = (token_near.astype(F32) + plane_swap(token_far, 1).astype(F32)).reshape(4, SPAN, WIDTH)
    pair = near_sum[:2] + plane_swap(near_sum[2:].astype(BF16), 2).astype(F32)
    for_other = plane_swap(pair[1].astype(BF16), 4)
    for_mine, for_other = pair[0], for_other.astype(F32)
    tokens_grad = jnp.where(
        y == 0, jnp.stack([for_mine, for_other]), jnp.stack([for_other, for_mine])
    )
    up_grad, down_grad, out_grad, proj_grad, late_rows, bias_rows = call(
        rest_shard_kernel,
        (scal, *gather_plane(shard_part)),
        (SM, *[VM] * 5),
        [
            ((SHARD, INNER), F32),
            ((WIDTH, WIDTH), F32),
            ((SHARD, WIDTH), F32),
            ((SHARD, EMBED), F32),
            ((8, SHARD), F32),
            ((PLANE, PIECE), F32),
        ],
        [pltpu.VMEM((PLANE, 2 * HALF + 32, WIDTH), BF16)],
        name="rest_shard",
    )
    bias_grad = bias_rows.reshape(-1)
    qkv_grad, vectors_grad = call(
        qkv_shard_kernel,
        (scal, late_rows, *gather_plane(qkv_part)),
        (SM, *[VM] * 6),
        [((SHARD, 3 * WIDTH), F32), ((8, SHARD), F32)],
        [pltpu.VMEM((PLANE, HALF + 16, 3 * WIDE), BF16)],
        name="qkv_shard",
    )
    return (
        embeddings,
        tokens_grad,
        qkv_grad,
        out_grad,
        up_grad,
        bias_grad,
        down_grad,
        proj_grad,
        vectors_grad,
    )


def body(*arrays):
    sequences, span, width = arrays[0].shape
    fits = (
        lax.axis_size("ctx") == PLANE
        and lax.axis_size("wa") == LINE
        and sequences == 2
        and span == SPAN
        and width == WIDTH
    )
    return (plane_body if fits else general_body)(*arrays)


def solution(mesh):
    in_specs = (
        P("wa", "ctx", None),
        P(),
        P(),
        P("wa", None),
        P("wa", None),
        P("wa", None),
        P("wa"),
        P("wa", None),
        P("wa", None),
        P(None, "wa"),
        P("wa", "ctx", None),
    )
    out_specs = (
        P("wa", "ctx", None),
        P("wa", "ctx", None),
        P("wa", None),
        P("wa", None),
        P("wa", None),
        P("wa"),
        P("wa", None),
        P("wa", None),
        P(None, "wa"),
    )
    return jax.shard_map(body, mesh=mesh, in_specs=in_specs, out_specs=out_specs, check_vma=False)
```

```python
from functools import partial

import jax
import jax.numpy as jnp
from jax import lax
from jax.experimental import pallas as pl
from jax.experimental.pallas import tpu as pltpu
from jax.sharding import PartitionSpec as P

H = 12
HEAD = 64


NEG_FILL = -1e30
NORM_EPS = 1e-06
ROOT_HALF = 0.7071067811865476
DENSITY_SCALE = 0.3989422804014327


def norm_rows(inputs, gain_row, shift_row):
    middle = jnp.mean(inputs, axis=-1, keepdims=True)
    center = inputs - middle
    spread = jnp.mean(center * center, axis=-1, keepdims=True)
    scaled = lax.rsqrt(spread + NORM_EPS)
    unit_rows = center * scaled
    return (unit_rows * gain_row + shift_row, unit_rows, scaled)


def norm_back(grad_in, unit_rows, scaled, gain_row):
    gain_grad = jnp.sum(grad_in * unit_rows, axis=(0, 1))
    shift_grad = jnp.sum(grad_in, axis=(0, 1))
    inner_grad = grad_in * gain_row
    centered = inner_grad - jnp.mean(inner_grad, axis=-1, keepdims=True)
    result = scaled * (
        centered - unit_rows * jnp.mean(inner_grad * unit_rows, axis=-1, keepdims=True)
    )
    return (result, gain_grad, shift_grad)


def gelu_both(inner_sum):
    normal_cdf = 0.5 * (1.0 + lax.erf(inner_sum * ROOT_HALF))
    density = jnp.exp(-0.5 * inner_sum * inner_sum) * DENSITY_SCALE
    return (inner_sum * normal_cdf, normal_cdf + inner_sum * density)


def split_tiles(key_rows, value_rows, key_valid):
    key_count = key_rows.shape[0]
    tile_width = 512
    tile_count = key_count // tile_width
    return (
        key_rows.reshape(tile_count, tile_width, H, HEAD),
        value_rows.reshape(tile_count, tile_width, H, HEAD),
        key_valid.reshape(tile_count, tile_width),
    )


def masked_scores(queries, key_tile, mask_tile):
    products = jnp.einsum("qhd,khd->hqk", queries, key_tile, preferred_element_type=jnp.float32)
    return jnp.where(mask_tile[None, None, :], products, NEG_FILL)


def attend_forward(queries, key_rows, value_rows, key_valid):
    key_tiles, value_tiles, mask_tiles = split_tiles(key_rows, value_rows, key_valid)
    row_span = queries.shape[0]

    def stats_step(running, portion):
        highest, summed = running
        key_tile, mask_tile = portion
        scores = masked_scores(queries, key_tile, mask_tile)
        new_peak = jnp.maximum(highest, jnp.max(scores, axis=-1))
        raised = jnp.where(mask_tile[None, None, :], jnp.exp(scores - new_peak[:, :, None]), 0.0)
        return ((new_peak, summed * jnp.exp(highest - new_peak) + jnp.sum(raised, axis=-1)), None)

    start_peak = jnp.full((H, row_span), NEG_FILL, jnp.float32)
    start_sum = jnp.zeros((H, row_span), jnp.float32)
    (highest, summed), _ = lax.scan(stats_step, (start_peak, start_sum), (key_tiles, mask_tiles))
    logsum = highest + jnp.log(summed)

    def value_step(running, portion):
        key_tile, value_tile, mask_tile = portion
        scores = masked_scores(queries, key_tile, mask_tile)
        prob_low = jnp.where(
            mask_tile[None, None, :], jnp.exp(scores - logsum[:, :, None]), 0.0
        ).astype(jnp.bfloat16)
        return (
            running
            + jnp.einsum("hqk,khd->qhd", prob_low, value_tile, preferred_element_type=jnp.float32),
            None,
        )

    attended, _ = lax.scan(
        value_step,
        jnp.zeros((row_span, H, HEAD), jnp.float32),
        (key_tiles, value_tiles, mask_tiles),
    )
    return (attended, logsum)


def attend_backward(
    queries, key_rows, value_rows, key_valid, logsum, delta_rows, grad_heads, with_keys
):
    key_tiles, value_tiles, mask_tiles = split_tiles(key_rows, value_rows, key_valid)

    def back_step(running, portion):
        key_tile, value_tile, mask_tile = portion
        scores = masked_scores(queries, key_tile, mask_tile)
        prob_rows = jnp.where(mask_tile[None, None, :], jnp.exp(scores - logsum[:, :, None]), 0.0)
        prob_grad = jnp.einsum(
            "qhd,khd->hqk", grad_heads, value_tile, preferred_element_type=jnp.float32
        )
        score_low = (prob_rows * (prob_grad - delta_rows[:, :, None])).astype(jnp.bfloat16)
        running = running + jnp.einsum(
            "hqk,khd->qhd", score_low, key_tile, preferred_element_type=jnp.float32
        )
        value_part = jnp.einsum(
            "hqk,qhd->khd",
            prob_rows.astype(jnp.bfloat16),
            grad_heads,
            preferred_element_type=jnp.float32,
        )
        key_part = jnp.einsum(
            "hqk,qhd->khd", score_low, queries, preferred_element_type=jnp.float32
        )
        return (running, (key_part, value_part))

    start_grad = jnp.zeros(queries.shape, jnp.float32)
    query_grad, pieces = lax.scan(back_step, start_grad, (key_tiles, value_tiles, mask_tiles))
    key_count = key_rows.shape[0]
    return (
        query_grad,
        pieces[0].reshape(key_count, H * HEAD),
        pieces[1].reshape(key_count, H * HEAD),
    )


def general_body(
    tokens,
    doc_lengths,
    group_deal,
    qkv_weight,
    out_weight,
    up_weight,
    up_bias,
    down_weight,
    proj_weight,
    vectors,
    cotangent,
):
    gathered = (
        lax.all_gather(qkv_weight, "wa", axis=0, tiled=True),
        lax.all_gather(out_weight, "wa", axis=0, tiled=True),
        lax.all_gather(up_weight, "wa", axis=0, tiled=True),
        lax.all_gather(up_bias, "wa", axis=0, tiled=True),
        lax.all_gather(down_weight, "wa", axis=0, tiled=True),
        lax.all_gather(proj_weight, "wa", axis=0, tiled=True),
        lax.all_gather(vectors, "wa", axis=1, tiled=True),
    )
    qkv_full, out_full, up_full, bias_full, down_full, proj_full, vector_full = gathered
    seq_count, group_rows, model_width = tokens.shape
    ctx_count = lax.axis_size("ctx")
    seq_start = lax.axis_index("wa") * seq_count
    my_lengths = lax.dynamic_slice_in_dim(doc_lengths, seq_start, seq_count, 0)
    my_deal = lax.dynamic_slice_in_dim(group_deal, seq_start, seq_count, 0)
    offsets = jnp.tile(jnp.arange(group_rows, dtype=jnp.int32), ctx_count)
    positions = jnp.repeat(my_deal, group_rows, axis=1) * group_rows + offsets[None, :]
    key_valid = positions < my_lengths[:, None]
    query_valid = lax.dynamic_slice_in_dim(
        key_valid, lax.axis_index("ctx") * group_rows, group_rows, 1
    )
    row_mask = query_valid.astype(jnp.float32)[:, :, None]
    query_scale = HEAD ** (-0.5)
    mixed_rows = jnp.einsum("scd,de->sce", tokens, qkv_full, preferred_element_type=jnp.float32)
    queries = ((mixed_rows[:, :, :model_width] + vector_full[0]) * query_scale).astype(jnp.bfloat16)
    key_rows = mixed_rows[:, :, model_width : 2 * model_width].astype(jnp.bfloat16)
    value_rows = (mixed_rows[:, :, 2 * model_width :] + vector_full[1]).astype(jnp.bfloat16)
    all_keys, all_values = (
        lax.all_gather(key_rows, "ctx", axis=1, tiled=True),
        lax.all_gather(value_rows, "ctx", axis=1, tiled=True),
    )
    query_heads = queries.reshape(seq_count, group_rows, H, HEAD)
    attended, logsum = jax.vmap(attend_forward)(query_heads, all_keys, all_values, key_valid)
    attended_low = attended.reshape(seq_count, group_rows, model_width).astype(jnp.bfloat16)
    first_sum = tokens.astype(jnp.float32) + (
        jnp.einsum("scd,de->sce", attended_low, out_full, preferred_element_type=jnp.float32)
        + vector_full[2]
    )
    normed, unit_one, scale_one = norm_rows(first_sum, vector_full[3], vector_full[4])
    normed_low = normed.astype(jnp.bfloat16)
    inner_sum = (
        jnp.einsum("scd,df->scf", normed_low, up_full, preferred_element_type=jnp.float32)
        + bias_full
    )
    active, gelu_slope = gelu_both(inner_sum)
    active_low = active.astype(jnp.bfloat16)
    second_sum = normed + (
        jnp.einsum("scf,fd->scd", active_low, down_full, preferred_element_type=jnp.float32)
        + vector_full[5]
    )
    final_sum, unit_two, scale_two = norm_rows(second_sum, vector_full[6], vector_full[7])
    final_low = final_sum.astype(jnp.bfloat16)
    project = jnp.einsum("scd,de->sce", final_low, proj_full, preferred_element_type=jnp.float32)
    inverse = lax.rsqrt(jnp.sum(project * project, axis=-1, keepdims=True) + NORM_EPS)
    direction = project * inverse
    embeddings = (direction * row_mask).astype(jnp.bfloat16)
    upstream = cotangent.astype(jnp.float32) * row_mask
    project_grad = (
        inverse * (upstream - direction * jnp.sum(upstream * direction, axis=-1, keepdims=True))
    ).astype(jnp.bfloat16)
    proj_grad = jnp.einsum(
        "scd,sce->de", final_low, project_grad, preferred_element_type=jnp.float32
    )
    final_grad = jnp.einsum(
        "sce,de->scd", project_grad, proj_full, preferred_element_type=jnp.float32
    )
    second_grad, gain_two, shift_two = norm_back(final_grad, unit_two, scale_two, vector_full[6])
    down_low = second_grad.astype(jnp.bfloat16)
    down_grad = jnp.einsum("scf,scd->fd", active_low, down_low, preferred_element_type=jnp.float32)
    inner_grad = (
        jnp.einsum("scd,fd->scf", down_low, down_full, preferred_element_type=jnp.float32)
        * gelu_slope
    )
    bias_grad = jnp.sum(inner_grad, axis=(0, 1))
    inner_low = inner_grad.astype(jnp.bfloat16)
    up_grad = jnp.einsum("scd,scf->df", normed_low, inner_low, preferred_element_type=jnp.float32)
    normed_grad = second_grad + jnp.einsum(
        "scf,df->scd", inner_low, up_full, preferred_element_type=jnp.float32
    )
    first_grad, gain_one, shift_one = norm_back(normed_grad, unit_one, scale_one, vector_full[3])
    first_low = first_grad.astype(jnp.bfloat16)
    out_grad = jnp.einsum(
        "scd,sce->de", attended_low, first_low, preferred_element_type=jnp.float32
    )
    attended_grad = jnp.einsum(
        "sce,de->scd", first_low, out_full, preferred_element_type=jnp.float32
    ).astype(jnp.bfloat16)
    grad_heads = attended_grad.reshape(seq_count, group_rows, H, HEAD)
    delta_rows = jnp.sum(grad_heads.astype(jnp.float32) * attended, axis=-1)
    delta_heads = jnp.swapaxes(delta_rows, 1, 2)
    query_grad, key_terms, value_terms = jax.vmap(partial(attend_backward, with_keys=True))(
        query_heads, all_keys, all_values, key_valid, logsum, delta_heads, grad_heads
    )
    key_grad, value_grad = (
        lax.psum_scatter(
            key_terms.astype(jnp.bfloat16), "ctx", scatter_dimension=1, tiled=True
        ).astype(jnp.float32),
        lax.psum_scatter(
            value_terms.astype(jnp.bfloat16), "ctx", scatter_dimension=1, tiled=True
        ).astype(jnp.float32),
    )
    query_part = (
        query_grad.reshape(seq_count, group_rows, model_width).astype(jnp.bfloat16) * query_scale
    )
    value_part = value_grad.astype(jnp.bfloat16)
    mixed_grad = jnp.concatenate([query_part, key_grad.astype(jnp.bfloat16), value_part], axis=-1)
    qkv_grad = jnp.einsum("scd,sce->de", tokens, mixed_grad, preferred_element_type=jnp.float32)
    tokens_grad = first_grad + jnp.einsum(
        "sce,de->scd", mixed_grad, qkv_full, preferred_element_type=jnp.float32
    )
    vectors_grad = jnp.stack(
        [
            jnp.sum(query_part.astype(jnp.float32), axis=(0, 1)),
            jnp.sum(value_part.astype(jnp.float32), axis=(0, 1)),
            jnp.sum(first_grad, axis=(0, 1)),
            gain_one,
            shift_one,
            jnp.sum(second_grad, axis=(0, 1)),
            gain_two,
            shift_two,
        ],
        axis=0,
    )
    owned = (
        lax.psum_scatter(
            qkv_grad.astype(jnp.bfloat16), "wa", scatter_dimension=0, tiled=True
        ).astype(jnp.float32),
        lax.psum_scatter(
            out_grad.astype(jnp.bfloat16), "wa", scatter_dimension=0, tiled=True
        ).astype(jnp.float32),
        lax.psum_scatter(
            up_grad.astype(jnp.bfloat16), "wa", scatter_dimension=0, tiled=True
        ).astype(jnp.float32),
        lax.psum_scatter(
            bias_grad.astype(jnp.bfloat16), "wa", scatter_dimension=0, tiled=True
        ).astype(jnp.float32),
        lax.psum_scatter(
            down_grad.astype(jnp.bfloat16), "wa", scatter_dimension=0, tiled=True
        ).astype(jnp.float32),
        lax.psum_scatter(
            proj_grad.astype(jnp.bfloat16), "wa", scatter_dimension=0, tiled=True
        ).astype(jnp.float32),
        lax.psum_scatter(
            vectors_grad.astype(jnp.bfloat16), "wa", scatter_dimension=1, tiled=True
        ).astype(jnp.float32),
    )
    summed = (
        lax.psum(owned[0].astype(jnp.bfloat16), "ctx").astype(jnp.float32),
        lax.psum(owned[1].astype(jnp.bfloat16), "ctx").astype(jnp.float32),
        lax.psum(owned[2].astype(jnp.bfloat16), "ctx").astype(jnp.float32),
        lax.psum(owned[3].astype(jnp.bfloat16), "ctx").astype(jnp.float32),
        lax.psum(owned[4].astype(jnp.bfloat16), "ctx").astype(jnp.float32),
        lax.psum(owned[5].astype(jnp.bfloat16), "ctx").astype(jnp.float32),
        lax.psum(owned[6].astype(jnp.bfloat16), "ctx").astype(jnp.float32),
    )
    return (
        embeddings,
        tokens_grad,
        summed[0],
        summed[1],
        summed[2],
        summed[3],
        summed[4],
        summed[5],
        summed[6],
    )


PLANE = 8
LINE = 4
SPAN = 128
OWN = 2 * SPAN
WIDTH = H * HEAD
INNER = 4 * WIDTH
SHARD = WIDTH // LINE
HALF = SHARD // 2
PIECE = INNER // LINE // PLANE
SLICE = LINE * PIECE
HEADS = 3
WIDE = HEADS * HEAD
PAD = 256
SLOTS = PLANE * SPAN
BLOCK = SHARD // 4
FIRST = SHARD + BLOCK
SIDE = PIECE
PARTS = FIRST + 2 * SIDE
QUARTER = HALF // 2
COLS = HALF + QUARTER
EMBED = 128
ORDER = (0, 4, 2, 6, 1, 5, 3, 7)
NEAR = (0, 2, 1, 3)
F32 = jnp.float32
BF16 = jnp.bfloat16

NN = ((1,), (0,))
NT = ((1,), (1,))
TN = ((0,), (0,))


def dot(left, right, dims):
    return lax.dot_general(left, right, (dims, ((), ())), preferred_element_type=F32)


def plane_swap(array, bits):
    return lax.ppermute(array, "ctx", [(i, i ^ bits) for i in range(PLANE)])


def line_turn(array, step):
    return lax.ppermute(array, "wa", [(i, (i + step) % LINE) for i in range(LINE)])


def line_turns(array):
    return [line_turn(array, step) for step in range(1, LINE)]


def relay(from_x, from_y, core):
    passed = jnp.where(core == 0, from_y, from_x)
    pairs = [(i, i ^ 2 if i % 2 == 0 else i ^ 4) for i in range(PLANE)]
    return lax.ppermute(passed, "ctx", pairs)


def pick(array, index):
    return lax.dynamic_index_in_dim(array, index, 0, keepdims=False)


COST = {'cut': 3, 'vectors': 1, 'attend': 12, 'out': 3, 'middle': 17, 'attend_back': 18, 'rest_shard': 4, 'qkv_shard': 2, 'slice_other': 3.0, 'slice_mine': 3.0}
VM = pl.BlockSpec(memory_space=pltpu.VMEM)
SM = pl.BlockSpec(memory_space=pltpu.SMEM)
HB = pl.BlockSpec(memory_space=pl.ANY)
BIG = 56


def call(kernel, inputs, spaces, outputs, scratch=(), mebibytes=32, name=None, own=()):
    shapes = [jax.ShapeDtypeStruct(shape, kind) for shape, kind in outputs]
    return pl.pallas_call(
        kernel,
        out_shape=shapes,
        in_specs=list(spaces),
        out_specs=[HB if i in own else VM for i in range(len(shapes))],
        scratch_shapes=list(scratch),
        compiler_params=pltpu.CompilerParams(vmem_limit_bytes=mebibytes << 20),
        cost_estimate=pl.CostEstimate(flops=int(COST[name] * 1e9), bytes_accessed=1, transcendentals=0),
        name=name,
    )(*inputs)


def place_of(scal):
    return scal[0], scal[1]


def shard_of_turn(line, turn):
    return lax.rem(line - turn + LINE, LINE)


def turn_ahead(line, turn):
    return lax.rem(line + turn, LINE)


def norm_forward(rows):
    middle = jnp.mean(rows, axis=-1, keepdims=True)
    center = rows - middle
    scaled = lax.rsqrt(jnp.mean(center * center, axis=-1, keepdims=True) + NORM_EPS)
    return center * scaled, scaled


def norm_reverse(grad, unit, scaled, gain):
    inner = grad * gain
    return scaled * (
        inner
        - jnp.mean(inner, axis=-1, keepdims=True)
        - unit * jnp.mean(inner * unit, axis=-1, keepdims=True)
    )


def cut_kernel(
    scal, vectors, bias, proj, qkv, up, down, out,
    cols_ref, ups_ref, own_ref,
    qkv_held, up_held, down_held, out_held, sems,
):
    me, line = place_of(scal)
    core = lax.rem(me, 2)
    copies = [
        pltpu.make_async_copy(qkv, qkv_held, sems.at[0]),
        pltpu.make_async_copy(up, up_held, sems.at[1]),
        pltpu.make_async_copy(
            down.at[pl.ds(pl.multiple_of(me * PIECE, 16), PIECE)], down_held, sems.at[2]
        ),
        pltpu.make_async_copy(
            out.at[pl.ds(pl.multiple_of(lax.div(me, 2) * BLOCK, 16), BLOCK)], out_held, sems.at[3]
        ),
    ]
    for copy in copies:
        copy.start()
    rows = [vectors[...].astype(F32)]
    flat = bias[...].astype(F32).reshape(1, WIDTH)
    rows += [flat[:, a * SHARD : (a + 1) * SHARD] for a in range(LINE)]
    rows = jnp.concatenate(rows + [jnp.zeros((4, SHARD), F32)])
    own_ref[PARTS + COLS : PARTS + COLS + 16, :SHARD] = rows.astype(BF16)
    own_ref[PARTS + COLS : PARTS + COLS + 16, SHARD:] = jnp.zeros((16, SLICE - SHARD), BF16)
    for side in range(2):
        start = PARTS + COLS + 16 * (1 + side)
        for t in range(3):
            own_ref[start : start + 16, t * EMBED : (t + 1) * EMBED] = proj[
                pl.ds(pl.multiple_of(core * HALF + 16 * (3 * side + t), 16), 16), :
            ]
    copies[0].wait()
    for g in range(4):

        @pl.when(lax.rem(me, 4) == g)
        def _():
            for part in range(3):
                start = part * WIDTH + g * WIDE
                cols_ref[:, part * WIDE : (part + 1) * WIDE] = qkv_held[:, start : start + WIDE]

    base = lax.div(me, 4) * HALF
    rows = cols_ref[pl.ds(pl.multiple_of(base, 16), HALF), :]
    own_ref[PARTS : PARTS + HALF, :] = rows[:, :SLICE]
    for side in range(2):
        own_ref[PARTS + HALF : PARTS + COLS, side * WIDE : (side + 1) * WIDE] = rows[
            side * QUARTER : (side + 1) * QUARTER, SLICE:
        ]
    copies[1].wait()
    for k in range(PLANE):
        for s in range(LINE):
            start = s * PLANE * PIECE + k * PIECE
            ups_ref[k, :, s * PIECE : (s + 1) * PIECE] = up_held[:, start : start + PIECE]
    own_ref[:SHARD] = ups_ref[me]
    copies[2].wait()
    for side in range(2):
        start = FIRST + side * SIDE
        own_ref[start : start + PIECE] = down_held[:, side * SLICE : (side + 1) * SLICE]
    copies[3].wait()
    own_ref[SHARD:FIRST] = out_held[:, pl.ds(pl.multiple_of(core * SLICE, 128), SLICE)]


def vectors_kernel(scal, own, halves, full_ref, bias_ref, ends_ref, held):
    me, line = place_of(scal)
    held[line] = own[PARTS + COLS : PARTS + COLS + 16, :SHARD].astype(F32)
    for turn in range(1, LINE):
        held[shard_of_turn(line, turn)] = halves[turn - 1, COLS:, :SHARD].astype(F32)
    for a in range(LINE):
        full_ref[:, a * SHARD : (a + 1) * SHARD] = held[a, :8, :]
        for k in range(PLANE):
            start = (k % 2) * PIECE
            bias_ref[k : k + 1, a * PIECE : (a + 1) * PIECE] = held[
                a, 8 + k // 2 : 9 + k // 2, start : start + PIECE
            ]
    ends_ref[...] = jnp.zeros((8, PAD), F32)
    ends_ref[:, :WIDE] = held[lax.rem(me, 4), :8, :]


def slots_left(scal, lengths, deal, place):
    me, line = place_of(scal)
    seq = 2 * line + lax.div(me, 4)
    return lengths[seq] - deal[seq, me ^ ORDER[place]] * SPAN


def fill_mask(scal, lengths, deal, mask):
    rows = lax.broadcasted_iota(jnp.int32, (SPAN, SPAN), 0)
    for place in range(PLANE):
        limit = slots_left(scal, lengths, deal, place)
        mask[place * SPAN : (place + 1) * SPAN, :] = jnp.where(rows < limit, 0.0, NEG_FILL)


def head_lanes(h):
    lanes = lax.broadcasted_iota(jnp.int32, (OWN, 128), 1)
    return (lanes >= HEAD) if h % 2 else (lanes < HEAD)


def attend_kernel(
    scal, lengths, deal, ends, own_cols, halves, others, near, far,
    q_out, k_out, v_out, w_out, own_ref, core_ref, x_ref, lse_ref,
    raw, mask, v_turned, o_turned, att, q_ref, k_ref, v_ref, w_ref, sems,
):
    me, line = place_of(scal)
    y = lax.div(me, 4)
    raw[pl.ds(pl.multiple_of(line * SHARD, 16), SHARD), :] = own_cols[...]
    for turn in range(1, LINE):
        base = shard_of_turn(line, turn) * SHARD
        for source, side in ((halves, y), (others, 1 - y)):
            start = base + side * HALF
            at = pl.ds(pl.multiple_of(start, 16), HALF)
            raw[at, :SLICE] = source[turn - 1, :HALF, :]
            for i in range(2):
                at = pl.ds(pl.multiple_of(start + i * QUARTER, 16), QUARTER)
                raw[at, SLICE:] = source[turn - 1, HALF:COLS, i * WIDE : (i + 1) * WIDE]
    fill_mask(scal, lengths, deal, mask)
    for part in range(3):
        w_ref[:, part * PAD : part * PAD + WIDE] = raw[:, part * WIDE : (part + 1) * WIDE]
        w_ref[:, part * PAD + WIDE : (part + 1) * PAD] = jnp.zeros((WIDTH, PAD - WIDE), BF16)
    for t in range(4):
        source = (near, far)[t // 2]
        rows = source[(t % 2) * OWN : (t % 2 + 1) * OWN, :]
        mixed = dot(rows, w_ref[...], NN)
        at = slice(t * OWN, (t + 1) * OWN)
        q_ref[at, :] = ((mixed[:, :PAD] + ends[0:1, :]) * (HEAD ** (-0.5))).astype(BF16)
        k_ref[at, :] = mixed[:, PAD : 2 * PAD].astype(BF16)
        values = mixed[:, 2 * PAD :] + ends[1:2, :]
        v_ref[at, :] = values.astype(BF16)
        v_turned[:, at] = values.T.astype(BF16)

    copies = [
        pltpu.make_async_copy(source, target, sems.at[i])
        for i, (source, target) in enumerate(
            ((q_ref, q_out), (k_ref, k_out), (v_ref, v_out), (w_ref, w_out))
        )
    ]
    for copy in copies:
        copy.start()
    o_turned[WIDE:, :] = jnp.zeros((PAD - WIDE, OWN), F32)

    def tile(t, carry):
        at = pl.ds(pl.multiple_of(t * OWN, OWN), OWN)
        for h in range(HEADS):
            cut = slice((h // 2) * 128, (h // 2 + 1) * 128)
            q_tile = jnp.where(head_lanes(h), q_ref[at, cut], jnp.zeros((), BF16))
            scores = dot(k_ref[:, cut], q_tile, NT)
            scores = scores + jnp.concatenate([mask[...], mask[...]], axis=1)
            peak = jnp.max(scores, axis=0, keepdims=True)
            raised = jnp.exp(scores - peak)
            total = jnp.sum(raised, axis=0, keepdims=True)
            rows = slice(h * HEAD, (h + 1) * HEAD)
            o_turned[rows, :] = dot(v_turned[rows, :], raised.astype(BF16), NN) * (1.0 / total)
            lse_ref[t, h : h + 1, :] = peak + jnp.log(total)
        att[t] = o_turned[...].T.astype(BF16)
        return carry

    lax.fori_loop(0, 4, tile, 0)
    own_ref[...] = att[0]
    core_ref[...] = att[2]
    x_ref[0] = att[1]
    x_ref[1] = att[3]
    for copy in copies:
        copy.wait()


def attend_back_kernel(
    scal, lengths, deal, q_ref, k_ref, v_ref, lse, weights, near, far, first_grad, g0, g1, g2, g3,
    mine_out, other_out, near_out, far_out,
    mine_ref, other_ref, near_ref, far_ref,
    q_held, k_held, v_held, w_held, near_held, far_held, first_held, grads,
    mask, k_turned, q_turned, mixed, key_sum, value_sum, part, sems,
):
    sources = (k_ref, q_ref, v_ref, g0, g1.at[0], g2, g3, weights, near, far, first_grad)
    targets = (k_held, q_held, v_held, grads.at[0], grads.at[1], grads.at[2], grads.at[3])
    targets += (w_held, near_held, far_held, first_held)
    copies = [
        pltpu.make_async_copy(source, target, sems.at[i])
        for i, (source, target) in enumerate(zip(sources, targets, strict=True))
    ]
    for copy in copies:
        copy.start()
    fill_mask(scal, lengths, deal, mask)
    copies[0].wait()
    for t in range(4):
        at = slice(t * OWN, (t + 1) * OWN)
        k_turned[:, at] = k_held[at, :].astype(F32).T.astype(BF16)
    key_sum[...] = jnp.zeros_like(key_sum)
    value_sum[...] = jnp.zeros_like(value_sum)
    q_turned[WIDE:, :] = jnp.zeros((PAD - WIDE, OWN), F32)
    for copy in copies[1:7]:
        copy.wait()

    def tile(t, carry):
        at = pl.ds(pl.multiple_of(t * OWN, OWN), OWN)
        for h in range(HEADS):
            cut = slice((h // 2) * 128, (h // 2 + 1) * 128)
            rows = slice(h * HEAD, (h + 1) * HEAD)
            q_tile = jnp.where(head_lanes(h), q_held[at, cut], jnp.zeros((), BF16))
            g_tile = jnp.where(head_lanes(h), grads[t, :, cut], jnp.zeros((), BF16))
            scores = dot(k_held[:, cut], q_tile, NT)
            scores = scores + jnp.concatenate([mask[...], mask[...]], axis=1)
            probs = jnp.exp(scores - lse[t, h : h + 1, :])
            prob_grad = dot(v_held[:, cut], g_tile, NT)
            delta = jnp.sum(probs * prob_grad, axis=0, keepdims=True)
            score_low = (probs * (prob_grad - delta)).astype(BF16)
            q_turned[rows, :] = dot(k_turned[rows, :], score_low, NN)
            key_sum[:, cut] += dot(score_low, q_tile, NN)
            value_sum[:, cut] += dot(probs.astype(BF16), g_tile, NN)
        low = q_turned[...].T.astype(BF16)
        mixed[at, :PAD] = (low.astype(F32) * (HEAD ** (-0.5))).astype(BF16)
        return carry

    lax.fori_loop(0, 4, tile, 0)
    mixed[:, PAD : 2 * PAD] = key_sum[...].astype(BF16)
    mixed[:, 2 * PAD :] = value_sum[...].astype(BF16)

    me, line = place_of(scal)
    y = lax.div(me, 4)
    for copy in copies[7:]:
        copy.wait()
    for i in range(3):
        cut = slice(i * 256, (i + 1) * 256)
        part[cut, :] = (
            dot(near_held[:, cut], mixed[: 2 * OWN, :], TN) + dot(far_held[:, cut], mixed[2 * OWN :, :], TN)
        ).astype(BF16)
    sums = jnp.sum(mixed[...].astype(F32), axis=0, keepdims=True)
    sums = jnp.concatenate([sums, jnp.zeros((15, 3 * PAD), F32)]).astype(BF16)
    for turn in range(LINE):
        base = turn_ahead(line, turn) * SHARD
        for target, side in ((mine_ref, y), (other_ref, 1 - y)):
            rows = part[pl.ds(pl.multiple_of(base + side * HALF, 16), HALF), :]
            for p in range(3):
                to = slice(p * WIDE, (p + 1) * WIDE)
                target[turn, :HALF, to] = rows[:, p * PAD : p * PAD + WIDE]
                target[turn, HALF:, to] = sums[:, p * PAD : p * PAD + WIDE]
    outs = [
        pltpu.make_async_copy(source, target, sems.at[11 + i])
        for i, (source, target) in enumerate(
            (
                (other_ref, other_out),
                (mine_ref, mine_out),
                (far_ref, far_out),
                (near_ref, near_out),
            )
        )
    ]
    outs[0].start()
    outs[1].start()
    for t in (2, 3, 0, 1):
        at = slice(t * OWN, (t + 1) * OWN)
        token_part = dot(mixed[at, :], w_held[...], NT)
        if t == 0:
            near_ref[at, :] = (token_part + first_held[...]).astype(BF16)
        elif t == 1:
            near_ref[at, :] = token_part.astype(BF16)
        else:
            far_ref[(t - 2) * OWN : (t - 1) * OWN, :] = token_part.astype(BF16)
        if t == 3:
            outs[2].start()
    outs[3].start()
    for copy in outs:
        copy.wait()


def out_kernel(
    scal, near, full, out_shard, a0, a1, a2, a3, p0, p1, p2, p3, p4, p5, p6, p7,
    sum_ref, low_ref,
    out_ref, sem,
):
    me, line = place_of(scal)
    group = lax.rem(me, 4)
    pieces = (p0, p1, p2, p3, p4, p5, p6, p7)
    copies = []
    for place, bits in enumerate(ORDER):
        k = me ^ bits
        rows = pl.ds(pl.multiple_of(lax.div(k, 2) * BLOCK, 16), BLOCK)
        lanes = pl.ds(pl.multiple_of(lax.rem(k, 2) * SLICE, 128), SLICE)
        for turn in range(1, LINE):
            copies.append(
                pltpu.make_async_copy(
                    pieces[place].at[turn - 1, pl.ds(SHARD, BLOCK)],
                    out_ref.at[shard_of_turn(line, turn), rows, lanes],
                    sem,
                )
            )
    for copy in copies:
        copy.start()
    for z in range(LINE):
        out_ref[z, SHARD:, :] = jnp.zeros((PAD - SHARD, WIDTH), BF16)
    out_ref[line, :SHARD, :] = out_shard[...]
    rows = near[:OWN, :].astype(F32) + full[2:3, :]
    filled = out_ref.at[pl.ds(0, LINE - 1), pl.ds(0, SHARD)]
    pltpu.make_async_copy(filled, filled, sem).wait()
    for i, source in enumerate((a0[...], a1[0], a2[...], a3[...])):
        rows = rows + dot(source, out_ref[group ^ NEAR[i]], NN)
    sum_ref[...] = rows
    unit, _ = norm_forward(rows)
    low_ref[...] = (unit * full[3:4, :] + full[4:5, :]).astype(BF16)


def place_up(scal, place, up_own, held, up_all):
    me, line = place_of(scal)
    at = pl.ds(pl.multiple_of(line * SHARD, 16), SHARD)
    up_all[place, at, :] = up_own[me ^ ORDER[place]]
    for turn in range(1, LINE):
        at = pl.ds(pl.multiple_of(shard_of_turn(line, turn) * SHARD, 16), SHARD)
        up_all[place, at, :] = held[place][turn - 1, :SHARD, :]


def place_down(scal, place, down_own, held, down_all):
    me, line = place_of(scal)
    at = pl.ds(pl.multiple_of(line * PIECE, 16), PIECE)
    start = pl.multiple_of((me ^ ORDER[place]) * PIECE, 16)
    down_all[place, at, :] = down_own[pl.ds(start, PIECE), :]
    for turn in range(1, LINE):
        at = pl.ds(pl.multiple_of(shard_of_turn(line, turn) * PIECE, 16), PIECE)
        for side in range(2):
            start = FIRST + side * SIDE
            down_all[place, at, side * SLICE : (side + 1) * SLICE] = held[place][
                turn - 1, start : start + PIECE, :
            ]


def place_out(scal, place, held, out_all):
    me, line = place_of(scal)
    k = me ^ ORDER[place]
    rows = pl.ds(pl.multiple_of(lax.div(k, 2) * BLOCK, 16), BLOCK)
    lanes = pl.ds(pl.multiple_of(lax.rem(k, 2) * SLICE, 128), SLICE)
    for turn in range(1, LINE):
        out_all[shard_of_turn(line, turn), rows, lanes] = held[place][turn - 1, SHARD:FIRST, :]


def middle_kernel(
    scal, lengths, deal, first_sum, full, bias, proj_shard, out_shard, cot_mine, cot_other,
    proj_near, proj_far, a0, a1, a2, a3, ups, down, p0, p1, p2, p3, p4, p5, p6, p7,
    embed_ref, low_out, first_out, own_out, core_out, x_out, mine_out, other_out,
    low_ref, first_ref, own_ref, core_ref, x_ref, mine_ref, other_ref,
    up_all, down_all, out_all, proj_all, slopes, proj_part, bias_sum, out_part, sems,
):
    held = (p0, p1, p2, p3, p4, p5, p6, p7)
    up_own, down_own = ups, down
    me, line = place_of(scal)
    core, group = lax.rem(me, 2), lax.rem(me, 4)
    proj_all[pl.ds(pl.multiple_of(line * SHARD, 16), SHARD), :] = proj_shard[...]

    unit_one, scale_one = norm_forward(first_sum[...])
    normed = unit_one * full[3:4, :] + full[4:5, :]
    normed_low = normed.astype(BF16)
    second_sum = normed + full[5:6, :]
    for z in range(LINE):
        out_all[z, SHARD:, :] = jnp.zeros((PAD - SHARD, WIDTH), BF16)
    out_all[line, :SHARD, :] = out_shard[...]
    for place, bits in enumerate(ORDER):
        place_up(scal, place, up_own, held, up_all)
        place_down(scal, place, down_own, held, down_all)
        place_out(scal, place, held, out_all)
        inner = dot(normed_low, up_all[place], NN) + bias[pl.ds(me ^ bits, 1), :]
        active, slope = gelu_both(inner)
        slopes[place] = slope
        second_sum = second_sum + dot(active.astype(BF16), down_all[place], NN)
    unit, scaled = norm_forward(second_sum)
    final_low = (unit * full[6:7, :] + full[7:8, :]).astype(BF16)
    for half, source in ((core, proj_near), (1 - core, proj_far)):
        for turn in range(1, LINE):
            base = shard_of_turn(line, turn) * SHARD + half * HALF
            for t in range(6):
                start = 16 * (t // 3)
                proj_all[pl.ds(pl.multiple_of(base + 16 * t, 16), 16), :] = source[
                    turn - 1, start : start + 16, (t % 3) * EMBED : (t % 3 + 1) * EMBED
                ]
    project = dot(final_low, proj_all[...], NN)
    inverse = lax.rsqrt(jnp.sum(project * project, axis=-1, keepdims=True) + NORM_EPS)
    direction = project * inverse
    rows = lax.broadcasted_iota(jnp.int32, (SPAN, EMBED), 0)
    keep = jnp.concatenate(
        [
            jnp.where(rows < slots_left(scal, lengths, deal, i), 1.0, 0.0).astype(F32)
            for i in range(2)
        ]
    )
    embed_ref[...] = (direction * keep).astype(BF16)
    upstream = jnp.concatenate([cot_mine[...], cot_other[...]]).astype(F32) * keep
    project_grad = (
        inverse * (upstream - direction * jnp.sum(upstream * direction, axis=-1, keepdims=True))
    ).astype(BF16)
    proj_part[...] = dot(final_low, project_grad, TN).astype(BF16)
    final_grad = dot(project_grad, proj_all[...], NT)
    second_grad = norm_reverse(final_grad, unit, scaled, full[6:7, :])
    down_low = second_grad.astype(BF16)
    low_ref[...] = down_low
    outs = [
        pltpu.make_async_copy(source, target, sems.at[i])
        for i, (source, target) in enumerate(
            (
                (low_ref, low_out),
                (x_ref, x_out),
                (core_ref, core_out),
                (own_ref, own_out),
                (first_ref, first_out),
                (other_ref, other_out),
                (mine_ref, mine_out),
            )
        )
    ]
    outs[0].start()

    normed_grad = second_grad
    for place, bits in enumerate(ORDER):
        inner_grad = dot(down_low, down_all[place], NT) * slopes[place]
        bias_sum[pl.ds(me ^ bits, 1), :] = jnp.sum(inner_grad, axis=0, keepdims=True)
        normed_grad = normed_grad + dot(inner_grad.astype(BF16), up_all[place], NT)
    first_grad = norm_reverse(normed_grad, unit_one, scale_one, full[3:4, :])
    first_ref[...] = first_grad
    first_low = first_grad.astype(BF16)
    for i, target in enumerate((own_ref, x_ref.at[0], core_ref, x_ref.at[1])):
        target[...] = dot(first_low, out_all[group ^ NEAR[i]], NT).astype(BF16)
    for copy in outs[1:5]:
        copy.start()
    small = jnp.concatenate(
        [
            jnp.sum(first_grad, axis=0, keepdims=True),
            jnp.sum(normed_grad * unit_one, axis=0, keepdims=True),
            jnp.sum(normed_grad, axis=0, keepdims=True),
            jnp.sum(second_grad, axis=0, keepdims=True),
            jnp.sum(final_grad * unit, axis=0, keepdims=True),
            jnp.sum(final_grad, axis=0, keepdims=True),
            jnp.zeros((2, WIDTH), F32),
        ]
    )
    tail = jnp.concatenate([bias_sum[...], jnp.zeros((8, WIDTH - SLICE), F32)], axis=1)
    small = jnp.concatenate([small, tail]).astype(BF16)
    for i, source in enumerate((a0[...], a1[0], a2[...], a3[...])):
        z = group ^ NEAR[i]
        turn = lax.rem(z - line + LINE, LINE)
        out_part[i] = dot(source, first_low, TN).astype(BF16)
        for target, half in ((mine_ref, core), (other_ref, 1 - core)):
            base = half * HALF
            target[turn, :HALF, :] = out_part[i, pl.ds(pl.multiple_of(base, 16), HALF), :]
            for t in range(6):
                target[turn, HALF : HALF + 16, t * EMBED : (t + 1) * EMBED] = proj_part[
                    pl.ds(pl.multiple_of(z * SHARD + base + 16 * t, 16), 16), :
                ]
            target[turn, HALF + 16 :, :] = small
    outs[5].start()
    outs[6].start()
    for copy in outs:
        copy.wait()


def slice_grad_kernel(
    other, scal, bias, turns, ups, down, n0, n1, n2, n3, d0, d1, d2, d3,
    part_ref,
    held, ups_held, down_held, slots, up_rows, up_turned, down_rows, up_sum, down_sum, up_back,
    sems,
):
    me, line = place_of(scal)
    k = me ^ 1 if other else me
    copies = [
        pltpu.make_async_copy(turns, held, sems.at[0]),
        pltpu.make_async_copy(ups.at[k], ups_held, sems.at[1]),
        pltpu.make_async_copy(
            down.at[pl.ds(pl.multiple_of(k * PIECE, 16), PIECE)], down_held, sems.at[2]
        ),
    ]
    for j, source in enumerate((n0, d0, n1, d1, n2, d2, n3, d3)):
        copies.append(pltpu.make_async_copy(source, slots.at[j], sems.at[3 + j]))
    for copy in copies:
        copy.start()
    for copy in copies[:3]:
        copy.wait()
    for turn in range(LINE):
        z = shard_of_turn(line, turn)
        rows = held[turn - 1, :SHARD, :] if turn else ups_held[...]
        up_rows[pl.ds(pl.multiple_of(z * SHARD, 16), SHARD), :] = rows.astype(F32)
        at = pl.ds(pl.multiple_of(z * PIECE, 16), PIECE)
        if turn == 0:
            down_rows[at, :] = down_held[...]
            continue
        for side in range(2):
            start = FIRST + side * SIDE
            down_rows[at, side * SLICE : (side + 1) * SLICE] = held[
                turn - 1, start : start + PIECE, :
            ]
    up_turned[...] = up_rows[...].T.astype(BF16)
    bias_rows = jnp.broadcast_to(bias[pl.ds(k, 1), :], (128, SLICE)).T
    bias_rows = jnp.concatenate([bias_rows, bias_rows], axis=1)
    for j in range(4):
        copies[3 + 2 * j].wait()
        copies[4 + 2 * j].wait()
        normed, low = slots[2 * j], slots[2 * j + 1]
        inner = dot(up_turned[...], normed, NT) + bias_rows
        active, slope = gelu_both(inner)
        inner_low = (dot(down_rows[...], low, NT) * slope).astype(BF16)
        up_part = dot(inner_low, normed, NN)
        down_part = dot(active.astype(BF16), low, NN)
        if j == 0:
            up_sum[...] = up_part
            down_sum[...] = down_part
        else:
            up_sum[...] += up_part
            down_sum[...] += down_part
    up_back[...] = up_sum[...].T
    for turn in range(LINE):
        z = turn_ahead(line, turn)
        for side in range(2):
            at = pl.ds(pl.multiple_of(z * SHARD + side * HALF, 16), HALF)
            part_ref[turn, :HALF, side * SLICE : (side + 1) * SLICE] = up_back[at, :].astype(BF16)
        at = pl.ds(pl.multiple_of(z * PIECE, 16), PIECE)
        part_ref[turn, HALF:, :] = down_sum[at, :].astype(BF16)


def hold_parts(me, close, far, held):
    for place in range(4):
        held[me ^ ORDER[place]] = close[place][...]
        held[me ^ ORDER[place + 4]] = far[place]


def rest_shard_kernel(
    scal, p0, p1, p2, p3, far,
    up_ref, down_ref, out_ref, proj_ref, rows_ref, bias_ref, held,
):
    me, line = place_of(scal)
    hold_parts(me, (p0, p1, p2, p3), far, held)
    for k in range(PLANE):
        core, x, y = k % 2, (k // 2) % 2, k // 4
        for side in range(2):
            rows = held[k, :HALF, side * SLICE : (side + 1) * SLICE].astype(F32)
            for s in range(LINE):
                start = s * PLANE * PIECE + k * PIECE
                up_ref[side * HALF : (side + 1) * HALF, start : start + PIECE] = rows[
                    :, s * PIECE : (s + 1) * PIECE
                ]
        down_ref[k * PIECE : (k + 1) * PIECE, :] = held[k, HALF : 2 * HALF, :].astype(F32)
        tail = held[k, 2 * HALF :, :].astype(F32)
        block = 2 * x + y
        if block < 3:
            start = core * HALF + 32 * block
            out_ref[start : start + 32, :] = tail
        else:
            for t in range(6):
                start = core * HALF + 16 * t
                proj_ref[start : start + 16, :] = tail[:16, t * EMBED : (t + 1) * EMBED]
            if core == 0:
                small = tail[16:, :]
    for z in range(LINE):

        @pl.when(line == z)
        def _():
            rows_ref[...] = small[:8, z * SHARD : (z + 1) * SHARD]
            flat = [small[8 + k : 9 + k, z * PIECE : (z + 1) * PIECE] for k in range(PLANE)]
            bias_ref[...] = jnp.concatenate(flat, axis=1).reshape(WIDTH)


def qkv_shard_kernel(scal, late, p0, p1, p2, p3, far, qkv_ref, rows_ref, held):
    me, line = place_of(scal)
    hold_parts(me, (p0, p1, p2, p3), far, held)
    for k in range(PLANE):
        y, g = k // 4, k % 4
        for part in range(3):
            start = part * WIDTH + g * WIDE
            qkv_ref[y * HALF : (y + 1) * HALF, start : start + WIDE] = held[
                k, :HALF, part * WIDE : (part + 1) * WIDE
            ].astype(F32)
    sums = held[line, HALF:, :].astype(F32)
    rows_ref[...] = jnp.concatenate(
        [sums[:1, :WIDE], sums[:1, 2 * WIDE : 3 * WIDE], late[:6, :]]
    )


def gather_side(array):
    return [array, plane_swap(array, 4), plane_swap(array, 2), plane_swap(array, 6)]


def gather_plane(array):
    close = gather_side(array)
    return close + [plane_swap(jnp.stack(close), 1)]


def turn_parts(parts):
    return [parts[0]] + [line_turn(parts[turn], turn) for turn in range(1, LINE)]


def sum_parts(parts):
    total = parts[0].astype(F32)
    for part in parts[1:]:
        total = total + part.astype(F32)
    return total.astype(BF16)


def swap_groups(own, from_x, for_core):
    return own, from_x, plane_swap(for_core, 1), plane_swap(from_x[1], 1)


def plane_body(
    tokens,
    doc_lengths,
    group_deal,
    qkv_weight,
    out_weight,
    up_weight,
    up_bias,
    down_weight,
    proj_weight,
    vectors,
    cotangent,
):
    me = lax.axis_index("ctx").astype(jnp.int32)
    line = lax.axis_index("wa").astype(jnp.int32)
    y, x, core = me // 4, (me // 2) % 2, me % 2
    scal = jnp.stack([me, line])
    spots = (scal, doc_lengths, group_deal)

    own_cols, ups, own_parts = call(
        cut_kernel,
        (scal, vectors, up_bias, proj_weight)
        + (qkv_weight, up_weight, down_weight, out_weight),
        (SM, VM, VM, VM, HB, HB, HB, HB),
        [
            ((SHARD, 3 * WIDE), BF16),
            ((PLANE, SHARD, SLICE), BF16),
            ((PARTS + COLS + 48, SLICE), BF16),
        ],
        [
            pltpu.VMEM((SHARD, 3 * WIDTH), BF16),
            pltpu.VMEM((SHARD, INNER), BF16),
            pltpu.VMEM((PIECE, WIDTH), BF16),
            pltpu.VMEM((BLOCK, WIDTH), BF16),
            pltpu.SemaphoreType.DMA((4,)),
        ],
        mebibytes=BIG,
        name="cut",
    )
    line_parts = line_turns(own_parts)
    tokens, own_parts = lax.optimization_barrier((tokens, own_parts))
    mine, other = pick(tokens, y), pick(tokens, 1 - y)
    got = [plane_swap(other, 4), plane_swap(mine, 2), plane_swap(other, 6)]
    *line_parts, got_y, got_x, got_d = lax.optimization_barrier((*line_parts, *got))
    near = jnp.concatenate([mine, got_y, got_x, got_d])
    far = plane_swap(near, 1)
    cot_mine, cot_other = pick(cotangent, y), plane_swap(pick(cotangent, 1 - y), 4)
    far, cot_other = lax.optimization_barrier((far, cot_other))
    halves = jnp.stack([part[PARTS : PARTS + COLS + 16] for part in line_parts])
    proj_near = jnp.stack([part[PARTS + COLS + 16 :] for part in line_parts])
    proj_far = plane_swap(proj_near, 1)
    others = plane_swap(halves, 4)
    turns = jnp.stack([part[:PARTS] for part in line_parts])
    from_x = plane_swap(turns, 2)
    from_y = plane_swap(turns, 4)

    full, bias, ends = call(
        vectors_kernel,
        (scal, own_parts, halves),
        (SM, VM, VM),
        [((8, WIDTH), F32), ((PLANE, SLICE), F32), ((8, PAD), F32)],
        [pltpu.VMEM((LINE, 16, SHARD), F32)],
        name="vectors",
    )

    queries, keys, values, weights, att_own, att_core, att_x, lse = call(
        attend_kernel,
        (*spots, ends, own_cols, halves, others, near, far),
        (SM, SM, SM, *[VM] * 6),
        [
            ((SLOTS, PAD), BF16),
            ((SLOTS, PAD), BF16),
            ((SLOTS, PAD), BF16),
            ((WIDTH, 3 * PAD), BF16),
            ((OWN, PAD), BF16),
            ((OWN, PAD), BF16),
            ((2, OWN, PAD), BF16),
            ((4, 8, OWN), F32),
        ],
        [
            pltpu.VMEM((WIDTH, 3 * WIDE), BF16),
            pltpu.VMEM((SLOTS, SPAN), F32),
            pltpu.VMEM((PAD, SLOTS), BF16),
            pltpu.VMEM((PAD, OWN), F32),
            pltpu.VMEM((4, OWN, PAD), BF16),
            *[pltpu.VMEM((SLOTS, PAD), BF16)] * 3,
            pltpu.VMEM((WIDTH, 3 * PAD), BF16),
            pltpu.SemaphoreType.DMA((4,)),
        ],
        mebibytes=BIG,
        own=(0, 1, 2, 3),
        name="attend",
    )
    att_x = plane_swap(att_x, 2)
    from_x, from_y, att_x = lax.optimization_barrier((from_x, from_y, att_x))
    from_d = relay(from_x, from_y, core)
    groups = list(swap_groups(att_own, att_x, att_core))
    from_d, groups[2], groups[3] = lax.optimization_barrier((from_d, groups[2], groups[3]))
    parts = [turns, from_y, from_x, from_d]
    parts += [plane_swap(part, 1) for part in parts]

    first_sum, normed_low = call(
        out_kernel,
        (scal, near, full, out_weight, *groups, *parts),
        (SM, VM, VM, VM, *[VM] * 4, *[HB] * 8),
        [
            ((OWN, WIDTH), F32),
            ((OWN, WIDTH), BF16),
        ],
        [pltpu.VMEM((LINE, PAD, WIDTH), BF16), pltpu.SemaphoreType.DMA],
        name="out",
    )
    normed_side = gather_side(normed_low)
    embedded, down_low, first_grad, grad_own, grad_core, grad_x, rest_mine, rest_other = call(
        middle_kernel,
        (*spots, first_sum, full, bias, proj_weight, out_weight, cot_mine, cot_other)
        + (proj_near, proj_far, *groups, ups, down_weight, *parts),
        (SM, SM, SM, *[VM] * 23),
        [
            ((OWN, EMBED), BF16),
            ((OWN, WIDTH), BF16),
            ((OWN, WIDTH), F32),
            *[((OWN, PAD), BF16)] * 2,
            ((2, OWN, PAD), BF16),
            *[((LINE, SPAN, WIDTH), BF16)] * 2,
        ],
        [
            pltpu.VMEM((OWN, WIDTH), BF16),
            pltpu.VMEM((OWN, WIDTH), F32),
            *[pltpu.VMEM((OWN, PAD), BF16)] * 2,
            pltpu.VMEM((2, OWN, PAD), BF16),
            *[pltpu.VMEM((LINE, SPAN, WIDTH), BF16)] * 2,
            pltpu.VMEM((PLANE, WIDTH, SLICE), BF16),
            pltpu.VMEM((PLANE, SLICE, WIDTH), BF16),
            pltpu.VMEM((LINE, PAD, WIDTH), BF16),
            pltpu.VMEM((WIDTH, EMBED), BF16),
            pltpu.VMEM((PLANE, OWN, SLICE), F32),
            pltpu.VMEM((WIDTH, EMBED), BF16),
            pltpu.VMEM((PLANE, SLICE), F32),
            pltpu.VMEM((4, PAD, WIDTH), BF16),
            pltpu.SemaphoreType.DMA((7,)),
        ],
        mebibytes=48,
        own=(1, 2, 3, 4, 5, 6, 7),
        name="middle",
    )
    *normed_side, down_low, embedded, grad_core, grad_x, rest_other = lax.optimization_barrier(
        (*normed_side, down_low, embedded, grad_core, grad_x, rest_other)
    )
    down_side = gather_side(down_low)
    embed_other = plane_swap(embedded[SPAN:], 4)
    embeddings = jnp.where(
        y == 0,
        jnp.stack([embedded[:SPAN], embed_other]),
        jnp.stack([embed_other, embedded[:SPAN]]),
    )

    grad_x = plane_swap(grad_x, 2)
    grads = swap_groups(grad_own, grad_x, grad_core)

    rest = rest_mine.astype(F32) + plane_swap(rest_other, 1).astype(F32)
    rest = rest.astype(BF16).reshape(LINE, 2, 64, WIDTH)
    rest_kept = lax.dynamic_index_in_dim(rest, x, 1, keepdims=False)
    rest_sent = lax.dynamic_index_in_dim(rest, 1 - x, 1, keepdims=False)
    rest_sent, first_grad = lax.optimization_barrier((rest_sent, first_grad))
    rest_sent = plane_swap(rest_sent, 2)

    qkv_mine, qkv_other, token_near, token_far = call(
        attend_back_kernel,
        (*spots, queries, keys, values, lse, weights, near, far, first_grad, *grads),
        (SM, SM, SM, HB, HB, HB, VM, *[HB] * 8),
        [
            *[((LINE, HALF + 16, 3 * WIDE), BF16)] * 2,
            *[((2 * OWN, WIDTH), BF16)] * 2,
        ],
        [
            *[pltpu.VMEM((LINE, HALF + 16, 3 * WIDE), BF16)] * 2,
            *[pltpu.VMEM((2 * OWN, WIDTH), BF16)] * 2,
            *[pltpu.VMEM((SLOTS, PAD), BF16)] * 3,
            pltpu.VMEM((WIDTH, 3 * PAD), BF16),
            *[pltpu.VMEM((2 * OWN, WIDTH), BF16)] * 2,
            pltpu.VMEM((OWN, WIDTH), F32),
            pltpu.VMEM((4, OWN, PAD), BF16),
            pltpu.VMEM((SLOTS, SPAN), F32),
            pltpu.VMEM((PAD, SLOTS), BF16),
            pltpu.VMEM((PAD, OWN), F32),
            pltpu.VMEM((SLOTS, 3 * PAD), BF16),
            pltpu.VMEM((SLOTS, PAD), F32),
            pltpu.VMEM((SLOTS, PAD), F32),
            pltpu.VMEM((WIDTH, 3 * PAD), BF16),
            pltpu.SemaphoreType.DMA((15,)),
        ],
        mebibytes=BIG,
        own=(0, 1, 2, 3),
        name="attend_back",
    )

    rest = (rest_kept.astype(F32) + rest_sent.astype(F32)).astype(BF16)
    rest = rest.reshape(LINE, 2, 32, WIDTH)
    rest_kept = lax.dynamic_index_in_dim(rest, y, 1, keepdims=False)
    rest_sent = lax.dynamic_index_in_dim(rest, 1 - y, 1, keepdims=False)
    rest_sent = plane_swap(rest_sent, 4)

    *down_side, token_near = lax.optimization_barrier((*down_side, token_near))

    def slice_grad(turns, ups, down, name):
        (parts,) = call(
            partial(slice_grad_kernel, name == "slice_other"),
            (scal, bias, turns, ups, down, *normed_side, *down_side),
            (SM, VM, *[HB] * 11),
            [((LINE, 2 * HALF, WIDTH), BF16)],
            [
                pltpu.VMEM((LINE - 1, PARTS, SLICE), BF16),
                pltpu.VMEM((SHARD, SLICE), BF16),
                pltpu.VMEM((PIECE, WIDTH), BF16),
                pltpu.VMEM((PLANE, OWN, WIDTH), BF16),
                pltpu.VMEM((WIDTH, SLICE), F32),
                *[pltpu.VMEM((SLICE, WIDTH), BF16)] * 2,
                *[pltpu.VMEM((SLICE, WIDTH), F32)] * 2,
                pltpu.VMEM((WIDTH, SLICE), F32),
                pltpu.SemaphoreType.DMA((11,)),
            ],
            mebibytes=BIG,
            name=name,
        )
        return parts

    slices_other = slice_grad(parts[4], ups, down_weight, "slice_other")
    *down_side, slices_other = lax.optimization_barrier((*down_side, slices_other))
    slices_mine = slice_grad(turns, ups, down_weight, "slice_mine")
    slices_other = plane_swap(slices_other, 1)
    slices_mine, rest_sent = lax.optimization_barrier((slices_mine, rest_sent))
    rest = (rest_kept.astype(F32) + rest_sent.astype(F32)).astype(BF16)
    shard_parts = []
    for turn in range(LINE):
        total = slices_mine[turn].astype(F32) + slices_other[turn].astype(F32)
        shard_parts.append(jnp.concatenate([total.astype(BF16), rest[turn]]))
    shard_part = sum_parts(turn_parts(shard_parts))

    qkv_other = plane_swap(qkv_other, 4)
    qkv_parts = [
        (qkv_mine[turn].astype(F32) + qkv_other[turn].astype(F32)).astype(BF16)
        for turn in range(LINE)
    ]
    qkv_part = sum_parts(turn_parts(qkv_parts))

    near_sum = (token_near.astype(F32) + plane_swap(token_far, 1).astype(F32)).reshape(4, SPAN, WIDTH)
    pair = near_sum[:2] + plane_swap(near_sum[2:].astype(BF16), 2).astype(F32)
    for_other = plane_swap(pair[1].astype(BF16), 4)
    for_mine, for_other = pair[0], for_other.astype(F32)
    tokens_grad = jnp.where(
        y == 0, jnp.stack([for_mine, for_other]), jnp.stack([for_other, for_mine])
    )
    up_grad, down_grad, out_grad, proj_grad, late_rows, bias_rows = call(
        rest_shard_kernel,
        (scal, *gather_plane(shard_part)),
        (SM, *[VM] * 5),
        [
            ((SHARD, INNER), F32),
            ((WIDTH, WIDTH), F32),
            ((SHARD, WIDTH), F32),
            ((SHARD, EMBED), F32),
            ((8, SHARD), F32),
            ((PLANE * PIECE,), F32),
        ],
        [pltpu.VMEM((PLANE, 2 * HALF + 32, WIDTH), BF16)],
        name="rest_shard",
    )
    bias_grad = bias_rows
    qkv_grad, vectors_grad = call(
        qkv_shard_kernel,
        (scal, late_rows, *gather_plane(qkv_part)),
        (SM, *[VM] * 6),
        [((SHARD, 3 * WIDTH), F32), ((8, SHARD), F32)],
        [pltpu.VMEM((PLANE, HALF + 16, 3 * WIDE), BF16)],
        name="qkv_shard",
    )
    return (
        embeddings,
        tokens_grad,
        qkv_grad,
        out_grad,
        up_grad,
        bias_grad,
        down_grad,
        proj_grad,
        vectors_grad,
    )


def body(*arrays):
    sequences, span, width = arrays[0].shape
    fits = (
        lax.axis_size("ctx") == PLANE
        and lax.axis_size("wa") == LINE
        and sequences == 2
        and span == SPAN
        and width == WIDTH
    )
    return (plane_body if fits else general_body)(*arrays)


def solution(mesh):
    in_specs = (
        P("wa", "ctx", None),
        P(),
        P(),
        P("wa", None),
        P("wa", None),
        P("wa", None),
        P("wa"),
        P("wa", None),
        P("wa", None),
        P(None, "wa"),
        P("wa", "ctx", None),
    )
    out_specs = (
        P("wa", "ctx", None),
        P("wa", "ctx", None),
        P("wa", None),
        P("wa", None),
        P("wa", None),
        P("wa"),
        P("wa", None),
        P("wa", None),
        P(None, "wa"),
    )
    return jax.shard_map(body, mesh=mesh, in_specs=in_specs, out_specs=out_specs, check_vma=False)
```
